128 devices in a mesh: ctx: 16 (over z_lo, x, core), ep: 8 (over z_hi, y).
Axes of the slice: x: 4, y: 4, z: 4 (z_hi: 2, z_lo: 2; z = z_hi * 2 + z_lo), core: 2. Of those that a mesh axis runs over, the one named last changes fastest.
Arguments:
- queries: bfloat16 [2048, 12288], P('ctx', 'ep'), may hold values from -8 to 8
- latents: bfloat16 [576, 2048], P(None, 'ctx'), may hold values from -8 to 8
- w_kv: bfloat16 [512, 16384], P(None, 'ep'), may hold values from -0.25 to 0.25
- w_out: bfloat16 [8192, 3584], P(('ep', 'ctx')), may hold values from -0.75 to 0.75
- resid: bfloat16 [2048, 3584], P(('ctx', 'ep')), may hold values from -3 to 3
- norm_gain: float32 [3584], replicated, may hold values from 0.1 to 1.9
- routes: int32 [2048, 8], P(('ctx', 'ep')), may hold values from 0 to 63, all different within a row; in each aligned block of 16 rows (0 to 15, 16 to 31, ...) at most 3 rows name the same one
- codes: int32 [2048, 8], P(('ctx', 'ep')), may hold values from 1 to 64
- w_gate: bfloat16 [128, 3584, 512], P(('ctx', 'ep')), may hold values from -0.09375 to 0.09375
- w_up: bfloat16 [128, 3584, 512], P(('ctx', 'ep')), may hold values from -0.09375 to 0.09375
- w_down: bfloat16 [128, 512, 3584], P(('ctx', 'ep')), may hold values from -0.1875 to 0.1875
Outputs:
- attended: bfloat16 [2048, 3584], P(('ctx', 'ep'))
- layer_out: bfloat16 [2048, 3584], P(('ctx', 'ep'))
The draws below stay inside these ranges and needn't reach their ends.
Inputs may be any that keep to these rules, and one draw needn't show every extreme that they name: `routes`: each token names 8 different experts; the 16 rows of one device name any one expert at most 3 times.
All inputs are finite; a program needn't handle non-finite values.
Results may differ from the reference program's by a relative error of at most 0.02.
Values may be sent and summed in bfloat16 or wider, within the bound.
No kernel may reach another device: no remote copies, remote signals or barrier semaphores. Data moves between devices by JAX's collectives and lax.ppermute only.
A program may use at most 128 MiB of HBM per device.

```python
import math
import jax
import jax.numpy as jnp
import numpy as np
from jax import lax

D = 3584
FF = 1024
HEADS = 64
NOPE = 128
VD = 128
KV_RANK = 512
TOP = 8
QK = 192
LAT = 576
SEQ = 2048
TOK_DEV = 16
EXPERTS = 64
CAP = 3
N_CTX = 16
N_EP = 8


def draw_queries(key, part):
    key = jax.random.fold_in(key, 11)
    values = jnp.clip(jax.random.normal(key, (SEQ, HEADS * QK), jnp.float32), -6.0, 6.0)
    return values.astype(jnp.bfloat16)


def draw_latents(key, part):
    key = jax.random.fold_in(key, 23)
    values = jnp.clip(jax.random.normal(key, (LAT, SEQ), jnp.float32), -6.0, 6.0)
    return values.astype(jnp.bfloat16)


def with_ends(values, stream_key, least, top_value):
    spot = [jax.random.randint(jax.random.fold_in(stream_key, axis), (), 0, length) for axis, length in enumerate(values.shape)]
    main_axis = values.shape.index(max(values.shape))
    beside = spot[:main_axis] + [(spot[main_axis] + 1) % values.shape[main_axis]] + spot[main_axis + 1:]
    return values.at[tuple(spot)].set(least).at[tuple(beside)].set(top_value)


def steps_of(rng, extent, cuts, smallest, largest):
    factor_of = 1.0
    for dim, shards_of in cuts:
        steps = jax.random.uniform(jax.random.fold_in(jax.random.fold_in(rng, 6), dim), (shards_of,), jnp.float32, smallest / len(cuts), largest / len(cuts))
        factor_of = factor_of * jnp.repeat(jnp.exp(steps), extent[dim] // shards_of).reshape((-1,) + (1,) * (len(extent) - 1 - dim))
    return factor_of


def routed_block(own_key, own, number, rows, amount, top, reach, lean):
    sequence = jax.random.permutation(own_key, amount)
    heavy_load, usual = load_shares(amount, rows * top, reach, lean, True), load_shares(amount, rows * top, reach, lean, False)
    places = jnp.arange(amount)

    def named(sizes, turn):
        used = int((sizes > 0).sum())
        fixed = max(1, used // 4)
        shifted = fixed + (places - fixed + turn * (used - fixed)) % max(1, amount - fixed)
        return jnp.zeros((amount,), jnp.int32).at[sequence[jnp.where(places < fixed, places, shifted)]].set(jnp.asarray(sizes, jnp.int32))

    sizes = jnp.where(number % 4 == 0, named(heavy_load, number // 4), named(usual, number - number // 4 - 1))
    mixed = jax.random.permutation(jax.random.fold_in(own, 3), amount)
    source_of, sink = mixed[0:amount // 2 * 2:2], mixed[1:amount // 2 * 2:2]
    slack = jnp.minimum(sizes[source_of] - 1, reach - sizes[sink]) // 2
    slack = jnp.where((source_of == sequence[0]) | (sink == sequence[0]) | (sizes[sink] == 0), 0, jnp.maximum(slack, 0))
    shifted = jax.random.randint(jax.random.fold_in(own, 4), (amount // 2,), 0, 1 << 20) % (slack + 1)
    sizes = sizes.at[source_of].add(-shifted).at[sink].add(shifted)
    members = jnp.searchsorted(jnp.cumsum(sizes), jnp.arange(rows * top), side="right").astype(jnp.int32)
    table = members.reshape(top, rows).T
    table = table[jax.random.permutation(jax.random.fold_in(own, 1), rows)]
    turn = jax.random.randint(jax.random.fold_in(own, 2), (rows, 1), 0, top)
    return jnp.take_along_axis(table, (jnp.arange(top)[None, :] + turn) % top, axis=1)


def load_shares(amount, total, most, lean, full):
    loads = [(1 << 20) // math.isqrt(rank ** lean) + 1 for rank in range(1, amount + 1)]
    largest = most if full else min(most, max(-(-total // amount), total * loads[0] // sum(loads)))
    least = 1 if total - largest >= amount - 1 else 0
    holding, surplus = [largest] + [least] * (amount - 1), total - largest - least * (amount - 1)
    while surplus > 0:
        free = [i for i in range(1, amount) if holding[i] < largest] or [i for i in range(1, amount) if holding[i] < most]
        whole, remaining = sum([loads[i] for i in free]), surplus
        for i in free:
            addition = min(most - holding[i], max(1, remaining * loads[i] // whole), surplus)
            holding[i] = holding[i] + addition
            surplus = surplus - addition
    return np.array(holding)


def noise(stream_key, dims, spread, most, pieces=(), kind=jnp.bfloat16):
    array = spread * jax.random.normal(stream_key, dims, jnp.float32)
    if pieces:
        array = array * steps_of(stream_key, dims, pieces, -0.22, 0.18)
    return jnp.clip(array, -most, most).astype(kind)


def setup_inputs(seed: int = 0) -> dict:
    arg_keys = jax.random.split(jax.random.key(seed), 12)
    queries = draw_queries(jax.random.fold_in(arg_keys[11], 71), 0)
    latents = draw_latents(jax.random.fold_in(arg_keys[11], 71), 0)
    w_kv = noise(arg_keys[2], (KV_RANK, HEADS * (NOPE + VD)), KV_RANK ** -0.5, 0.25, ((1, 8),))
    w_out = noise(arg_keys[3], (HEADS * VD, D), HEADS ** -0.5, 0.75, ((0, 128),))
    resid = noise(arg_keys[4], (SEQ, D), 0.5, 3.0, ((0, 128),))
    norm_gain = jnp.clip(1.0 + 0.18 * jax.random.normal(arg_keys[5], (D,), jnp.float32), 0.1, 1.9)
    routes_keys = jax.random.split(jax.random.fold_in(arg_keys[6], 1), SEQ // TOK_DEV)
    routes_turns = jax.random.permutation(jax.random.fold_in(arg_keys[6], 3), SEQ // TOK_DEV)
    routes = jax.vmap(lambda own, number: routed_block(jax.random.fold_in(arg_keys[6], 2), own, number, TOK_DEV, EXPERTS, TOP, CAP, 2))(routes_keys, routes_turns).reshape((SEQ, TOP))
    codes = with_ends(jax.random.randint(arg_keys[7], (SEQ, TOP), 1, 65), jax.random.fold_in(arg_keys[7], 1), 1, 64).astype(jnp.int32)
    w_gate = noise(arg_keys[8], (2 * EXPERTS, D, FF // 2), D ** -0.5, 0.09375, ((0, 128),))
    w_up = noise(arg_keys[9], (2 * EXPERTS, D, FF // 2), D ** -0.5, 0.09375, ((0, 128),))
    w_down = noise(arg_keys[10], (2 * EXPERTS, FF // 2, D), FF ** -0.5, 0.1875, ((0, 128),))
    return {"queries": queries, "latents": latents, "w_kv": w_kv, "w_out": w_out, "resid": resid, "norm_gain": norm_gain, "routes": routes, "codes": codes, "w_gate": w_gate, "w_up": w_up, "w_down": w_down}


def reference(queries, latents, w_kv, w_out, resid, norm_gain, routes, codes, w_gate, w_up, w_down):
    latent_rows = latents[:KV_RANK].T
    rotary_keys = latents[KV_RANK:].T
    positions = jnp.arange(SEQ, dtype=jnp.int32)
    allowed = positions[None, :] <= positions[:, None]
    scale = QK ** (-0.5)

    def one_head(head):
        columns = lax.dynamic_slice_in_dim(w_kv, head * (NOPE + VD), NOPE + VD, 1)
        expanded = jnp.dot(latent_rows, columns, preferred_element_type=jnp.float32).astype(jnp.bfloat16)
        keys = jnp.concatenate([expanded[:, :NOPE], rotary_keys], axis=1)
        values = expanded[:, NOPE:]
        head_queries = lax.dynamic_slice_in_dim(queries, head * QK, QK, 1)
        scores = jnp.dot(head_queries, keys.T, preferred_element_type=jnp.float32) * scale
        masked = jnp.where(allowed, scores, jnp.float32(-1e+30))
        peak = lax.optimization_barrier(jnp.max(masked, axis=1))
        probs = jnp.where(allowed, jnp.exp(scores - peak[:, None]), jnp.float32(0.0))
        total = lax.optimization_barrier(jnp.sum(probs, axis=1))
        weighted = jnp.dot(probs.astype(jnp.bfloat16), values, preferred_element_type=jnp.float32)
        return (weighted / total[:, None]).astype(jnp.bfloat16)
    heads_out = lax.map(one_head, jnp.arange(HEADS, dtype=jnp.int32))
    attention = heads_out.transpose(1, 0, 2).reshape(SEQ, HEADS * VD)
    attn = jnp.dot(attention, w_out, preferred_element_type=jnp.float32)
    attended = (resid.astype(jnp.float32) + attn).astype(jnp.bfloat16)
    wide = attended.astype(jnp.float32)
    meansq = lax.optimization_barrier(jnp.mean(wide * wide, axis=1, keepdims=True))
    normed = (wide * lax.rsqrt(meansq + 1e-06) * norm_gain[None, :]).astype(jnp.bfloat16)
    code_float = codes.astype(jnp.float32)
    mix = code_float / lax.optimization_barrier(jnp.sum(code_float, axis=1, keepdims=True))
    flat_routes = routes.reshape(-1).astype(jnp.int32)
    order = jnp.argsort(flat_routes, stable=True).astype(jnp.int32)
    counts = lax.optimization_barrier(jnp.sum((flat_routes[:, None] == jnp.arange(EXPERTS, dtype=jnp.int32)[None, :]).astype(jnp.int32), axis=0)).astype(jnp.int32)
    starts = (jnp.cumsum(counts) - counts).astype(jnp.int32)
    most = CAP * N_CTX * N_EP
    padded = jnp.concatenate([order, jnp.zeros((most,), jnp.int32)])
    mix_flat = mix.reshape(-1)

    def one_expert(accum, expert):
        index = lax.dynamic_slice_in_dim(padded, starts[expert], most)
        live = jnp.arange(most, dtype=jnp.int32) < counts[expert]
        token = (index // TOP).astype(jnp.int32)
        rows = normed[token]
        produced = jnp.zeros((most, D), jnp.float32)
        for half in range(2):
            holder = 2 * expert + half
            gate = jnp.dot(rows, w_gate[holder], preferred_element_type=jnp.float32)
            upward = jnp.dot(rows, w_up[holder], preferred_element_type=jnp.float32)
            hidden = (jax.nn.silu(gate) * upward).astype(jnp.bfloat16)
            partial_out = jnp.dot(hidden, w_down[holder], preferred_element_type=jnp.float32).astype(jnp.bfloat16)
            produced = produced + partial_out.astype(jnp.float32)
        produced = produced.astype(jnp.bfloat16)
        weight = jnp.where(live, mix_flat[index], jnp.float32(0.0))
        accum = accum.at[token].add(weight[:, None] * produced.astype(jnp.float32))
        return (accum, None)
    moe, _ = lax.scan(one_expert, jnp.zeros((SEQ, D), jnp.float32), jnp.arange(EXPERTS, dtype=jnp.int32))
    layer_out = (attended.astype(jnp.float32) + moe).astype(jnp.bfloat16)
    return (attended, layer_out)
```

```python
import jax
import jax.numpy as jnp
from jax import lax
from jax.sharding import Mesh, PartitionSpec as P

NOPE = 128
VD = 128
KV_RANK = 512
TOP = 8
QK = 192
CAP = 3

CTX = ("z_lo", "x", "core")
CTX_CHIPS = ("z_lo", "x")
EP = ("z_hi", "y")
CHIPS = ("z_lo", "x", "z_hi", "y")
SIZES = (2, 4, 2, 2, 4)
NAMES = ("z_lo", "x", "core", "z_hi", "y")
SWAP = ((0, 1), (1, 0))
BF = jnp.bfloat16
F32 = jnp.float32


def both_cores(mine):
    other = lax.ppermute(mine, "core", SWAP)
    first = lax.axis_index("core") == 0
    return jnp.stack([jnp.where(first, mine, other), jnp.where(first, other, mine)])


def attention(queries, lat, w_kv):
    rows = queries.shape[0]
    heads = queries.shape[1] // QK
    q = queries.reshape(rows, heads, QK)
    w = w_kv.reshape(KV_RANK, heads, NOPE + VD)
    q_lat = jnp.einsum("qhd,rhd->hqr", q[:, :, :NOPE], w[:, :, :NOPE], preferred_element_type=F32).astype(BF)
    q_all = jnp.concatenate([q_lat, q[:, :, NOPE:].transpose(1, 0, 2)], axis=2)
    scores = jnp.einsum("hqr,rn->hqn", q_all, lat, preferred_element_type=F32) * QK ** (-0.5)
    ctx = lax.axis_index(CTX)
    query_pos = ctx * rows + jnp.arange(rows, dtype=jnp.int32)
    key_pos = jnp.arange(lat.shape[1], dtype=jnp.int32)
    allowed = key_pos[None, None, :] <= query_pos[None, :, None]
    peak = jnp.max(jnp.where(allowed, scores, F32(-1e30)), axis=2, keepdims=True)
    probs = jnp.where(allowed, jnp.exp(scores - peak), F32(0.0))
    total = jnp.sum(probs, axis=2, keepdims=True)
    mixed = jnp.einsum("hqn,rn->hqr", probs.astype(BF), lat[:KV_RANK], preferred_element_type=F32)
    mixed = (mixed / total).astype(BF)
    out = jnp.einsum("hqr,rhd->qhd", mixed, w[:, :, NOPE:], preferred_element_type=F32).astype(BF)
    return out.reshape(rows, heads * VD)


def local(queries, latents, w_kv, w_out, resid, norm_gain, routes, codes, w_gate, w_up, w_down):
    tok, width = resid.shape
    chips = 64
    w_full = lax.all_gather(w_out, CTX, axis=0, tiled=True)
    parts = 16
    lat = lax.all_to_all(
        jnp.broadcast_to(latents[None], (parts,) + latents.shape), CTX, split_axis=0, concat_axis=0, tiled=True
    )
    lat = lat.transpose(1, 0, 2).reshape(latents.shape[0], -1)
    heads_out = attention(queries, lat, w_kv)
    attn = jnp.dot(heads_out, w_full, preferred_element_type=F32).astype(BF)
    attn = lax.all_to_all(attn.reshape(8, tok, width), EP, split_axis=0, concat_axis=0, tiled=True)
    attended = (resid.astype(F32) + jnp.sum(attn.astype(F32), axis=0)).astype(BF)
    wide = attended.astype(F32)
    meansq = jnp.mean(wide * wide, axis=1, keepdims=True)
    normed = (wide * lax.rsqrt(meansq + 1e-06) * norm_gain[None, :]).astype(BF)
    normed2 = both_cores(normed).reshape(2 * tok, width)

    core = lax.axis_index("core")
    code_float = codes.astype(F32)
    mix = code_float / jnp.sum(code_float, axis=1, keepdims=True)
    routes2 = both_cores(routes)
    mix2 = both_cores(mix)
    chosen = routes2[:, :, :, None] == jnp.arange(64, dtype=jnp.int32)
    weight = jnp.sum(jnp.where(chosen, mix2[..., None], F32(0.0)), axis=2)
    has = jnp.any(chosen, axis=2)

    def of_core(a):
        a = a.reshape(2, tok, 8, 2, 4)
        return jnp.where(core == 0, a[:, :, :, 0], a[:, :, :, 1]).reshape(2, tok, 32)

    weight, has = of_core(weight), of_core(has)
    count = has.astype(jnp.int32)
    slot = jnp.cumsum(count, axis=1) - count
    place = has[:, :, :, None] & (slot[:, :, :, None] == jnp.arange(CAP, dtype=jnp.int32))
    place = place.transpose(2, 3, 0, 1)[:, :, :, None, :]
    same = jnp.arange(2)[:, None, None] == jnp.arange(2)[None, :, None]
    place = (place & same).reshape(32, CAP, 2, 2 * tok)
    place = jnp.broadcast_to(place[:, None], (32, 2, CAP, 2, 2 * tok)).reshape(chips * CAP * 2, 2 * tok)
    gains = weight.transpose(2, 0, 1).reshape(32, 2 * tok)
    gains = jnp.broadcast_to(gains[:, None], (32, 2 * CAP * 2, 2 * tok)).reshape(chips * CAP * 2, 2 * tok)
    combine = jnp.where(place, gains, F32(0.0))

    outgoing = jnp.dot(place.astype(BF), normed2, preferred_element_type=F32).astype(BF)
    arrived = lax.all_to_all(
        outgoing.reshape(chips, CAP, 2, width), CHIPS, split_axis=0, concat_axis=0, tiled=True
    ).reshape(chips * CAP * 2, width)
    gate = jnp.dot(arrived, w_gate[0], preferred_element_type=F32)
    upward = jnp.dot(arrived, w_up[0], preferred_element_type=F32)
    hidden = (jax.nn.silu(gate) * upward).astype(BF)
    produced = jnp.dot(hidden, w_down[0], preferred_element_type=F32).astype(BF)
    returned = lax.all_to_all(
        produced.reshape(chips, CAP, 2, width), CHIPS, split_axis=0, concat_axis=0, tiled=True
    ).reshape(chips * CAP * 2, width)

    high = lax.reduce_precision(combine, 8, 7)
    factors = jnp.concatenate([high, combine - high], axis=1).astype(BF)
    moe = lax.dot_general(factors, returned, (((0,), (0,)), ((), ())), preferred_element_type=F32)
    moe = moe[: 2 * tok] + moe[2 * tok :]
    moe = moe.reshape(2, tok, width)
    own = jnp.where(core == 0, moe[0], moe[1])
    far = lax.ppermute(jnp.where(core == 0, moe[1], moe[0]), "core", SWAP)
    layer_out = (wide + own + far).astype(BF)
    return (attended, layer_out)


def solution(mesh):
    fine = Mesh(mesh.devices.reshape(SIZES), NAMES)
    rows = P(CTX + EP, None)
    heads = P(CTX + EP, None, None)
    placed = (
        P(CTX, EP),
        P(None, CTX),
        P(None, EP),
        P(EP + CTX, None),
        rows,
        P(),
        rows,
        rows,
        heads,
        heads,
        heads,
    )
    return jax.shard_map(local, mesh=fine, in_specs=placed, out_specs=(rows, rows), check_vma=False)
```

```python
import functools

import jax
import jax.numpy as jnp
from jax import lax
from jax.experimental import pallas as pl
from jax.experimental.pallas import tpu as pltpu
from jax.sharding import Mesh, PartitionSpec as P

NOPE = 128
VD = 128
KV_RANK = 512
TOP = 8
QK = 192
CAP = 3

CTX = ("z_lo", "x", "core")
CTX_CHIPS = ("z_lo", "x")
EP = ("z_hi", "y")
CHIPS = ("z_lo", "x", "z_hi", "y")
SIZES = (2, 4, 2, 2, 4)
NAMES = ("z_lo", "x", "core", "z_hi", "y")
SWAP = ((0, 1), (1, 0))
BF = jnp.bfloat16
F32 = jnp.float32
LOG2E = 1.4426950408889634


def attend_kernel(ids_ref, q_ref, near_ref, far_ref, w_ref, out_ref, lat_ref, s_ref, p_ref, *, rows, cuts):
    heads = w_ref.shape[1] // (NOPE + VD)
    m = q_ref.shape[0]
    pairs = near_ref.shape[0]
    keys = 2 * rows * pairs

    @pl.when(pl.program_id(0) == 0)
    def _():
        for i in range(pairs):
            lat_ref[:, 2 * i * rows : (2 * i + 1) * rows] = near_ref[i]
            lat_ref[:, (2 * i + 1) * rows : (2 * i + 2) * rows] = far_ref[i]

    ctx, core = ids_ref[0], ids_ref[1]
    span = keys // cuts
    lane = lax.broadcasted_iota(jnp.int32, (m, rows), 1)
    query = lax.broadcasted_iota(jnp.int32, (m, rows), 0) % rows
    ahead = lane - query
    peak = jnp.full((m, rows), -1e30, F32)
    for j in range(cuts):
        s = jnp.dot(q_ref[...], lat_ref[:, j * span : (j + 1) * span], preferred_element_type=F32)
        for b in range(span // rows):
            block = j * (span // rows) + b
            pos = 2 * (block // 2) + (core if block % 2 == 0 else 1 - core)
            part = s[:, b * rows : (b + 1) * rows]
            part = jnp.where(ahead <= (ctx - pos) * rows, part, F32(-1e30))
            peak = jnp.maximum(peak, part)
            s_ref[:, block * rows : (block + 1) * rows] = part
    top = jnp.max(peak, axis=1, keepdims=True)
    total = jnp.zeros((m, rows), F32)
    for j in range(keys // rows):
        p = jnp.exp2((s_ref[:, j * rows : (j + 1) * rows] - top) * (QK ** (-0.5) * LOG2E))
        total = total + p
        p_ref[:, j * rows : (j + 1) * rows] = p.astype(BF)
    mixed = lax.dot_general(p_ref[...], lat_ref[:KV_RANK], (((1,), (1,)), ((), ())), preferred_element_type=F32)
    mixed = (mixed / jnp.sum(total, axis=1, keepdims=True)).astype(BF)
    for h in range(heads):
        values = w_ref[:, h * (NOPE + VD) + NOPE : (h + 1) * (NOPE + VD)]
        o = jnp.dot(mixed[h * rows : (h + 1) * rows], values, preferred_element_type=F32)
        out_ref[:, h * VD : (h + 1) * VD] = o.astype(BF)


def attend(ids, q, near, far, w_kv, group, cuts):
    pairs, depth, rows = near.shape
    heads = w_kv.shape[1] // (NOPE + VD)
    keys = 2 * rows * pairs
    m = group * rows
    return pl.pallas_call(
        functools.partial(attend_kernel, rows=rows, cuts=cuts),
        grid=(heads // group,),
        in_specs=[
            pl.BlockSpec(memory_space=pltpu.SMEM),
            pl.BlockSpec((m, depth), lambda g: (g, 0)),
            pl.BlockSpec(near.shape, lambda g: (0, 0, 0)),
            pl.BlockSpec(far.shape, lambda g: (0, 0, 0)),
            pl.BlockSpec((KV_RANK, group * (NOPE + VD)), lambda g: (0, g)),
        ],
        out_specs=pl.BlockSpec((rows, group * VD), lambda g: (0, g)),
        out_shape=jax.ShapeDtypeStruct((rows, heads * VD), BF),
        scratch_shapes=[pltpu.VMEM((depth, keys), BF), pltpu.VMEM((m, keys), F32), pltpu.VMEM((m, keys), BF)],
        compiler_params=pltpu.CompilerParams(vmem_limit_bytes=40 * 2**20),
        cost_estimate=pl.CostEstimate(
            flops=2 * heads * rows * keys * (depth + KV_RANK),
            bytes_accessed=8_000_000,
            transcendentals=heads * rows * keys,
        ),
    )(ids, q, near, far, w_kv)


def expert_kernel(x_ref, g_ref, u_ref, d_ref, out_ref, rows_ref, hid_ref, *, first):
    step = pl.program_id(0)

    @pl.when(step == 0)
    def _():
        rows_ref[...] = x_ref[...].reshape(rows_ref.shape)

    @pl.when(step < first)
    def _():
        rows = rows_ref[...]
        gate = jnp.dot(rows, g_ref[...], preferred_element_type=F32)
        upward = jnp.dot(rows, u_ref[...], preferred_element_type=F32)
        hid = (gate / (1.0 + jnp.exp(-gate)) * upward).astype(BF)
        n = g_ref.shape[1]
        for f in range(first):

            @pl.when(step == f)
            def _(f=f):
                hid_ref[:, f * n : (f + 1) * n] = hid

    @pl.when(step >= first)
    def _():
        y = jnp.dot(hid_ref[...], d_ref[...], preferred_element_type=F32).astype(BF)
        out_ref[...] = y.reshape(out_ref.shape)


def expert(x, w_gate, w_up, w_down, first, last):
    units, pair, width = x.shape
    m = units * pair
    hidden = w_gate.shape[1]
    n1, n2 = hidden // first, width // last
    return pl.pallas_call(
        functools.partial(expert_kernel, first=first),
        grid=(first + last,),
        in_specs=[
            pl.BlockSpec(x.shape, lambda i: (0, 0, 0)),
            pl.BlockSpec((width, n1), lambda i: (0, jnp.minimum(i, first - 1))),
            pl.BlockSpec((width, n1), lambda i: (0, jnp.minimum(i, first - 1))),
            pl.BlockSpec((hidden, n2), lambda i: (0, jnp.maximum(i - first, 0))),
        ],
        out_specs=pl.BlockSpec((units, pair, n2), lambda i: (0, 0, jnp.maximum(i - first, 0))),
        out_shape=jax.ShapeDtypeStruct(x.shape, BF),
        scratch_shapes=[pltpu.VMEM((m, width), BF), pltpu.VMEM((m, hidden), BF)],
        compiler_params=pltpu.CompilerParams(vmem_limit_bytes=40 * 2**20),
        cost_estimate=pl.CostEstimate(
            flops=6 * m * width * hidden, bytes_accessed=17_000_000, transcendentals=m * hidden
        ),
    )(x, w_gate, w_up, w_down)


def dispatch_kernel(place_ref, x_ref, out_ref):
    y = jnp.dot(place_ref[...], x_ref[...], preferred_element_type=F32).astype(BF)
    out_ref[...] = y.reshape(out_ref.shape)


def dispatch(place, x, cuts):
    m = place.shape[0]
    tokens, width = x.shape
    n = width // cuts
    return pl.pallas_call(
        dispatch_kernel,
        grid=(cuts,),
        in_specs=[pl.BlockSpec(place.shape, lambda i: (0, 0)), pl.BlockSpec((tokens, n), lambda i: (0, i))],
        out_specs=pl.BlockSpec((m // 2, 2, n), lambda i: (0, 0, i)),
        out_shape=jax.ShapeDtypeStruct((m // 2, 2, width), BF),
        compiler_params=pltpu.CompilerParams(vmem_limit_bytes=32 * 2**20),
        cost_estimate=pl.CostEstimate(
            flops=2 * m * tokens * width, bytes_accessed=2 * m * width + 2 * tokens * width, transcendentals=0
        ),
    )(place, x)


def combine_kernel(factors_ref, x_ref, own_ref, far_ref):
    tok = own_ref.shape[0]
    rows = x_ref[...].reshape(factors_ref.shape[1], x_ref.shape[2])
    y = jnp.dot(factors_ref[...], rows, preferred_element_type=F32)
    y = y[: 2 * tok] + y[2 * tok :]
    own_ref[...] = y[:tok]
    far_ref[...] = y[tok:]


def combine(factors, x, cuts):
    width = x.shape[2]
    n = width // cuts
    tok = factors.shape[0] // 4
    part = pl.BlockSpec((tok, n), lambda i: (0, i))
    return pl.pallas_call(
        combine_kernel,
        grid=(cuts,),
        in_specs=[
            pl.BlockSpec(factors.shape, lambda i: (0, 0)),
            pl.BlockSpec((x.shape[0], 2, n), lambda i: (0, 0, i)),
        ],
        out_specs=(part, part),
        out_shape=(jax.ShapeDtypeStruct((tok, width), F32),) * 2,
        compiler_params=pltpu.CompilerParams(vmem_limit_bytes=32 * 2**20),
        cost_estimate=pl.CostEstimate(
            flops=2 * factors.size * width, bytes_accessed=4 * x.shape[0] * width, transcendentals=0
        ),
    )(factors, x)


def both_cores(mine):
    other = lax.ppermute(mine, "core", SWAP)
    first = lax.axis_index("core") == 0
    return jnp.stack([jnp.where(first, mine, other), jnp.where(first, other, mine)])


def latent_queries(queries, w_kv):
    rows = queries.shape[0]
    heads = queries.shape[1] // QK
    q = queries.reshape(rows, heads, QK)
    keys = w_kv.reshape(KV_RANK, heads, NOPE + VD)[:, :, :NOPE]
    q_lat = jnp.einsum("qhd,rhd->hqr", q[:, :, :NOPE], keys, preferred_element_type=F32).astype(BF)
    q_all = jnp.concatenate([q_lat, q[:, :, NOPE:].transpose(1, 0, 2)], axis=2)
    return q_all.reshape(heads * rows, -1)


def routing(routes, codes):
    tok = routes.shape[0]
    core = lax.axis_index("core")
    code_float = codes.astype(F32)
    mix = code_float / jnp.sum(code_float, axis=1, keepdims=True)
    routes2, mix2 = both_cores(routes), both_cores(mix)
    chosen = routes2[:, :, :, None] == jnp.arange(64, dtype=jnp.int32)
    weight = jnp.sum(jnp.where(chosen, mix2[..., None], F32(0.0)), axis=2)
    has = jnp.any(chosen, axis=2)

    def of_core(a):
        a = a.reshape(2, tok, 8, 2, 4)
        return jnp.where(core == 0, a[:, :, :, 0], a[:, :, :, 1]).reshape(2, tok, 32)

    weight, has = of_core(weight), of_core(has)
    count = has.astype(jnp.int32)
    slot = jnp.cumsum(count, axis=1) - count
    place = has[:, :, :, None] & (slot[:, :, :, None] == jnp.arange(CAP, dtype=jnp.int32))
    place = place.transpose(2, 3, 0, 1)[:, :, :, None, :]
    same = jnp.arange(2)[:, None, None] == jnp.arange(2)[None, :, None]
    place = (place & same).reshape(32, CAP, 2, 2 * tok)
    place = jnp.broadcast_to(place[:, None], (32, 2, CAP, 2, 2 * tok)).reshape(64 * CAP * 2, 2 * tok)
    gains = weight.transpose(2, 0, 1).reshape(32, 2 * tok)
    gains = jnp.broadcast_to(gains[:, None], (32, 2 * CAP * 2, 2 * tok)).reshape(64 * CAP * 2, 2 * tok)
    factors = jnp.where(place, gains, F32(0.0)).T.reshape(2, tok, -1)
    factors = jnp.where(core == 0, factors, factors[::-1]).reshape(2 * tok, -1)
    high = lax.reduce_precision(factors, 8, 7)
    factors = jnp.concatenate([high, factors - high], axis=0).astype(BF)
    return place.astype(BF), factors


def local(queries, latents, w_kv, w_out, resid, norm_gain, routes, codes, w_gate, w_up, w_down):
    tok, width = resid.shape
    chips = 64
    w_full = lax.all_gather(w_out, CTX, axis=0, tiled=True)
    near = lax.all_to_all(
        jnp.broadcast_to(latents[None], (8,) + latents.shape), CTX_CHIPS, split_axis=0, concat_axis=0, tiled=True
    )
    far = lax.ppermute(near, "core", SWAP)
    ids = jnp.stack([lax.axis_index(CTX), lax.axis_index("core")]).astype(jnp.int32)
    heads_out = attend(ids, latent_queries(queries, w_kv), near, far, w_kv, 4, 4)
    attn = jnp.dot(heads_out, w_full, preferred_element_type=F32).astype(BF)
    attn = lax.all_to_all(attn.reshape(8, tok, width), EP, split_axis=0, concat_axis=0, tiled=True)
    attended = (resid.astype(F32) + jnp.sum(attn.astype(F32), axis=0)).astype(BF)
    wide = attended.astype(F32)
    meansq = jnp.mean(wide * wide, axis=1, keepdims=True)
    normed = (wide * lax.rsqrt(meansq + 1e-06) * norm_gain[None, :]).astype(BF)
    normed2 = both_cores(normed).reshape(2 * tok, width)

    place, factors = routing(routes, codes)
    outgoing = dispatch(place, normed2, 7)
    arrived = lax.all_to_all(
        outgoing.reshape(chips, CAP, 2, width), CHIPS, split_axis=0, concat_axis=0, tiled=True
    ).reshape(chips * CAP, 2, width)
    produced = expert(arrived, w_gate[0], w_up[0], w_down[0], 2, 7)
    returned = lax.all_to_all(
        produced.reshape(chips, CAP, 2, width), CHIPS, split_axis=0, concat_axis=0, tiled=True
    ).reshape(chips * CAP, 2, width)
    own, theirs = combine(factors, returned, 7)
    layer_out = (wide + own + lax.ppermute(theirs, "core", SWAP)).astype(BF)
    return (attended, layer_out)


def solution(mesh):
    fine = Mesh(mesh.devices.reshape(SIZES), NAMES)
    rows = P(CTX + EP, None)
    heads = P(CTX + EP, None, None)
    placed = (
        P(CTX, EP),
        P(None, CTX),
        P(None, EP),
        P(EP + CTX, None),
        rows,
        P(),
        rows,
        rows,
        heads,
        heads,
        heads,
    )
    return jax.shard_map(local, mesh=fine, in_specs=placed, out_specs=(rows, rows), check_vma=False)
```

```python
import functools

import jax
import jax.numpy as jnp
from jax import lax
from jax.experimental import pallas as pl
from jax.experimental.pallas import tpu as pltpu
from jax.sharding import Mesh, PartitionSpec as P

NOPE = 128
VD = 128
KV_RANK = 512
TOP = 8
QK = 192
CAP = 3

CTX = ("z_lo", "x", "core")
CTX_CHIPS = ("z_lo", "x")
EP = ("z_hi", "y")
CHIPS = ("z_lo", "x", "z_hi", "y")
SIZES = (2, 4, 2, 2, 4)
NAMES = ("z_lo", "x", "core", "z_hi", "y")
SWAP = ((0, 1), (1, 0))
BF = jnp.bfloat16
F32 = jnp.float32
LOG2E = 1.4426950408889634


def attend_kernel(ids_ref, q_ref, near_ref, far_ref, w_ref, out_ref, lat_ref, s_ref, p_ref, *, rows, cuts):
    heads = w_ref.shape[1] // (NOPE + VD)
    m = q_ref.shape[0]
    pairs = near_ref.shape[0]
    keys = 2 * rows * pairs

    @pl.when(pl.program_id(0) == 0)
    def _():
        for i in range(pairs):
            lat_ref[:, 2 * i * rows : (2 * i + 1) * rows] = near_ref[i]
            lat_ref[:, (2 * i + 1) * rows : (2 * i + 2) * rows] = far_ref[i]

    ctx, core = ids_ref[0], ids_ref[1]
    span = keys // cuts
    lane = lax.broadcasted_iota(jnp.int32, (m, rows), 1)
    query = lax.broadcasted_iota(jnp.int32, (m, rows), 0) % rows
    ahead = lane - query
    peak = jnp.full((m, rows), -1e30, F32)
    for j in range(cuts):
        s = jnp.dot(q_ref[...], lat_ref[:, j * span : (j + 1) * span], preferred_element_type=F32)
        for b in range(span // rows):
            block = j * (span // rows) + b
            pos = 2 * (block // 2) + (core if block % 2 == 0 else 1 - core)
            part = s[:, b * rows : (b + 1) * rows]
            part = jnp.where(ahead <= (ctx - pos) * rows, part, F32(-1e30))
            peak = jnp.maximum(peak, part)
            s_ref[:, block * rows : (block + 1) * rows] = part
    top = jnp.max(peak, axis=1, keepdims=True)
    total = jnp.zeros((m, rows), F32)
    for j in range(keys // rows):
        p = jnp.exp2((s_ref[:, j * rows : (j + 1) * rows] - top) * (QK ** (-0.5) * LOG2E))
        total = total + p
        p_ref[:, j * rows : (j + 1) * rows] = p.astype(BF)
    mixed = lax.dot_general(p_ref[...], lat_ref[:KV_RANK], (((1,), (1,)), ((), ())), preferred_element_type=F32)
    mixed = (mixed / jnp.sum(total, axis=1, keepdims=True)).astype(BF)
    for h in range(heads):
        values = w_ref[:, h * (NOPE + VD) + NOPE : (h + 1) * (NOPE + VD)]
        o = jnp.dot(mixed[h * rows : (h + 1) * rows], values, preferred_element_type=F32)
        out_ref[:, h * VD : (h + 1) * VD] = o.astype(BF)


def attend(ids, q, near, far, w_kv, group, cuts):
    pairs, depth, rows = near.shape
    heads = w_kv.shape[1] // (NOPE + VD)
    keys = 2 * rows * pairs
    m = group * rows
    return pl.pallas_call(
        functools.partial(attend_kernel, rows=rows, cuts=cuts),
        grid=(heads // group,),
        in_specs=[
            pl.BlockSpec(memory_space=pltpu.SMEM),
            pl.BlockSpec((m, depth), lambda g: (g, 0)),
            pl.BlockSpec(near.shape, lambda g: (0, 0, 0)),
            pl.BlockSpec(far.shape, lambda g: (0, 0, 0)),
            pl.BlockSpec((KV_RANK, group * (NOPE + VD)), lambda g: (0, g)),
        ],
        out_specs=pl.BlockSpec((rows, group * VD), lambda g: (0, g)),
        out_shape=jax.ShapeDtypeStruct((rows, heads * VD), BF),
        scratch_shapes=[pltpu.VMEM((depth, keys), BF), pltpu.VMEM((m, keys), F32), pltpu.VMEM((m, keys), BF)],
        compiler_params=pltpu.CompilerParams(vmem_limit_bytes=40 * 2**20),
        cost_estimate=pl.CostEstimate(
            flops=2 * heads * rows * keys * (depth + KV_RANK),
            bytes_accessed=8_000_000,
            transcendentals=heads * rows * keys,
        ),
    )(ids, q, near, far, w_kv)


def expert_kernel(x_ref, g_ref, u_ref, d_ref, out_ref, rows_ref, hid_ref, *, first):
    step = pl.program_id(0)

    @pl.when(step == 0)
    def _():
        rows_ref[...] = x_ref[...].reshape(rows_ref.shape)

    @pl.when(step < first)
    def _():
        rows = rows_ref[...]
        gate = jnp.dot(rows, g_ref[...], preferred_element_type=F32)
        upward = jnp.dot(rows, u_ref[...], preferred_element_type=F32)
        hid = (gate / (1.0 + jnp.exp(-gate)) * upward).astype(BF)
        n = g_ref.shape[1]
        for f in range(first):

            @pl.when(step == f)
            def _(f=f):
                hid_ref[:, f * n : (f + 1) * n] = hid

    @pl.when(step >= first)
    def _():
        y = jnp.dot(hid_ref[...], d_ref[...], preferred_element_type=F32).astype(BF)
        out_ref[...] = y.reshape(out_ref.shape)


def expert(x, w_gate, w_up, w_down, first, last):
    units, pair, width = x.shape
    m = units * pair
    hidden = w_gate.shape[1]
    n1, n2 = hidden // first, width // last
    return pl.pallas_call(
        functools.partial(expert_kernel, first=first),
        grid=(first + last,),
        in_specs=[
            pl.BlockSpec(x.shape, lambda i: (0, 0, 0)),
            pl.BlockSpec((width, n1), lambda i: (0, jnp.minimum(i, first - 1))),
            pl.BlockSpec((width, n1), lambda i: (0, jnp.minimum(i, first - 1))),
            pl.BlockSpec((hidden, n2), lambda i: (0, jnp.maximum(i - first, 0))),
        ],
        out_specs=pl.BlockSpec((units, pair, n2), lambda i: (0, 0, jnp.maximum(i - first, 0))),
        out_shape=jax.ShapeDtypeStruct(x.shape, BF),
        scratch_shapes=[pltpu.VMEM((m, width), BF), pltpu.VMEM((m, hidden), BF)],
        compiler_params=pltpu.CompilerParams(vmem_limit_bytes=40 * 2**20),
        cost_estimate=pl.CostEstimate(
            flops=6 * m * width * hidden, bytes_accessed=17_000_000, transcendentals=m * hidden
        ),
    )(x, w_gate, w_up, w_down)


def dispatch_kernel(place_ref, x_ref, out_ref):
    y = jnp.dot(place_ref[...], x_ref[...], preferred_element_type=F32).astype(BF)
    out_ref[...] = y.reshape(out_ref.shape)


def dispatch(place, x, cuts):
    m = place.shape[0]
    tokens, width = x.shape
    n = width // cuts
    return pl.pallas_call(
        dispatch_kernel,
        grid=(cuts,),
        in_specs=[pl.BlockSpec(place.shape, lambda i: (0, 0)), pl.BlockSpec((tokens, n), lambda i: (0, i))],
        out_specs=pl.BlockSpec((m // 2, 2, n), lambda i: (0, 0, i)),
        out_shape=jax.ShapeDtypeStruct((m // 2, 2, width), BF),
        compiler_params=pltpu.CompilerParams(vmem_limit_bytes=32 * 2**20),
        cost_estimate=pl.CostEstimate(
            flops=2 * m * tokens * width, bytes_accessed=2 * m * width + 2 * tokens * width, transcendentals=0
        ),
    )(place, x)


def combine_kernel(factors_ref, x_ref, own_ref, far_ref):
    tok = own_ref.shape[0]
    rows = x_ref[...].reshape(factors_ref.shape[1], x_ref.shape[2])
    y = jnp.dot(factors_ref[...], rows, preferred_element_type=F32)
    y = y[: 2 * tok] + y[2 * tok :]
    own_ref[...] = y[:tok]
    far_ref[...] = y[tok:]


def combine(factors, x, cuts):
    width = x.shape[2]
    n = width // cuts
    tok = factors.shape[0] // 4
    part = pl.BlockSpec((tok, n), lambda i: (0, i))
    return pl.pallas_call(
        combine_kernel,
        grid=(cuts,),
        in_specs=[
            pl.BlockSpec(factors.shape, lambda i: (0, 0)),
            pl.BlockSpec((x.shape[0], 2, n), lambda i: (0, 0, i)),
        ],
        out_specs=(part, part),
        out_shape=(jax.ShapeDtypeStruct((tok, width), F32),) * 2,
        compiler_params=pltpu.CompilerParams(vmem_limit_bytes=32 * 2**20),
        cost_estimate=pl.CostEstimate(
            flops=2 * factors.size * width, bytes_accessed=4 * x.shape[0] * width, transcendentals=0
        ),
    )(factors, x)


def project_kernel(order_ref, own_ref, far_ref, *refs):
    *chunk_refs, left_ref, right_ref, out_ref, x_ref, w_ref = refs
    rows = own_ref.shape[0]
    parts = out_ref.shape[0]
    tok = rows // parts
    for i in range(len(chunk_refs) + 1):
        columns = pl.ds(pl.multiple_of(order_ref[i] * VD, VD), VD)
        x_ref[:rows, i * VD : (i + 1) * VD] = own_ref[:, columns]
        x_ref[rows:, i * VD : (i + 1) * VD] = far_ref[:, columns]
    for i, ref in enumerate(chunk_refs):
        w_ref[i * VD : (i + 1) * VD] = ref[...]
    half = left_ref.shape[1]
    w_ref[len(chunk_refs) * VD :, :half] = left_ref[...]
    w_ref[len(chunk_refs) * VD :, half:] = right_ref[...]
    n = 256
    for c in range(0, w_ref.shape[1], n):
        y = jnp.dot(x_ref[...], w_ref[:, c : c + n], preferred_element_type=F32).astype(BF)
        for e in range(parts):
            out_ref[e, 0, :, c : c + n] = y[e * tok : (e + 1) * tok]
            out_ref[e, 1, :, c : c + n] = y[rows + e * tok : rows + (e + 1) * tok]


def project(order, own, far, chunks, parts):
    rows, depth = own.shape
    width = chunks[0].shape[1]
    whole = pl.BlockSpec(memory_space=pltpu.VMEM)
    return pl.pallas_call(
        project_kernel,
        in_specs=[pl.BlockSpec(memory_space=pltpu.SMEM)] + [whole] * (2 + len(chunks)),
        out_specs=whole,
        out_shape=jax.ShapeDtypeStruct((parts, 2, rows // parts, width), BF),
        scratch_shapes=[pltpu.VMEM((2 * rows, depth), BF), pltpu.VMEM((depth, width), BF)],
        compiler_params=pltpu.CompilerParams(vmem_limit_bytes=32 * 2**20),
        cost_estimate=pl.CostEstimate(
            flops=4 * rows * depth * width, bytes_accessed=2 * depth * width, transcendentals=0
        ),
    )(order, own, far, *chunks)


def swap(mine):
    return lax.ppermute(mine, "core", SWAP)


def gather_w_out(w_out):
    core, x, z = (lax.axis_index(n) for n in ("core", "x", "z_lo"))
    half = w_out.shape[1] // 2
    lower, upper = w_out[:, :half], w_out[:, half:]
    mine = jnp.where(core == 0, lower, upper)
    other = swap(jnp.where(core == 0, upper, lower))
    own = jnp.concatenate([jnp.where(core == 0, mine, other), jnp.where(core == 0, other, mine)], axis=0)
    up = lambda a: lax.ppermute(a, "x", [(i, (i + 1) % 4) for i in range(4)])
    down = lambda a: lax.ppermute(a, "x", [(i, (i + 3) % 4) for i in range(4)])
    across = lambda a: lax.ppermute(a, "z_lo", SWAP)
    mate, before, after = across(own), up(own), down(own)
    mate_before, mate_after, opposite = up(mate), across(after), down(after)
    part = half // 2
    left, right = up(mate_before[:, :part]), down(mate_after[:, part:])
    chunks = (own, mate, before, after, mate_before, mate_after, opposite, left, right)
    chip = lambda zz, dx: zz * 4 + lax.rem(x + 4 + dx, 4)
    order = (chip(z, 0), chip(1 - z, 0), chip(z, -1), chip(z, 1), chip(1 - z, -1), chip(1 - z, 1), chip(z, 2), chip(1 - z, 2))
    return jnp.stack(order).astype(jnp.int32), chunks


def latent_queries(queries, w_kv):
    rows = queries.shape[0]
    heads = queries.shape[1] // QK
    q = queries.reshape(rows, heads, QK)
    keys = w_kv.reshape(KV_RANK, heads, NOPE + VD)[:, :, :NOPE]
    q_lat = jnp.einsum("qhd,rhd->hqr", q[:, :, :NOPE], keys, preferred_element_type=F32).astype(BF)
    q_all = jnp.concatenate([q_lat, q[:, :, NOPE:].transpose(1, 0, 2)], axis=2)
    return q_all.reshape(heads * rows, -1)


def routing(routes, codes):
    tok = routes.shape[0]
    core = lax.axis_index("core")
    code_float = codes.astype(F32)
    mix = code_float / jnp.sum(code_float, axis=1, keepdims=True)
    routes2, mix2 = jnp.stack([routes, swap(routes)]), jnp.stack([mix, swap(mix)])
    chosen = routes2[:, :, :, None] == jnp.arange(64, dtype=jnp.int32)
    weight = jnp.sum(jnp.where(chosen, mix2[..., None], F32(0.0)), axis=2)
    has = jnp.any(chosen, axis=2)

    def of_core(a):
        a = a.reshape(2, tok, 8, 2, 4)
        return jnp.where(core == 0, a[:, :, :, 0], a[:, :, :, 1]).reshape(2, tok, 32)

    weight, has = of_core(weight), of_core(has)
    count = has.astype(jnp.int32)
    slot = jnp.cumsum(count, axis=1) - count
    place = has[:, :, :, None] & (slot[:, :, :, None] == jnp.arange(CAP, dtype=jnp.int32))
    place = place.transpose(2, 3, 0, 1)[:, :, :, None, :]
    same = jnp.arange(2)[:, None, None] == jnp.arange(2)[None, :, None]
    place = (place & same).reshape(32, CAP, 2, 2 * tok)
    place = jnp.broadcast_to(place[:, None], (32, 2, CAP, 2, 2 * tok)).reshape(64 * CAP * 2, 2 * tok)
    gains = weight.transpose(2, 0, 1).reshape(32, 2 * tok)
    gains = jnp.broadcast_to(gains[:, None], (32, 2 * CAP * 2, 2 * tok)).reshape(64 * CAP * 2, 2 * tok)
    factors = jnp.where(place, gains, F32(0.0)).T
    high = lax.reduce_precision(factors, 8, 7)
    factors = jnp.concatenate([high, factors - high], axis=0).astype(BF)
    return place.astype(BF), factors


def local(queries, latents, w_kv, w_out, resid, norm_gain, routes, codes, w_gate, w_up, w_down):
    tok, width = resid.shape
    chips = 64
    core = lax.axis_index("core")
    order, chunks = gather_w_out(w_out)
    near = lax.all_to_all(
        jnp.broadcast_to(latents[None], (8,) + latents.shape), CTX_CHIPS, split_axis=0, concat_axis=0, tiled=True
    )
    far = swap(near)
    ids = jnp.stack([lax.axis_index(CTX), core]).astype(jnp.int32)
    heads_out = attend(ids, latent_queries(queries, w_kv), near, far, w_kv, 4, 4)
    half = width // 2
    lower, upper = resid[:, :half], resid[:, half:]
    resid2 = jnp.stack([jnp.where(core == 0, lower, upper), swap(jnp.where(core == 0, upper, lower))])
    attn = project(order, heads_out, swap(heads_out), chunks, 8)
    attn = lax.all_to_all(attn, EP, split_axis=0, concat_axis=0, tiled=True)
    summed = (resid2.astype(F32) + jnp.sum(attn.astype(F32), axis=0)).astype(BF)
    others = swap(summed)[::-1]
    attended2 = jnp.concatenate(
        [jnp.where(core == 0, summed, others), jnp.where(core == 0, others, summed)], axis=2
    ).reshape(2 * tok, width)
    attended = attended2[:tok]
    wide2 = attended2.astype(F32)
    meansq = jnp.mean(wide2 * wide2, axis=1, keepdims=True)
    normed2 = (wide2 * lax.rsqrt(meansq + 1e-06) * norm_gain[None, :]).astype(BF)

    place, factors = routing(routes, codes)
    outgoing = dispatch(place, normed2, 7)
    arrived = lax.all_to_all(
        outgoing.reshape(chips, CAP, 2, width), CHIPS, split_axis=0, concat_axis=0, tiled=True
    ).reshape(chips * CAP, 2, width)
    produced = expert(arrived, w_gate[0], w_up[0], w_down[0], 2, 7)
    returned = lax.all_to_all(
        produced.reshape(chips, CAP, 2, width), CHIPS, split_axis=0, concat_axis=0, tiled=True
    ).reshape(chips * CAP, 2, width)
    own, theirs = combine(factors, returned, 7)
    layer_out = (wide2[:tok] + own + swap(theirs)).astype(BF)
    return (attended, layer_out)


def solution(mesh):
    fine = Mesh(mesh.devices.reshape(SIZES), NAMES)
    rows = P(CTX + EP, None)
    heads = P(CTX + EP, None, None)
    placed = (
        P(CTX, EP),
        P(None, CTX),
        P(None, EP),
        P(EP + CTX, None),
        rows,
        P(),
        rows,
        rows,
        heads,
        heads,
        heads,
    )
    return jax.shard_map(local, mesh=fine, in_specs=placed, out_specs=(rows, rows), check_vma=False)
```

```python
import functools

import jax
import jax.numpy as jnp
from jax import lax
from jax.experimental import pallas as pl
from jax.experimental.pallas import tpu as pltpu
from jax.sharding import Mesh, PartitionSpec as P

NOPE = 128
VD = 128
KV_RANK = 512
TOP = 8
QK = 192
CAP = 3
SLOTS = (slice(0, 2), slice(2, 3))

CTX = ("z_lo", "x", "core")
CTX_CHIPS = ("z_lo", "x")
EP = ("z_hi", "y")
CHIPS = ("z_lo", "x", "z_hi", "y")
SIZES = (2, 4, 2, 2, 4)
NAMES = ("z_lo", "x", "core", "z_hi", "y")
SWAP = ((0, 1), (1, 0))
BF = jnp.bfloat16
F32 = jnp.float32
LOG2E = 1.4426950408889634


def attend_kernel(ids_ref, q_ref, near_ref, far_ref, w_ref, out_ref, lat_ref, s_ref, p_ref, *, rows, cuts):
    heads = w_ref.shape[1] // (NOPE + VD)
    m = q_ref.shape[0]
    pairs = near_ref.shape[0]
    keys = 2 * rows * pairs

    @pl.when(pl.program_id(0) == 0)
    def _():
        for i in range(pairs):
            lat_ref[:, 2 * i * rows : (2 * i + 1) * rows] = near_ref[i]
            lat_ref[:, (2 * i + 1) * rows : (2 * i + 2) * rows] = far_ref[i]

    ctx, core = ids_ref[0], ids_ref[1]
    span = keys // cuts
    lane = lax.broadcasted_iota(jnp.int32, (m, rows), 1)
    query = lax.broadcasted_iota(jnp.int32, (m, rows), 0) % rows
    ahead = lane - query
    peak = jnp.full((m, rows), -1e30, F32)
    for j in range(cuts):
        s = jnp.dot(q_ref[...], lat_ref[:, j * span : (j + 1) * span], preferred_element_type=F32)
        for b in range(span // rows):
            block = j * (span // rows) + b
            pos = 2 * (block // 2) + (core if block % 2 == 0 else 1 - core)
            part = s[:, b * rows : (b + 1) * rows]
            part = jnp.where(ahead <= (ctx - pos) * rows, part, F32(-1e30))
            peak = jnp.maximum(peak, part)
            s_ref[:, block * rows : (block + 1) * rows] = part
    top = jnp.max(peak, axis=1, keepdims=True)
    total = jnp.zeros((m, rows), F32)
    for j in range(keys // rows):
        p = jnp.exp2((s_ref[:, j * rows : (j + 1) * rows] - top) * (QK ** (-0.5) * LOG2E))
        total = total + p
        p_ref[:, j * rows : (j + 1) * rows] = p.astype(BF)
    mixed = lax.dot_general(p_ref[...], lat_ref[:KV_RANK], (((1,), (1,)), ((), ())), preferred_element_type=F32)
    mixed = (mixed / jnp.sum(total, axis=1, keepdims=True)).astype(BF)
    for h in range(heads):
        values = w_ref[:, h * (NOPE + VD) + NOPE : (h + 1) * (NOPE + VD)]
        o = jnp.dot(mixed[h * rows : (h + 1) * rows], values, preferred_element_type=F32)
        out_ref[:, h * VD : (h + 1) * VD] = o.astype(BF)


def attend(ids, q, near, far, w_kv, group, cuts):
    pairs, depth, rows = near.shape
    heads = w_kv.shape[1] // (NOPE + VD)
    keys = 2 * rows * pairs
    m = group * rows
    return pl.pallas_call(
        functools.partial(attend_kernel, rows=rows, cuts=cuts),
        grid=(heads // group,),
        in_specs=[
            pl.BlockSpec(memory_space=pltpu.SMEM),
            pl.BlockSpec((m, depth), lambda g: (g, 0)),
            pl.BlockSpec(near.shape, lambda g: (0, 0, 0)),
            pl.BlockSpec(far.shape, lambda g: (0, 0, 0)),
            pl.BlockSpec((KV_RANK, group * (NOPE + VD)), lambda g: (0, g)),
        ],
        out_specs=pl.BlockSpec((rows, group * VD), lambda g: (0, g)),
        out_shape=jax.ShapeDtypeStruct((rows, heads * VD), BF),
        scratch_shapes=[pltpu.VMEM((depth, keys), BF), pltpu.VMEM((m, keys), F32), pltpu.VMEM((m, keys), BF)],
        compiler_params=pltpu.CompilerParams(vmem_limit_bytes=40 * 2**20),
        cost_estimate=pl.CostEstimate(
            flops=2 * heads * rows * keys * (depth + KV_RANK),
            bytes_accessed=8_000_000,
            transcendentals=heads * rows * keys,
        ),
    )(ids, q, near, far, w_kv)


def expert_kernel(x_ref, g_ref, u_ref, d_ref, out_ref, rows_ref, hid_ref, *, first):
    step = pl.program_id(0)

    @pl.when(step == 0)
    def _():
        rows_ref[...] = x_ref[...].reshape(rows_ref.shape)

    @pl.when(step < first)
    def _():
        rows = rows_ref[...]
        gate = jnp.dot(rows, g_ref[...], preferred_element_type=F32)
        upward = jnp.dot(rows, u_ref[...], preferred_element_type=F32)
        hid = (gate / (1.0 + jnp.exp(-gate)) * upward).astype(BF)
        n = g_ref.shape[1]
        for f in range(first):

            @pl.when(step == f)
            def _(f=f):
                hid_ref[:, f * n : (f + 1) * n] = hid

    @pl.when(step >= first)
    def _():
        y = jnp.dot(hid_ref[...], d_ref[...], preferred_element_type=F32).astype(BF)
        out_ref[...] = y.reshape(out_ref.shape)


def expert(x, w_gate, w_up, w_down, first, last):
    units, pair, width = x.shape
    m = units * pair
    hidden = w_gate.shape[1]
    n1, n2 = hidden // first, width // last
    return pl.pallas_call(
        functools.partial(expert_kernel, first=first),
        grid=(first + last,),
        in_specs=[
            pl.BlockSpec(x.shape, lambda i: (0, 0, 0)),
            pl.BlockSpec((width, n1), lambda i: (0, jnp.minimum(i, first - 1))),
            pl.BlockSpec((width, n1), lambda i: (0, jnp.minimum(i, first - 1))),
            pl.BlockSpec((hidden, n2), lambda i: (0, jnp.maximum(i - first, 0))),
        ],
        out_specs=pl.BlockSpec((units, pair, n2), lambda i: (0, 0, jnp.maximum(i - first, 0))),
        out_shape=jax.ShapeDtypeStruct(x.shape, BF),
        scratch_shapes=[pltpu.VMEM((m, width), BF), pltpu.VMEM((m, hidden), BF)],
        compiler_params=pltpu.CompilerParams(vmem_limit_bytes=40 * 2**20),
        cost_estimate=pl.CostEstimate(
            flops=6 * m * width * hidden, bytes_accessed=17_000_000, transcendentals=m * hidden
        ),
    )(x, w_gate, w_up, w_down)


def dispatch_kernel(place_ref, x_ref, out_ref):
    y = jnp.dot(place_ref[...], x_ref[...], preferred_element_type=F32).astype(BF)
    out_ref[...] = y.reshape(out_ref.shape)


def dispatch(place, x, cuts):
    m = place.shape[0]
    tokens, width = x.shape
    n = width // cuts
    return pl.pallas_call(
        dispatch_kernel,
        grid=(cuts,),
        in_specs=[pl.BlockSpec(place.shape, lambda i: (0, 0)), pl.BlockSpec((tokens, n), lambda i: (0, i))],
        out_specs=pl.BlockSpec((m // 2, 2, n), lambda i: (0, 0, i)),
        out_shape=jax.ShapeDtypeStruct((m // 2, 2, width), BF),
        compiler_params=pltpu.CompilerParams(vmem_limit_bytes=32 * 2**20),
        cost_estimate=pl.CostEstimate(
            flops=2 * m * tokens * width, bytes_accessed=2 * m * width + 2 * tokens * width, transcendentals=0
        ),
    )(place, x)


def combine_kernel(*refs):
    *in_refs, own_ref, far_ref = refs
    tok = own_ref.shape[0]
    y = None
    for factors_ref, x_ref in zip(in_refs[::2], in_refs[1::2]):
        rows = x_ref[...].reshape(factors_ref.shape[1], x_ref.shape[2])
        part = jnp.dot(factors_ref[...], rows, preferred_element_type=F32)
        y = part if y is None else y + part
    y = y[: 2 * tok] + y[2 * tok :]
    own_ref[...] = y[:tok]
    far_ref[...] = y[tok:]


def combine(parts, cuts):
    width = parts[0][1].shape[2]
    n = width // cuts
    tok = parts[0][0].shape[0] // 4
    half = pl.BlockSpec((tok, n), lambda i: (0, i))
    in_specs = []
    for factors, x in parts:
        in_specs.append(pl.BlockSpec(factors.shape, lambda i: (0, 0)))
        in_specs.append(pl.BlockSpec((x.shape[0], 2, n), lambda i: (0, 0, i)))
    rows = sum(2 * x.shape[0] for _, x in parts)
    return pl.pallas_call(
        combine_kernel,
        grid=(cuts,),
        in_specs=in_specs,
        out_specs=(half, half),
        out_shape=(jax.ShapeDtypeStruct((tok, width), F32),) * 2,
        compiler_params=pltpu.CompilerParams(vmem_limit_bytes=32 * 2**20),
        cost_estimate=pl.CostEstimate(
            flops=8 * tok * rows * width, bytes_accessed=2 * rows * width, transcendentals=0
        ),
    )(*[a for part in parts for a in part])


def project_kernel(order_ref, own_ref, far_ref, *refs):
    *chunk_refs, left_ref, right_ref, out_ref, x_ref, w_ref = refs
    rows = own_ref.shape[0]
    parts = out_ref.shape[0]
    tok = rows // parts
    for i in range(len(chunk_refs) + 1):
        columns = pl.ds(pl.multiple_of(order_ref[i] * VD, VD), VD)
        x_ref[:rows, i * VD : (i + 1) * VD] = own_ref[:, columns]
        x_ref[rows:, i * VD : (i + 1) * VD] = far_ref[:, columns]
    for i, ref in enumerate(chunk_refs):
        w_ref[i * VD : (i + 1) * VD] = ref[...]
    half = left_ref.shape[1]
    w_ref[len(chunk_refs) * VD :, :half] = left_ref[...]
    w_ref[len(chunk_refs) * VD :, half:] = right_ref[...]
    n = 256
    for c in range(0, w_ref.shape[1], n):
        y = jnp.dot(x_ref[...], w_ref[:, c : c + n], preferred_element_type=F32).astype(BF)
        for e in range(parts):
            out_ref[e, 0, :, c : c + n] = y[e * tok : (e + 1) * tok]
            out_ref[e, 1, :, c : c + n] = y[rows + e * tok : rows + (e + 1) * tok]


def project(order, own, far, chunks, parts):
    rows, depth = own.shape
    width = chunks[0].shape[1]
    whole = pl.BlockSpec(memory_space=pltpu.VMEM)
    return pl.pallas_call(
        project_kernel,
        in_specs=[pl.BlockSpec(memory_space=pltpu.SMEM)] + [whole] * (2 + len(chunks)),
        out_specs=whole,
        out_shape=jax.ShapeDtypeStruct((parts, 2, rows // parts, width), BF),
        scratch_shapes=[pltpu.VMEM((2 * rows, depth), BF), pltpu.VMEM((depth, width), BF)],
        compiler_params=pltpu.CompilerParams(vmem_limit_bytes=32 * 2**20),
        cost_estimate=pl.CostEstimate(
            flops=4 * rows * depth * width, bytes_accessed=2 * depth * width, transcendentals=0
        ),
    )(order, own, far, *chunks)


def swap(mine):
    return lax.ppermute(mine, "core", SWAP)


def gather_w_out(w_out):
    core, x, z = (lax.axis_index(n) for n in ("core", "x", "z_lo"))
    half = w_out.shape[1] // 2
    lower, upper = w_out[:, :half], w_out[:, half:]
    mine = jnp.where(core == 0, lower, upper)
    other = swap(jnp.where(core == 0, upper, lower))
    own = jnp.concatenate([jnp.where(core == 0, mine, other), jnp.where(core == 0, other, mine)], axis=0)
    up = lambda a: lax.ppermute(a, "x", [(i, (i + 1) % 4) for i in range(4)])
    down = lambda a: lax.ppermute(a, "x", [(i, (i + 3) % 4) for i in range(4)])
    across = lambda a: lax.ppermute(a, "z_lo", SWAP)
    mate, before, after = across(own), up(own), down(own)
    mate_before, mate_after, opposite = up(mate), across(after), down(after)
    part = half // 2
    left, right = up(mate_before[:, :part]), down(mate_after[:, part:])
    chunks = (own, mate, before, after, mate_before, mate_after, opposite, left, right)
    chip = lambda zz, dx: zz * 4 + lax.rem(x + 4 + dx, 4)
    order = (chip(z, 0), chip(1 - z, 0), chip(z, -1), chip(z, 1), chip(1 - z, -1), chip(1 - z, 1), chip(z, 2), chip(1 - z, 2))
    return own, jnp.stack(order).astype(jnp.int32), chunks


def latent_queries(queries, w_kv):
    rows = queries.shape[0]
    heads = queries.shape[1] // QK
    q = queries.reshape(rows, heads, QK)
    keys = w_kv.reshape(KV_RANK, heads, NOPE + VD)[:, :, :NOPE]
    q_lat = jnp.einsum("qhd,rhd->hqr", q[:, :, :NOPE], keys, preferred_element_type=F32).astype(BF)
    q_all = jnp.concatenate([q_lat, q[:, :, NOPE:].transpose(1, 0, 2)], axis=2)
    return q_all.reshape(heads * rows, -1)


def routing(routes, codes):
    tok = routes.shape[0]
    core = lax.axis_index("core")
    code_float = codes.astype(F32)
    mix = code_float / jnp.sum(code_float, axis=1, keepdims=True)
    routes2, mix2 = jnp.stack([routes, swap(routes)]), jnp.stack([mix, swap(mix)])
    chosen = routes2[:, :, :, None] == jnp.arange(64, dtype=jnp.int32)
    weight = jnp.sum(jnp.where(chosen, mix2[..., None], F32(0.0)), axis=2)
    has = jnp.any(chosen, axis=2)

    def of_core(a):
        a = a.reshape(2, tok, 8, 2, 4)
        return jnp.where(core == 0, a[:, :, :, 0], a[:, :, :, 1]).reshape(2, tok, 32)

    weight, has = of_core(weight), of_core(has)
    count = has.astype(jnp.int32)
    slot = jnp.cumsum(count, axis=1) - count
    place = has[:, :, :, None] & (slot[:, :, :, None] == jnp.arange(CAP, dtype=jnp.int32))
    place = place.transpose(2, 3, 0, 1)[:, :, :, None, :]
    same = jnp.arange(2)[:, None, None] == jnp.arange(2)[None, :, None]
    place = (place & same).reshape(32, CAP, 2, 2 * tok)
    place = jnp.broadcast_to(place[:, None], (32, 2, CAP, 2, 2 * tok)).reshape(64, CAP, 2, 2 * tok)
    gains = weight.transpose(2, 0, 1).reshape(32, 2 * tok)
    gains = jnp.broadcast_to(gains[:, None], (32, 2, 2 * tok)).reshape(64, 1, 1, 2 * tok)
    factors = jnp.where(place, gains, F32(0.0))
    high = lax.reduce_precision(factors, 8, 7)
    factors = jnp.concatenate([high, factors - high], axis=3).astype(BF)
    place = place.astype(BF)
    parts = []
    for slots in SLOTS:
        parts.append((place[:, slots].reshape(-1, 2 * tok), factors[:, slots].reshape(-1, 4 * tok).T))
    return parts


def local(queries, latents, w_kv, w_out, resid, norm_gain, routes, codes, w_gate, w_up, w_down):
    tok, width = resid.shape
    chips = 64
    core = lax.axis_index("core")
    own_rows, order, chunks = gather_w_out(w_out)
    latents, _ = lax.optimization_barrier((latents, own_rows))
    near = lax.all_to_all(
        jnp.broadcast_to(latents[None], (8,) + latents.shape), CTX_CHIPS, split_axis=0, concat_axis=0, tiled=True
    )
    far = swap(near)
    ids = jnp.stack([lax.axis_index(CTX), core]).astype(jnp.int32)
    heads_out = attend(ids, latent_queries(queries, w_kv), near, far, w_kv, 4, 4)
    half = width // 2
    lower, upper = resid[:, :half], resid[:, half:]
    resid2 = jnp.stack([jnp.where(core == 0, lower, upper), swap(jnp.where(core == 0, upper, lower))])
    attn = project(order, heads_out, swap(heads_out), chunks, 8)
    attn = lax.all_to_all(attn, EP, split_axis=0, concat_axis=0, tiled=True)
    summed = (resid2.astype(F32) + jnp.sum(attn.astype(F32), axis=0)).astype(BF)
    others = swap(summed)[::-1]
    attended2 = jnp.concatenate(
        [jnp.where(core == 0, summed, others), jnp.where(core == 0, others, summed)], axis=2
    ).reshape(2 * tok, width)
    attended = attended2[:tok]
    wide2 = attended2.astype(F32)
    meansq = jnp.mean(wide2 * wide2, axis=1, keepdims=True)
    normed2 = (wide2 * lax.rsqrt(meansq + 1e-06) * norm_gain[None, :]).astype(BF)

    def exchange(rows):
        units = rows.reshape(chips, -1, 2, width)
        units = lax.all_to_all(units, CHIPS, split_axis=0, concat_axis=0, tiled=True)
        return units.reshape(rows.shape)

    parts = routing(routes, codes)
    arrived = [exchange(dispatch(place, normed2, 7)) for place, _ in parts]
    returned = [exchange(expert(rows, w_gate[0], w_up[0], w_down[0], 2, 7)) for rows in arrived]
    own, theirs = combine([(factors, rows) for (_, factors), rows in zip(parts, returned)], 7)
    layer_out = (wide2[:tok] + own + swap(theirs)).astype(BF)
    return (attended, layer_out)


def solution(mesh):
    fine = Mesh(mesh.devices.reshape(SIZES), NAMES)
    rows = P(CTX + EP, None)
    heads = P(CTX + EP, None, None)
    placed = (
        P(CTX, EP),
        P(None, CTX),
        P(None, EP),
        P(EP + CTX, None),
        rows,
        P(),
        rows,
        rows,
        heads,
        heads,
        heads,
    )
    return jax.shard_map(local, mesh=fine, in_specs=placed, out_specs=(rows, rows), check_vma=False)
```

```python
import functools

import jax
import jax.numpy as jnp
from jax import lax
from jax.experimental import pallas as pl
from jax.experimental.pallas import tpu as pltpu
from jax.sharding import Mesh, PartitionSpec as P

NOPE = 128
VD = 128
KV_RANK = 512
TOP = 8
QK = 192
CAP = 3
SLOTS = (slice(0, 3),)

CTX = ("z_lo", "x", "core")
CTX_CHIPS = ("z_lo", "x")
EP = ("z_hi", "y")
CHIPS = ("z_lo", "x", "z_hi", "y")
SIZES = (2, 4, 2, 2, 4)
NAMES = ("z_lo", "x", "core", "z_hi", "y")
SWAP = ((0, 1), (1, 0))
BF = jnp.bfloat16
F32 = jnp.float32
LOG2E = 1.4426950408889634


def attend_kernel(order_ref, q_ref, w_ref, *refs, rows, cuts):
    *piece_refs, out_ref, lat_ref, s_ref, p_ref = refs
    heads = w_ref.shape[1] // (NOPE + VD)
    m = q_ref.shape[0]
    keys = lat_ref.shape[1]
    count = len(piece_refs) // 2

    @pl.when(pl.program_id(0) == 0)
    def _():
        for side in range(2):
            for i in range(count - 2):
                first = (2 * i + side) * rows
                lat_ref[:, first : first + rows] = piece_refs[side * count + i][...]
            first = (2 * (count - 2) + side) * rows
            depth = piece_refs[count - 1].shape[0]
            lat_ref[:depth, first : first + rows] = piece_refs[side * count + count - 2][...]
            lat_ref[depth:, first : first + rows] = piece_refs[side * count + count - 1][...]

    core = order_ref[count - 1]
    ctx = 2 * order_ref[0] + core
    span = keys // cuts
    lane = lax.broadcasted_iota(jnp.int32, (m, rows), 1)
    query = lax.broadcasted_iota(jnp.int32, (m, rows), 0) % rows
    ahead = lane - query
    peak = jnp.full((m, rows), -1e30, F32)
    for j in range(cuts):
        s = jnp.dot(q_ref[...], lat_ref[:, j * span : (j + 1) * span], preferred_element_type=F32)
        for b in range(span // rows):
            block = j * (span // rows) + b
            pos = 2 * order_ref[block // 2] + (core if block % 2 == 0 else 1 - core)
            part = s[:, b * rows : (b + 1) * rows]
            part = jnp.where(ahead <= (ctx - pos) * rows, part, F32(-1e30))
            peak = jnp.maximum(peak, part)
            s_ref[:, block * rows : (block + 1) * rows] = part
    top = jnp.max(peak, axis=1, keepdims=True)
    total = jnp.zeros((m, rows), F32)
    for j in range(keys // rows):
        p = jnp.exp2((s_ref[:, j * rows : (j + 1) * rows] - top) * (QK ** (-0.5) * LOG2E))
        total = total + p
        p_ref[:, j * rows : (j + 1) * rows] = p.astype(BF)
    mixed = lax.dot_general(p_ref[...], lat_ref[:KV_RANK], (((1,), (1,)), ((), ())), preferred_element_type=F32)
    mixed = (mixed / jnp.sum(total, axis=1, keepdims=True)).astype(BF)
    for h in range(heads):
        values = w_ref[:, h * (NOPE + VD) + NOPE : (h + 1) * (NOPE + VD)]
        o = jnp.dot(mixed[h * rows : (h + 1) * rows], values, preferred_element_type=F32)
        out_ref[:, h * VD : (h + 1) * VD] = o.astype(BF)


def attend(order, q, w_kv, near, far, group, cuts):
    depth, rows = near[0].shape
    heads = w_kv.shape[1] // (NOPE + VD)
    keys = 2 * rows * (len(near) - 1)
    m = group * rows
    pieces = (*near, *far)
    return pl.pallas_call(
        functools.partial(attend_kernel, rows=rows, cuts=cuts),
        grid=(heads // group,),
        in_specs=[
            pl.BlockSpec(memory_space=pltpu.SMEM),
            pl.BlockSpec((m, depth), lambda g: (g, 0)),
            pl.BlockSpec((KV_RANK, group * (NOPE + VD)), lambda g: (0, g)),
        ]
        + [pl.BlockSpec(a.shape, lambda g: (0, 0)) for a in pieces],
        out_specs=pl.BlockSpec((rows, group * VD), lambda g: (0, g)),
        out_shape=jax.ShapeDtypeStruct((rows, heads * VD), BF),
        scratch_shapes=[pltpu.VMEM((depth, keys), BF), pltpu.VMEM((m, keys), F32), pltpu.VMEM((m, keys), BF)],
        compiler_params=pltpu.CompilerParams(vmem_limit_bytes=40 * 2**20),
        cost_estimate=pl.CostEstimate(
            flops=2 * heads * rows * keys * (depth + KV_RANK),
            bytes_accessed=8_000_000,
            transcendentals=heads * rows * keys,
        ),
    )(order, q, w_kv, *pieces)


def expert_kernel(x_ref, g_ref, u_ref, d_ref, out_ref, rows_ref, hid_ref, *, first):
    step = pl.program_id(0)

    @pl.when(step == 0)
    def _():
        rows_ref[...] = x_ref[...].reshape(rows_ref.shape)

    @pl.when(step < first)
    def _():
        rows = rows_ref[...]
        gate = jnp.dot(rows, g_ref[...], preferred_element_type=F32)
        upward = jnp.dot(rows, u_ref[...], preferred_element_type=F32)
        hid = (gate / (1.0 + jnp.exp(-gate)) * upward).astype(BF)
        n = g_ref.shape[1]
        for f in range(first):

            @pl.when(step == f)
            def _(f=f):
                hid_ref[:, f * n : (f + 1) * n] = hid

    @pl.when(step >= first)
    def _():
        y = jnp.dot(hid_ref[...], d_ref[...], preferred_element_type=F32).astype(BF)
        out_ref[...] = y.reshape(out_ref.shape)


def expert(x, w_gate, w_up, w_down, first, last):
    units, pair, width = x.shape
    m = units * pair
    hidden = w_gate.shape[1]
    n1, n2 = hidden // first, width // last
    return pl.pallas_call(
        functools.partial(expert_kernel, first=first),
        grid=(first + last,),
        in_specs=[
            pl.BlockSpec(x.shape, lambda i: (0, 0, 0)),
            pl.BlockSpec((width, n1), lambda i: (0, jnp.minimum(i, first - 1))),
            pl.BlockSpec((width, n1), lambda i: (0, jnp.minimum(i, first - 1))),
            pl.BlockSpec((hidden, n2), lambda i: (0, jnp.maximum(i - first, 0))),
        ],
        out_specs=pl.BlockSpec((units, pair, n2), lambda i: (0, 0, jnp.maximum(i - first, 0))),
        out_shape=jax.ShapeDtypeStruct(x.shape, BF),
        scratch_shapes=[pltpu.VMEM((m, width), BF), pltpu.VMEM((m, hidden), BF)],
        compiler_params=pltpu.CompilerParams(vmem_limit_bytes=40 * 2**20),
        cost_estimate=pl.CostEstimate(
            flops=6 * m * width * hidden, bytes_accessed=17_000_000, transcendentals=m * hidden
        ),
    )(x, w_gate, w_up, w_down)


def dispatch_kernel(place_ref, x_ref, out_ref):
    y = jnp.dot(place_ref[...], x_ref[...], preferred_element_type=F32).astype(BF)
    out_ref[...] = y.reshape(out_ref.shape)


def dispatch(place, x, cuts):
    m = place.shape[0]
    tokens, width = x.shape
    n = width // cuts
    return pl.pallas_call(
        dispatch_kernel,
        grid=(cuts,),
        in_specs=[pl.BlockSpec(place.shape, lambda i: (0, 0)), pl.BlockSpec((tokens, n), lambda i: (0, i))],
        out_specs=pl.BlockSpec((m // 2, 2, n), lambda i: (0, 0, i)),
        out_shape=jax.ShapeDtypeStruct((m // 2, 2, width), BF),
        compiler_params=pltpu.CompilerParams(vmem_limit_bytes=32 * 2**20),
        cost_estimate=pl.CostEstimate(
            flops=2 * m * tokens * width, bytes_accessed=2 * m * width + 2 * tokens * width, transcendentals=0
        ),
    )(place, x)


def combine_kernel(*refs):
    *in_refs, own_ref, far_ref = refs
    tok = own_ref.shape[0]
    y = None
    for factors_ref, x_ref in zip(in_refs[::2], in_refs[1::2]):
        rows = x_ref[...].reshape(factors_ref.shape[1], x_ref.shape[2])
        part = jnp.dot(factors_ref[...], rows, preferred_element_type=F32)
        y = part if y is None else y + part
    y = y[: 2 * tok] + y[2 * tok :]
    own_ref[...] = y[:tok]
    far_ref[...] = y[tok:]


def combine(parts, cuts):
    width = parts[0][1].shape[2]
    n = width // cuts
    tok = parts[0][0].shape[0] // 4
    half = pl.BlockSpec((tok, n), lambda i: (0, i))
    in_specs = []
    for factors, x in parts:
        in_specs.append(pl.BlockSpec(factors.shape, lambda i: (0, 0)))
        in_specs.append(pl.BlockSpec((x.shape[0], 2, n), lambda i: (0, 0, i)))
    rows = sum(2 * x.shape[0] for _, x in parts)
    return pl.pallas_call(
        combine_kernel,
        grid=(cuts,),
        in_specs=in_specs,
        out_specs=(half, half),
        out_shape=(jax.ShapeDtypeStruct((tok, width), F32),) * 2,
        compiler_params=pltpu.CompilerParams(vmem_limit_bytes=32 * 2**20),
        cost_estimate=pl.CostEstimate(
            flops=8 * tok * rows * width, bytes_accessed=2 * rows * width, transcendentals=0
        ),
    )(*[a for part in parts for a in part])


def project_kernel(order_ref, own_ref, far_ref, *refs):
    *chunk_refs, left_ref, right_ref, out_ref, x_ref, w_ref = refs
    rows = own_ref.shape[0]
    parts = out_ref.shape[0]
    tok = rows // parts
    for i in range(len(chunk_refs) + 1):
        columns = pl.ds(pl.multiple_of(order_ref[i] * VD, VD), VD)
        x_ref[:rows, i * VD : (i + 1) * VD] = own_ref[:, columns]
        x_ref[rows:, i * VD : (i + 1) * VD] = far_ref[:, columns]
    for i, ref in enumerate(chunk_refs):
        w_ref[i * VD : (i + 1) * VD] = ref[...]
    half = left_ref.shape[1]
    w_ref[len(chunk_refs) * VD :, :half] = left_ref[...]
    w_ref[len(chunk_refs) * VD :, half:] = right_ref[...]
    n = 256
    for c in range(0, w_ref.shape[1], n):
        y = jnp.dot(x_ref[...], w_ref[:, c : c + n], preferred_element_type=F32).astype(BF)
        for e in range(parts):
            out_ref[e, 0, :, c : c + n] = y[e * tok : (e + 1) * tok]
            out_ref[e, 1, :, c : c + n] = y[rows + e * tok : rows + (e + 1) * tok]


def project(order, own, far, chunks, parts):
    rows, depth = own.shape
    width = chunks[0].shape[1]
    whole = pl.BlockSpec(memory_space=pltpu.VMEM)
    return pl.pallas_call(
        project_kernel,
        in_specs=[pl.BlockSpec(memory_space=pltpu.SMEM)] + [whole] * (2 + len(chunks)),
        out_specs=whole,
        out_shape=jax.ShapeDtypeStruct((parts, 2, rows // parts, width), BF),
        scratch_shapes=[pltpu.VMEM((2 * rows, depth), BF), pltpu.VMEM((depth, width), BF)],
        compiler_params=pltpu.CompilerParams(vmem_limit_bytes=32 * 2**20),
        cost_estimate=pl.CostEstimate(
            flops=4 * rows * depth * width, bytes_accessed=2 * depth * width, transcendentals=0
        ),
    )(order, own, far, *chunks)


def swap(mine):
    return lax.ppermute(mine, "core", SWAP)


def gather(own, axis):
    up = lambda a: lax.ppermute(a, "x", [(i, (i + 1) % 4) for i in range(4)])
    down = lambda a: lax.ppermute(a, "x", [(i, (i + 3) % 4) for i in range(4)])
    across = lambda a: lax.ppermute(a, "z_lo", SWAP)
    mate, before, after = across(own), up(own), down(own)
    mate_before, mate_after, opposite = up(mate), across(after), down(after)
    half = own.shape[axis] // 2
    left = up(lax.slice_in_dim(mate_before, 0, half, axis=axis))
    right = down(lax.slice_in_dim(mate_after, half, 2 * half, axis=axis))
    return own, mate, before, after, mate_before, mate_after, opposite, left, right


def chip_order():
    core, x, z = (lax.axis_index(n) for n in ("core", "x", "z_lo"))
    chip = lambda zz, dx: zz * 4 + lax.rem(x + 4 + dx, 4)
    near, far = z, 1 - z
    order = [chip(near, 0), chip(far, 0), chip(near, -1), chip(near, 1)]
    order += [chip(far, -1), chip(far, 1), chip(near, 2), chip(far, 2), core]
    return jnp.stack(order).astype(jnp.int32)


def own_w_out(w_out):
    core = lax.axis_index("core")
    half = w_out.shape[1] // 2
    lower, upper = w_out[:, :half], w_out[:, half:]
    mine = jnp.where(core == 0, lower, upper)
    other = swap(jnp.where(core == 0, upper, lower))
    return jnp.concatenate([jnp.where(core == 0, mine, other), jnp.where(core == 0, other, mine)], axis=0)


def latent_queries(queries, w_kv):
    rows = queries.shape[0]
    heads = queries.shape[1] // QK
    q = queries.reshape(rows, heads, QK)
    keys = w_kv.reshape(KV_RANK, heads, NOPE + VD)[:, :, :NOPE]
    q_lat = jnp.einsum("qhd,rhd->hqr", q[:, :, :NOPE], keys, preferred_element_type=F32).astype(BF)
    q_all = jnp.concatenate([q_lat, q[:, :, NOPE:].transpose(1, 0, 2)], axis=2)
    return q_all.reshape(heads * rows, -1)


def routing(routes, codes):
    tok = routes.shape[0]
    core = lax.axis_index("core")
    code_float = codes.astype(F32)
    mix = code_float / jnp.sum(code_float, axis=1, keepdims=True)
    routes2, mix2 = jnp.stack([routes, swap(routes)]), jnp.stack([mix, swap(mix)])
    chosen = routes2[:, :, :, None] == jnp.arange(64, dtype=jnp.int32)
    weight = jnp.sum(jnp.where(chosen, mix2[..., None], F32(0.0)), axis=2)
    has = jnp.any(chosen, axis=2)

    def of_core(a):
        a = a.reshape(2, tok, 8, 2, 4)
        return jnp.where(core == 0, a[:, :, :, 0], a[:, :, :, 1]).reshape(2, tok, 32)

    weight, has = of_core(weight), of_core(has)
    count = has.astype(jnp.int32)
    slot = jnp.cumsum(count, axis=1) - count
    place = has[:, :, :, None] & (slot[:, :, :, None] == jnp.arange(CAP, dtype=jnp.int32))
    place = place.transpose(2, 3, 0, 1)[:, :, :, None, :]
    same = jnp.arange(2)[:, None, None] == jnp.arange(2)[None, :, None]
    place = (place & same).reshape(32, CAP, 2, 2 * tok)
    place = jnp.broadcast_to(place[:, None], (32, 2, CAP, 2, 2 * tok)).reshape(64, CAP, 2, 2 * tok)
    gains = weight.transpose(2, 0, 1).reshape(32, 2 * tok)
    gains = jnp.broadcast_to(gains[:, None], (32, 2, 2 * tok)).reshape(64, 1, 1, 2 * tok)
    factors = jnp.where(place, gains, F32(0.0))
    high = lax.reduce_precision(factors, 8, 7)
    factors = jnp.concatenate([high, factors - high], axis=3).astype(BF)
    place = place.astype(BF)
    parts = []
    for slots in SLOTS:
        parts.append((place[:, slots].reshape(-1, 2 * tok), factors[:, slots].reshape(-1, 4 * tok).T))
    return parts


def local(queries, latents, w_kv, w_out, resid, norm_gain, routes, codes, w_gate, w_up, w_down):
    tok, width = resid.shape
    chips = 64
    core = lax.axis_index("core")
    order = chip_order()
    near = gather(latents, 0)
    far = [swap(a) for a in near]
    chunks = gather(own_w_out(w_out), 1)
    heads_out = attend(order, latent_queries(queries, w_kv), w_kv, near, far, 4, 4)
    half = width // 2
    lower, upper = resid[:, :half], resid[:, half:]
    resid2 = jnp.stack([jnp.where(core == 0, lower, upper), swap(jnp.where(core == 0, upper, lower))])
    attn = project(order, heads_out, swap(heads_out), chunks, 8)
    attn = lax.all_to_all(attn, EP, split_axis=0, concat_axis=0, tiled=True)
    summed = (resid2.astype(F32) + jnp.sum(attn.astype(F32), axis=0)).astype(BF)
    others = swap(summed)[::-1]
    attended2 = jnp.concatenate(
        [jnp.where(core == 0, summed, others), jnp.where(core == 0, others, summed)], axis=2
    ).reshape(2 * tok, width)
    attended = attended2[:tok]
    wide2 = attended2.astype(F32)
    meansq = jnp.mean(wide2 * wide2, axis=1, keepdims=True)
    normed2 = (wide2 * lax.rsqrt(meansq + 1e-06) * norm_gain[None, :]).astype(BF)

    def exchange(rows):
        units = rows.reshape(chips, -1, 2, width)
        units = lax.all_to_all(units, CHIPS, split_axis=0, concat_axis=0, tiled=True)
        return units.reshape(rows.shape)

    parts = routing(routes, codes)
    arrived = [exchange(dispatch(place, normed2, 7)) for place, _ in parts]
    returned = [exchange(expert(rows, w_gate[0], w_up[0], w_down[0], 2, 7)) for rows in arrived]
    own, theirs = combine([(factors, rows) for (_, factors), rows in zip(parts, returned)], 7)
    layer_out = (wide2[:tok] + own + swap(theirs)).astype(BF)
    return (attended, layer_out)


def solution(mesh):
    fine = Mesh(mesh.devices.reshape(SIZES), NAMES)
    rows = P(CTX + EP, None)
    heads = P(CTX + EP, None, None)
    placed = (
        P(CTX, EP),
        P(None, CTX),
        P(None, EP),
        P(EP + CTX, None),
        rows,
        P(),
        rows,
        rows,
        heads,
        heads,
        heads,
    )
    return jax.shard_map(local, mesh=fine, in_specs=placed, out_specs=(rows, rows), check_vma=False)
```

```python
import functools

import jax
import jax.numpy as jnp
from jax import lax
from jax.experimental import pallas as pl
from jax.experimental.pallas import tpu as pltpu
from jax.sharding import Mesh, PartitionSpec as P

NOPE = 128
VD = 128
KV_RANK = 512
TOP = 8
QK = 192
CAP = 3
SLOTS = (slice(0, 3),)

CTX = ("z_lo", "x", "core")
CTX_CHIPS = ("z_lo", "x")
EP = ("z_hi", "y")
CHIPS = ("z_lo", "x", "z_hi", "y")
SIZES = (2, 4, 2, 2, 4)
NAMES = ("z_lo", "x", "core", "z_hi", "y")
SWAP = ((0, 1), (1, 0))
BF = jnp.bfloat16
F32 = jnp.float32
LOG2E = 1.4426950408889634


def attend_kernel(ids_ref, q_ref, near_ref, far_ref, w_ref, out_ref, lat_ref, s_ref, p_ref, *, rows, cuts):
    heads = w_ref.shape[1] // (NOPE + VD)
    m = q_ref.shape[0]
    pairs = near_ref.shape[0]
    keys = 2 * rows * pairs

    @pl.when(pl.program_id(0) == 0)
    def _():
        for i in range(pairs):
            lat_ref[:, 2 * i * rows : (2 * i + 1) * rows] = near_ref[i]
            lat_ref[:, (2 * i + 1) * rows : (2 * i + 2) * rows] = far_ref[i]

    ctx, core = ids_ref[0], ids_ref[1]
    span = keys // cuts
    lane = lax.broadcasted_iota(jnp.int32, (m, rows), 1)
    query = lax.broadcasted_iota(jnp.int32, (m, rows), 0) % rows
    ahead = lane - query
    peak = jnp.full((m, rows), -1e30, F32)
    for j in range(cuts):
        s = jnp.dot(q_ref[...], lat_ref[:, j * span : (j + 1) * span], preferred_element_type=F32)
        for b in range(span // rows):
            block = j * (span // rows) + b
            pos = 2 * (block // 2) + (core if block % 2 == 0 else 1 - core)
            part = s[:, b * rows : (b + 1) * rows]
            part = jnp.where(ahead <= (ctx - pos) * rows, part, F32(-1e30))
            peak = jnp.maximum(peak, part)
            s_ref[:, block * rows : (block + 1) * rows] = part
    top = jnp.max(peak, axis=1, keepdims=True)
    total = jnp.zeros((m, rows), F32)
    for j in range(keys // rows):
        p = jnp.exp2((s_ref[:, j * rows : (j + 1) * rows] - top) * (QK ** (-0.5) * LOG2E))
        total = total + p
        p_ref[:, j * rows : (j + 1) * rows] = p.astype(BF)
    mixed = lax.dot_general(p_ref[...], lat_ref[:KV_RANK], (((1,), (1,)), ((), ())), preferred_element_type=F32)
    mixed = (mixed / jnp.sum(total, axis=1, keepdims=True)).astype(BF)
    for h in range(heads):
        values = w_ref[:, h * (NOPE + VD) + NOPE : (h + 1) * (NOPE + VD)]
        o = jnp.dot(mixed[h * rows : (h + 1) * rows], values, preferred_element_type=F32)
        out_ref[:, h * VD : (h + 1) * VD] = o.astype(BF)


def attend(ids, q, near, far, w_kv, group, cuts):
    pairs, depth, rows = near.shape
    heads = w_kv.shape[1] // (NOPE + VD)
    keys = 2 * rows * pairs
    m = group * rows
    return pl.pallas_call(
        functools.partial(attend_kernel, rows=rows, cuts=cuts),
        grid=(heads // group,),
        in_specs=[
            pl.BlockSpec(memory_space=pltpu.SMEM),
            pl.BlockSpec((m, depth), lambda g: (g, 0)),
            pl.BlockSpec(near.shape, lambda g: (0, 0, 0)),
            pl.BlockSpec(far.shape, lambda g: (0, 0, 0)),
            pl.BlockSpec((KV_RANK, group * (NOPE + VD)), lambda g: (0, g)),
        ],
        out_specs=pl.BlockSpec((rows, group * VD), lambda g: (0, g)),
        out_shape=jax.ShapeDtypeStruct((rows, heads * VD), BF),
        scratch_shapes=[pltpu.VMEM((depth, keys), BF), pltpu.VMEM((m, keys), F32), pltpu.VMEM((m, keys), BF)],
        compiler_params=pltpu.CompilerParams(vmem_limit_bytes=40 * 2**20),
        cost_estimate=pl.CostEstimate(
            flops=2 * heads * rows * keys * (depth + KV_RANK),
            bytes_accessed=8_000_000,
            transcendentals=heads * rows * keys,
        ),
    )(ids, q, near, far, w_kv)


def expert_kernel(x_ref, g_ref, u_ref, d_ref, out_ref, rows_ref, hid_ref, *, first):
    step = pl.program_id(0)

    @pl.when(step == 0)
    def _():
        rows_ref[...] = x_ref[...].reshape(rows_ref.shape)

    @pl.when(step < first)
    def _():
        rows = rows_ref[...]
        gate = jnp.dot(rows, g_ref[...], preferred_element_type=F32)
        upward = jnp.dot(rows, u_ref[...], preferred_element_type=F32)
        hid = (gate / (1.0 + jnp.exp(-gate)) * upward).astype(BF)
        n = g_ref.shape[1]
        for f in range(first):

            @pl.when(step == f)
            def _(f=f):
                hid_ref[:, f * n : (f + 1) * n] = hid

    @pl.when(step >= first)
    def _():
        y = jnp.dot(hid_ref[...], d_ref[...], preferred_element_type=F32).astype(BF)
        out_ref[...] = y.reshape(out_ref.shape)


def expert(x, w_gate, w_up, w_down, first, last):
    units, pair, width = x.shape
    m = units * pair
    hidden = w_gate.shape[1]
    n1, n2 = hidden // first, width // last
    return pl.pallas_call(
        functools.partial(expert_kernel, first=first),
        grid=(first + last,),
        in_specs=[
            pl.BlockSpec(x.shape, lambda i: (0, 0, 0)),
            pl.BlockSpec((width, n1), lambda i: (0, jnp.minimum(i, first - 1))),
            pl.BlockSpec((width, n1), lambda i: (0, jnp.minimum(i, first - 1))),
            pl.BlockSpec((hidden, n2), lambda i: (0, jnp.maximum(i - first, 0))),
        ],
        out_specs=pl.BlockSpec((units, pair, n2), lambda i: (0, 0, jnp.maximum(i - first, 0))),
        out_shape=jax.ShapeDtypeStruct(x.shape, BF),
        scratch_shapes=[pltpu.VMEM((m, width), BF), pltpu.VMEM((m, hidden), BF)],
        compiler_params=pltpu.CompilerParams(vmem_limit_bytes=40 * 2**20),
        cost_estimate=pl.CostEstimate(
            flops=6 * m * width * hidden, bytes_accessed=17_000_000, transcendentals=m * hidden
        ),
    )(x, w_gate, w_up, w_down)


def dispatch_kernel(place_ref, x_ref, out_ref):
    y = jnp.dot(place_ref[...], x_ref[...], preferred_element_type=F32).astype(BF)
    out_ref[...] = y.reshape(out_ref.shape)


def dispatch(place, x, cuts):
    m = place.shape[0]
    tokens, width = x.shape
    n = width // cuts
    return pl.pallas_call(
        dispatch_kernel,
        grid=(cuts,),
        in_specs=[pl.BlockSpec(place.shape, lambda i: (0, 0)), pl.BlockSpec((tokens, n), lambda i: (0, i))],
        out_specs=pl.BlockSpec((m // 2, 2, n), lambda i: (0, 0, i)),
        out_shape=jax.ShapeDtypeStruct((m // 2, 2, width), BF),
        compiler_params=pltpu.CompilerParams(vmem_limit_bytes=32 * 2**20),
        cost_estimate=pl.CostEstimate(
            flops=2 * m * tokens * width, bytes_accessed=2 * m * width + 2 * tokens * width, transcendentals=0
        ),
    )(place, x)


def combine_kernel(*refs):
    *in_refs, own_ref, far_ref = refs
    tok = own_ref.shape[0]
    y = None
    for factors_ref, x_ref in zip(in_refs[::2], in_refs[1::2]):
        rows = x_ref[...].reshape(factors_ref.shape[1], x_ref.shape[2])
        part = jnp.dot(factors_ref[...], rows, preferred_element_type=F32)
        y = part if y is None else y + part
    y = y[: 2 * tok] + y[2 * tok :]
    own_ref[...] = y[:tok]
    far_ref[...] = y[tok:]


def combine(parts, cuts):
    width = parts[0][1].shape[2]
    n = width // cuts
    tok = parts[0][0].shape[0] // 4
    half = pl.BlockSpec((tok, n), lambda i: (0, i))
    in_specs = []
    for factors, x in parts:
        in_specs.append(pl.BlockSpec(factors.shape, lambda i: (0, 0)))
        in_specs.append(pl.BlockSpec((x.shape[0], 2, n), lambda i: (0, 0, i)))
    rows = sum(2 * x.shape[0] for _, x in parts)
    return pl.pallas_call(
        combine_kernel,
        grid=(cuts,),
        in_specs=in_specs,
        out_specs=(half, half),
        out_shape=(jax.ShapeDtypeStruct((tok, width), F32),) * 2,
        compiler_params=pltpu.CompilerParams(vmem_limit_bytes=32 * 2**20),
        cost_estimate=pl.CostEstimate(
            flops=8 * tok * rows * width, bytes_accessed=2 * rows * width, transcendentals=0
        ),
    )(*[a for part in parts for a in part])


def project_kernel(order_ref, own_ref, far_ref, *refs):
    *chunk_refs, left_ref, right_ref, out_ref, x_ref, w_ref = refs
    rows = own_ref.shape[0]
    parts = out_ref.shape[0]
    tok = rows // parts
    for i in range(len(chunk_refs) + 1):
        columns = pl.ds(pl.multiple_of(order_ref[i] * VD, VD), VD)
        x_ref[:rows, i * VD : (i + 1) * VD] = own_ref[:, columns]
        x_ref[rows:, i * VD : (i + 1) * VD] = far_ref[:, columns]
    for i, ref in enumerate(chunk_refs):
        w_ref[i * VD : (i + 1) * VD] = ref[...]
    half = left_ref.shape[1]
    w_ref[len(chunk_refs) * VD :, :half] = left_ref[...]
    w_ref[len(chunk_refs) * VD :, half:] = right_ref[...]
    n = 256
    for c in range(0, w_ref.shape[1], n):
        y = jnp.dot(x_ref[...], w_ref[:, c : c + n], preferred_element_type=F32).astype(BF)
        for e in range(parts):
            out_ref[e, 0, :, c : c + n] = y[e * tok : (e + 1) * tok]
            out_ref[e, 1, :, c : c + n] = y[rows + e * tok : rows + (e + 1) * tok]


def project(order, own, far, chunks, parts):
    rows, depth = own.shape
    width = chunks[0].shape[1]
    whole = pl.BlockSpec(memory_space=pltpu.VMEM)
    return pl.pallas_call(
        project_kernel,
        in_specs=[pl.BlockSpec(memory_space=pltpu.SMEM)] + [whole] * (2 + len(chunks)),
        out_specs=whole,
        out_shape=jax.ShapeDtypeStruct((parts, 2, rows // parts, width), BF),
        scratch_shapes=[pltpu.VMEM((2 * rows, depth), BF), pltpu.VMEM((depth, width), BF)],
        compiler_params=pltpu.CompilerParams(vmem_limit_bytes=32 * 2**20),
        cost_estimate=pl.CostEstimate(
            flops=4 * rows * depth * width, bytes_accessed=2 * depth * width, transcendentals=0
        ),
    )(order, own, far, *chunks)


def swap(mine):
    return lax.ppermute(mine, "core", SWAP)


def own_w_out(w_out):
    core = lax.axis_index("core")
    half = w_out.shape[1] // 2
    lower, upper = w_out[:, :half], w_out[:, half:]
    mine = jnp.where(core == 0, lower, upper)
    other = swap(jnp.where(core == 0, upper, lower))
    return jnp.concatenate([jnp.where(core == 0, mine, other), jnp.where(core == 0, other, mine)], axis=0)


def up(a):
    return lax.ppermute(a, "x", [(i, (i + 1) % 4) for i in range(4)])


def down(a):
    return lax.ppermute(a, "x", [(i, (i + 3) % 4) for i in range(4)])


def across(a):
    return lax.ppermute(a, "z_lo", SWAP)


def chip_order():
    x, z = lax.axis_index("x"), lax.axis_index("z_lo")
    chip = lambda zz, dx: zz * 4 + lax.rem(x + 4 + dx, 4)
    near, far = z, 1 - z
    order = [chip(near, 0), chip(far, 0), chip(near, -1), chip(near, 1)]
    order += [chip(far, -1), chip(far, 1), chip(near, 2), chip(far, 2)]
    return jnp.stack(order).astype(jnp.int32)


def latent_queries(queries, w_kv):
    rows = queries.shape[0]
    heads = queries.shape[1] // QK
    q = queries.reshape(rows, heads, QK)
    keys = w_kv.reshape(KV_RANK, heads, NOPE + VD)[:, :, :NOPE]
    q_lat = jnp.einsum("qhd,rhd->hqr", q[:, :, :NOPE], keys, preferred_element_type=F32).astype(BF)
    q_all = jnp.concatenate([q_lat, q[:, :, NOPE:].transpose(1, 0, 2)], axis=2)
    return q_all.reshape(heads * rows, -1)


def routing(routes, codes):
    tok = routes.shape[0]
    core = lax.axis_index("core")
    code_float = codes.astype(F32)
    mix = code_float / jnp.sum(code_float, axis=1, keepdims=True)
    routes2, mix2 = jnp.stack([routes, swap(routes)]), jnp.stack([mix, swap(mix)])
    chosen = routes2[:, :, :, None] == jnp.arange(64, dtype=jnp.int32)
    weight = jnp.sum(jnp.where(chosen, mix2[..., None], F32(0.0)), axis=2)
    has = jnp.any(chosen, axis=2)

    def of_core(a):
        a = a.reshape(2, tok, 8, 2, 4)
        return jnp.where(core == 0, a[:, :, :, 0], a[:, :, :, 1]).reshape(2, tok, 32)

    weight, has = of_core(weight), of_core(has)
    count = has.astype(jnp.int32)
    slot = jnp.cumsum(count, axis=1) - count
    place = has[:, :, :, None] & (slot[:, :, :, None] == jnp.arange(CAP, dtype=jnp.int32))
    place = place.transpose(2, 3, 0, 1)[:, :, :, None, :]
    same = jnp.arange(2)[:, None, None] == jnp.arange(2)[None, :, None]
    place = (place & same).reshape(32, CAP, 2, 2 * tok)
    place = jnp.broadcast_to(place[:, None], (32, 2, CAP, 2, 2 * tok)).reshape(64, CAP, 2, 2 * tok)
    gains = weight.transpose(2, 0, 1).reshape(32, 2 * tok)
    gains = jnp.broadcast_to(gains[:, None], (32, 2, 2 * tok)).reshape(64, 1, 1, 2 * tok)
    factors = jnp.where(place, gains, F32(0.0))
    high = lax.reduce_precision(factors, 8, 7)
    factors = jnp.concatenate([high, factors - high], axis=3).astype(BF)
    place = place.astype(BF)
    parts = []
    for slots in SLOTS:
        parts.append((place[:, slots].reshape(-1, 2 * tok), factors[:, slots].reshape(-1, 4 * tok).T))
    return parts


def local(queries, latents, w_kv, w_out, resid, norm_gain, routes, codes, w_gate, w_up, w_down):
    tok, width = resid.shape
    chips = 64
    core = lax.axis_index("core")
    chunk = own_w_out(w_out)
    mate, before, after = across(chunk), up(chunk), down(chunk)
    near = lax.all_to_all(
        jnp.broadcast_to(latents[None], (8,) + latents.shape), CTX_CHIPS, split_axis=0, concat_axis=0, tiled=True
    )
    q = latent_queries(queries, w_kv)
    near, q, mate, before, after = lax.optimization_barrier((near, q, mate, before, after))
    far = swap(near)
    mate_before, mate_after, opposite = up(mate), across(after), down(after)
    ids = jnp.stack([lax.axis_index(CTX), core]).astype(jnp.int32)
    heads_out = attend(ids, q, near, far, w_kv, 4, 4)
    heads_out, mate_before, mate_after, opposite = lax.optimization_barrier(
        (heads_out, mate_before, mate_after, opposite)
    )
    part = chunk.shape[1] // 2
    left, right = up(mate_before[:, :part]), down(mate_after[:, part:])
    chunks = (chunk, mate, before, after, mate_before, mate_after, opposite, left, right)
    order = chip_order()
    half = width // 2
    lower, upper = resid[:, :half], resid[:, half:]
    resid2 = jnp.stack([jnp.where(core == 0, lower, upper), swap(jnp.where(core == 0, upper, lower))])
    attn = project(order, heads_out, swap(heads_out), chunks, 8)
    attn = lax.all_to_all(attn, EP, split_axis=0, concat_axis=0, tiled=True)
    summed = (resid2.astype(F32) + jnp.sum(attn.astype(F32), axis=0)).astype(BF)
    others = swap(summed)[::-1]
    attended2 = jnp.concatenate(
        [jnp.where(core == 0, summed, others), jnp.where(core == 0, others, summed)], axis=2
    ).reshape(2 * tok, width)
    attended = attended2[:tok]
    wide2 = attended2.astype(F32)
    meansq = jnp.mean(wide2 * wide2, axis=1, keepdims=True)
    normed2 = (wide2 * lax.rsqrt(meansq + 1e-06) * norm_gain[None, :]).astype(BF)

    def exchange(rows):
        units = rows.reshape(chips, -1, 2, width)
        units = lax.all_to_all(units, CHIPS, split_axis=0, concat_axis=0, tiled=True)
        return units.reshape(rows.shape)

    parts = routing(routes, codes)
    arrived = [exchange(dispatch(place, normed2, 7)) for place, _ in parts]
    returned = [exchange(expert(rows, w_gate[0], w_up[0], w_down[0], 2, 7)) for rows in arrived]
    own, theirs = combine([(factors, rows) for (_, factors), rows in zip(parts, returned)], 7)
    layer_out = (wide2[:tok] + own + swap(theirs)).astype(BF)
    return (attended, layer_out)


def solution(mesh):
    fine = Mesh(mesh.devices.reshape(SIZES), NAMES)
    rows = P(CTX + EP, None)
    heads = P(CTX + EP, None, None)
    placed = (
        P(CTX, EP),
        P(None, CTX),
        P(None, EP),
        P(EP + CTX, None),
        rows,
        P(),
        rows,
        rows,
        heads,
        heads,
        heads,
    )
    return jax.shard_map(local, mesh=fine, in_specs=placed, out_specs=(rows, rows), check_vma=False)
```

```python
import functools

import jax
import jax.numpy as jnp
from jax import lax
from jax.experimental import pallas as pl
from jax.experimental.pallas import tpu as pltpu
from jax.sharding import Mesh, PartitionSpec as P

NOPE = 128
VD = 128
KV_RANK = 512
TOP = 8
QK = 192
CAP = 3
SLOTS = (slice(0, 3),)

CTX = ("z_lo", "x", "core")
CTX_CHIPS = ("z_lo", "x")
EP = ("z_hi", "y")
CHIPS = ("z_lo", "x", "z_hi", "y")
SIZES = (2, 4, 2, 2, 4)
NAMES = ("z_lo", "x", "core", "z_hi", "y")
SWAP = ((0, 1), (1, 0))
BF = jnp.bfloat16
F32 = jnp.float32
LOG2E = 1.4426950408889634


def attend_kernel(ids_ref, q_ref, w_ref, *refs, rows, cuts):
    *piece_refs, out_ref, lat_ref, s_ref, p_ref = refs
    heads = w_ref.shape[1] // (NOPE + VD)
    m = q_ref.shape[0]
    keys = lat_ref.shape[1]
    ctx, core, odd = ids_ref[0], ids_ref[1], ids_ref[2]

    @pl.when(pl.program_id(0) == 0)
    def _():
        for side in range(2):
            whole, lower, upper = piece_refs[3 * side : 3 * side + 3]
            pairs, depth, _ = whole.shape
            mine = pl.ds(pl.multiple_of(odd * depth, 32), depth)
            rest = pl.ds(pl.multiple_of((1 - odd) * depth, 32), depth)
            for i in range(pairs):
                first = (2 * i + side) * rows
                lat_ref[mine, first : first + rows] = whole[i]
                half = lower if i < pairs // 2 else upper
                lat_ref[rest, first : first + rows] = half[i % (pairs // 2)]

    span = keys // cuts
    lane = lax.broadcasted_iota(jnp.int32, (m, rows), 1)
    query = lax.broadcasted_iota(jnp.int32, (m, rows), 0) % rows
    ahead = lane - query
    peak = jnp.full((m, rows), -1e30, F32)
    for j in range(cuts):
        s = jnp.dot(q_ref[...], lat_ref[:, j * span : (j + 1) * span], preferred_element_type=F32)
        for b in range(span // rows):
            block = j * (span // rows) + b
            pos = 2 * (block // 2) + (core if block % 2 == 0 else 1 - core)
            part = s[:, b * rows : (b + 1) * rows]
            part = jnp.where(ahead <= (ctx - pos) * rows, part, F32(-1e30))
            peak = jnp.maximum(peak, part)
            s_ref[:, block * rows : (block + 1) * rows] = part
    top = jnp.max(peak, axis=1, keepdims=True)
    total = jnp.zeros((m, rows), F32)
    for j in range(keys // rows):
        p = jnp.exp2((s_ref[:, j * rows : (j + 1) * rows] - top) * (QK ** (-0.5) * LOG2E))
        total = total + p
        p_ref[:, j * rows : (j + 1) * rows] = p.astype(BF)
    mixed = lax.dot_general(p_ref[...], lat_ref[:KV_RANK], (((1,), (1,)), ((), ())), preferred_element_type=F32)
    mixed = (mixed / jnp.sum(total, axis=1, keepdims=True)).astype(BF)
    for h in range(heads):
        values = w_ref[:, h * (NOPE + VD) + NOPE : (h + 1) * (NOPE + VD)]
        o = jnp.dot(mixed[h * rows : (h + 1) * rows], values, preferred_element_type=F32)
        out_ref[:, h * VD : (h + 1) * VD] = o.astype(BF)


def attend(ids, q, w_kv, near, far, group, cuts):
    pairs, half, rows = near[0].shape
    depth = 2 * half
    heads = w_kv.shape[1] // (NOPE + VD)
    keys = 2 * rows * pairs
    m = group * rows
    pieces = (*near, *far)
    return pl.pallas_call(
        functools.partial(attend_kernel, rows=rows, cuts=cuts),
        grid=(heads // group,),
        in_specs=[
            pl.BlockSpec(memory_space=pltpu.SMEM),
            pl.BlockSpec((m, depth), lambda g: (g, 0)),
            pl.BlockSpec((KV_RANK, group * (NOPE + VD)), lambda g: (0, g)),
        ]
        + [pl.BlockSpec(a.shape, lambda g: (0, 0, 0)) for a in pieces],
        out_specs=pl.BlockSpec((rows, group * VD), lambda g: (0, g)),
        out_shape=jax.ShapeDtypeStruct((rows, heads * VD), BF),
        scratch_shapes=[pltpu.VMEM((depth, keys), BF), pltpu.VMEM((m, keys), F32), pltpu.VMEM((m, keys), BF)],
        compiler_params=pltpu.CompilerParams(vmem_limit_bytes=28 * 2**20),
        cost_estimate=pl.CostEstimate(
            flops=2 * heads * rows * keys * (depth + KV_RANK),
            bytes_accessed=8_000_000,
            transcendentals=heads * rows * keys,
        ),
    )(ids, q, w_kv, *pieces)


def expert_kernel(x_ref, g_ref, u_ref, d_ref, out_ref, rows_ref, hid_ref, *, first):
    step = pl.program_id(0)

    @pl.when(step == 0)
    def _():
        rows_ref[...] = x_ref[...].reshape(rows_ref.shape)

    @pl.when(step < first)
    def _():
        rows = rows_ref[...]
        gate = jnp.dot(rows, g_ref[...], preferred_element_type=F32)
        upward = jnp.dot(rows, u_ref[...], preferred_element_type=F32)
        hid = (gate / (1.0 + jnp.exp(-gate)) * upward).astype(BF)
        n = g_ref.shape[1]
        for f in range(first):

            @pl.when(step == f)
            def _(f=f):
                hid_ref[:, f * n : (f + 1) * n] = hid

    @pl.when(step >= first)
    def _():
        y = jnp.dot(hid_ref[...], d_ref[...], preferred_element_type=F32).astype(BF)
        out_ref[...] = y.reshape(out_ref.shape)


def expert(x, w_gate, w_up, w_down, first, last):
    units, pair, width = x.shape
    m = units * pair
    hidden = w_gate.shape[1]
    n1, n2 = hidden // first, width // last
    return pl.pallas_call(
        functools.partial(expert_kernel, first=first),
        grid=(first + last,),
        in_specs=[
            pl.BlockSpec(x.shape, lambda i: (0, 0, 0)),
            pl.BlockSpec((width, n1), lambda i: (0, jnp.minimum(i, first - 1))),
            pl.BlockSpec((width, n1), lambda i: (0, jnp.minimum(i, first - 1))),
            pl.BlockSpec((hidden, n2), lambda i: (0, jnp.maximum(i - first, 0))),
        ],
        out_specs=pl.BlockSpec((units, pair, n2), lambda i: (0, 0, jnp.maximum(i - first, 0))),
        out_shape=jax.ShapeDtypeStruct(x.shape, BF),
        scratch_shapes=[pltpu.VMEM((m, width), BF), pltpu.VMEM((m, hidden), BF)],
        compiler_params=pltpu.CompilerParams(vmem_limit_bytes=28 * 2**20),
        cost_estimate=pl.CostEstimate(
            flops=6 * m * width * hidden, bytes_accessed=17_000_000, transcendentals=m * hidden
        ),
    )(x, w_gate, w_up, w_down)


def dispatch_kernel(place_ref, x_ref, out_ref):
    y = jnp.dot(place_ref[...], x_ref[...], preferred_element_type=F32).astype(BF)
    out_ref[...] = y.reshape(out_ref.shape)


def dispatch(place, x, cuts):
    m = place.shape[0]
    tokens, width = x.shape
    n = width // cuts
    return pl.pallas_call(
        dispatch_kernel,
        grid=(cuts,),
        in_specs=[pl.BlockSpec(place.shape, lambda i: (0, 0)), pl.BlockSpec((tokens, n), lambda i: (0, i))],
        out_specs=pl.BlockSpec((m // 2, 2, n), lambda i: (0, 0, i)),
        out_shape=jax.ShapeDtypeStruct((m // 2, 2, width), BF),
        compiler_params=pltpu.CompilerParams(vmem_limit_bytes=16 * 2**20),
        cost_estimate=pl.CostEstimate(
            flops=2 * m * tokens * width, bytes_accessed=2 * m * width + 2 * tokens * width, transcendentals=0
        ),
    )(place, x)


def combine_kernel(*refs):
    *in_refs, own_ref, far_ref = refs
    tok = own_ref.shape[0]
    y = None
    for factors_ref, x_ref in zip(in_refs[::2], in_refs[1::2]):
        rows = x_ref[...].reshape(factors_ref.shape[1], x_ref.shape[2])
        part = jnp.dot(factors_ref[...], rows, preferred_element_type=F32)
        y = part if y is None else y + part
    y = y[: 2 * tok] + y[2 * tok :]
    own_ref[...] = y[:tok]
    far_ref[...] = y[tok:]


def combine(parts, cuts):
    width = parts[0][1].shape[2]
    n = width // cuts
    tok = parts[0][0].shape[0] // 4
    half = pl.BlockSpec((tok, n), lambda i: (0, i))
    in_specs = []
    for factors, x in parts:
        in_specs.append(pl.BlockSpec(factors.shape, lambda i: (0, 0)))
        in_specs.append(pl.BlockSpec((x.shape[0], 2, n), lambda i: (0, 0, i)))
    rows = sum(2 * x.shape[0] for _, x in parts)
    return pl.pallas_call(
        combine_kernel,
        grid=(cuts,),
        in_specs=in_specs,
        out_specs=(half, half),
        out_shape=(jax.ShapeDtypeStruct((tok, width), F32),) * 2,
        compiler_params=pltpu.CompilerParams(vmem_limit_bytes=16 * 2**20),
        cost_estimate=pl.CostEstimate(
            flops=8 * tok * rows * width, bytes_accessed=2 * rows * width, transcendentals=0
        ),
    )(*[a for part in parts for a in part])


def project_kernel(order_ref, own_ref, far_ref, *refs):
    *chunk_refs, left_ref, right_ref, out_ref, x_ref, w_ref = refs
    rows = own_ref.shape[0]
    parts = out_ref.shape[0]
    tok = rows // parts
    for i in range(len(chunk_refs) + 1):
        columns = pl.ds(pl.multiple_of(order_ref[i] * VD, VD), VD)
        x_ref[:rows, i * VD : (i + 1) * VD] = own_ref[:, columns]
        x_ref[rows:, i * VD : (i + 1) * VD] = far_ref[:, columns]
    for i, ref in enumerate(chunk_refs):
        w_ref[i * VD : (i + 1) * VD] = ref[...]
    half = left_ref.shape[1]
    w_ref[len(chunk_refs) * VD :, :half] = left_ref[...]
    w_ref[len(chunk_refs) * VD :, half:] = right_ref[...]
    n = 256
    for c in range(0, w_ref.shape[1], n):
        y = jnp.dot(x_ref[...], w_ref[:, c : c + n], preferred_element_type=F32).astype(BF)
        for e in range(parts):
            out_ref[e, 0, :, c : c + n] = y[e * tok : (e + 1) * tok]
            out_ref[e, 1, :, c : c + n] = y[rows + e * tok : rows + (e + 1) * tok]


def project(order, own, far, chunks, parts):
    rows, depth = own.shape
    width = chunks[0].shape[1]
    whole = pl.BlockSpec(memory_space=pltpu.VMEM)
    return pl.pallas_call(
        project_kernel,
        in_specs=[pl.BlockSpec(memory_space=pltpu.SMEM)] + [whole] * (2 + len(chunks)),
        out_specs=whole,
        out_shape=jax.ShapeDtypeStruct((parts, 2, rows // parts, width), BF),
        scratch_shapes=[pltpu.VMEM((2 * rows, depth), BF), pltpu.VMEM((depth, width), BF)],
        compiler_params=pltpu.CompilerParams(vmem_limit_bytes=16 * 2**20),
        cost_estimate=pl.CostEstimate(
            flops=4 * rows * depth * width, bytes_accessed=2 * depth * width, transcendentals=0
        ),
    )(order, own, far, *chunks)


def swap(mine):
    return lax.ppermute(mine, "core", SWAP)


def own_w_out(w_out):
    core = lax.axis_index("core")
    half = w_out.shape[1] // 2
    lower, upper = w_out[:, :half], w_out[:, half:]
    mine = jnp.where(core == 0, lower, upper)
    other = swap(jnp.where(core == 0, upper, lower))
    return jnp.concatenate([jnp.where(core == 0, mine, other), jnp.where(core == 0, other, mine)], axis=0)


def up(a):
    return lax.ppermute(a, "x", [(i, (i + 1) % 4) for i in range(4)])


def down(a):
    return lax.ppermute(a, "x", [(i, (i + 3) % 4) for i in range(4)])


def across(a):
    return lax.ppermute(a, "z_lo", SWAP)


def chip_order():
    x, z = lax.axis_index("x"), lax.axis_index("z_lo")
    chip = lambda zz, dx: zz * 4 + lax.rem(x + 4 + dx, 4)
    near, far = z, 1 - z
    order = [chip(near, 0), chip(far, 0), chip(near, -1), chip(near, 1)]
    order += [chip(far, -1), chip(far, 1), chip(near, 2), chip(far, 2)]
    return jnp.stack(order).astype(jnp.int32)


def latent_queries(queries, w_kv):
    rows = queries.shape[0]
    heads = queries.shape[1] // QK
    q = queries.reshape(rows, heads, QK)
    keys = w_kv.reshape(KV_RANK, heads, NOPE + VD)[:, :, :NOPE]
    q_lat = jnp.einsum("qhd,rhd->hqr", q[:, :, :NOPE], keys, preferred_element_type=F32).astype(BF)
    q_all = jnp.concatenate([q_lat, q[:, :, NOPE:].transpose(1, 0, 2)], axis=2)
    return q_all.reshape(heads * rows, -1)


def routing(routes, codes):
    tok = routes.shape[0]
    core = lax.axis_index("core")
    code_float = codes.astype(F32)
    mix = code_float / jnp.sum(code_float, axis=1, keepdims=True)
    routes2, mix2 = jnp.stack([routes, swap(routes)]), jnp.stack([mix, swap(mix)])
    chosen = routes2[:, :, :, None] == jnp.arange(64, dtype=jnp.int32)
    weight = jnp.sum(jnp.where(chosen, mix2[..., None], F32(0.0)), axis=2)
    has = jnp.any(chosen, axis=2)

    def of_core(a):
        a = a.reshape(2, tok, 8, 2, 4)
        return jnp.where(core == 0, a[:, :, :, 0], a[:, :, :, 1]).reshape(2, tok, 32)

    weight, has = of_core(weight), of_core(has)
    count = has.astype(jnp.int32)
    slot = jnp.cumsum(count, axis=1) - count
    place = has[:, :, :, None] & (slot[:, :, :, None] == jnp.arange(CAP, dtype=jnp.int32))
    place = place.transpose(2, 3, 0, 1)[:, :, :, None, :]
    same = jnp.arange(2)[:, None, None] == jnp.arange(2)[None, :, None]
    place = (place & same).reshape(32, CAP, 2, 2 * tok)
    place = jnp.broadcast_to(place[:, None], (32, 2, CAP, 2, 2 * tok)).reshape(64, CAP, 2, 2 * tok)
    gains = weight.transpose(2, 0, 1).reshape(32, 2 * tok)
    gains = jnp.broadcast_to(gains[:, None], (32, 2, 2 * tok)).reshape(64, 1, 1, 2 * tok)
    factors = jnp.where(place, gains, F32(0.0))
    high = lax.reduce_precision(factors, 8, 7)
    factors = jnp.concatenate([high, factors - high], axis=3).astype(BF)
    place = place.astype(BF)
    parts = []
    for slots in SLOTS:
        parts.append((place[:, slots].reshape(-1, 2 * tok), factors[:, slots].reshape(-1, 4 * tok).T))
    return parts


def local(queries, latents, w_kv, w_out, resid, norm_gain, routes, codes, w_gate, w_up, w_down):
    tok, width = resid.shape
    chips = 64
    core = lax.axis_index("core")
    odd = lax.rem(lax.axis_index("y"), 2)
    depth = latents.shape[0] // 2
    mine = lax.dynamic_slice_in_dim(latents, odd * depth, depth, axis=0)
    fetched = lax.all_to_all(
        jnp.broadcast_to(mine[None], (8,) + mine.shape), CTX_CHIPS, split_axis=0, concat_axis=0, tiled=True
    )
    chunk = own_w_out(w_out)
    q = latent_queries(queries, w_kv)
    fetched, chunk, q = lax.optimization_barrier((fetched, chunk, q))
    lower = lax.ppermute(fetched[:4], "y", [(i, (i + 1) % 4) for i in range(4)])
    upper = lax.ppermute(fetched[4:], "y", [(i, (i + 3) % 4) for i in range(4)])
    far = swap(fetched)
    mate, before, after = across(chunk), up(chunk), down(chunk)
    lower, upper, far, mate, before, after = lax.optimization_barrier((lower, upper, far, mate, before, after))
    ids = jnp.stack([lax.axis_index(CTX), core, odd]).astype(jnp.int32)
    mate_before, mate_after, opposite = up(mate), across(after), down(after)
    heads_out = attend(ids, q, w_kv, (fetched, lower, upper), (far, swap(lower), swap(upper)), 4, 4)
    heads_out, mate_before, mate_after, opposite = lax.optimization_barrier(
        (heads_out, mate_before, mate_after, opposite)
    )
    part = chunk.shape[1] // 2
    left, right = up(mate_before[:, :part]), down(mate_after[:, part:])
    chunks = (chunk, mate, before, after, mate_before, mate_after, opposite, left, right)
    order = chip_order()
    half = width // 2
    lower, upper = resid[:, :half], resid[:, half:]
    resid2 = jnp.stack([jnp.where(core == 0, lower, upper), swap(jnp.where(core == 0, upper, lower))])
    attn = project(order, heads_out, swap(heads_out), chunks, 8)
    attn = lax.all_to_all(attn, EP, split_axis=0, concat_axis=0, tiled=True)
    summed = (resid2.astype(F32) + jnp.sum(attn.astype(F32), axis=0)).astype(BF)
    others = swap(summed)[::-1]
    attended2 = jnp.concatenate(
        [jnp.where(core == 0, summed, others), jnp.where(core == 0, others, summed)], axis=2
    ).reshape(2 * tok, width)
    attended = attended2[:tok]
    wide2 = attended2.astype(F32)
    meansq = jnp.mean(wide2 * wide2, axis=1, keepdims=True)
    normed2 = (wide2 * lax.rsqrt(meansq + 1e-06) * norm_gain[None, :]).astype(BF)

    def exchange(rows):
        units = rows.reshape(chips, -1, 2, width)
        units = lax.all_to_all(units, CHIPS, split_axis=0, concat_axis=0, tiled=True)
        return units.reshape(rows.shape)

    parts = routing(routes, codes)
    arrived = [exchange(dispatch(place, normed2, 7)) for place, _ in parts]
    returned = [exchange(expert(rows, w_gate[0], w_up[0], w_down[0], 2, 7)) for rows in arrived]
    own, theirs = combine([(factors, rows) for (_, factors), rows in zip(parts, returned)], 7)
    layer_out = (wide2[:tok] + own + swap(theirs)).astype(BF)
    return (attended, layer_out)


def solution(mesh):
    fine = Mesh(mesh.devices.reshape(SIZES), NAMES)
    rows = P(CTX + EP, None)
    heads = P(CTX + EP, None, None)
    placed = (
        P(CTX, EP),
        P(None, CTX),
        P(None, EP),
        P(EP + CTX, None),
        rows,
        P(),
        rows,
        rows,
        heads,
        heads,
        heads,
    )
    return jax.shard_map(local, mesh=fine, in_specs=placed, out_specs=(rows, rows), check_vma=False)
```

```python
import functools

import jax
import jax.numpy as jnp
from jax import lax
from jax.experimental import pallas as pl
from jax.experimental.pallas import tpu as pltpu
from jax.sharding import Mesh, PartitionSpec as P

NOPE = 128
VD = 128
KV_RANK = 512
TOP = 8
QK = 192
CAP = 3
CARRIED = 1024
SLOTS = (slice(0, 3),)

CTX = ("z_lo", "x", "core")
CTX_CHIPS = ("z_lo", "x")
EP = ("z_hi", "y")
CHIPS = ("z_lo", "x", "z_hi", "y")
SIZES = (2, 4, 2, 2, 4)
NAMES = ("z_lo", "x", "core", "z_hi", "y")
SWAP = ((0, 1), (1, 0))
BF = jnp.bfloat16
F32 = jnp.float32
LOG2E = 1.4426950408889634


def attend_kernel(ids_ref, q_ref, near_ref, far_ref, w_ref, out_ref, lat_ref, s_ref, p_ref, *, rows, cuts):
    heads = w_ref.shape[1] // (NOPE + VD)
    m = q_ref.shape[0]
    pairs = near_ref.shape[0]
    keys = 2 * rows * pairs

    @pl.when(pl.program_id(0) == 0)
    def _():
        for i in range(pairs):
            lat_ref[:, 2 * i * rows : (2 * i + 1) * rows] = near_ref[i]
            lat_ref[:, (2 * i + 1) * rows : (2 * i + 2) * rows] = far_ref[i]

    ctx, core = ids_ref[0], ids_ref[1]
    span = keys // cuts
    lane = lax.broadcasted_iota(jnp.int32, (m, rows), 1)
    query = lax.broadcasted_iota(jnp.int32, (m, rows), 0) % rows
    ahead = lane - query
    peak = jnp.full((m, rows), -1e30, F32)
    for j in range(cuts):
        s = jnp.dot(q_ref[...], lat_ref[:, j * span : (j + 1) * span], preferred_element_type=F32)
        for b in range(span // rows):
            block = j * (span // rows) + b
            pos = 2 * (block // 2) + (core if block % 2 == 0 else 1 - core)
            part = s[:, b * rows : (b + 1) * rows]
            part = jnp.where(ahead <= (ctx - pos) * rows, part, F32(-1e30))
            peak = jnp.maximum(peak, part)
            s_ref[:, block * rows : (block + 1) * rows] = part
    top = jnp.max(peak, axis=1, keepdims=True)
    total = jnp.zeros((m, rows), F32)
    for j in range(keys // rows):
        p = jnp.exp2((s_ref[:, j * rows : (j + 1) * rows] - top) * (QK ** (-0.5) * LOG2E))
        total = total + p
        p_ref[:, j * rows : (j + 1) * rows] = p.astype(BF)
    mixed = lax.dot_general(p_ref[...], lat_ref[:KV_RANK], (((1,), (1,)), ((), ())), preferred_element_type=F32)
    mixed = (mixed / jnp.sum(total, axis=1, keepdims=True)).astype(BF)
    for h in range(heads):
        values = w_ref[:, h * (NOPE + VD) + NOPE : (h + 1) * (NOPE + VD)]
        o = jnp.dot(mixed[h * rows : (h + 1) * rows], values, preferred_element_type=F32)
        out_ref[:, h * VD : (h + 1) * VD] = o.astype(BF)


def attend(ids, q, near, far, w_kv, group, cuts):
    pairs, depth, rows = near.shape
    heads = w_kv.shape[1] // (NOPE + VD)
    keys = 2 * rows * pairs
    m = group * rows
    return pl.pallas_call(
        functools.partial(attend_kernel, rows=rows, cuts=cuts),
        grid=(heads // group,),
        in_specs=[
            pl.BlockSpec(memory_space=pltpu.SMEM),
            pl.BlockSpec((m, depth), lambda g: (g, 0)),
            pl.BlockSpec(near.shape, lambda g: (0, 0, 0)),
            pl.BlockSpec(far.shape, lambda g: (0, 0, 0)),
            pl.BlockSpec((KV_RANK, group * (NOPE + VD)), lambda g: (0, g)),
        ],
        out_specs=pl.BlockSpec((rows, group * VD), lambda g: (0, g)),
        out_shape=jax.ShapeDtypeStruct((rows, heads * VD), BF),
        scratch_shapes=[pltpu.VMEM((depth, keys), BF), pltpu.VMEM((m, keys), F32), pltpu.VMEM((m, keys), BF)],
        compiler_params=pltpu.CompilerParams(vmem_limit_bytes=40 * 2**20),
        cost_estimate=pl.CostEstimate(
            flops=2 * heads * rows * keys * (depth + KV_RANK),
            bytes_accessed=8_000_000,
            transcendentals=heads * rows * keys,
        ),
    )(ids, q, near, far, w_kv)


def expert_kernel(x_ref, g_ref, u_ref, d_ref, out_ref, rows_ref, hid_ref, *, first):
    step = pl.program_id(0)

    @pl.when(step == 0)
    def _():
        rows_ref[...] = x_ref[...].reshape(rows_ref.shape)

    @pl.when(step < first)
    def _():
        rows = rows_ref[...]
        gate = jnp.dot(rows, g_ref[...], preferred_element_type=F32)
        upward = jnp.dot(rows, u_ref[...], preferred_element_type=F32)
        hid = (gate / (1.0 + jnp.exp(-gate)) * upward).astype(BF)
        n = g_ref.shape[1]
        for f in range(first):

            @pl.when(step == f)
            def _(f=f):
                hid_ref[:, f * n : (f + 1) * n] = hid

    @pl.when(step >= first)
    def _():
        y = jnp.dot(hid_ref[...], d_ref[...], preferred_element_type=F32).astype(BF)
        out_ref[...] = y.reshape(out_ref.shape)


def expert(x, w_gate, w_up, w_down, first, last):
    units, pair, width = x.shape
    m = units * pair
    hidden = w_gate.shape[1]
    n1, n2 = hidden // first, width // last
    return pl.pallas_call(
        functools.partial(expert_kernel, first=first),
        grid=(first + last,),
        in_specs=[
            pl.BlockSpec(x.shape, lambda i: (0, 0, 0)),
            pl.BlockSpec((width, n1), lambda i: (0, jnp.minimum(i, first - 1))),
            pl.BlockSpec((width, n1), lambda i: (0, jnp.minimum(i, first - 1))),
            pl.BlockSpec((hidden, n2), lambda i: (0, jnp.maximum(i - first, 0))),
        ],
        out_specs=pl.BlockSpec((units, pair, n2), lambda i: (0, 0, jnp.maximum(i - first, 0))),
        out_shape=jax.ShapeDtypeStruct(x.shape, BF),
        scratch_shapes=[pltpu.VMEM((m, width), BF), pltpu.VMEM((m, hidden), BF)],
        compiler_params=pltpu.CompilerParams(vmem_limit_bytes=40 * 2**20),
        cost_estimate=pl.CostEstimate(
            flops=6 * m * width * hidden, bytes_accessed=17_000_000, transcendentals=m * hidden
        ),
    )(x, w_gate, w_up, w_down)


def dispatch_kernel(place_ref, x_ref, out_ref):
    y = jnp.dot(place_ref[...], x_ref[...], preferred_element_type=F32).astype(BF)
    out_ref[...] = y.reshape(out_ref.shape)


def dispatch(place, x, cuts):
    m = place.shape[0]
    tokens, width = x.shape
    n = width // cuts
    return pl.pallas_call(
        dispatch_kernel,
        grid=(cuts,),
        in_specs=[pl.BlockSpec(place.shape, lambda i: (0, 0)), pl.BlockSpec((tokens, n), lambda i: (0, i))],
        out_specs=pl.BlockSpec((m // 2, 2, n), lambda i: (0, 0, i)),
        out_shape=jax.ShapeDtypeStruct((m // 2, 2, width), BF),
        compiler_params=pltpu.CompilerParams(vmem_limit_bytes=32 * 2**20),
        cost_estimate=pl.CostEstimate(
            flops=2 * m * tokens * width, bytes_accessed=2 * m * width + 2 * tokens * width, transcendentals=0
        ),
    )(place, x)


def combine_kernel(*refs):
    *in_refs, own_ref, far_ref = refs
    tok = own_ref.shape[0]
    y = None
    for factors_ref, x_ref in zip(in_refs[::2], in_refs[1::2]):
        rows = x_ref[...].reshape(factors_ref.shape[1], x_ref.shape[2])
        part = jnp.dot(factors_ref[...], rows, preferred_element_type=F32)
        y = part if y is None else y + part
    y = y[: 2 * tok] + y[2 * tok :]
    own_ref[...] = y[:tok]
    far_ref[...] = y[tok:]


def combine(parts, cuts):
    width = parts[0][1].shape[2]
    n = width // cuts
    tok = parts[0][0].shape[0] // 4
    half = pl.BlockSpec((tok, n), lambda i: (0, i))
    in_specs = []
    for factors, x in parts:
        in_specs.append(pl.BlockSpec(factors.shape, lambda i: (0, 0)))
        in_specs.append(pl.BlockSpec((x.shape[0], 2, n), lambda i: (0, 0, i)))
    rows = sum(2 * x.shape[0] for _, x in parts)
    return pl.pallas_call(
        combine_kernel,
        grid=(cuts,),
        in_specs=in_specs,
        out_specs=(half, half),
        out_shape=(jax.ShapeDtypeStruct((tok, width), F32),) * 2,
        compiler_params=pltpu.CompilerParams(vmem_limit_bytes=32 * 2**20),
        cost_estimate=pl.CostEstimate(
            flops=8 * tok * rows * width, bytes_accessed=2 * rows * width, transcendentals=0
        ),
    )(*[a for part in parts for a in part])


def project_kernel(order_ref, own_ref, far_ref, gathered_ref, *refs):
    *chunk_refs, left_ref, right_ref, out_ref, x_ref, w_ref = refs
    rows = own_ref.shape[0]
    parts = out_ref.shape[0]
    tok = rows // parts

    def multiply(weights_ref, first):
        n = 256
        for c in range(0, weights_ref.shape[1], n):
            y = jnp.dot(x_ref[...], weights_ref[:, c : c + n], preferred_element_type=F32).astype(BF)
            for e in range(parts):
                out_ref[e, 0, :, first + c : first + c + n] = y[e * tok : (e + 1) * tok]
                out_ref[e, 1, :, first + c : first + c + n] = y[rows + e * tok : rows + (e + 1) * tok]

    x_ref[:rows] = own_ref[...]
    x_ref[rows:] = far_ref[...]
    multiply(gathered_ref, w_ref.shape[1])
    for i in range(len(chunk_refs) + 1):
        columns = pl.ds(pl.multiple_of(order_ref[i] * VD, VD), VD)
        x_ref[:rows, i * VD : (i + 1) * VD] = own_ref[:, columns]
        x_ref[rows:, i * VD : (i + 1) * VD] = far_ref[:, columns]
    for i, ref in enumerate(chunk_refs):
        w_ref[i * VD : (i + 1) * VD] = ref[...]
    half = left_ref.shape[1]
    w_ref[len(chunk_refs) * VD :, :half] = left_ref[...]
    w_ref[len(chunk_refs) * VD :, half:] = right_ref[...]
    multiply(w_ref, 0)


def project(order, own, far, gathered, chunks, parts):
    rows, depth = own.shape
    carried = chunks[0].shape[1]
    width = carried + gathered.shape[1]
    whole = pl.BlockSpec(memory_space=pltpu.VMEM)
    return pl.pallas_call(
        project_kernel,
        in_specs=[pl.BlockSpec(memory_space=pltpu.SMEM)] + [whole] * (3 + len(chunks)),
        out_specs=whole,
        out_shape=jax.ShapeDtypeStruct((parts, 2, rows // parts, width), BF),
        scratch_shapes=[pltpu.VMEM((2 * rows, depth), BF), pltpu.VMEM((depth, carried), BF)],
        compiler_params=pltpu.CompilerParams(vmem_limit_bytes=32 * 2**20),
        cost_estimate=pl.CostEstimate(
            flops=4 * rows * depth * width, bytes_accessed=2 * depth * width, transcendentals=0
        ),
    )(order, own, far, gathered, *chunks)


def swap(mine):
    return lax.ppermute(mine, "core", SWAP)


def own_w_out(w_out):
    core = lax.axis_index("core")
    half = w_out.shape[1] // 2
    lower, upper = w_out[:, :half], w_out[:, half:]
    mine = jnp.where(core == 0, lower, upper)
    other = swap(jnp.where(core == 0, upper, lower))
    return jnp.concatenate([jnp.where(core == 0, mine, other), jnp.where(core == 0, other, mine)], axis=0)


def up(a):
    return lax.ppermute(a, "x", [(i, (i + 1) % 4) for i in range(4)])


def down(a):
    return lax.ppermute(a, "x", [(i, (i + 3) % 4) for i in range(4)])


def across(a):
    return lax.ppermute(a, "z_lo", SWAP)


def chip_order():
    x, z = lax.axis_index("x"), lax.axis_index("z_lo")
    chip = lambda zz, dx: zz * 4 + lax.rem(x + 4 + dx, 4)
    near, far = z, 1 - z
    order = [chip(near, 0), chip(far, 0), chip(near, -1), chip(near, 1)]
    order += [chip(far, -1), chip(far, 1), chip(near, 2), chip(far, 2)]
    return jnp.stack(order).astype(jnp.int32)


def latent_queries(queries, w_kv):
    rows = queries.shape[0]
    heads = queries.shape[1] // QK
    q = queries.reshape(rows, heads, QK)
    keys = w_kv.reshape(KV_RANK, heads, NOPE + VD)[:, :, :NOPE]
    q_lat = jnp.einsum("qhd,rhd->hqr", q[:, :, :NOPE], keys, preferred_element_type=F32).astype(BF)
    q_all = jnp.concatenate([q_lat, q[:, :, NOPE:].transpose(1, 0, 2)], axis=2)
    return q_all.reshape(heads * rows, -1)


def routing(routes, codes):
    tok = routes.shape[0]
    core = lax.axis_index("core")
    code_float = codes.astype(F32)
    mix = code_float / jnp.sum(code_float, axis=1, keepdims=True)
    routes2, mix2 = jnp.stack([routes, swap(routes)]), jnp.stack([mix, swap(mix)])
    chosen = routes2[:, :, :, None] == jnp.arange(64, dtype=jnp.int32)
    weight = jnp.sum(jnp.where(chosen, mix2[..., None], F32(0.0)), axis=2)
    has = jnp.any(chosen, axis=2)

    def of_core(a):
        a = a.reshape(2, tok, 8, 2, 4)
        return jnp.where(core == 0, a[:, :, :, 0], a[:, :, :, 1]).reshape(2, tok, 32)

    weight, has = of_core(weight), of_core(has)
    count = has.astype(jnp.int32)
    slot = jnp.cumsum(count, axis=1) - count
    place = has[:, :, :, None] & (slot[:, :, :, None] == jnp.arange(CAP, dtype=jnp.int32))
    place = place.transpose(2, 3, 0, 1)[:, :, :, None, :]
    same = jnp.arange(2)[:, None, None] == jnp.arange(2)[None, :, None]
    place = (place & same).reshape(32, CAP, 2, 2 * tok)
    place = jnp.broadcast_to(place[:, None], (32, 2, CAP, 2, 2 * tok)).reshape(64, CAP, 2, 2 * tok)
    gains = weight.transpose(2, 0, 1).reshape(32, 2 * tok)
    gains = jnp.broadcast_to(gains[:, None], (32, 2, 2 * tok)).reshape(64, 1, 1, 2 * tok)
    factors = jnp.where(place, gains, F32(0.0))
    high = lax.reduce_precision(factors, 8, 7)
    factors = jnp.concatenate([high, factors - high], axis=3).astype(BF)
    place = place.astype(BF)
    parts = []
    for slots in SLOTS:
        parts.append((place[:, slots].reshape(-1, 2 * tok), factors[:, slots].reshape(-1, 4 * tok).T))
    return parts


def local(queries, latents, w_kv, w_out, resid, norm_gain, routes, codes, w_gate, w_up, w_down):
    tok, width = resid.shape
    chips = 64
    core = lax.axis_index("core")
    chunk = own_w_out(w_out)
    gathered = lax.all_gather(chunk[:, CARRIED:], CTX_CHIPS, axis=0, tiled=True)
    chunk = chunk[:, :CARRIED]
    mate, before, after = across(chunk), up(chunk), down(chunk)
    near = lax.all_to_all(
        jnp.broadcast_to(latents[None], (8,) + latents.shape), CTX_CHIPS, split_axis=0, concat_axis=0, tiled=True
    )
    q = latent_queries(queries, w_kv)
    near, q, mate, before, after = lax.optimization_barrier((near, q, mate, before, after))
    far = swap(near)
    mate_before, mate_after, opposite = up(mate), across(after), down(after)
    ids = jnp.stack([lax.axis_index(CTX), core]).astype(jnp.int32)
    heads_out = attend(ids, q, near, far, w_kv, 4, 4)
    heads_out, mate_before, mate_after, opposite = lax.optimization_barrier(
        (heads_out, mate_before, mate_after, opposite)
    )
    part = chunk.shape[1] // 2
    left, right = up(mate_before[:, :part]), down(mate_after[:, part:])
    chunks = (chunk, mate, before, after, mate_before, mate_after, opposite, left, right)
    order = chip_order()
    half = width // 2
    lower, upper = resid[:, :half], resid[:, half:]
    resid2 = jnp.stack([jnp.where(core == 0, lower, upper), swap(jnp.where(core == 0, upper, lower))])
    attn = project(order, heads_out, swap(heads_out), gathered, chunks, 8)
    attn = lax.all_to_all(attn, EP, split_axis=0, concat_axis=0, tiled=True)
    summed = (resid2.astype(F32) + jnp.sum(attn.astype(F32), axis=0)).astype(BF)
    others = swap(summed)[::-1]
    attended2 = jnp.concatenate(
        [jnp.where(core == 0, summed, others), jnp.where(core == 0, others, summed)], axis=2
    ).reshape(2 * tok, width)
    attended = attended2[:tok]
    wide2 = attended2.astype(F32)
    meansq = jnp.mean(wide2 * wide2, axis=1, keepdims=True)
    normed2 = (wide2 * lax.rsqrt(meansq + 1e-06) * norm_gain[None, :]).astype(BF)

    def exchange(rows):
        units = rows.reshape(chips, -1, 2, width)
        units = lax.all_to_all(units, CHIPS, split_axis=0, concat_axis=0, tiled=True)
        return units.reshape(rows.shape)

    parts = routing(routes, codes)
    arrived = [exchange(dispatch(place, normed2, 7)) for place, _ in parts]
    returned = [exchange(expert(rows, w_gate[0], w_up[0], w_down[0], 2, 7)) for rows in arrived]
    own, theirs = combine([(factors, rows) for (_, factors), rows in zip(parts, returned)], 7)
    layer_out = (wide2[:tok] + own + swap(theirs)).astype(BF)
    return (attended, layer_out)


def solution(mesh):
    fine = Mesh(mesh.devices.reshape(SIZES), NAMES)
    rows = P(CTX + EP, None)
    heads = P(CTX + EP, None, None)
    placed = (
        P(CTX, EP),
        P(None, CTX),
        P(None, EP),
        P(EP + CTX, None),
        rows,
        P(),
        rows,
        rows,
        heads,
        heads,
        heads,
    )
    return jax.shard_map(local, mesh=fine, in_specs=placed, out_specs=(rows, rows), check_vma=False)
```

```python
import functools

import jax
import jax.numpy as jnp
from jax import lax
from jax.experimental import pallas as pl
from jax.experimental.pallas import tpu as pltpu
from jax.sharding import Mesh, PartitionSpec as P

NOPE = 128
VD = 128
KV_RANK = 512
TOP = 8
QK = 192
CAP = 3
SLOTS = (slice(0, 3),)

CTX = ("z_lo", "x", "core")
CTX_CHIPS = ("z_lo", "x")
EP = ("z_hi", "y")
CHIPS = ("z_lo", "x", "z_hi", "y")
SIZES = (2, 4, 2, 2, 4)
NAMES = ("z_lo", "x", "core", "z_hi", "y")
SWAP = ((0, 1), (1, 0))
BF = jnp.bfloat16
F32 = jnp.float32
LOG2E = 1.4426950408889634


def attend_kernel(ids_ref, q_ref, near_ref, far_ref, w_ref, out_ref, lat_ref, s_ref, p_ref, *, rows, cuts):
    heads = w_ref.shape[1] // (NOPE + VD)
    m = q_ref.shape[0]
    pairs = near_ref.shape[0]
    keys = 2 * rows * pairs

    @pl.when(pl.program_id(0) == 0)
    def _():
        for i in range(pairs):
            lat_ref[:, 2 * i * rows : (2 * i + 1) * rows] = near_ref[i]
            lat_ref[:, (2 * i + 1) * rows : (2 * i + 2) * rows] = far_ref[i]

    ctx, core = ids_ref[0], ids_ref[1]
    span = keys // cuts
    lane = lax.broadcasted_iota(jnp.int32, (m, rows), 1)
    query = lax.broadcasted_iota(jnp.int32, (m, rows), 0) % rows
    ahead = lane - query
    peak = jnp.full((m, rows), -1e30, F32)
    for j in range(cuts):
        s = jnp.dot(q_ref[...], lat_ref[:, j * span : (j + 1) * span], preferred_element_type=F32)
        for b in range(span // rows):
            block = j * (span // rows) + b
            pos = 2 * (block // 2) + (core if block % 2 == 0 else 1 - core)
            part = s[:, b * rows : (b + 1) * rows]
            part = jnp.where(ahead <= (ctx - pos) * rows, part, F32(-1e30))
            peak = jnp.maximum(peak, part)
            s_ref[:, block * rows : (block + 1) * rows] = part
    top = jnp.max(peak, axis=1, keepdims=True)
    total = jnp.zeros((m, rows), F32)
    for j in range(keys // rows):
        p = jnp.exp2((s_ref[:, j * rows : (j + 1) * rows] - top) * (QK ** (-0.5) * LOG2E))
        total = total + p
        p_ref[:, j * rows : (j + 1) * rows] = p.astype(BF)
    mixed = lax.dot_general(p_ref[...], lat_ref[:KV_RANK], (((1,), (1,)), ((), ())), preferred_element_type=F32)
    mixed = (mixed / jnp.sum(total, axis=1, keepdims=True)).astype(BF)
    for h in range(heads):
        values = w_ref[:, h * (NOPE + VD) + NOPE : (h + 1) * (NOPE + VD)]
        o = jnp.dot(mixed[h * rows : (h + 1) * rows], values, preferred_element_type=F32)
        out_ref[:, h * VD : (h + 1) * VD] = o.astype(BF)


def attend(ids, q, near, far, w_kv, group, cuts):
    pairs, depth, rows = near.shape
    heads = w_kv.shape[1] // (NOPE + VD)
    keys = 2 * rows * pairs
    m = group * rows
    return pl.pallas_call(
        functools.partial(attend_kernel, rows=rows, cuts=cuts),
        grid=(heads // group,),
        in_specs=[
            pl.BlockSpec(memory_space=pltpu.SMEM),
            pl.BlockSpec((m, depth), lambda g: (g, 0)),
            pl.BlockSpec(near.shape, lambda g: (0, 0, 0)),
            pl.BlockSpec(far.shape, lambda g: (0, 0, 0)),
            pl.BlockSpec((KV_RANK, group * (NOPE + VD)), lambda g: (0, g)),
        ],
        out_specs=pl.BlockSpec((rows, group * VD), lambda g: (0, g)),
        out_shape=jax.ShapeDtypeStruct((rows, heads * VD), BF),
        scratch_shapes=[pltpu.VMEM((depth, keys), BF), pltpu.VMEM((m, keys), F32), pltpu.VMEM((m, keys), BF)],
        compiler_params=pltpu.CompilerParams(vmem_limit_bytes=40 * 2**20),
        cost_estimate=pl.CostEstimate(
            flops=2 * heads * rows * keys * (depth + KV_RANK),
            bytes_accessed=8_000_000,
            transcendentals=heads * rows * keys,
        ),
    )(ids, q, near, far, w_kv)


def expert_kernel(x_ref, g_ref, u_ref, d_ref, out_ref, rows_ref, hid_ref, *, first):
    step = pl.program_id(0)

    @pl.when(step == 0)
    def _():
        rows_ref[...] = x_ref[...].reshape(rows_ref.shape)

    @pl.when(step < first)
    def _():
        rows = rows_ref[...]
        gate = jnp.dot(rows, g_ref[...], preferred_element_type=F32)
        upward = jnp.dot(rows, u_ref[...], preferred_element_type=F32)
        hid = (gate / (1.0 + jnp.exp(-gate)) * upward).astype(BF)
        n = g_ref.shape[1]
        for f in range(first):

            @pl.when(step == f)
            def _(f=f):
                hid_ref[:, f * n : (f + 1) * n] = hid

    @pl.when(step >= first)
    def _():
        y = jnp.dot(hid_ref[...], d_ref[...], preferred_element_type=F32).astype(BF)
        out_ref[...] = y.reshape(out_ref.shape)


def expert(x, w_gate, w_up, w_down, first, last):
    units, pair, width = x.shape
    m = units * pair
    hidden = w_gate.shape[1]
    n1, n2 = hidden // first, width // last
    return pl.pallas_call(
        functools.partial(expert_kernel, first=first),
        grid=(first + last,),
        in_specs=[
            pl.BlockSpec(x.shape, lambda i: (0, 0, 0)),
            pl.BlockSpec((width, n1), lambda i: (0, jnp.minimum(i, first - 1))),
            pl.BlockSpec((width, n1), lambda i: (0, jnp.minimum(i, first - 1))),
            pl.BlockSpec((hidden, n2), lambda i: (0, jnp.maximum(i - first, 0))),
        ],
        out_specs=pl.BlockSpec((units, pair, n2), lambda i: (0, 0, jnp.maximum(i - first, 0))),
        out_shape=jax.ShapeDtypeStruct(x.shape, BF),
        scratch_shapes=[pltpu.VMEM((m, width), BF), pltpu.VMEM((m, hidden), BF)],
        compiler_params=pltpu.CompilerParams(vmem_limit_bytes=40 * 2**20),
        cost_estimate=pl.CostEstimate(
            flops=6 * m * width * hidden, bytes_accessed=17_000_000, transcendentals=m * hidden
        ),
    )(x, w_gate, w_up, w_down)


def dispatch_kernel(place_ref, x_ref, out_ref):
    y = jnp.dot(place_ref[...], x_ref[...], preferred_element_type=F32).astype(BF)
    out_ref[...] = y.reshape(out_ref.shape)


def dispatch(place, x, cuts):
    m = place.shape[0]
    tokens, width = x.shape
    n = width // cuts
    return pl.pallas_call(
        dispatch_kernel,
        grid=(cuts,),
        in_specs=[pl.BlockSpec(place.shape, lambda i: (0, 0)), pl.BlockSpec((tokens, n), lambda i: (0, i))],
        out_specs=pl.BlockSpec((m // 2, 2, n), lambda i: (0, 0, i)),
        out_shape=jax.ShapeDtypeStruct((m // 2, 2, width), BF),
        compiler_params=pltpu.CompilerParams(vmem_limit_bytes=32 * 2**20),
        cost_estimate=pl.CostEstimate(
            flops=2 * m * tokens * width, bytes_accessed=2 * m * width + 2 * tokens * width, transcendentals=0
        ),
    )(place, x)


def combine_kernel(*refs):
    *in_refs, own_ref, far_ref = refs
    tok = own_ref.shape[0]
    y = None
    for factors_ref, x_ref in zip(in_refs[::2], in_refs[1::2]):
        rows = x_ref[...].reshape(factors_ref.shape[1], x_ref.shape[2])
        part = jnp.dot(factors_ref[...], rows, preferred_element_type=F32)
        y = part if y is None else y + part
    y = y[: 2 * tok] + y[2 * tok :]
    own_ref[...] = y[:tok]
    far_ref[...] = y[tok:]


def combine(parts, cuts):
    width = parts[0][1].shape[2]
    n = width // cuts
    tok = parts[0][0].shape[0] // 4
    half = pl.BlockSpec((tok, n), lambda i: (0, i))
    in_specs = []
    for factors, x in parts:
        in_specs.append(pl.BlockSpec(factors.shape, lambda i: (0, 0)))
        in_specs.append(pl.BlockSpec((x.shape[0], 2, n), lambda i: (0, 0, i)))
    rows = sum(2 * x.shape[0] for _, x in parts)
    return pl.pallas_call(
        combine_kernel,
        grid=(cuts,),
        in_specs=in_specs,
        out_specs=(half, half),
        out_shape=(jax.ShapeDtypeStruct((tok, width), F32),) * 2,
        compiler_params=pltpu.CompilerParams(vmem_limit_bytes=32 * 2**20),
        cost_estimate=pl.CostEstimate(
            flops=8 * tok * rows * width, bytes_accessed=2 * rows * width, transcendentals=0
        ),
    )(*[a for part in parts for a in part])


def project_kernel(order_ref, *refs):
    *head_refs, chunk_refs, (left_ref, right_ref), out_ref, x_ref, w_ref, sems = refs
    parts = out_ref.shape[0]
    rows = head_refs[0].shape[0]
    tok = rows // parts
    whole = len(chunk_refs)
    half = left_ref.shape[1]
    copies = [
        pltpu.make_async_copy(ref, w_ref.at[i * VD : (i + 1) * VD], sems.at[i]) for i, ref in enumerate(chunk_refs)
    ]
    copies.append(pltpu.make_async_copy(left_ref, w_ref.at[whole * VD :, :half], sems.at[whole]))
    copies.append(pltpu.make_async_copy(right_ref, w_ref.at[whole * VD :, half:], sems.at[whole + 1]))
    for copy in copies:
        copy.start()
    lower, upper, far_lower, far_upper = head_refs
    count = lower.shape[1] // VD
    for i in range(whole + 1):
        chip = order_ref[i]
        columns = pl.ds(pl.multiple_of(lax.rem(chip, count) * VD, VD), VD)
        here = slice(i * VD, (i + 1) * VD)

        @pl.when(chip < count)
        def _():
            x_ref[:rows, here] = lower[:, columns]
            x_ref[rows:, here] = far_lower[:, columns]

        @pl.when(chip >= count)
        def _():
            x_ref[:rows, here] = upper[:, columns]
            x_ref[rows:, here] = far_upper[:, columns]

    for copy in copies:
        copy.wait()
    n = 256
    for c in range(0, w_ref.shape[1], n):
        y = jnp.dot(x_ref[...], w_ref[:, c : c + n], preferred_element_type=F32).astype(BF)
        for e in range(parts):
            out_ref[e, 0, :, c : c + n] = y[e * tok : (e + 1) * tok]
            out_ref[e, 1, :, c : c + n] = y[rows + e * tok : rows + (e + 1) * tok]


def project(order, heads, chunks, parts):
    *whole, left, right = chunks
    rows = heads[0].shape[0]
    width = whole[0].shape[1]
    depth = VD * (len(whole) + 1)
    vmem = pl.BlockSpec(memory_space=pltpu.VMEM)
    hbm = pl.BlockSpec(memory_space=pl.ANY)

    def kernel(*refs):
        order_ref, *refs = refs
        head_refs, refs = refs[: len(heads)], refs[len(heads) :]
        chunk_refs, refs = refs[: len(whole)], refs[len(whole) :]
        project_kernel(order_ref, *head_refs, chunk_refs, refs[:2], *refs[2:])

    return pl.pallas_call(
        kernel,
        in_specs=[pl.BlockSpec(memory_space=pltpu.SMEM)] + [vmem] * len(heads) + [hbm] * len(chunks),
        out_specs=vmem,
        out_shape=jax.ShapeDtypeStruct((parts, 2, rows // parts, width), BF),
        scratch_shapes=[
            pltpu.VMEM((2 * rows, depth), BF),
            pltpu.VMEM((depth, width), BF),
            pltpu.SemaphoreType.DMA((len(chunks),)),
        ],
        compiler_params=pltpu.CompilerParams(vmem_limit_bytes=32 * 2**20),
        cost_estimate=pl.CostEstimate(
            flops=4 * rows * depth * width, bytes_accessed=2 * depth * width, transcendentals=0
        ),
    )(order, *heads, *chunks)


def swap(mine):
    return lax.ppermute(mine, "core", SWAP)


def own_w_out(w_out):
    core = lax.axis_index("core")
    half = w_out.shape[1] // 2
    lower, upper = w_out[:, :half], w_out[:, half:]
    mine = jnp.where(core == 0, lower, upper)
    other = swap(jnp.where(core == 0, upper, lower))
    return jnp.concatenate([jnp.where(core == 0, mine, other), jnp.where(core == 0, other, mine)], axis=0)


def up(a):
    return lax.ppermute(a, "x", [(i, (i + 1) % 4) for i in range(4)])


def down(a):
    return lax.ppermute(a, "x", [(i, (i + 3) % 4) for i in range(4)])


def across(a):
    return lax.ppermute(a, "z_lo", SWAP)


def chip_order():
    x, z = lax.axis_index("x"), lax.axis_index("z_lo")
    chip = lambda zz, dx: zz * 4 + lax.rem(x + 4 + dx, 4)
    near, far = z, 1 - z
    order = [chip(near, 0), chip(far, 0), chip(near, -1), chip(near, 1)]
    order += [chip(far, -1), chip(far, 1), chip(near, 2), chip(far, 2)]
    return jnp.stack(order).astype(jnp.int32)


def latent_queries(queries, w_kv):
    rows = queries.shape[0]
    heads = queries.shape[1] // QK
    q = queries.reshape(rows, heads, QK)
    keys = w_kv.reshape(KV_RANK, heads, NOPE + VD)[:, :, :NOPE]
    q_lat = jnp.einsum("qhd,rhd->hqr", q[:, :, :NOPE], keys, preferred_element_type=F32).astype(BF)
    q_all = jnp.concatenate([q_lat, q[:, :, NOPE:].transpose(1, 0, 2)], axis=2)
    return q_all.reshape(heads * rows, -1)


def routing(routes, codes):
    tok = routes.shape[0]
    core = lax.axis_index("core")
    code_float = codes.astype(F32)
    mix = code_float / jnp.sum(code_float, axis=1, keepdims=True)
    routes2, mix2 = jnp.stack([routes, swap(routes)]), jnp.stack([mix, swap(mix)])
    chosen = routes2[:, :, :, None] == jnp.arange(64, dtype=jnp.int32)
    weight = jnp.sum(jnp.where(chosen, mix2[..., None], F32(0.0)), axis=2)
    has = jnp.any(chosen, axis=2)

    def of_core(a):
        a = a.reshape(2, tok, 8, 2, 4)
        return jnp.where(core == 0, a[:, :, :, 0], a[:, :, :, 1]).reshape(2, tok, 32)

    weight, has = of_core(weight), of_core(has)
    count = has.astype(jnp.int32)
    slot = jnp.cumsum(count, axis=1) - count
    place = has[:, :, :, None] & (slot[:, :, :, None] == jnp.arange(CAP, dtype=jnp.int32))
    place = place.transpose(2, 3, 0, 1)[:, :, :, None, :]
    same = jnp.arange(2)[:, None, None] == jnp.arange(2)[None, :, None]
    place = (place & same).reshape(32, CAP, 2, 2 * tok)
    place = jnp.broadcast_to(place[:, None], (32, 2, CAP, 2, 2 * tok)).reshape(64, CAP, 2, 2 * tok)
    gains = weight.transpose(2, 0, 1).reshape(32, 2 * tok)
    gains = jnp.broadcast_to(gains[:, None], (32, 2, 2 * tok)).reshape(64, 1, 1, 2 * tok)
    factors = jnp.where(place, gains, F32(0.0))
    high = lax.reduce_precision(factors, 8, 7)
    factors = jnp.concatenate([high, factors - high], axis=3).astype(BF)
    place = place.astype(BF)
    parts = []
    for slots in SLOTS:
        parts.append((place[:, slots].reshape(-1, 2 * tok), factors[:, slots].reshape(-1, 4 * tok).T))
    return parts


def local(queries, latents, w_kv, w_out, resid, norm_gain, routes, codes, w_gate, w_up, w_down):
    tok, width = resid.shape
    chips = 64
    core = lax.axis_index("core")
    chunk = own_w_out(w_out)
    mate, before, after = across(chunk), up(chunk), down(chunk)
    near = lax.all_to_all(
        jnp.broadcast_to(latents[None], (8,) + latents.shape), CTX_CHIPS, split_axis=0, concat_axis=0, tiled=True
    )
    q = latent_queries(queries, w_kv)
    near, q, mate, before, after = lax.optimization_barrier((near, q, mate, before, after))
    far = swap(near)
    mate_before, mate_after, opposite = up(mate), across(after), down(after)
    ids = jnp.stack([lax.axis_index(CTX), core]).astype(jnp.int32)
    wide_half, tall_half = w_kv.shape[1] // 2, q.shape[0] // 2
    heads_lower = attend(ids, q[:tall_half], near, far, w_kv[:, :wide_half], 4, 4)
    heads_lower, q_upper, mate_before, mate_after, opposite = lax.optimization_barrier(
        (heads_lower, q[tall_half:], mate_before, mate_after, opposite)
    )
    part = chunk.shape[1] // 2
    left, right = up(mate_before[:, :part]), down(mate_after[:, part:])
    heads_upper = attend(ids, q_upper, near, far, w_kv[:, wide_half:], 4, 4)
    chunks = (chunk, mate, before, after, mate_before, mate_after, opposite, left, right)
    order = chip_order()
    half = width // 2
    lower, upper = resid[:, :half], resid[:, half:]
    resid2 = jnp.stack([jnp.where(core == 0, lower, upper), swap(jnp.where(core == 0, upper, lower))])
    attn = project(order, (heads_lower, heads_upper, swap(heads_lower), swap(heads_upper)), chunks, 8)
    attn = lax.all_to_all(attn, EP, split_axis=0, concat_axis=0, tiled=True)
    summed = (resid2.astype(F32) + jnp.sum(attn.astype(F32), axis=0)).astype(BF)
    others = swap(summed)[::-1]
    attended2 = jnp.concatenate(
        [jnp.where(core == 0, summed, others), jnp.where(core == 0, others, summed)], axis=2
    ).reshape(2 * tok, width)
    attended = attended2[:tok]
    wide2 = attended2.astype(F32)
    meansq = jnp.mean(wide2 * wide2, axis=1, keepdims=True)
    normed2 = (wide2 * lax.rsqrt(meansq + 1e-06) * norm_gain[None, :]).astype(BF)

    def exchange(rows):
        units = rows.reshape(chips, -1, 2, width)
        units = lax.all_to_all(units, CHIPS, split_axis=0, concat_axis=0, tiled=True)
        return units.reshape(rows.shape)

    parts = routing(routes, codes)
    arrived = [exchange(dispatch(place, normed2, 2)) for place, _ in parts]
    returned = [exchange(expert(rows, w_gate[0], w_up[0], w_down[0], 2, 7)) for rows in arrived]
    own, theirs = combine([(factors, rows) for (_, factors), rows in zip(parts, returned)], 4)
    layer_out = (wide2[:tok] + own + swap(theirs)).astype(BF)
    return (attended, layer_out)


def solution(mesh):
    fine = Mesh(mesh.devices.reshape(SIZES), NAMES)
    rows = P(CTX + EP, None)
    heads = P(CTX + EP, None, None)
    placed = (
        P(CTX, EP),
        P(None, CTX),
        P(None, EP),
        P(EP + CTX, None),
        rows,
        P(),
        rows,
        rows,
        heads,
        heads,
        heads,
    )
    return jax.shard_map(local, mesh=fine, in_specs=placed, out_specs=(rows, rows), check_vma=False)
```

```python
import functools

import jax
import jax.numpy as jnp
from jax import lax
from jax.experimental import pallas as pl
from jax.experimental.pallas import tpu as pltpu
from jax.sharding import Mesh, PartitionSpec as P

NOPE = 128
VD = 128
KV_RANK = 512
TOP = 8
QK = 192
CAP = 3
SLOTS = (slice(0, 3),)

CTX = ("z_lo", "x", "core")
CTX_CHIPS = ("z_lo", "x")
EP = ("z_hi", "y")
CHIPS = ("z_lo", "x", "z_hi", "y")
SIZES = (2, 4, 2, 2, 4)
NAMES = ("z_lo", "x", "core", "z_hi", "y")
SWAP = ((0, 1), (1, 0))
BF = jnp.bfloat16
F32 = jnp.float32
LOG2E = 1.4426950408889634


def attend_kernel(ids_ref, q_ref, near_ref, far_ref, w_ref, out_ref, lat_ref, s_ref, p_ref, *, rows, cuts):
    heads = w_ref.shape[1] // (NOPE + VD)
    m = q_ref.shape[0]
    pairs = near_ref.shape[0]
    keys = 2 * rows * pairs

    @pl.when(pl.program_id(0) == 0)
    def _():
        for i in range(pairs):
            lat_ref[:, 2 * i * rows : (2 * i + 1) * rows] = near_ref[i]
            lat_ref[:, (2 * i + 1) * rows : (2 * i + 2) * rows] = far_ref[i]

    ctx, core = ids_ref[0], ids_ref[1]
    span = keys // cuts
    lane = lax.broadcasted_iota(jnp.int32, (m, rows), 1)
    query = lax.broadcasted_iota(jnp.int32, (m, rows), 0) % rows
    ahead = lane - query
    peak = jnp.full((m, rows), -1e30, F32)
    for j in range(cuts):
        s = jnp.dot(q_ref[...], lat_ref[:, j * span : (j + 1) * span], preferred_element_type=F32)
        for b in range(span // rows):
            block = j * (span // rows) + b
            pos = 2 * (block // 2) + (core if block % 2 == 0 else 1 - core)
            part = s[:, b * rows : (b + 1) * rows]
            part = jnp.where(ahead <= (ctx - pos) * rows, part, F32(-1e30))
            peak = jnp.maximum(peak, part)
            s_ref[:, block * rows : (block + 1) * rows] = part
    top = jnp.max(peak, axis=1, keepdims=True)
    total = jnp.zeros((m, rows), F32)
    for j in range(keys // rows):
        p = jnp.exp2((s_ref[:, j * rows : (j + 1) * rows] - top) * (QK ** (-0.5) * LOG2E))
        total = total + p
        p_ref[:, j * rows : (j + 1) * rows] = p.astype(BF)
    mixed = lax.dot_general(p_ref[...], lat_ref[:KV_RANK], (((1,), (1,)), ((), ())), preferred_element_type=F32)
    mixed = (mixed / jnp.sum(total, axis=1, keepdims=True)).astype(BF)
    for h in range(heads):
        values = w_ref[:, h * (NOPE + VD) + NOPE : (h + 1) * (NOPE + VD)]
        o = jnp.dot(mixed[h * rows : (h + 1) * rows], values, preferred_element_type=F32)
        out_ref[:, h * VD : (h + 1) * VD] = o.astype(BF)


def attend(ids, q, near, far, w_kv, group, cuts):
    pairs, _, rows = near.shape
    depth = q.shape[1]
    heads = w_kv.shape[1] // (NOPE + VD)
    keys = 2 * rows * pairs
    m = group * rows
    return pl.pallas_call(
        functools.partial(attend_kernel, rows=rows, cuts=cuts),
        grid=(heads // group,),
        in_specs=[
            pl.BlockSpec(memory_space=pltpu.SMEM),
            pl.BlockSpec((m, depth), lambda g: (g, 0)),
            pl.BlockSpec((pairs, depth, rows), lambda g: (0, 0, 0)),
            pl.BlockSpec((pairs, depth, rows), lambda g: (0, 0, 0)),
            pl.BlockSpec((KV_RANK, group * (NOPE + VD)), lambda g: (0, g)),
        ],
        out_specs=pl.BlockSpec((rows, group * VD), lambda g: (0, g)),
        out_shape=jax.ShapeDtypeStruct((rows, heads * VD), BF),
        scratch_shapes=[pltpu.VMEM((depth, keys), BF), pltpu.VMEM((m, keys), F32), pltpu.VMEM((m, keys), BF)],
        compiler_params=pltpu.CompilerParams(vmem_limit_bytes=40 * 2**20),
        cost_estimate=pl.CostEstimate(
            flops=2 * heads * rows * keys * (depth + KV_RANK),
            bytes_accessed=8_000_000,
            transcendentals=heads * rows * keys,
        ),
    )(ids, q, near, far, w_kv)


def expert_kernel(x_ref, g_ref, u_ref, d_ref, out_ref, rows_ref, hid_ref, *, first):
    step = pl.program_id(0)

    @pl.when(step == 0)
    def _():
        rows_ref[...] = x_ref[...].reshape(rows_ref.shape)

    @pl.when(step < first)
    def _():
        rows = rows_ref[...]
        gate = jnp.dot(rows, g_ref[...], preferred_element_type=F32)
        upward = jnp.dot(rows, u_ref[...], preferred_element_type=F32)
        hid = (gate / (1.0 + jnp.exp(-gate)) * upward).astype(BF)
        n = g_ref.shape[1]
        for f in range(first):

            @pl.when(step == f)
            def _(f=f):
                hid_ref[:, f * n : (f + 1) * n] = hid

    @pl.when(step >= first)
    def _():
        y = jnp.dot(hid_ref[...], d_ref[...], preferred_element_type=F32).astype(BF)
        out_ref[...] = y.reshape(out_ref.shape)


def expert(x, w_gate, w_up, w_down, first, last):
    units, pair, width = x.shape
    m = units * pair
    hidden = w_gate.shape[1]
    n1, n2 = hidden // first, width // last
    return pl.pallas_call(
        functools.partial(expert_kernel, first=first),
        grid=(first + last,),
        in_specs=[
            pl.BlockSpec(x.shape, lambda i: (0, 0, 0)),
            pl.BlockSpec((width, n1), lambda i: (0, jnp.minimum(i, first - 1))),
            pl.BlockSpec((width, n1), lambda i: (0, jnp.minimum(i, first - 1))),
            pl.BlockSpec((hidden, n2), lambda i: (0, jnp.maximum(i - first, 0))),
        ],
        out_specs=pl.BlockSpec((units, pair, n2), lambda i: (0, 0, jnp.maximum(i - first, 0))),
        out_shape=jax.ShapeDtypeStruct(x.shape, BF),
        scratch_shapes=[pltpu.VMEM((m, width), BF), pltpu.VMEM((m, hidden), BF)],
        compiler_params=pltpu.CompilerParams(vmem_limit_bytes=40 * 2**20),
        cost_estimate=pl.CostEstimate(
            flops=6 * m * width * hidden, bytes_accessed=17_000_000, transcendentals=m * hidden
        ),
    )(x, w_gate, w_up, w_down)


def dispatch_kernel(place_ref, x_ref, out_ref):
    y = jnp.dot(place_ref[...], x_ref[...], preferred_element_type=F32).astype(BF)
    out_ref[...] = y.reshape(out_ref.shape)


def dispatch(place, x, cuts):
    m = place.shape[0]
    tokens, width = x.shape
    n = width // cuts
    return pl.pallas_call(
        dispatch_kernel,
        grid=(cuts,),
        in_specs=[pl.BlockSpec(place.shape, lambda i: (0, 0)), pl.BlockSpec((tokens, n), lambda i: (0, i))],
        out_specs=pl.BlockSpec((m // 2, 2, n), lambda i: (0, 0, i)),
        out_shape=jax.ShapeDtypeStruct((m // 2, 2, width), BF),
        compiler_params=pltpu.CompilerParams(vmem_limit_bytes=32 * 2**20),
        cost_estimate=pl.CostEstimate(
            flops=2 * m * tokens * width, bytes_accessed=2 * m * width + 2 * tokens * width, transcendentals=0
        ),
    )(place, x)


def combine_kernel(*refs):
    *in_refs, own_ref, far_ref = refs
    tok = own_ref.shape[0]
    y = None
    for factors_ref, x_ref in zip(in_refs[::2], in_refs[1::2]):
        rows = x_ref[...].reshape(factors_ref.shape[1], x_ref.shape[2])
        part = jnp.dot(factors_ref[...], rows, preferred_element_type=F32)
        y = part if y is None else y + part
    y = y[: 2 * tok] + y[2 * tok :]
    own_ref[...] = y[:tok]
    far_ref[...] = y[tok:]


def combine(parts, cuts):
    width = parts[0][1].shape[2]
    n = width // cuts
    tok = parts[0][0].shape[0] // 4
    half = pl.BlockSpec((tok, n), lambda i: (0, i))
    in_specs = []
    for factors, x in parts:
        in_specs.append(pl.BlockSpec(factors.shape, lambda i: (0, 0)))
        in_specs.append(pl.BlockSpec((x.shape[0], 2, n), lambda i: (0, 0, i)))
    rows = sum(2 * x.shape[0] for _, x in parts)
    return pl.pallas_call(
        combine_kernel,
        grid=(cuts,),
        in_specs=in_specs,
        out_specs=(half, half),
        out_shape=(jax.ShapeDtypeStruct((tok, width), F32),) * 2,
        compiler_params=pltpu.CompilerParams(vmem_limit_bytes=32 * 2**20),
        cost_estimate=pl.CostEstimate(
            flops=8 * tok * rows * width, bytes_accessed=2 * rows * width, transcendentals=0
        ),
    )(*[a for part in parts for a in part])


def project_kernel(ids_ref, own_ref, before_ref, after_ref, left_ref, right_ref, near_ref, far_ref, out_ref, x_ref, w_ref):
    rows = own_ref.shape[0]
    group, tok = 4, out_ref.shape[1]
    parts = out_ref.shape[0] // group
    core, x = ids_ref[1], ids_ref[2]
    half = left_ref.shape[1]
    x_ref[:rows] = own_ref[...]
    x_ref[rows : 2 * rows] = after_ref[...]
    x_ref[2 * rows : 3 * rows, :half] = left_ref[...]
    x_ref[2 * rows : 3 * rows, half:] = right_ref[...]
    x_ref[3 * rows :] = before_ref[...]
    deep = VD // 2
    blocks = w_ref.shape[1] // 128
    first = near_ref.shape[1] - blocks * deep
    for side, ref in enumerate((near_ref, far_ref)):
        offset = (core if side == 0 else 1 - core) * deep
        for j in range(ref.shape[0]):
            here = pl.ds(pl.multiple_of(j * VD + offset, deep), deep)
            for b in range(blocks):
                w_ref[here, b * 128 : (b + 1) * 128] = ref[j, first + b * deep : first + (b + 1) * deep]
    for d in range(group):
        y = jnp.dot(x_ref[d * rows : (d + 1) * rows], w_ref[...], preferred_element_type=F32).astype(BF)
        target = lax.rem(x + d, group)
        for e in range(parts):
            out_ref[e * group + target] = y[e * tok : (e + 1) * tok]


def project(ids, pieces, near, far, parts, width):
    rows, depth = pieces[0].shape
    whole = pl.BlockSpec(memory_space=pltpu.VMEM)
    group = 4
    return pl.pallas_call(
        project_kernel,
        in_specs=[pl.BlockSpec(memory_space=pltpu.SMEM)] + [whole] * (len(pieces) + 2),
        out_specs=whole,
        out_shape=jax.ShapeDtypeStruct((parts * group, rows // parts, width), BF),
        scratch_shapes=[pltpu.VMEM((group * rows, depth), BF), pltpu.VMEM((depth, width), BF)],
        compiler_params=pltpu.CompilerParams(vmem_limit_bytes=32 * 2**20),
        cost_estimate=pl.CostEstimate(
            flops=2 * group * rows * depth * width, bytes_accessed=2 * depth * width, transcendentals=0
        ),
    )(ids, *pieces, near, far)


def swap(mine):
    return lax.ppermute(mine, "core", SWAP)


def up(a):
    return lax.ppermute(a, "x", [(i, (i + 1) % 4) for i in range(4)])


def down(a):
    return lax.ppermute(a, "x", [(i, (i + 3) % 4) for i in range(4)])


def latent_queries(queries, w_kv):
    rows = queries.shape[0]
    heads = queries.shape[1] // QK
    q = queries.reshape(rows, heads, QK)
    keys = w_kv.reshape(KV_RANK, heads, NOPE + VD)[:, :, :NOPE]
    q_lat = jnp.einsum("qhd,rhd->hqr", q[:, :, :NOPE], keys, preferred_element_type=F32).astype(BF)
    q_all = jnp.concatenate([q_lat, q[:, :, NOPE:].transpose(1, 0, 2)], axis=2)
    return q_all.reshape(heads * rows, -1)


def routing(routes, codes):
    tok = routes.shape[0]
    core = lax.axis_index("core")
    code_float = codes.astype(F32)
    mix = code_float / jnp.sum(code_float, axis=1, keepdims=True)
    routes2, mix2 = jnp.stack([routes, swap(routes)]), jnp.stack([mix, swap(mix)])
    chosen = routes2[:, :, :, None] == jnp.arange(64, dtype=jnp.int32)
    weight = jnp.sum(jnp.where(chosen, mix2[..., None], F32(0.0)), axis=2)
    has = jnp.any(chosen, axis=2)

    def of_core(a):
        a = a.reshape(2, tok, 8, 2, 4)
        return jnp.where(core == 0, a[:, :, :, 0], a[:, :, :, 1]).reshape(2, tok, 32)

    weight, has = of_core(weight), of_core(has)
    count = has.astype(jnp.int32)
    slot = jnp.cumsum(count, axis=1) - count
    place = has[:, :, :, None] & (slot[:, :, :, None] == jnp.arange(CAP, dtype=jnp.int32))
    place = place.transpose(2, 3, 0, 1)[:, :, :, None, :]
    same = jnp.arange(2)[:, None, None] == jnp.arange(2)[None, :, None]
    place = (place & same).reshape(32, CAP, 2, 2 * tok)
    place = jnp.broadcast_to(place[:, None], (32, 2, CAP, 2, 2 * tok)).reshape(64, CAP, 2, 2 * tok)
    gains = weight.transpose(2, 0, 1).reshape(32, 2 * tok)
    gains = jnp.broadcast_to(gains[:, None], (32, 2, 2 * tok)).reshape(64, 1, 1, 2 * tok)
    factors = jnp.where(place, gains, F32(0.0))
    high = lax.reduce_precision(factors, 8, 7)
    factors = jnp.concatenate([high, factors - high], axis=3).astype(BF)
    place = place.astype(BF)
    parts = []
    for slots in SLOTS:
        parts.append((place[:, slots].reshape(-1, 2 * tok), factors[:, slots].reshape(-1, 4 * tok).T))
    return parts


def local(queries, latents, w_kv, w_out, resid, norm_gain, routes, codes, w_gate, w_up, w_down):
    tok, width = resid.shape
    chips = 64
    core = lax.axis_index("core")
    group = 4
    columns = width // group
    w_blocks = w_out.reshape(-1, group, columns // 128, 128).transpose(1, 2, 0, 3).reshape(group, -1, 128)
    payload = jnp.concatenate(
        [jnp.broadcast_to(latents[None], (group,) + latents.shape), w_blocks], axis=1
    )
    near = lax.all_to_all(
        jnp.concatenate([payload, payload], axis=0), CTX_CHIPS, split_axis=0, concat_axis=0, tiled=True
    )
    far = swap(near)
    ids = jnp.stack([lax.axis_index(CTX), core, lax.axis_index("x")]).astype(jnp.int32)
    own = attend(ids, latent_queries(queries, w_kv), near, far, w_kv, 4, 4)
    before, after = up(own), down(own)
    half = own.shape[1] // 2
    left, right = up(before[:, :half]), down(after[:, half:])
    attn = project(ids, (own, before, after, left, right), near, far, 8, columns)
    attn = lax.all_to_all(attn, EP + ("x",), split_axis=0, concat_axis=0, tiled=True)
    attn = jnp.sum(attn.reshape(8, group, tok, columns).astype(F32), axis=0)
    attn = attn.transpose(1, 0, 2).reshape(tok, width)
    attended = (resid.astype(F32) + attn).astype(BF)
    wide = attended.astype(F32)
    meansq = jnp.mean(wide * wide, axis=1, keepdims=True)
    normed = (wide * lax.rsqrt(meansq + 1e-06) * norm_gain[None, :]).astype(BF)
    normed2 = jnp.concatenate([normed, swap(normed)], axis=0)

    def exchange(rows):
        units = rows.reshape(chips, -1, 2, width)
        units = lax.all_to_all(units, CHIPS, split_axis=0, concat_axis=0, tiled=True)
        return units.reshape(rows.shape)

    parts = routing(routes, codes)
    arrived = [exchange(dispatch(place, normed2, 2)) for place, _ in parts]
    returned = [exchange(expert(rows, w_gate[0], w_up[0], w_down[0], 2, 7)) for rows in arrived]
    mine, theirs = combine([(factors, rows) for (_, factors), rows in zip(parts, returned)], 4)
    layer_out = (wide + mine + swap(theirs)).astype(BF)
    return (attended, layer_out)


def solution(mesh):
    fine = Mesh(mesh.devices.reshape(SIZES), NAMES)
    rows = P(CTX + EP, None)
    heads = P(CTX + EP, None, None)
    placed = (
        P(CTX, EP),
        P(None, CTX),
        P(None, EP),
        P(EP + CTX, None),
        rows,
        P(),
        rows,
        rows,
        heads,
        heads,
        heads,
    )
    return jax.shard_map(local, mesh=fine, in_specs=placed, out_specs=(rows, rows), check_vma=False)
```

```python
import functools

import jax
import jax.numpy as jnp
from jax import lax
from jax.experimental import pallas as pl
from jax.experimental.pallas import tpu as pltpu
from jax.sharding import Mesh, PartitionSpec as P

NOPE = 128
VD = 128
KV_RANK = 512
TOP = 8
QK = 192
CAP = 3
SLOTS = (slice(0, 3),)

CTX = ("z_lo", "x", "core")
CTX_CHIPS = ("z_lo", "x")
EP = ("z_hi", "y")
CHIPS = ("z_lo", "x", "z_hi", "y")
SIZES = (2, 4, 2, 2, 4)
NAMES = ("z_lo", "x", "core", "z_hi", "y")
SWAP = ((0, 1), (1, 0))
BF = jnp.bfloat16
F32 = jnp.float32
LOG2E = 1.4426950408889634


def attend_kernel(ids_ref, q_ref, w_ref, near_ref, far_ref, out_ref, lat_ref, s_ref, latq_ref, mixed_ref, *, cuts):
    heads = w_ref.shape[1] // (NOPE + VD)
    rows = q_ref.shape[0]
    m = heads * rows
    pairs = near_ref.shape[0]
    keys = 2 * rows * pairs
    for i in range(pairs):
        lat_ref[:, 2 * i * rows : (2 * i + 1) * rows] = near_ref[i]
        lat_ref[:, (2 * i + 1) * rows : (2 * i + 2) * rows] = far_ref[i]
    for h in range(heads):
        here = slice(h * rows, (h + 1) * rows)
        key_weights = w_ref[:, h * (NOPE + VD) : h * (NOPE + VD) + NOPE]
        plain = q_ref[:, h * QK : h * QK + NOPE]
        latq = lax.dot_general(plain, key_weights, (((1,), (1,)), ((), ())), preferred_element_type=F32)
        latq_ref[here, :KV_RANK] = latq.astype(BF)
        latq_ref[here, KV_RANK:] = q_ref[:, h * QK + NOPE : (h + 1) * QK]
    ctx, core = ids_ref[0], ids_ref[1]
    span = keys // cuts
    lane = lax.broadcasted_iota(jnp.int32, (m, rows), 1)
    query = lax.broadcasted_iota(jnp.int32, (m, rows), 0) % rows
    ahead = lane - query
    peak = jnp.full((m, rows), -1e30, F32)
    for j in range(cuts):
        s = jnp.dot(latq_ref[...], lat_ref[:, j * span : (j + 1) * span], preferred_element_type=F32)
        for b in range(span // rows):
            block = j * (span // rows) + b
            pos = 2 * (block // 2) + (core if block % 2 == 0 else 1 - core)
            part = s[:, b * rows : (b + 1) * rows]
            part = jnp.where(ahead <= (ctx - pos) * rows, part, F32(-1e30))
            peak = jnp.maximum(peak, part)
            s_ref[:, block * rows : (block + 1) * rows] = part
    top = jnp.max(peak, axis=1, keepdims=True)
    total = jnp.zeros((m, rows), F32)
    for j in range(cuts):
        probs = []
        for b in range(span // rows):
            first = j * span + b * rows
            p = jnp.exp2((s_ref[:, first : first + rows] - top) * (QK ** (-0.5) * LOG2E))
            total = total + p
            probs.append(p.astype(BF))
        part = lax.dot_general(
            jnp.concatenate(probs, axis=1),
            lat_ref[:KV_RANK, j * span : (j + 1) * span],
            (((1,), (1,)), ((), ())),
            preferred_element_type=F32,
        )
        mixed_ref[...] = part if j == 0 else mixed_ref[...] + part
    mixed = (mixed_ref[...] / jnp.sum(total, axis=1, keepdims=True)).astype(BF)
    for h in range(heads):
        values = w_ref[:, h * (NOPE + VD) + NOPE : (h + 1) * (NOPE + VD)]
        o = jnp.dot(mixed[h * rows : (h + 1) * rows], values, preferred_element_type=F32)
        out_ref[:, h * VD : (h + 1) * VD] = o.astype(BF)


def attend(ids, q, w_kv, near, far, cuts):
    pairs, depth, rows = near.shape
    heads = w_kv.shape[1] // (NOPE + VD)
    keys = 2 * rows * pairs
    m = heads * rows
    whole = pl.BlockSpec(memory_space=pltpu.VMEM)
    return pl.pallas_call(
        functools.partial(attend_kernel, cuts=cuts),
        in_specs=[pl.BlockSpec(memory_space=pltpu.SMEM)] + [whole] * 4,
        out_specs=whole,
        out_shape=jax.ShapeDtypeStruct((rows, heads * VD), BF),
        scratch_shapes=[
            pltpu.VMEM((depth, keys), BF),
            pltpu.VMEM((m, keys), F32),
            pltpu.VMEM((m, depth), BF),
            pltpu.VMEM((m, KV_RANK), F32),
        ],
        compiler_params=pltpu.CompilerParams(vmem_limit_bytes=36 * 2**20),
        cost_estimate=pl.CostEstimate(
            flops=2 * m * keys * (depth + KV_RANK), bytes_accessed=8_000_000, transcendentals=m * keys
        ),
    )(ids, q, w_kv, near, far)


def expert_kernel(x_hbm, g_ref, u_ref, d_ref, out_hbm, x_ref, hid_ref, gate_ref, up_ref, y_ref, sem_in, sem_out):
    units, pair, width = x_ref.shape
    m = units * pair
    first, last = sem_in.shape[0], sem_out.shape[0]
    depth, wide = width // first, width // last
    arrivals = []
    for k in range(first):
        part = slice(k * depth, (k + 1) * depth)
        arrivals.append(pltpu.make_async_copy(x_hbm.at[:, :, part], x_ref.at[:, :, part], sem_in.at[k]))
        arrivals[-1].start()
    for k in range(first):
        part = slice(k * depth, (k + 1) * depth)
        arrivals[k].wait()
        rows = x_ref[:, :, part].reshape(m, depth)
        gate = jnp.dot(rows, g_ref[part], preferred_element_type=F32)
        upward = jnp.dot(rows, u_ref[part], preferred_element_type=F32)
        gate_ref[...] = gate if k == 0 else gate_ref[...] + gate
        up_ref[...] = upward if k == 0 else up_ref[...] + upward
    gate = gate_ref[...]
    hid_ref[...] = (gate / (1.0 + jnp.exp(-gate)) * up_ref[...]).astype(BF)
    departures = []
    for n in range(last):
        part = slice(n * wide, (n + 1) * wide)
        y = jnp.dot(hid_ref[...], d_ref[:, part], preferred_element_type=F32).astype(BF)
        y_ref[:, :, part] = y.reshape(units, pair, wide)
        departures.append(pltpu.make_async_copy(y_ref.at[:, :, part], out_hbm.at[:, :, part], sem_out.at[n]))
        departures[-1].start()
    for copy in departures:
        copy.wait()


def expert(x, w_gate, w_up, w_down, first, last):
    units, pair, width = x.shape
    m = units * pair
    hidden = w_gate.shape[1]
    whole = pl.BlockSpec(memory_space=pltpu.VMEM)
    far = pl.BlockSpec(memory_space=pltpu.HBM)
    return pl.pallas_call(
        expert_kernel,
        in_specs=[far, whole, whole, whole],
        out_specs=far,
        out_shape=jax.ShapeDtypeStruct(x.shape, BF),
        scratch_shapes=[
            pltpu.VMEM(x.shape, BF),
            pltpu.VMEM((m, hidden), BF),
            pltpu.VMEM((m, hidden), F32),
            pltpu.VMEM((m, hidden), F32),
            pltpu.VMEM(x.shape, BF),
            pltpu.SemaphoreType.DMA((first,)),
            pltpu.SemaphoreType.DMA((last,)),
        ],
        compiler_params=pltpu.CompilerParams(vmem_limit_bytes=32 * 2**20),
        cost_estimate=pl.CostEstimate(
            flops=6 * m * width * hidden, bytes_accessed=17_000_000, transcendentals=m * hidden
        ),
    )(x, w_gate, w_up, w_down)


def dispatch_kernel(place_ref, x_ref, out_ref):
    y = jnp.dot(place_ref[...], x_ref[...], preferred_element_type=F32).astype(BF)
    out_ref[...] = y.reshape(out_ref.shape)


def dispatch(place, x, cuts):
    m = place.shape[0]
    tokens, width = x.shape
    n = width // cuts
    return pl.pallas_call(
        dispatch_kernel,
        grid=(cuts,),
        in_specs=[pl.BlockSpec(place.shape, lambda i: (0, 0)), pl.BlockSpec((tokens, n), lambda i: (0, i))],
        out_specs=pl.BlockSpec((m // 2, 2, n), lambda i: (0, 0, i)),
        out_shape=jax.ShapeDtypeStruct((m // 2, 2, width), BF),
        compiler_params=pltpu.CompilerParams(vmem_limit_bytes=32 * 2**20),
        cost_estimate=pl.CostEstimate(
            flops=2 * m * tokens * width, bytes_accessed=2 * m * width + 2 * tokens * width, transcendentals=0
        ),
    )(place, x)


def combine_kernel(*refs):
    *in_refs, own_ref, far_ref = refs
    tok = own_ref.shape[0]
    y = None
    for factors_ref, x_ref in zip(in_refs[::2], in_refs[1::2]):
        rows = x_ref[...].reshape(factors_ref.shape[1], x_ref.shape[2])
        part = jnp.dot(factors_ref[...], rows, preferred_element_type=F32)
        y = part if y is None else y + part
    y = y[: 2 * tok] + y[2 * tok :]
    own_ref[...] = y[:tok]
    far_ref[...] = y[tok:]


def combine(parts, cuts):
    width = parts[0][1].shape[2]
    n = width // cuts
    tok = parts[0][0].shape[0] // 4
    half = pl.BlockSpec((tok, n), lambda i: (0, i))
    in_specs = []
    for factors, x in parts:
        in_specs.append(pl.BlockSpec(factors.shape, lambda i: (0, 0)))
        in_specs.append(pl.BlockSpec((x.shape[0], 2, n), lambda i: (0, 0, i)))
    rows = sum(2 * x.shape[0] for _, x in parts)
    return pl.pallas_call(
        combine_kernel,
        grid=(cuts,),
        in_specs=in_specs,
        out_specs=(half, half),
        out_shape=(jax.ShapeDtypeStruct((tok, width), F32),) * 2,
        compiler_params=pltpu.CompilerParams(vmem_limit_bytes=32 * 2**20),
        cost_estimate=pl.CostEstimate(
            flops=8 * tok * rows * width, bytes_accessed=2 * rows * width, transcendentals=0
        ),
    )(*[a for part in parts for a in part])


def project_kernel(ids_ref, own_ref, before_ref, after_ref, left_ref, right_ref, near_ref, far_ref, out_ref, x_ref, w_ref):
    rows = own_ref.shape[0]
    group, tok = 4, out_ref.shape[1]
    parts = out_ref.shape[0] // group
    core, x = ids_ref[1], ids_ref[2]
    half = left_ref.shape[1]
    x_ref[:rows] = own_ref[...]
    x_ref[rows : 2 * rows] = after_ref[...]
    x_ref[2 * rows : 3 * rows, :half] = left_ref[...]
    x_ref[2 * rows : 3 * rows, half:] = right_ref[...]
    x_ref[3 * rows :] = before_ref[...]
    deep = VD // 2
    blocks = w_ref.shape[1] // 128
    for side, ref in enumerate((near_ref, far_ref)):
        offset = (core if side == 0 else 1 - core) * deep
        for j in range(ref.shape[0]):
            here = pl.ds(pl.multiple_of(j * VD + offset, deep), deep)
            for b in range(blocks):
                w_ref[here, b * 128 : (b + 1) * 128] = ref[j, b * deep : (b + 1) * deep]
    for d in range(group):
        y = jnp.dot(x_ref[d * rows : (d + 1) * rows], w_ref[...], preferred_element_type=F32).astype(BF)
        target = lax.rem(x + d, group)
        for e in range(parts):
            out_ref[e * group + target] = y[e * tok : (e + 1) * tok]


def project(ids, pieces, near, far, parts, width):
    rows, depth = pieces[0].shape
    whole = pl.BlockSpec(memory_space=pltpu.VMEM)
    group = 4
    return pl.pallas_call(
        project_kernel,
        in_specs=[pl.BlockSpec(memory_space=pltpu.SMEM)] + [whole] * (len(pieces) + 2),
        out_specs=whole,
        out_shape=jax.ShapeDtypeStruct((parts * group, rows // parts, width), BF),
        scratch_shapes=[pltpu.VMEM((group * rows, depth), BF), pltpu.VMEM((depth, width), BF)],
        compiler_params=pltpu.CompilerParams(vmem_limit_bytes=32 * 2**20),
        cost_estimate=pl.CostEstimate(
            flops=2 * group * rows * depth * width, bytes_accessed=2 * depth * width, transcendentals=0
        ),
    )(ids, *pieces, near, far)


def swap(mine):
    return lax.ppermute(mine, "core", SWAP)


def up(a):
    return lax.ppermute(a, "x", [(i, (i + 1) % 4) for i in range(4)])


def down(a):
    return lax.ppermute(a, "x", [(i, (i + 3) % 4) for i in range(4)])


def routing(routes, codes):
    tok = routes.shape[0]
    core = lax.axis_index("core")
    code_float = codes.astype(F32)
    mix = code_float / jnp.sum(code_float, axis=1, keepdims=True)
    routes2, mix2 = jnp.stack([routes, swap(routes)]), jnp.stack([mix, swap(mix)])
    chosen = routes2[:, :, :, None] == jnp.arange(64, dtype=jnp.int32)
    weight = jnp.sum(jnp.where(chosen, mix2[..., None], F32(0.0)), axis=2)
    has = jnp.any(chosen, axis=2)

    def of_core(a):
        a = a.reshape(2, tok, 8, 2, 4)
        return jnp.where(core == 0, a[:, :, :, 0], a[:, :, :, 1]).reshape(2, tok, 32)

    weight, has = of_core(weight), of_core(has)
    count = has.astype(jnp.int32)
    slot = jnp.cumsum(count, axis=1) - count
    place = has[:, :, :, None] & (slot[:, :, :, None] == jnp.arange(CAP, dtype=jnp.int32))
    place = place.transpose(2, 3, 0, 1)[:, :, :, None, :]
    same = jnp.arange(2)[:, None, None] == jnp.arange(2)[None, :, None]
    place = (place & same).reshape(32, CAP, 2, 2 * tok)
    place = jnp.broadcast_to(place[:, None], (32, 2, CAP, 2, 2 * tok)).reshape(64, CAP, 2, 2 * tok)
    gains = weight.transpose(2, 0, 1).reshape(32, 2 * tok)
    gains = jnp.broadcast_to(gains[:, None], (32, 2, 2 * tok)).reshape(64, 1, 1, 2 * tok)
    factors = jnp.where(place, gains, F32(0.0))
    high = lax.reduce_precision(factors, 8, 7)
    factors = jnp.concatenate([high, factors - high], axis=3).astype(BF)
    place = place.astype(BF)
    parts = []
    for slots in SLOTS:
        parts.append((place[:, slots].reshape(-1, 2 * tok), factors[:, slots].reshape(-1, 4 * tok).T))
    return parts


def local(queries, latents, w_kv, w_out, resid, norm_gain, routes, codes, w_gate, w_up, w_down):
    tok, width = resid.shape
    chips = 64
    core = lax.axis_index("core")
    group = 4
    columns = width // group
    near = lax.all_to_all(
        jnp.broadcast_to(latents[None], (8,) + latents.shape), CTX_CHIPS, split_axis=0, concat_axis=0, tiled=True
    )
    far = swap(near)
    w_blocks = w_out.reshape(-1, group, columns // 128, 128).transpose(1, 2, 0, 3).reshape(group, -1, 128)
    w_blocks, _ = lax.optimization_barrier((w_blocks, near[0, :8]))
    w_near = lax.all_to_all(
        jnp.concatenate([w_blocks, w_blocks], axis=0), CTX_CHIPS, split_axis=0, concat_axis=0, tiled=True
    )
    w_far = swap(w_near)
    ids = jnp.stack([lax.axis_index(CTX), core, lax.axis_index("x")]).astype(jnp.int32)
    own = attend(ids, queries, w_kv, near, far, 4)
    before, after = up(own), down(own)
    half = own.shape[1] // 2
    left, right = up(before[:, :half]), down(after[:, half:])
    attn = project(ids, (own, before, after, left, right), w_near, w_far, 8, columns)
    attn = lax.all_to_all(attn, EP + ("x",), split_axis=0, concat_axis=0, tiled=True)
    attn = jnp.sum(attn.reshape(8, group, tok, columns).astype(F32), axis=0)
    attn = attn.transpose(1, 0, 2).reshape(tok, width)
    attended = (resid.astype(F32) + attn).astype(BF)
    wide = attended.astype(F32)
    meansq = jnp.mean(wide * wide, axis=1, keepdims=True)
    normed = (wide * lax.rsqrt(meansq + 1e-06) * norm_gain[None, :]).astype(BF)
    normed2 = jnp.concatenate([normed, swap(normed)], axis=0)

    def exchange(rows):
        units = rows.reshape(chips, -1, 2, width)
        units = lax.all_to_all(units, CHIPS, split_axis=0, concat_axis=0, tiled=True)
        return units.reshape(rows.shape)

    parts = routing(routes, codes)
    arrived = [exchange(dispatch(place, normed2, 2)) for place, _ in parts]
    returned = [exchange(expert(rows, w_gate[0], w_up[0], w_down[0], 2, 7)) for rows in arrived]
    mine, theirs = combine([(factors, rows) for (_, factors), rows in zip(parts, returned)], 4)
    layer_out = (wide + mine + swap(theirs)).astype(BF)
    return (attended, layer_out)


def solution(mesh):
    fine = Mesh(mesh.devices.reshape(SIZES), NAMES)
    rows = P(CTX + EP, None)
    heads = P(CTX + EP, None, None)
    placed = (
        P(CTX, EP),
        P(None, CTX),
        P(None, EP),
        P(EP + CTX, None),
        rows,
        P(),
        rows,
        rows,
        heads,
        heads,
        heads,
    )
    return jax.shard_map(local, mesh=fine, in_specs=placed, out_specs=(rows, rows), check_vma=False)
```

```python
import functools

import jax
import jax.numpy as jnp
from jax import lax
from jax.experimental import pallas as pl
from jax.experimental.pallas import tpu as pltpu
from jax.sharding import Mesh, PartitionSpec as P

NOPE = 128
VD = 128
KV_RANK = 512
TOP = 8
QK = 192
CAP = 3
SLOTS = (slice(0, 3),)

CTX = ("z_lo", "x", "core")
CTX_CHIPS = ("z_lo", "x")
EP = ("z_hi", "y")
CHIPS = ("z_lo", "x", "z_hi", "y")
SIZES = (2, 4, 2, 2, 4)
NAMES = ("z_lo", "x", "core", "z_hi", "y")
SWAP = ((0, 1), (1, 0))
BF = jnp.bfloat16
F32 = jnp.float32
LOG2E = 1.4426950408889634


def attend_kernel(ids_ref, q_ref, w_ref, near_ref, far_ref, out_ref, lat_ref, s_ref, latq_ref, mixed_ref, *, cuts):
    heads = w_ref.shape[1] // (NOPE + VD)
    rows = q_ref.shape[0]
    m = heads * rows
    pairs = near_ref.shape[0]
    keys = 2 * rows * pairs
    for i in range(pairs):
        lat_ref[:, 2 * i * rows : (2 * i + 1) * rows] = near_ref[i]
        lat_ref[:, (2 * i + 1) * rows : (2 * i + 2) * rows] = far_ref[i]
    for h in range(heads):
        here = slice(h * rows, (h + 1) * rows)
        key_weights = w_ref[:, h * (NOPE + VD) : h * (NOPE + VD) + NOPE]
        plain = q_ref[:, h * QK : h * QK + NOPE]
        latq = lax.dot_general(plain, key_weights, (((1,), (1,)), ((), ())), preferred_element_type=F32)
        latq_ref[here, :KV_RANK] = latq.astype(BF)
        latq_ref[here, KV_RANK:] = q_ref[:, h * QK + NOPE : (h + 1) * QK]
    ctx, core = ids_ref[0], ids_ref[1]
    span = keys // cuts
    lane = lax.broadcasted_iota(jnp.int32, (m, rows), 1)
    query = lax.broadcasted_iota(jnp.int32, (m, rows), 0) % rows
    ahead = lane - query
    peak = jnp.full((m, rows), -1e30, F32)
    for j in range(cuts):
        s = jnp.dot(latq_ref[...], lat_ref[:, j * span : (j + 1) * span], preferred_element_type=F32)
        for b in range(span // rows):
            block = j * (span // rows) + b
            pos = 2 * (block // 2) + (core if block % 2 == 0 else 1 - core)
            part = s[:, b * rows : (b + 1) * rows]
            part = jnp.where(ahead <= (ctx - pos) * rows, part, F32(-1e30))
            peak = jnp.maximum(peak, part)
            s_ref[:, block * rows : (block + 1) * rows] = part
    top = jnp.max(peak, axis=1, keepdims=True)
    total = jnp.zeros((m, rows), F32)
    for j in range(cuts):
        probs = []
        for b in range(span // rows):
            first = j * span + b * rows
            p = jnp.exp2((s_ref[:, first : first + rows] - top) * (QK ** (-0.5) * LOG2E))
            total = total + p
            probs.append(p.astype(BF))
        part = lax.dot_general(
            jnp.concatenate(probs, axis=1),
            lat_ref[:KV_RANK, j * span : (j + 1) * span],
            (((1,), (1,)), ((), ())),
            preferred_element_type=F32,
        )
        mixed_ref[...] = part if j == 0 else mixed_ref[...] + part
    mixed = (mixed_ref[...] / jnp.sum(total, axis=1, keepdims=True)).astype(BF)
    for h in range(heads):
        values = w_ref[:, h * (NOPE + VD) + NOPE : (h + 1) * (NOPE + VD)]
        o = jnp.dot(mixed[h * rows : (h + 1) * rows], values, preferred_element_type=F32)
        out_ref[:, h * VD : (h + 1) * VD] = o.astype(BF)


def attend(ids, q, w_kv, near, far, cuts):
    pairs, depth, rows = near.shape
    heads = w_kv.shape[1] // (NOPE + VD)
    keys = 2 * rows * pairs
    m = heads * rows
    whole = pl.BlockSpec(memory_space=pltpu.VMEM)
    return pl.pallas_call(
        functools.partial(attend_kernel, cuts=cuts),
        in_specs=[pl.BlockSpec(memory_space=pltpu.SMEM)] + [whole] * 4,
        out_specs=whole,
        out_shape=jax.ShapeDtypeStruct((rows, heads * VD), BF),
        scratch_shapes=[
            pltpu.VMEM((depth, keys), BF),
            pltpu.VMEM((m, keys), F32),
            pltpu.VMEM((m, depth), BF),
            pltpu.VMEM((m, KV_RANK), F32),
        ],
        compiler_params=pltpu.CompilerParams(vmem_limit_bytes=24 * 2**20),
        cost_estimate=pl.CostEstimate(
            flops=2 * m * keys * (depth + KV_RANK), bytes_accessed=8_000_000, transcendentals=m * keys
        ),
    )(ids, q, w_kv, near, far)


def expert_kernel(x_hbm, g_ref, u_ref, d_ref, out_hbm, x_ref, hid_ref, gate_ref, up_ref, y_ref, sem_in, sem_out):
    units, pair, width = x_ref.shape
    m = units * pair
    first, last = sem_in.shape[0], sem_out.shape[0]
    depth, wide = width // first, width // last
    arrivals = []
    for k in range(first):
        part = slice(k * depth, (k + 1) * depth)
        arrivals.append(pltpu.make_async_copy(x_hbm.at[:, :, part], x_ref.at[:, :, part], sem_in.at[k]))
        arrivals[-1].start()
    for k in range(first):
        part = slice(k * depth, (k + 1) * depth)
        arrivals[k].wait()
        rows = x_ref[:, :, part].reshape(m, depth)
        gate = jnp.dot(rows, g_ref[part], preferred_element_type=F32)
        upward = jnp.dot(rows, u_ref[part], preferred_element_type=F32)
        gate_ref[...] = gate if k == 0 else gate_ref[...] + gate
        up_ref[...] = upward if k == 0 else up_ref[...] + upward
    gate = gate_ref[...]
    hid_ref[...] = (gate / (1.0 + jnp.exp(-gate)) * up_ref[...]).astype(BF)
    departures = []
    for n in range(last):
        part = slice(n * wide, (n + 1) * wide)
        y = jnp.dot(hid_ref[...], d_ref[:, part], preferred_element_type=F32).astype(BF)
        y_ref[:, :, part] = y.reshape(units, pair, wide)
        departures.append(pltpu.make_async_copy(y_ref.at[:, :, part], out_hbm.at[:, :, part], sem_out.at[n]))
        departures[-1].start()
    for copy in departures:
        copy.wait()


def expert(x, w_gate, w_up, w_down, first, last):
    units, pair, width = x.shape
    m = units * pair
    hidden = w_gate.shape[1]
    whole = pl.BlockSpec(memory_space=pltpu.VMEM)
    far = pl.BlockSpec(memory_space=pltpu.HBM)
    return pl.pallas_call(
        expert_kernel,
        in_specs=[far, whole, whole, whole],
        out_specs=far,
        out_shape=jax.ShapeDtypeStruct(x.shape, BF),
        scratch_shapes=[
            pltpu.VMEM(x.shape, BF),
            pltpu.VMEM((m, hidden), BF),
            pltpu.VMEM((m, hidden), F32),
            pltpu.VMEM((m, hidden), F32),
            pltpu.VMEM(x.shape, BF),
            pltpu.SemaphoreType.DMA((first,)),
            pltpu.SemaphoreType.DMA((last,)),
        ],
        compiler_params=pltpu.CompilerParams(vmem_limit_bytes=20 * 2**20),
        cost_estimate=pl.CostEstimate(
            flops=6 * m * width * hidden, bytes_accessed=17_000_000, transcendentals=m * hidden
        ),
    )(x, w_gate, w_up, w_down)


def dispatch_kernel(place_ref, x_ref, out_ref):
    y = jnp.dot(place_ref[...], x_ref[...], preferred_element_type=F32).astype(BF)
    out_ref[...] = y.reshape(out_ref.shape)


def dispatch(place, x, cuts):
    m = place.shape[0]
    tokens, width = x.shape
    n = width // cuts
    return pl.pallas_call(
        dispatch_kernel,
        grid=(cuts,),
        in_specs=[pl.BlockSpec(place.shape, lambda i: (0, 0)), pl.BlockSpec((tokens, n), lambda i: (0, i))],
        out_specs=pl.BlockSpec((m // 2, 2, n), lambda i: (0, 0, i)),
        out_shape=jax.ShapeDtypeStruct((m // 2, 2, width), BF),
        compiler_params=pltpu.CompilerParams(vmem_limit_bytes=32 * 2**20),
        cost_estimate=pl.CostEstimate(
            flops=2 * m * tokens * width, bytes_accessed=2 * m * width + 2 * tokens * width, transcendentals=0
        ),
    )(place, x)


def combine_kernel(*refs):
    *in_refs, own_ref, far_ref = refs
    tok = own_ref.shape[0]
    y = None
    for factors_ref, x_ref in zip(in_refs[::2], in_refs[1::2]):
        rows = x_ref[...].reshape(factors_ref.shape[1], x_ref.shape[2])
        part = jnp.dot(factors_ref[...], rows, preferred_element_type=F32)
        y = part if y is None else y + part
    y = y[: 2 * tok] + y[2 * tok :]
    own_ref[...] = y[:tok]
    far_ref[...] = y[tok:]


def combine(parts, cuts):
    width = parts[0][1].shape[2]
    n = width // cuts
    tok = parts[0][0].shape[0] // 4
    half = pl.BlockSpec((tok, n), lambda i: (0, i))
    in_specs = []
    for factors, x in parts:
        in_specs.append(pl.BlockSpec(factors.shape, lambda i: (0, 0)))
        in_specs.append(pl.BlockSpec((x.shape[0], 2, n), lambda i: (0, 0, i)))
    rows = sum(2 * x.shape[0] for _, x in parts)
    return pl.pallas_call(
        combine_kernel,
        grid=(cuts,),
        in_specs=in_specs,
        out_specs=(half, half),
        out_shape=(jax.ShapeDtypeStruct((tok, width), F32),) * 2,
        compiler_params=pltpu.CompilerParams(vmem_limit_bytes=32 * 2**20),
        cost_estimate=pl.CostEstimate(
            flops=8 * tok * rows * width, bytes_accessed=2 * rows * width, transcendentals=0
        ),
    )(*[a for part in parts for a in part])


def project_kernel(ids_ref, own_ref, before_ref, after_ref, left_ref, right_ref, near_ref, far_ref, out_ref, x_ref, w_ref):
    rows = own_ref.shape[0]
    group, tok = 4, out_ref.shape[1]
    parts = out_ref.shape[0] // group
    core, x = ids_ref[1], ids_ref[2]
    half = left_ref.shape[1]
    x_ref[:rows] = own_ref[...]
    x_ref[rows : 2 * rows] = after_ref[...]
    x_ref[2 * rows : 3 * rows, :half] = left_ref[...]
    x_ref[2 * rows : 3 * rows, half:] = right_ref[...]
    x_ref[3 * rows :] = before_ref[...]
    deep = VD // 2
    blocks = w_ref.shape[1] // 128
    for side, ref in enumerate((near_ref, far_ref)):
        offset = (core if side == 0 else 1 - core) * deep
        for j in range(ref.shape[0]):
            here = pl.ds(pl.multiple_of(j * VD + offset, deep), deep)
            for b in range(blocks):
                w_ref[here, b * 128 : (b + 1) * 128] = ref[j, b * deep : (b + 1) * deep]
    for d in range(group):
        y = jnp.dot(x_ref[d * rows : (d + 1) * rows], w_ref[...], preferred_element_type=F32).astype(BF)
        target = lax.rem(x + d, group)
        for e in range(parts):
            out_ref[e * group + target] = y[e * tok : (e + 1) * tok]


def project(ids, pieces, near, far, parts, width):
    rows, depth = pieces[0].shape
    whole = pl.BlockSpec(memory_space=pltpu.VMEM)
    group = 4
    return pl.pallas_call(
        project_kernel,
        in_specs=[pl.BlockSpec(memory_space=pltpu.SMEM)] + [whole] * (len(pieces) + 2),
        out_specs=whole,
        out_shape=jax.ShapeDtypeStruct((parts * group, rows // parts, width), BF),
        scratch_shapes=[pltpu.VMEM((group * rows, depth), BF), pltpu.VMEM((depth, width), BF)],
        compiler_params=pltpu.CompilerParams(vmem_limit_bytes=32 * 2**20),
        cost_estimate=pl.CostEstimate(
            flops=2 * group * rows * depth * width, bytes_accessed=2 * depth * width, transcendentals=0
        ),
    )(ids, *pieces, near, far)


def swap(mine):
    return lax.ppermute(mine, "core", SWAP)


def up(a):
    return lax.ppermute(a, "x", [(i, (i + 1) % 4) for i in range(4)])


def down(a):
    return lax.ppermute(a, "x", [(i, (i + 3) % 4) for i in range(4)])


def routing(routes, codes):
    tok = routes.shape[0]
    core = lax.axis_index("core")
    code_float = codes.astype(F32)
    mix = code_float / jnp.sum(code_float, axis=1, keepdims=True)
    routes2, mix2 = jnp.stack([routes, swap(routes)]), jnp.stack([mix, swap(mix)])
    chosen = routes2[:, :, :, None] == jnp.arange(64, dtype=jnp.int32)
    weight = jnp.sum(jnp.where(chosen, mix2[..., None], F32(0.0)), axis=2)
    has = jnp.any(chosen, axis=2)

    def of_core(a):
        a = a.reshape(2, tok, 8, 2, 4)
        return jnp.where(core == 0, a[:, :, :, 0], a[:, :, :, 1]).reshape(2, tok, 32)

    weight, has = of_core(weight), of_core(has)
    count = has.astype(jnp.int32)
    slot = jnp.cumsum(count, axis=1) - count
    place = has[:, :, :, None] & (slot[:, :, :, None] == jnp.arange(CAP, dtype=jnp.int32))
    place = place.transpose(2, 3, 0, 1)[:, :, :, None, :]
    same = jnp.arange(2)[:, None, None] == jnp.arange(2)[None, :, None]
    place = (place & same).reshape(32, CAP, 2, 2 * tok)
    place = jnp.broadcast_to(place[:, None], (32, 2, CAP, 2, 2 * tok)).reshape(64, CAP, 2, 2 * tok)
    gains = weight.transpose(2, 0, 1).reshape(32, 2 * tok)
    gains = jnp.broadcast_to(gains[:, None], (32, 2, 2 * tok)).reshape(64, 1, 1, 2 * tok)
    factors = jnp.where(place, gains, F32(0.0))
    high = lax.reduce_precision(factors, 8, 7)
    factors = jnp.concatenate([high, factors - high], axis=3).astype(BF)
    place = place.astype(BF)
    parts = []
    for slots in SLOTS:
        parts.append((place[:, slots].reshape(-1, 2 * tok), factors[:, slots].reshape(-1, 4 * tok).T))
    return parts


def local(queries, latents, w_kv, w_out, resid, norm_gain, routes, codes, w_gate, w_up, w_down):
    tok, width = resid.shape
    chips = 64
    core = lax.axis_index("core")
    group = 4
    columns = width // group
    near = lax.all_to_all(
        jnp.broadcast_to(latents[None], (8,) + latents.shape), CTX_CHIPS, split_axis=0, concat_axis=0, tiled=True
    )
    far = swap(near)
    w_blocks = w_out.reshape(-1, group, columns // 128, 128).transpose(1, 2, 0, 3).reshape(group, -1, 128)
    w_blocks, _ = lax.optimization_barrier((jnp.concatenate([w_blocks, w_blocks], axis=0), near[0, :8]))
    w_near = lax.all_to_all(w_blocks, CTX_CHIPS, split_axis=0, concat_axis=0, tiled=True)
    ids = jnp.stack([lax.axis_index(CTX), core, lax.axis_index("x")]).astype(jnp.int32)
    own = attend(ids, queries, w_kv, near, far, 4)
    own, w_near = lax.optimization_barrier((own, w_near))
    w_far = swap(w_near)
    before, after = up(own), down(own)
    half = own.shape[1] // 2
    left, right = up(before[:, :half]), down(after[:, half:])
    attn = project(ids, (own, before, after, left, right), w_near, w_far, 8, columns)
    attn = lax.all_to_all(attn, EP + ("x",), split_axis=0, concat_axis=0, tiled=True)
    attn = jnp.sum(attn.reshape(8, group, tok, columns).astype(F32), axis=0)
    attn = attn.transpose(1, 0, 2).reshape(tok, width)
    attended = (resid.astype(F32) + attn).astype(BF)
    wide = attended.astype(F32)
    meansq = jnp.mean(wide * wide, axis=1, keepdims=True)
    normed = (wide * lax.rsqrt(meansq + 1e-06) * norm_gain[None, :]).astype(BF)
    normed2 = jnp.concatenate([normed, swap(normed)], axis=0)

    def exchange(rows):
        units = rows.reshape(chips, -1, 2, width)
        units = lax.all_to_all(units, CHIPS, split_axis=0, concat_axis=0, tiled=True)
        return units.reshape(rows.shape)

    parts = routing(routes, codes)
    arrived = [exchange(dispatch(place, normed2, 2)) for place, _ in parts]
    returned = [exchange(expert(rows, w_gate[0], w_up[0], w_down[0], 2, 7)) for rows in arrived]
    mine, theirs = combine([(factors, rows) for (_, factors), rows in zip(parts, returned)], 4)
    layer_out = (wide + mine + swap(theirs)).astype(BF)
    return (attended, layer_out)


def solution(mesh):
    fine = Mesh(mesh.devices.reshape(SIZES), NAMES)
    rows = P(CTX + EP, None)
    heads = P(CTX + EP, None, None)
    placed = (
        P(CTX, EP),
        P(None, CTX),
        P(None, EP),
        P(EP + CTX, None),
        rows,
        P(),
        rows,
        rows,
        heads,
        heads,
        heads,
    )
    return jax.shard_map(local, mesh=fine, in_specs=placed, out_specs=(rows, rows), check_vma=False)
```

```python
import functools

import jax
import jax.numpy as jnp
from jax import lax
from jax.experimental import pallas as pl
from jax.experimental.pallas import tpu as pltpu
from jax.sharding import Mesh, PartitionSpec as P

NOPE = 128
VD = 128
KV_RANK = 512
TOP = 8
QK = 192
CAP = 3
SLOTS = (slice(0, 3),)

CTX = ("z_lo", "x", "core")
CTX_CHIPS = ("z_lo", "x")
EP = ("z_hi", "y")
CHIPS = ("z_lo", "x", "z_hi", "y")
SIZES = (2, 4, 2, 2, 4)
NAMES = ("z_lo", "x", "core", "z_hi", "y")
SWAP = ((0, 1), (1, 0))
BF = jnp.bfloat16
F32 = jnp.float32
LOG2E = 1.4426950408889634


def in_hbm(a):
    return pltpu.with_memory_space_constraint(a, pltpu.HBM)


def attend_kernel(
    ids_ref, q_hbm, w_hbm, near_ref, far_ref, out_ref, q_ref, w_ref, lat_ref, s_ref, latq_ref, mixed_ref, sems, *, cuts
):
    heads = w_ref.shape[1] // (NOPE + VD)
    rows = q_ref.shape[0]
    m = heads * rows
    pairs = near_ref.shape[0]
    keys = 2 * rows * pairs
    q_copy = pltpu.make_async_copy(q_hbm, q_ref, sems.at[0])
    w_copy = pltpu.make_async_copy(w_hbm, w_ref, sems.at[1])
    q_copy.start()
    w_copy.start()
    for i in range(pairs):
        lat_ref[:, 2 * i * rows : (2 * i + 1) * rows] = near_ref[i]
        lat_ref[:, (2 * i + 1) * rows : (2 * i + 2) * rows] = far_ref[i]
    q_copy.wait()
    w_copy.wait()
    for h in range(heads):
        here = slice(h * rows, (h + 1) * rows)
        key_weights = w_ref[:, h * (NOPE + VD) : h * (NOPE + VD) + NOPE]
        plain = q_ref[:, h * QK : h * QK + NOPE]
        latq = lax.dot_general(plain, key_weights, (((1,), (1,)), ((), ())), preferred_element_type=F32)
        latq_ref[here, :KV_RANK] = latq.astype(BF)
        latq_ref[here, KV_RANK:] = q_ref[:, h * QK + NOPE : (h + 1) * QK]
    ctx, core = ids_ref[0], ids_ref[1]
    span = keys // cuts
    lane = lax.broadcasted_iota(jnp.int32, (m, rows), 1)
    query = lax.broadcasted_iota(jnp.int32, (m, rows), 0) % rows
    ahead = lane - query
    peak = jnp.full((m, rows), -1e30, F32)
    for j in range(cuts):
        s = jnp.dot(latq_ref[...], lat_ref[:, j * span : (j + 1) * span], preferred_element_type=F32)
        for b in range(span // rows):
            block = j * (span // rows) + b
            pos = 2 * (block // 2) + (core if block % 2 == 0 else 1 - core)
            part = s[:, b * rows : (b + 1) * rows]
            part = jnp.where(ahead <= (ctx - pos) * rows, part, F32(-1e30))
            peak = jnp.maximum(peak, part)
            s_ref[:, block * rows : (block + 1) * rows] = part
    top = jnp.max(peak, axis=1, keepdims=True)
    total = jnp.zeros((m, rows), F32)
    for j in range(cuts):
        probs = []
        for b in range(span // rows):
            first = j * span + b * rows
            p = jnp.exp2((s_ref[:, first : first + rows] - top) * (QK ** (-0.5) * LOG2E))
            total = total + p
            probs.append(p.astype(BF))
        part = lax.dot_general(
            jnp.concatenate(probs, axis=1),
            lat_ref[:KV_RANK, j * span : (j + 1) * span],
            (((1,), (1,)), ((), ())),
            preferred_element_type=F32,
        )
        mixed_ref[...] = part if j == 0 else mixed_ref[...] + part
    mixed = (mixed_ref[...] / jnp.sum(total, axis=1, keepdims=True)).astype(BF)
    for h in range(heads):
        values = w_ref[:, h * (NOPE + VD) + NOPE : (h + 1) * (NOPE + VD)]
        o = jnp.dot(mixed[h * rows : (h + 1) * rows], values, preferred_element_type=F32)
        out_ref[:, h * VD : (h + 1) * VD] = o.astype(BF)


def attend(ids, q, w_kv, near, far, cuts):
    pairs, depth, rows = near.shape
    heads = w_kv.shape[1] // (NOPE + VD)
    keys = 2 * rows * pairs
    m = heads * rows
    whole = pl.BlockSpec(memory_space=pltpu.VMEM)
    hbm = pl.BlockSpec(memory_space=pltpu.HBM)
    return pl.pallas_call(
        functools.partial(attend_kernel, cuts=cuts),
        in_specs=[pl.BlockSpec(memory_space=pltpu.SMEM), hbm, hbm, whole, whole],
        out_specs=whole,
        out_shape=jax.ShapeDtypeStruct((rows, heads * VD), BF),
        scratch_shapes=[
            pltpu.VMEM(q.shape, BF),
            pltpu.VMEM(w_kv.shape, BF),
            pltpu.VMEM((depth, keys), BF),
            pltpu.VMEM((m, keys), F32),
            pltpu.VMEM((m, depth), BF),
            pltpu.VMEM((m, KV_RANK), F32),
            pltpu.SemaphoreType.DMA((2,)),
        ],
        compiler_params=pltpu.CompilerParams(vmem_limit_bytes=28 * 2**20),
        cost_estimate=pl.CostEstimate(
            flops=2 * m * keys * (depth + KV_RANK), bytes_accessed=8_000_000, transcendentals=m * keys
        ),
    )(ids, in_hbm(q), in_hbm(w_kv), near, far)


def expert_kernel(x_hbm, g_ref, u_ref, d_hbm, out_hbm, d_ref, x_ref, hid_ref, gate_ref, up_ref, y_ref, sem_d, sem_in, sem_out):
    units, pair, width = x_ref.shape
    m = units * pair
    first, last = sem_in.shape[0], sem_out.shape[0]
    depth, wide = width // first, width // last
    arrivals = []
    for k in range(first):
        part = slice(k * depth, (k + 1) * depth)
        arrivals.append(pltpu.make_async_copy(x_hbm.at[:, :, part], x_ref.at[:, :, part], sem_in.at[k]))
        arrivals[-1].start()
    d_copy = pltpu.make_async_copy(d_hbm, d_ref, sem_d.at[0])
    d_copy.start()
    for k in range(first):
        part = slice(k * depth, (k + 1) * depth)
        arrivals[k].wait()
        rows = x_ref[:, :, part].reshape(m, depth)
        gate = jnp.dot(rows, g_ref[part], preferred_element_type=F32)
        upward = jnp.dot(rows, u_ref[part], preferred_element_type=F32)
        gate_ref[...] = gate if k == 0 else gate_ref[...] + gate
        up_ref[...] = upward if k == 0 else up_ref[...] + upward
    gate = gate_ref[...]
    hid_ref[...] = (gate / (1.0 + jnp.exp(-gate)) * up_ref[...]).astype(BF)
    d_copy.wait()
    departures = []
    for n in range(last):
        part = slice(n * wide, (n + 1) * wide)
        y = jnp.dot(hid_ref[...], d_ref[:, part], preferred_element_type=F32).astype(BF)
        y_ref[:, :, part] = y.reshape(units, pair, wide)
        departures.append(pltpu.make_async_copy(y_ref.at[:, :, part], out_hbm.at[:, :, part], sem_out.at[n]))
        departures[-1].start()
    for copy in departures:
        copy.wait()


def expert(x, w_gate, w_up, w_down, first, last):
    units, pair, width = x.shape
    m = units * pair
    hidden = w_gate.shape[1]
    whole = pl.BlockSpec(memory_space=pltpu.VMEM)
    far = pl.BlockSpec(memory_space=pltpu.HBM)
    return pl.pallas_call(
        expert_kernel,
        in_specs=[far, whole, whole, far],
        out_specs=far,
        out_shape=pltpu.HBM(x.shape, BF),
        scratch_shapes=[
            pltpu.VMEM(w_down.shape, BF),
            pltpu.VMEM(x.shape, BF),
            pltpu.VMEM((m, hidden), BF),
            pltpu.VMEM((m, hidden), F32),
            pltpu.VMEM((m, hidden), F32),
            pltpu.VMEM(x.shape, BF),
            pltpu.SemaphoreType.DMA((1,)),
            pltpu.SemaphoreType.DMA((first,)),
            pltpu.SemaphoreType.DMA((last,)),
        ],
        compiler_params=pltpu.CompilerParams(vmem_limit_bytes=24 * 2**20),
        cost_estimate=pl.CostEstimate(
            flops=6 * m * width * hidden, bytes_accessed=17_000_000, transcendentals=m * hidden
        ),
    )(x, w_gate, w_up, in_hbm(w_down))


def dispatch_kernel(place_ref, x_ref, out_ref):
    y = jnp.dot(place_ref[...], x_ref[...], preferred_element_type=F32).astype(BF)
    out_ref[...] = y.reshape(out_ref.shape)


def dispatch(place, x, cuts):
    m = place.shape[0]
    tokens, width = x.shape
    n = width // cuts
    return pl.pallas_call(
        dispatch_kernel,
        grid=(cuts,),
        in_specs=[pl.BlockSpec(place.shape, lambda i: (0, 0)), pl.BlockSpec((tokens, n), lambda i: (0, i))],
        out_specs=pl.BlockSpec((m // 2, 2, n), lambda i: (0, 0, i)),
        out_shape=jax.ShapeDtypeStruct((m // 2, 2, width), BF),
        compiler_params=pltpu.CompilerParams(vmem_limit_bytes=32 * 2**20),
        cost_estimate=pl.CostEstimate(
            flops=2 * m * tokens * width, bytes_accessed=2 * m * width + 2 * tokens * width, transcendentals=0
        ),
    )(place, x)


def combine_kernel(*refs):
    *in_refs, own_ref, far_ref = refs
    tok = own_ref.shape[0]
    y = None
    for factors_ref, x_ref in zip(in_refs[::2], in_refs[1::2]):
        rows = x_ref[...].reshape(factors_ref.shape[1], x_ref.shape[2])
        part = jnp.dot(factors_ref[...], rows, preferred_element_type=F32)
        y = part if y is None else y + part
    y = y[: 2 * tok] + y[2 * tok :]
    own_ref[...] = y[:tok]
    far_ref[...] = y[tok:]


def combine(parts, cuts):
    width = parts[0][1].shape[2]
    n = width // cuts
    tok = parts[0][0].shape[0] // 4
    half = pl.BlockSpec((tok, n), lambda i: (0, i))
    in_specs = []
    for factors, x in parts:
        in_specs.append(pl.BlockSpec(factors.shape, lambda i: (0, 0)))
        in_specs.append(pl.BlockSpec((x.shape[0], 2, n), lambda i: (0, 0, i)))
    rows = sum(2 * x.shape[0] for _, x in parts)
    return pl.pallas_call(
        combine_kernel,
        grid=(cuts,),
        in_specs=in_specs,
        out_specs=(half, half),
        out_shape=(jax.ShapeDtypeStruct((tok, width), F32),) * 2,
        compiler_params=pltpu.CompilerParams(vmem_limit_bytes=32 * 2**20),
        cost_estimate=pl.CostEstimate(
            flops=8 * tok * rows * width, bytes_accessed=2 * rows * width, transcendentals=0
        ),
    )(*[a for part in parts for a in part])


def project_kernel(ids_ref, own_ref, before_ref, after_ref, left_ref, right_ref, near_ref, far_ref, out_ref, x_ref, w_ref):
    rows = own_ref.shape[0]
    group, tok = 4, out_ref.shape[1]
    parts = out_ref.shape[0] // group
    core, x = ids_ref[1], ids_ref[2]
    half = left_ref.shape[1]
    x_ref[:rows] = own_ref[...]
    x_ref[rows : 2 * rows] = after_ref[...]
    x_ref[2 * rows : 3 * rows, :half] = left_ref[...]
    x_ref[2 * rows : 3 * rows, half:] = right_ref[...]
    x_ref[3 * rows :] = before_ref[...]
    deep = VD // 2
    for side, ref in enumerate((near_ref, far_ref)):
        offset = (core if side == 0 else 1 - core) * deep
        for j in range(ref.shape[0]):
            w_ref[pl.ds(pl.multiple_of(j * VD + offset, deep), deep)] = ref[j]
    for d in range(group):
        y = jnp.dot(x_ref[d * rows : (d + 1) * rows], w_ref[...], preferred_element_type=F32).astype(BF)
        target = lax.rem(x + d, group)
        for e in range(parts):
            out_ref[e * group + target] = y[e * tok : (e + 1) * tok]


def project(ids, pieces, near, far, parts, width):
    rows, depth = pieces[0].shape
    whole = pl.BlockSpec(memory_space=pltpu.VMEM)
    group = 4
    return pl.pallas_call(
        project_kernel,
        in_specs=[pl.BlockSpec(memory_space=pltpu.SMEM)] + [whole] * (len(pieces) + 2),
        out_specs=whole,
        out_shape=jax.ShapeDtypeStruct((parts * group, rows // parts, width), BF),
        scratch_shapes=[pltpu.VMEM((group * rows, depth), BF), pltpu.VMEM((depth, width), BF)],
        compiler_params=pltpu.CompilerParams(vmem_limit_bytes=32 * 2**20),
        cost_estimate=pl.CostEstimate(
            flops=2 * group * rows * depth * width, bytes_accessed=2 * depth * width, transcendentals=0
        ),
    )(ids, *pieces, near, far)


def swap(mine):
    return lax.ppermute(mine, "core", SWAP)


def up(a):
    return lax.ppermute(a, "x", [(i, (i + 1) % 4) for i in range(4)])


def down(a):
    return lax.ppermute(a, "x", [(i, (i + 3) % 4) for i in range(4)])


def routing(routes, codes):
    tok = routes.shape[0]
    core = lax.axis_index("core")
    code_float = codes.astype(F32)
    mix = code_float / jnp.sum(code_float, axis=1, keepdims=True)
    routes2, mix2 = jnp.stack([routes, swap(routes)]), jnp.stack([mix, swap(mix)])
    chosen = routes2[:, :, :, None] == jnp.arange(64, dtype=jnp.int32)
    weight = jnp.sum(jnp.where(chosen, mix2[..., None], F32(0.0)), axis=2)
    has = jnp.any(chosen, axis=2)

    def of_core(a):
        a = a.reshape(2, tok, 8, 2, 4)
        return jnp.where(core == 0, a[:, :, :, 0], a[:, :, :, 1]).reshape(2, tok, 32)

    weight, has = of_core(weight), of_core(has)
    count = has.astype(jnp.int32)
    slot = jnp.cumsum(count, axis=1) - count
    place = has[:, :, :, None] & (slot[:, :, :, None] == jnp.arange(CAP, dtype=jnp.int32))
    place = place.transpose(2, 3, 0, 1)[:, :, :, None, :]
    same = jnp.arange(2)[:, None, None] == jnp.arange(2)[None, :, None]
    place = (place & same).reshape(32, CAP, 2, 2 * tok)
    place = jnp.broadcast_to(place[:, None], (32, 2, CAP, 2, 2 * tok)).reshape(64, CAP, 2, 2 * tok)
    gains = weight.transpose(2, 0, 1).reshape(32, 2 * tok)
    gains = jnp.broadcast_to(gains[:, None], (32, 2, 2 * tok)).reshape(64, 1, 1, 2 * tok)
    factors = jnp.where(place, gains, F32(0.0))
    high = lax.reduce_precision(factors, 8, 7)
    factors = jnp.concatenate([high, factors - high], axis=3).astype(BF)
    place = place.astype(BF)
    parts = []
    for slots in SLOTS:
        parts.append((place[:, slots].reshape(-1, 2 * tok), factors[:, slots].reshape(-1, 4 * tok).T))
    return parts


def local(queries, latents, w_kv, w_out, resid, norm_gain, routes, codes, w_gate, w_up, w_down):
    tok, width = resid.shape
    chips = 64
    core = lax.axis_index("core")
    group = 4
    columns = width // group
    near = lax.all_to_all(
        jnp.broadcast_to(latents[None], (8,) + latents.shape), CTX_CHIPS, split_axis=0, concat_axis=0, tiled=True
    )
    far = swap(near)
    w_blocks = jnp.stack([w_out[:, i * columns : (i + 1) * columns] for i in range(group)] * 2)
    w_blocks, _ = lax.optimization_barrier((w_blocks, near[0, :8]))
    w_near = lax.all_to_all(w_blocks, CTX_CHIPS, split_axis=0, concat_axis=0, tiled=True)
    ids = jnp.stack([lax.axis_index(CTX), core, lax.axis_index("x")]).astype(jnp.int32)
    own = attend(ids, queries, w_kv, near, far, 4)
    own, w_near = lax.optimization_barrier((own, w_near))
    w_far = swap(w_near)
    before, after = up(own), down(own)
    half = own.shape[1] // 2
    left, right = up(before[:, :half]), down(after[:, half:])
    attn = project(ids, (own, before, after, left, right), w_near, w_far, 8, columns)
    attn = lax.all_to_all(attn, EP + ("x",), split_axis=0, concat_axis=0, tiled=True)
    attn = jnp.sum(attn.reshape(8, group, tok, columns).astype(F32), axis=0)
    attn = attn.transpose(1, 0, 2).reshape(tok, width)
    attended = (resid.astype(F32) + attn).astype(BF)
    wide = attended.astype(F32)
    meansq = jnp.mean(wide * wide, axis=1, keepdims=True)
    normed = (wide * lax.rsqrt(meansq + 1e-06) * norm_gain[None, :]).astype(BF)
    normed2 = jnp.concatenate([normed, swap(normed)], axis=0)

    def exchange(rows):
        units = rows.reshape(chips, -1, 2, width)
        units = lax.all_to_all(units, CHIPS, split_axis=0, concat_axis=0, tiled=True)
        return units.reshape(rows.shape)

    parts = routing(routes, codes)
    arrived = [exchange(dispatch(place, normed2, 2)) for place, _ in parts]
    returned = [exchange(expert(rows, w_gate[0], w_up[0], w_down[0], 2, 7)) for rows in arrived]
    mine, theirs = combine([(factors, rows) for (_, factors), rows in zip(parts, returned)], 4)
    layer_out = (wide + mine + swap(theirs)).astype(BF)
    return (attended, layer_out)


def solution(mesh):
    fine = Mesh(mesh.devices.reshape(SIZES), NAMES)
    rows = P(CTX + EP, None)
    heads = P(CTX + EP, None, None)
    placed = (
        P(CTX, EP),
        P(None, CTX),
        P(None, EP),
        P(EP + CTX, None),
        rows,
        P(),
        rows,
        rows,
        heads,
        heads,
        heads,
    )
    return jax.shard_map(local, mesh=fine, in_specs=placed, out_specs=(rows, rows), check_vma=False)
```

```python
import functools

import jax
import jax.numpy as jnp
from jax import lax
from jax.experimental import pallas as pl
from jax.experimental.pallas import tpu as pltpu
from jax.sharding import Mesh, PartitionSpec as P

NOPE = 128
VD = 128
KV_RANK = 512
TOP = 8
QK = 192
CAP = 3
SLOTS = (slice(0, 3),)

CTX = ("z_lo", "x", "core")
CTX_CHIPS = ("z_lo", "x")
EP = ("z_hi", "y")
CHIPS = ("z_lo", "x", "z_hi", "y")
SIZES = (2, 4, 2, 2, 4)
NAMES = ("z_lo", "x", "core", "z_hi", "y")
SWAP = ((0, 1), (1, 0))
BF = jnp.bfloat16
F32 = jnp.float32
LOG2E = 1.4426950408889634


def in_hbm(a):
    return pltpu.with_memory_space_constraint(a, pltpu.HBM)


def attend_kernel(
    ids_ref, q_hbm, w_hbm, near_ref, far_ref, out_ref, q_ref, w_ref, lat_ref, s_ref, latq_ref, mixed_ref, sems, *, turn, cuts
):
    heads = w_ref.shape[1] // (NOPE + VD)
    rows = q_ref.shape[0]
    m = heads * rows
    pairs = near_ref.shape[0]
    keys = 2 * rows * pairs
    q_part = q_hbm.at[:, turn * q_ref.shape[1] : (turn + 1) * q_ref.shape[1]]
    w_part = w_hbm.at[:, turn * w_ref.shape[1] : (turn + 1) * w_ref.shape[1]]
    q_copy = pltpu.make_async_copy(q_part, q_ref, sems.at[0])
    w_copy = pltpu.make_async_copy(w_part, w_ref, sems.at[1])
    q_copy.start()
    w_copy.start()
    for i in range(pairs):
        lat_ref[:, 2 * i * rows : (2 * i + 1) * rows] = near_ref[i]
        lat_ref[:, (2 * i + 1) * rows : (2 * i + 2) * rows] = far_ref[i]
    q_copy.wait()
    w_copy.wait()
    for h in range(heads):
        here = slice(h * rows, (h + 1) * rows)
        key_weights = w_ref[:, h * (NOPE + VD) : h * (NOPE + VD) + NOPE]
        plain = q_ref[:, h * QK : h * QK + NOPE]
        latq = lax.dot_general(plain, key_weights, (((1,), (1,)), ((), ())), preferred_element_type=F32)
        latq_ref[here, :KV_RANK] = latq.astype(BF)
        latq_ref[here, KV_RANK:] = q_ref[:, h * QK + NOPE : (h + 1) * QK]
    ctx, core = ids_ref[0], ids_ref[1]
    span = keys // cuts
    lane = lax.broadcasted_iota(jnp.int32, (m, rows), 1)
    query = lax.broadcasted_iota(jnp.int32, (m, rows), 0) % rows
    ahead = lane - query
    peak = jnp.full((m, rows), -1e30, F32)
    for j in range(cuts):
        s = jnp.dot(latq_ref[...], lat_ref[:, j * span : (j + 1) * span], preferred_element_type=F32)
        for b in range(span // rows):
            block = j * (span // rows) + b
            pos = 2 * (block // 2) + (core if block % 2 == 0 else 1 - core)
            part = s[:, b * rows : (b + 1) * rows]
            part = jnp.where(ahead <= (ctx - pos) * rows, part, F32(-1e30))
            peak = jnp.maximum(peak, part)
            s_ref[:, block * rows : (block + 1) * rows] = part
    top = jnp.max(peak, axis=1, keepdims=True)
    total = jnp.zeros((m, rows), F32)
    for j in range(cuts):
        probs = []
        for b in range(span // rows):
            first = j * span + b * rows
            p = jnp.exp2((s_ref[:, first : first + rows] - top) * (QK ** (-0.5) * LOG2E))
            total = total + p
            probs.append(p.astype(BF))
        part = lax.dot_general(
            jnp.concatenate(probs, axis=1),
            lat_ref[:KV_RANK, j * span : (j + 1) * span],
            (((1,), (1,)), ((), ())),
            preferred_element_type=F32,
        )
        mixed_ref[...] = part if j == 0 else mixed_ref[...] + part
    mixed = (mixed_ref[...] / jnp.sum(total, axis=1, keepdims=True)).astype(BF)
    for h in range(heads):
        values = w_ref[:, h * (NOPE + VD) + NOPE : (h + 1) * (NOPE + VD)]
        o = jnp.dot(mixed[h * rows : (h + 1) * rows], values, preferred_element_type=F32)
        out_ref[:, h * VD : (h + 1) * VD] = o.astype(BF)


def attend(ids, q, w_kv, near, far, turn, turns, cuts):
    pairs, depth, rows = near.shape
    heads = w_kv.shape[1] // (NOPE + VD) // turns
    keys = 2 * rows * pairs
    m = heads * rows
    whole = pl.BlockSpec(memory_space=pltpu.VMEM)
    hbm = pl.BlockSpec(memory_space=pltpu.HBM)
    return pl.pallas_call(
        functools.partial(attend_kernel, turn=turn, cuts=cuts),
        in_specs=[pl.BlockSpec(memory_space=pltpu.SMEM), hbm, hbm, whole, whole],
        out_specs=whole,
        out_shape=jax.ShapeDtypeStruct((rows, heads * VD), BF),
        scratch_shapes=[
            pltpu.VMEM((rows, heads * QK), BF),
            pltpu.VMEM((KV_RANK, heads * (NOPE + VD)), BF),
            pltpu.VMEM((depth, keys), BF),
            pltpu.VMEM((m, keys), F32),
            pltpu.VMEM((m, depth), BF),
            pltpu.VMEM((m, KV_RANK), F32),
            pltpu.SemaphoreType.DMA((2,)),
        ],
        compiler_params=pltpu.CompilerParams(vmem_limit_bytes=28 * 2**20),
        cost_estimate=pl.CostEstimate(
            flops=2 * m * keys * (depth + KV_RANK), bytes_accessed=8_000_000, transcendentals=m * keys
        ),
    )(ids, in_hbm(q), in_hbm(w_kv), near, far)


def expert_kernel(x_hbm, g_ref, u_ref, d_hbm, out_hbm, d_ref, x_ref, hid_ref, gate_ref, up_ref, y_ref, sem_d, sem_in, sem_out):
    units, pair, width = x_ref.shape
    m = units * pair
    first, last = sem_in.shape[0], sem_out.shape[0]
    depth, wide = width // first, width // last
    arrivals = []
    for k in range(first):
        part = slice(k * depth, (k + 1) * depth)
        arrivals.append(pltpu.make_async_copy(x_hbm.at[:, :, part], x_ref.at[:, :, part], sem_in.at[k]))
        arrivals[-1].start()
    d_copy = pltpu.make_async_copy(d_hbm, d_ref, sem_d.at[0])
    d_copy.start()
    for k in range(first):
        part = slice(k * depth, (k + 1) * depth)
        arrivals[k].wait()
        rows = x_ref[:, :, part].reshape(m, depth)
        gate = jnp.dot(rows, g_ref[part], preferred_element_type=F32)
        upward = jnp.dot(rows, u_ref[part], preferred_element_type=F32)
        gate_ref[...] = gate if k == 0 else gate_ref[...] + gate
        up_ref[...] = upward if k == 0 else up_ref[...] + upward
    gate = gate_ref[...]
    hid_ref[...] = (gate / (1.0 + jnp.exp(-gate)) * up_ref[...]).astype(BF)
    d_copy.wait()
    departures = []
    for n in range(last):
        part = slice(n * wide, (n + 1) * wide)
        y = jnp.dot(hid_ref[...], d_ref[:, part], preferred_element_type=F32).astype(BF)
        y_ref[:, :, part] = y.reshape(units, pair, wide)
        departures.append(pltpu.make_async_copy(y_ref.at[:, :, part], out_hbm.at[:, :, part], sem_out.at[n]))
        departures[-1].start()
    for copy in departures:
        copy.wait()


def expert(x, w_gate, w_up, w_down, first, last):
    units, pair, width = x.shape
    m = units * pair
    hidden = w_gate.shape[1]
    whole = pl.BlockSpec(memory_space=pltpu.VMEM)
    far = pl.BlockSpec(memory_space=pltpu.HBM)
    return pl.pallas_call(
        expert_kernel,
        in_specs=[far, whole, whole, far],
        out_specs=far,
        out_shape=pltpu.HBM(x.shape, BF),
        scratch_shapes=[
            pltpu.VMEM(w_down.shape, BF),
            pltpu.VMEM(x.shape, BF),
            pltpu.VMEM((m, hidden), BF),
            pltpu.VMEM((m, hidden), F32),
            pltpu.VMEM((m, hidden), F32),
            pltpu.VMEM(x.shape, BF),
            pltpu.SemaphoreType.DMA((1,)),
            pltpu.SemaphoreType.DMA((first,)),
            pltpu.SemaphoreType.DMA((last,)),
        ],
        compiler_params=pltpu.CompilerParams(vmem_limit_bytes=24 * 2**20),
        cost_estimate=pl.CostEstimate(
            flops=6 * m * width * hidden, bytes_accessed=17_000_000, transcendentals=m * hidden
        ),
    )(x, w_gate, w_up, in_hbm(w_down))


def dispatch_kernel(place_ref, x_ref, out_ref):
    y = jnp.dot(place_ref[...], x_ref[...], preferred_element_type=F32).astype(BF)
    out_ref[...] = y.reshape(out_ref.shape)


def dispatch(place, x, cuts):
    m = place.shape[0]
    tokens, width = x.shape
    n = width // cuts
    return pl.pallas_call(
        dispatch_kernel,
        grid=(cuts,),
        in_specs=[pl.BlockSpec(place.shape, lambda i: (0, 0)), pl.BlockSpec((tokens, n), lambda i: (0, i))],
        out_specs=pl.BlockSpec((m // 2, 2, n), lambda i: (0, 0, i)),
        out_shape=jax.ShapeDtypeStruct((m // 2, 2, width), BF),
        compiler_params=pltpu.CompilerParams(vmem_limit_bytes=32 * 2**20),
        cost_estimate=pl.CostEstimate(
            flops=2 * m * tokens * width, bytes_accessed=2 * m * width + 2 * tokens * width, transcendentals=0
        ),
    )(place, x)


def combine_kernel(*refs):
    *in_refs, own_ref, far_ref = refs
    tok = own_ref.shape[0]
    y = None
    for factors_ref, x_ref in zip(in_refs[::2], in_refs[1::2]):
        rows = x_ref[...].reshape(factors_ref.shape[1], x_ref.shape[2])
        part = jnp.dot(factors_ref[...], rows, preferred_element_type=F32)
        y = part if y is None else y + part
    y = y[: 2 * tok] + y[2 * tok :]
    own_ref[...] = y[:tok]
    far_ref[...] = y[tok:]


def combine(parts, cuts):
    width = parts[0][1].shape[2]
    n = width // cuts
    tok = parts[0][0].shape[0] // 4
    half = pl.BlockSpec((tok, n), lambda i: (0, i))
    in_specs = []
    for factors, x in parts:
        in_specs.append(pl.BlockSpec(factors.shape, lambda i: (0, 0)))
        in_specs.append(pl.BlockSpec((x.shape[0], 2, n), lambda i: (0, 0, i)))
    rows = sum(2 * x.shape[0] for _, x in parts)
    return pl.pallas_call(
        combine_kernel,
        grid=(cuts,),
        in_specs=in_specs,
        out_specs=(half, half),
        out_shape=(jax.ShapeDtypeStruct((tok, width), F32),) * 2,
        compiler_params=pltpu.CompilerParams(vmem_limit_bytes=32 * 2**20),
        cost_estimate=pl.CostEstimate(
            flops=8 * tok * rows * width, bytes_accessed=2 * rows * width, transcendentals=0
        ),
    )(*[a for part in parts for a in part])


def project_kernel(ids_ref, *refs):
    *piece_refs, near_ref, far_ref, out_ref, x_ref, w_ref = refs
    rows, half = piece_refs[0].shape
    group, tok = 4, out_ref.shape[1]
    parts = out_ref.shape[0] // group
    core, x = ids_ref[1], ids_ref[2]
    for i, ref in enumerate(piece_refs):
        x_ref[i // 2 * rows : (i // 2 + 1) * rows, i % 2 * half : (i % 2 + 1) * half] = ref[...]
    deep = VD // 2
    for side, ref in enumerate((near_ref, far_ref)):
        offset = (core if side == 0 else 1 - core) * deep
        for j in range(ref.shape[0]):
            w_ref[pl.ds(pl.multiple_of(j * VD + offset, deep), deep)] = ref[j]
    for d in range(group):
        y = jnp.dot(x_ref[d * rows : (d + 1) * rows], w_ref[...], preferred_element_type=F32).astype(BF)
        target = lax.rem(x + d, group)
        for e in range(parts):
            out_ref[e * group + target] = y[e * tok : (e + 1) * tok]


def project(ids, pieces, near, far, parts, width):
    rows, depth = pieces[0].shape[0], 2 * pieces[0].shape[1]
    whole = pl.BlockSpec(memory_space=pltpu.VMEM)
    group = 4
    return pl.pallas_call(
        project_kernel,
        in_specs=[pl.BlockSpec(memory_space=pltpu.SMEM)] + [whole] * (len(pieces) + 2),
        out_specs=whole,
        out_shape=jax.ShapeDtypeStruct((parts * group, rows // parts, width), BF),
        scratch_shapes=[pltpu.VMEM((group * rows, depth), BF), pltpu.VMEM((depth, width), BF)],
        compiler_params=pltpu.CompilerParams(vmem_limit_bytes=32 * 2**20),
        cost_estimate=pl.CostEstimate(
            flops=2 * group * rows * depth * width, bytes_accessed=2 * depth * width, transcendentals=0
        ),
    )(ids, *pieces, near, far)


def blocks_kernel(w_ref, out_ref, sems):
    wide = out_ref.shape[2]
    group = w_ref.shape[1] // wide
    copies = []
    for i in range(out_ref.shape[0]):
        first = i % group * wide
        copies.append(pltpu.make_async_copy(w_ref.at[:, first : first + wide], out_ref.at[i], sems.at[i]))
        copies[-1].start()
    for copy in copies:
        copy.wait()


def column_blocks(w, group, count):
    shape = (count, w.shape[0], w.shape[1] // group)
    hbm = pl.BlockSpec(memory_space=pltpu.HBM)
    return pl.pallas_call(
        blocks_kernel,
        in_specs=[hbm],
        out_specs=hbm,
        out_shape=pltpu.HBM(shape, w.dtype),
        scratch_shapes=[pltpu.SemaphoreType.DMA((count,))],
        cost_estimate=pl.CostEstimate(flops=0, bytes_accessed=6 * w.size, transcendentals=0),
    )(in_hbm(w))


def swap(mine):
    return lax.ppermute(mine, "core", SWAP)


def up(a):
    return lax.ppermute(a, "x", [(i, (i + 1) % 4) for i in range(4)])


def down(a):
    return lax.ppermute(a, "x", [(i, (i + 3) % 4) for i in range(4)])


def routing(routes, codes):
    tok = routes.shape[0]
    core = lax.axis_index("core")
    code_float = codes.astype(F32)
    mix = code_float / jnp.sum(code_float, axis=1, keepdims=True)
    routes2, mix2 = jnp.stack([routes, swap(routes)]), jnp.stack([mix, swap(mix)])
    chosen = routes2[:, :, :, None] == jnp.arange(64, dtype=jnp.int32)
    weight = jnp.sum(jnp.where(chosen, mix2[..., None], F32(0.0)), axis=2)
    has = jnp.any(chosen, axis=2)

    def of_core(a):
        a = a.reshape(2, tok, 8, 2, 4)
        return jnp.where(core == 0, a[:, :, :, 0], a[:, :, :, 1]).reshape(2, tok, 32)

    weight, has = of_core(weight), of_core(has)
    count = has.astype(jnp.int32)
    slot = jnp.cumsum(count, axis=1) - count
    place = has[:, :, :, None] & (slot[:, :, :, None] == jnp.arange(CAP, dtype=jnp.int32))
    place = place.transpose(2, 3, 0, 1)[:, :, :, None, :]
    same = jnp.arange(2)[:, None, None] == jnp.arange(2)[None, :, None]
    place = (place & same).reshape(32, CAP, 2, 2 * tok)
    place = jnp.broadcast_to(place[:, None], (32, 2, CAP, 2, 2 * tok)).reshape(64, CAP, 2, 2 * tok)
    gains = weight.transpose(2, 0, 1).reshape(32, 2 * tok)
    gains = jnp.broadcast_to(gains[:, None], (32, 2, 2 * tok)).reshape(64, 1, 1, 2 * tok)
    factors = jnp.where(place, gains, F32(0.0))
    high = lax.reduce_precision(factors, 8, 7)
    factors = jnp.concatenate([high, factors - high], axis=3).astype(BF)
    place = place.astype(BF)
    parts = []
    for slots in SLOTS:
        parts.append((place[:, slots].reshape(-1, 2 * tok), factors[:, slots].reshape(-1, 4 * tok).T))
    return parts


def local(queries, latents, w_kv, w_out, resid, norm_gain, routes, codes, w_gate, w_up, w_down):
    tok, width = resid.shape
    chips = 64
    core = lax.axis_index("core")
    group = 4
    columns = width // group
    near = lax.all_to_all(
        jnp.broadcast_to(latents[None], (8,) + latents.shape), CTX_CHIPS, split_axis=0, concat_axis=0, tiled=True
    )
    far = swap(near)
    w_blocks, _ = lax.optimization_barrier((column_blocks(w_out, group, 8), near[0, :8]))
    w_near = lax.all_to_all(w_blocks, CTX_CHIPS, split_axis=0, concat_axis=0, tiled=True)
    ids = jnp.stack([lax.axis_index(CTX), core, lax.axis_index("x")]).astype(jnp.int32)
    lower = attend(ids, queries, w_kv, near, far, 0, 2, 4)
    before_lower, after_lower = up(lower), down(lower)
    ids, _ = lax.optimization_barrier((ids, lower[:8, :128]))
    upper = attend(ids, queries, w_kv, near, far, 1, 2, 4)
    before_upper, after_upper = up(upper), down(upper)
    left, right = up(before_lower), down(after_upper)
    w_near, _ = lax.optimization_barrier((w_near, upper[:8, :128]))
    w_far = swap(w_near)
    pieces = (lower, upper, after_lower, after_upper, left, right, before_lower, before_upper)
    attn = project(ids, pieces, w_near, w_far, 8, columns)
    attn = lax.all_to_all(attn, EP + ("x",), split_axis=0, concat_axis=0, tiled=True)
    attn = jnp.sum(attn.reshape(8, group, tok, columns).astype(F32), axis=0)
    attn = attn.transpose(1, 0, 2).reshape(tok, width)
    attended = (resid.astype(F32) + attn).astype(BF)
    wide = attended.astype(F32)
    meansq = jnp.mean(wide * wide, axis=1, keepdims=True)
    normed = (wide * lax.rsqrt(meansq + 1e-06) * norm_gain[None, :]).astype(BF)
    normed2 = jnp.concatenate([normed, swap(normed)], axis=0)

    def exchange(rows):
        units = rows.reshape(chips, -1, 2, width)
        units = lax.all_to_all(units, CHIPS, split_axis=0, concat_axis=0, tiled=True)
        return units.reshape(rows.shape)

    parts = routing(routes, codes)
    arrived = [exchange(dispatch(place, normed2, 2)) for place, _ in parts]
    returned = [exchange(expert(rows, w_gate[0], w_up[0], w_down[0], 2, 7)) for rows in arrived]
    mine, theirs = combine([(factors, rows) for (_, factors), rows in zip(parts, returned)], 4)
    layer_out = (wide + mine + swap(theirs)).astype(BF)
    return (attended, layer_out)


def solution(mesh):
    fine = Mesh(mesh.devices.reshape(SIZES), NAMES)
    rows = P(CTX + EP, None)
    heads = P(CTX + EP, None, None)
    placed = (
        P(CTX, EP),
        P(None, CTX),
        P(None, EP),
        P(EP + CTX, None),
        rows,
        P(),
        rows,
        rows,
        heads,
        heads,
        heads,
    )
    return jax.shard_map(local, mesh=fine, in_specs=placed, out_specs=(rows, rows), check_vma=False)
```

```python
import functools

import jax
import jax.numpy as jnp
from jax import lax
from jax.experimental import pallas as pl
from jax.experimental.pallas import tpu as pltpu
from jax.sharding import Mesh, PartitionSpec as P

NOPE = 128
VD = 128
KV_RANK = 512
TOP = 8
QK = 192
CAP = 3
SLOTS = (slice(0, 3),)

CTX = ("z_lo", "x", "core")
CTX_CHIPS = ("z_lo", "x")
EP = ("z_hi", "y")
CHIPS = ("z_lo", "x", "z_hi", "y")
SIZES = (2, 4, 2, 2, 4)
NAMES = ("z_lo", "x", "core", "z_hi", "y")
SWAP = ((0, 1), (1, 0))
BF = jnp.bfloat16
F32 = jnp.float32
LOG2E = 1.4426950408889634


def in_hbm(a):
    return pltpu.with_memory_space_constraint(a, pltpu.HBM)


def attend_kernel(
    ids_ref, q_hbm, w_hbm, near_ref, far_ref, out_ref, q_ref, w_ref, lat_ref, s_ref, latq_ref, mixed_ref, sems, *, cuts
):
    heads = w_ref.shape[1] // (NOPE + VD)
    rows = q_ref.shape[0]
    m = heads * rows
    pairs = near_ref.shape[0]
    keys = 2 * rows * pairs
    q_copy = pltpu.make_async_copy(q_hbm, q_ref, sems.at[0])
    w_copy = pltpu.make_async_copy(w_hbm, w_ref, sems.at[1])
    q_copy.start()
    w_copy.start()
    for i in range(pairs):
        lat_ref[:, 2 * i * rows : (2 * i + 1) * rows] = near_ref[i]
        lat_ref[:, (2 * i + 1) * rows : (2 * i + 2) * rows] = far_ref[i]
    q_copy.wait()
    w_copy.wait()
    for h in range(heads):
        here = slice(h * rows, (h + 1) * rows)
        key_weights = w_ref[:, h * (NOPE + VD) : h * (NOPE + VD) + NOPE]
        plain = q_ref[:, h * QK : h * QK + NOPE]
        latq = lax.dot_general(plain, key_weights, (((1,), (1,)), ((), ())), preferred_element_type=F32)
        latq_ref[here, :KV_RANK] = latq.astype(BF)
        latq_ref[here, KV_RANK:] = q_ref[:, h * QK + NOPE : (h + 1) * QK]
    ctx, core = ids_ref[0], ids_ref[1]
    span = keys // cuts
    lane = lax.broadcasted_iota(jnp.int32, (m, rows), 1)
    query = lax.broadcasted_iota(jnp.int32, (m, rows), 0) % rows
    ahead = lane - query
    peak = jnp.full((m, rows), -1e30, F32)
    for j in range(cuts):
        s = jnp.dot(latq_ref[...], lat_ref[:, j * span : (j + 1) * span], preferred_element_type=F32)
        for b in range(span // rows):
            block = j * (span // rows) + b
            pos = 2 * (block // 2) + (core if block % 2 == 0 else 1 - core)
            part = s[:, b * rows : (b + 1) * rows]
            part = jnp.where(ahead <= (ctx - pos) * rows, part, F32(-1e30))
            peak = jnp.maximum(peak, part)
            s_ref[:, block * rows : (block + 1) * rows] = part
    top = jnp.max(peak, axis=1, keepdims=True)
    total = jnp.zeros((m, rows), F32)
    for j in range(cuts):
        probs = []
        for b in range(span // rows):
            first = j * span + b * rows
            p = jnp.exp2((s_ref[:, first : first + rows] - top) * (QK ** (-0.5) * LOG2E))
            total = total + p
            probs.append(p.astype(BF))
        part = lax.dot_general(
            jnp.concatenate(probs, axis=1),
            lat_ref[:KV_RANK, j * span : (j + 1) * span],
            (((1,), (1,)), ((), ())),
            preferred_element_type=F32,
        )
        mixed_ref[...] = part if j == 0 else mixed_ref[...] + part
    mixed = (mixed_ref[...] / jnp.sum(total, axis=1, keepdims=True)).astype(BF)
    for h in range(heads):
        values = w_ref[:, h * (NOPE + VD) + NOPE : (h + 1) * (NOPE + VD)]
        o = jnp.dot(mixed[h * rows : (h + 1) * rows], values, preferred_element_type=F32)
        out_ref[:, h * VD : (h + 1) * VD] = o.astype(BF)


def attend(ids, q, w_kv, near, far, cuts):
    pairs, depth, rows = near.shape
    heads = w_kv.shape[1] // (NOPE + VD)
    keys = 2 * rows * pairs
    m = heads * rows
    whole = pl.BlockSpec(memory_space=pltpu.VMEM)
    hbm = pl.BlockSpec(memory_space=pltpu.HBM)
    return pl.pallas_call(
        functools.partial(attend_kernel, cuts=cuts),
        in_specs=[pl.BlockSpec(memory_space=pltpu.SMEM), hbm, hbm, whole, whole],
        out_specs=whole,
        out_shape=jax.ShapeDtypeStruct((rows, heads * VD), BF),
        scratch_shapes=[
            pltpu.VMEM(q.shape, BF),
            pltpu.VMEM(w_kv.shape, BF),
            pltpu.VMEM((depth, keys), BF),
            pltpu.VMEM((m, keys), F32),
            pltpu.VMEM((m, depth), BF),
            pltpu.VMEM((m, KV_RANK), F32),
            pltpu.SemaphoreType.DMA((2,)),
        ],
        compiler_params=pltpu.CompilerParams(vmem_limit_bytes=28 * 2**20),
        cost_estimate=pl.CostEstimate(
            flops=2 * m * keys * (depth + KV_RANK), bytes_accessed=8_000_000, transcendentals=m * keys
        ),
    )(ids, in_hbm(q), in_hbm(w_kv), near, far)


def expert_kernel(x_hbm, g_ref, u_ref, d_hbm, out_hbm, d_ref, x_ref, hid_ref, gate_ref, up_ref, y_ref, sem_d, sem_in, sem_out):
    units, pair, width = x_ref.shape
    m = units * pair
    first, last = sem_in.shape[0], sem_out.shape[0]
    depth, wide = width // first, width // last
    arrivals = []
    for k in range(first):
        part = slice(k * depth, (k + 1) * depth)
        arrivals.append(pltpu.make_async_copy(x_hbm.at[:, :, part], x_ref.at[:, :, part], sem_in.at[k]))
        arrivals[-1].start()
    d_copy = pltpu.make_async_copy(d_hbm, d_ref, sem_d.at[0])
    d_copy.start()
    for k in range(first):
        part = slice(k * depth, (k + 1) * depth)
        arrivals[k].wait()
        rows = x_ref[:, :, part].reshape(m, depth)
        gate = jnp.dot(rows, g_ref[part], preferred_element_type=F32)
        upward = jnp.dot(rows, u_ref[part], preferred_element_type=F32)
        gate_ref[...] = gate if k == 0 else gate_ref[...] + gate
        up_ref[...] = upward if k == 0 else up_ref[...] + upward
    gate = gate_ref[...]
    hid_ref[...] = (gate / (1.0 + jnp.exp(-gate)) * up_ref[...]).astype(BF)
    d_copy.wait()
    departures = []
    for n in range(last):
        part = slice(n * wide, (n + 1) * wide)
        y = jnp.dot(hid_ref[...], d_ref[:, part], preferred_element_type=F32).astype(BF)
        y_ref[:, :, part] = y.reshape(units, pair, wide)
        departures.append(pltpu.make_async_copy(y_ref.at[:, :, part], out_hbm.at[:, :, part], sem_out.at[n]))
        departures[-1].start()
    for copy in departures:
        copy.wait()


def expert(x, w_gate, w_up, w_down, first, last):
    units, pair, width = x.shape
    m = units * pair
    hidden = w_gate.shape[1]
    whole = pl.BlockSpec(memory_space=pltpu.VMEM)
    far = pl.BlockSpec(memory_space=pltpu.HBM)
    return pl.pallas_call(
        expert_kernel,
        in_specs=[far, whole, whole, far],
        out_specs=far,
        out_shape=pltpu.HBM(x.shape, BF),
        scratch_shapes=[
            pltpu.VMEM(w_down.shape, BF),
            pltpu.VMEM(x.shape, BF),
            pltpu.VMEM((m, hidden), BF),
            pltpu.VMEM((m, hidden), F32),
            pltpu.VMEM((m, hidden), F32),
            pltpu.VMEM(x.shape, BF),
            pltpu.SemaphoreType.DMA((1,)),
            pltpu.SemaphoreType.DMA((first,)),
            pltpu.SemaphoreType.DMA((last,)),
        ],
        compiler_params=pltpu.CompilerParams(vmem_limit_bytes=24 * 2**20),
        cost_estimate=pl.CostEstimate(
            flops=6 * m * width * hidden, bytes_accessed=17_000_000, transcendentals=m * hidden
        ),
    )(x, w_gate, w_up, in_hbm(w_down))


def dispatch_kernel(place_ref, x_ref, out_ref):
    y = jnp.dot(place_ref[...], x_ref[...], preferred_element_type=F32).astype(BF)
    out_ref[...] = y.reshape(out_ref.shape)


def dispatch(place, x, cuts):
    m = place.shape[0]
    tokens, width = x.shape
    n = width // cuts
    return pl.pallas_call(
        dispatch_kernel,
        grid=(cuts,),
        in_specs=[pl.BlockSpec(place.shape, lambda i: (0, 0)), pl.BlockSpec((tokens, n), lambda i: (0, i))],
        out_specs=pl.BlockSpec((m // 2, 2, n), lambda i: (0, 0, i)),
        out_shape=jax.ShapeDtypeStruct((m // 2, 2, width), BF),
        compiler_params=pltpu.CompilerParams(vmem_limit_bytes=32 * 2**20),
        cost_estimate=pl.CostEstimate(
            flops=2 * m * tokens * width, bytes_accessed=2 * m * width + 2 * tokens * width, transcendentals=0
        ),
    )(place, x)


def combine_kernel(*refs):
    *in_refs, own_ref, far_ref = refs
    tok = own_ref.shape[0]
    y = None
    for factors_ref, x_ref in zip(in_refs[::2], in_refs[1::2]):
        rows = x_ref[...].reshape(factors_ref.shape[1], x_ref.shape[2])
        part = jnp.dot(factors_ref[...], rows, preferred_element_type=F32)
        y = part if y is None else y + part
    y = y[: 2 * tok] + y[2 * tok :]
    own_ref[...] = y[:tok]
    far_ref[...] = y[tok:]


def combine(parts, cuts):
    width = parts[0][1].shape[2]
    n = width // cuts
    tok = parts[0][0].shape[0] // 4
    half = pl.BlockSpec((tok, n), lambda i: (0, i))
    in_specs = []
    for factors, x in parts:
        in_specs.append(pl.BlockSpec(factors.shape, lambda i: (0, 0)))
        in_specs.append(pl.BlockSpec((x.shape[0], 2, n), lambda i: (0, 0, i)))
    rows = sum(2 * x.shape[0] for _, x in parts)
    return pl.pallas_call(
        combine_kernel,
        grid=(cuts,),
        in_specs=in_specs,
        out_specs=(half, half),
        out_shape=(jax.ShapeDtypeStruct((tok, width), F32),) * 2,
        compiler_params=pltpu.CompilerParams(vmem_limit_bytes=32 * 2**20),
        cost_estimate=pl.CostEstimate(
            flops=8 * tok * rows * width, bytes_accessed=2 * rows * width, transcendentals=0
        ),
    )(*[a for part in parts for a in part])


def project_kernel(ids_ref, own_ref, before_ref, after_ref, left_ref, right_ref, near_ref, far_ref, out_ref, x_ref, w_ref):
    rows = own_ref.shape[0]
    group, tok = 4, out_ref.shape[1]
    parts = out_ref.shape[0] // group
    core, x = ids_ref[1], ids_ref[2]
    half = left_ref.shape[1]
    x_ref[:rows] = own_ref[...]
    x_ref[rows : 2 * rows] = after_ref[...]
    x_ref[2 * rows : 3 * rows, :half] = left_ref[...]
    x_ref[2 * rows : 3 * rows, half:] = right_ref[...]
    x_ref[3 * rows :] = before_ref[...]
    deep = VD // 2
    for side, ref in enumerate((near_ref, far_ref)):
        offset = (core if side == 0 else 1 - core) * deep
        for j in range(ref.shape[0]):
            w_ref[pl.ds(pl.multiple_of(j * VD + offset, deep), deep)] = ref[j]
    for d in range(group):
        y = jnp.dot(x_ref[d * rows : (d + 1) * rows], w_ref[...], preferred_element_type=F32).astype(BF)
        target = lax.rem(x + d, group)
        for e in range(parts):
            out_ref[e * group + target] = y[e * tok : (e + 1) * tok]


def project(ids, pieces, near, far, parts, width):
    rows, depth = pieces[0].shape
    whole = pl.BlockSpec(memory_space=pltpu.VMEM)
    group = 4
    return pl.pallas_call(
        project_kernel,
        in_specs=[pl.BlockSpec(memory_space=pltpu.SMEM)] + [whole] * (len(pieces) + 2),
        out_specs=whole,
        out_shape=jax.ShapeDtypeStruct((parts * group, rows // parts, width), BF),
        scratch_shapes=[pltpu.VMEM((group * rows, depth), BF), pltpu.VMEM((depth, width), BF)],
        compiler_params=pltpu.CompilerParams(vmem_limit_bytes=32 * 2**20),
        cost_estimate=pl.CostEstimate(
            flops=2 * group * rows * depth * width, bytes_accessed=2 * depth * width, transcendentals=0
        ),
    )(ids, *pieces, near, far)


def blocks_kernel(w_ref, out_ref, sems):
    wide = out_ref.shape[2]
    group = w_ref.shape[1] // wide
    copies = []
    for i in range(out_ref.shape[0]):
        first = i % group * wide
        copies.append(pltpu.make_async_copy(w_ref.at[:, first : first + wide], out_ref.at[i], sems.at[i]))
        copies[-1].start()
    for copy in copies:
        copy.wait()


def column_blocks(w, group, count):
    shape = (count, w.shape[0], w.shape[1] // group)
    return pl.pallas_call(
        blocks_kernel,
        in_specs=[pl.BlockSpec(memory_space=pltpu.VMEM)],
        out_specs=pl.BlockSpec(memory_space=pltpu.HBM),
        out_shape=pltpu.HBM(shape, w.dtype),
        scratch_shapes=[pltpu.SemaphoreType.DMA((count,))],
        cost_estimate=pl.CostEstimate(flops=0, bytes_accessed=6 * w.size, transcendentals=0),
    )(w)


def swap(mine):
    return lax.ppermute(mine, "core", SWAP)


def up(a):
    return lax.ppermute(a, "x", [(i, (i + 1) % 4) for i in range(4)])


def down(a):
    return lax.ppermute(a, "x", [(i, (i + 3) % 4) for i in range(4)])


def routing(routes, codes):
    tok = routes.shape[0]
    core = lax.axis_index("core")
    code_float = codes.astype(F32)
    mix = code_float / jnp.sum(code_float, axis=1, keepdims=True)
    routes2, mix2 = jnp.stack([routes, swap(routes)]), jnp.stack([mix, swap(mix)])
    chosen = routes2[:, :, :, None] == jnp.arange(64, dtype=jnp.int32)
    weight = jnp.sum(jnp.where(chosen, mix2[..., None], F32(0.0)), axis=2)
    has = jnp.any(chosen, axis=2)

    def of_core(a):
        a = a.reshape(2, tok, 8, 2, 4)
        return jnp.where(core == 0, a[:, :, :, 0], a[:, :, :, 1]).reshape(2, tok, 32)

    weight, has = of_core(weight), of_core(has)
    count = has.astype(jnp.int32)
    slot = jnp.cumsum(count, axis=1) - count
    place = has[:, :, :, None] & (slot[:, :, :, None] == jnp.arange(CAP, dtype=jnp.int32))
    place = place.transpose(2, 3, 0, 1)[:, :, :, None, :]
    same = jnp.arange(2)[:, None, None] == jnp.arange(2)[None, :, None]
    place = (place & same).reshape(32, CAP, 2, 2 * tok)
    place = jnp.broadcast_to(place[:, None], (32, 2, CAP, 2, 2 * tok)).reshape(64, CAP, 2, 2 * tok)
    gains = weight.transpose(2, 0, 1).reshape(32, 2 * tok)
    gains = jnp.broadcast_to(gains[:, None], (32, 2, 2 * tok)).reshape(64, 1, 1, 2 * tok)
    factors = jnp.where(place, gains, F32(0.0))
    high = lax.reduce_precision(factors, 8, 7)
    factors = jnp.concatenate([high, factors - high], axis=3).astype(BF)
    place = place.astype(BF)
    parts = []
    for slots in SLOTS:
        parts.append((place[:, slots].reshape(-1, 2 * tok), factors[:, slots].reshape(-1, 4 * tok).T))
    return parts


def local(queries, latents, w_kv, w_out, resid, norm_gain, routes, codes, w_gate, w_up, w_down):
    tok, width = resid.shape
    chips = 64
    core = lax.axis_index("core")
    group = 4
    columns = width // group
    near = lax.all_to_all(
        jnp.broadcast_to(latents[None], (8,) + latents.shape), CTX_CHIPS, split_axis=0, concat_axis=0, tiled=True
    )
    far = swap(near)
    w_blocks, _ = lax.optimization_barrier((column_blocks(w_out, group, 8), near[0, :8]))
    w_near = lax.all_to_all(w_blocks, CTX_CHIPS, split_axis=0, concat_axis=0, tiled=True)
    ids = jnp.stack([lax.axis_index(CTX), core, lax.axis_index("x")]).astype(jnp.int32)
    own = attend(ids, queries, w_kv, near, far, 4)
    before, after, w_near = lax.optimization_barrier((up(own), down(own), w_near))
    w_far = swap(w_near)
    half = own.shape[1] // 2
    left, right = up(before[:, :half]), down(after[:, half:])
    attn = project(ids, (own, before, after, left, right), w_near, w_far, 8, columns)
    attn = lax.all_to_all(attn, EP + ("x",), split_axis=0, concat_axis=0, tiled=True)
    attn = jnp.sum(attn.reshape(8, group, tok, columns).astype(F32), axis=0)
    attn = attn.transpose(1, 0, 2).reshape(tok, width)
    attended = (resid.astype(F32) + attn).astype(BF)
    wide = attended.astype(F32)
    meansq = jnp.mean(wide * wide, axis=1, keepdims=True)
    normed = (wide * lax.rsqrt(meansq + 1e-06) * norm_gain[None, :]).astype(BF)
    normed2 = jnp.concatenate([normed, swap(normed)], axis=0)

    def exchange(rows):
        units = rows.reshape(chips, -1, 2, width)
        units = lax.all_to_all(units, CHIPS, split_axis=0, concat_axis=0, tiled=True)
        return units.reshape(rows.shape)

    parts = routing(routes, codes)
    arrived = [exchange(dispatch(place, normed2, 2)) for place, _ in parts]
    returned = [exchange(expert(rows, w_gate[0], w_up[0], w_down[0], 2, 7)) for rows in arrived]
    mine, theirs = combine([(factors, rows) for (_, factors), rows in zip(parts, returned)], 4)
    layer_out = (wide + mine + swap(theirs)).astype(BF)
    return (attended, layer_out)


def solution(mesh):
    fine = Mesh(mesh.devices.reshape(SIZES), NAMES)
    rows = P(CTX + EP, None)
    heads = P(CTX + EP, None, None)
    placed = (
        P(CTX, EP),
        P(None, CTX),
        P(None, EP),
        P(EP + CTX, None),
        rows,
        P(),
        rows,
        rows,
        heads,
        heads,
        heads,
    )
    return jax.shard_map(local, mesh=fine, in_specs=placed, out_specs=(rows, rows), check_vma=False)
```

```python
import functools

import jax
import jax.numpy as jnp
from jax import lax
from jax.experimental import pallas as pl
from jax.experimental.pallas import tpu as pltpu
from jax.sharding import Mesh, PartitionSpec as P

NOPE = 128
VD = 128
KV_RANK = 512
TOP = 8
QK = 192
CAP = 3
SLOTS = (slice(0, 3),)

CTX = ("z_lo", "x", "core")
CTX_CHIPS = ("z_lo", "x")
EP = ("z_hi", "y")
CHIPS = ("z_lo", "x", "z_hi", "y")
SIZES = (2, 4, 2, 2, 4)
NAMES = ("z_lo", "x", "core", "z_hi", "y")
SWAP = ((0, 1), (1, 0))
BF = jnp.bfloat16
F32 = jnp.float32
LOG2E = 1.4426950408889634


def in_hbm(a):
    return pltpu.with_memory_space_constraint(a, pltpu.HBM)


def attend_kernel(
    ids_ref, q_hbm, w_hbm, near_ref, far_ref, out_ref, q_ref, w_ref, lat_ref, s_ref, latq_ref, mixed_ref, sems, *, cuts
):
    heads = w_ref.shape[1] // (NOPE + VD)
    rows = q_ref.shape[0]
    m = heads * rows
    pairs = near_ref.shape[0]
    keys = 2 * rows * pairs
    q_copy = pltpu.make_async_copy(q_hbm, q_ref, sems.at[0])
    w_copy = pltpu.make_async_copy(w_hbm, w_ref, sems.at[1])
    q_copy.start()
    w_copy.start()
    for i in range(pairs):
        lat_ref[:, 2 * i * rows : (2 * i + 1) * rows] = near_ref[i]
        lat_ref[:, (2 * i + 1) * rows : (2 * i + 2) * rows] = far_ref[i]
    q_copy.wait()
    w_copy.wait()
    for h in range(heads):
        here = slice(h * rows, (h + 1) * rows)
        key_weights = w_ref[:, h * (NOPE + VD) : h * (NOPE + VD) + NOPE]
        plain = q_ref[:, h * QK : h * QK + NOPE]
        latq = lax.dot_general(plain, key_weights, (((1,), (1,)), ((), ())), preferred_element_type=F32)
        latq_ref[here, :KV_RANK] = latq.astype(BF)
        latq_ref[here, KV_RANK:] = q_ref[:, h * QK + NOPE : (h + 1) * QK]
    ctx, core = ids_ref[0], ids_ref[1]
    span = keys // cuts
    lane = lax.broadcasted_iota(jnp.int32, (m, rows), 1)
    query = lax.broadcasted_iota(jnp.int32, (m, rows), 0) % rows
    ahead = lane - query
    peak = jnp.full((m, rows), -1e30, F32)
    for j in range(cuts):
        s = jnp.dot(latq_ref[...], lat_ref[:, j * span : (j + 1) * span], preferred_element_type=F32)
        for b in range(span // rows):
            block = j * (span // rows) + b
            pos = 2 * (block // 2) + (core if block % 2 == 0 else 1 - core)
            part = s[:, b * rows : (b + 1) * rows]
            part = jnp.where(ahead <= (ctx - pos) * rows, part, F32(-1e30))
            peak = jnp.maximum(peak, part)
            s_ref[:, block * rows : (block + 1) * rows] = part
    top = jnp.max(peak, axis=1, keepdims=True)
    total = jnp.zeros((m, rows), F32)
    for j in range(cuts):
        probs = []
        for b in range(span // rows):
            first = j * span + b * rows
            p = jnp.exp2((s_ref[:, first : first + rows] - top) * (QK ** (-0.5) * LOG2E))
            total = total + p
            probs.append(p.astype(BF))
        part = lax.dot_general(
            jnp.concatenate(probs, axis=1),
            lat_ref[:KV_RANK, j * span : (j + 1) * span],
            (((1,), (1,)), ((), ())),
            preferred_element_type=F32,
        )
        mixed_ref[...] = part if j == 0 else mixed_ref[...] + part
    mixed = (mixed_ref[...] / jnp.sum(total, axis=1, keepdims=True)).astype(BF)
    for h in range(heads):
        values = w_ref[:, h * (NOPE + VD) + NOPE : (h + 1) * (NOPE + VD)]
        o = jnp.dot(mixed[h * rows : (h + 1) * rows], values, preferred_element_type=F32)
        out_ref[:, h * VD : (h + 1) * VD] = o.astype(BF)


def attend(ids, q, w_kv, near, far, cuts):
    pairs, depth, rows = near.shape
    heads = w_kv.shape[1] // (NOPE + VD)
    keys = 2 * rows * pairs
    m = heads * rows
    whole = pl.BlockSpec(memory_space=pltpu.VMEM)
    hbm = pl.BlockSpec(memory_space=pltpu.HBM)
    return pl.pallas_call(
        functools.partial(attend_kernel, cuts=cuts),
        in_specs=[pl.BlockSpec(memory_space=pltpu.SMEM), hbm, hbm, whole, whole],
        out_specs=whole,
        out_shape=jax.ShapeDtypeStruct((rows, heads * VD), BF),
        scratch_shapes=[
            pltpu.VMEM(q.shape, BF),
            pltpu.VMEM(w_kv.shape, BF),
            pltpu.VMEM((depth, keys), BF),
            pltpu.VMEM((m, keys), F32),
            pltpu.VMEM((m, depth), BF),
            pltpu.VMEM((m, KV_RANK), F32),
            pltpu.SemaphoreType.DMA((2,)),
        ],
        compiler_params=pltpu.CompilerParams(vmem_limit_bytes=28 * 2**20),
        cost_estimate=pl.CostEstimate(
            flops=2 * m * keys * (depth + KV_RANK), bytes_accessed=8_000_000, transcendentals=m * keys
        ),
    )(ids, in_hbm(q), in_hbm(w_kv), near, far)


def expert_kernel(x_hbm, g_ref, u_ref, d_hbm, out_hbm, d_ref, x_ref, hid_ref, gate_ref, up_ref, y_ref, sem_d, sem_in, sem_out):
    units, pair, width = x_ref.shape
    m = units * pair
    first, last = sem_in.shape[0], sem_out.shape[0]
    depth, wide = width // first, width // last
    arrivals = []
    for k in range(first):
        part = slice(k * depth, (k + 1) * depth)
        arrivals.append(pltpu.make_async_copy(x_hbm.at[:, :, part], x_ref.at[:, :, part], sem_in.at[k]))
        arrivals[-1].start()
    d_copy = pltpu.make_async_copy(d_hbm, d_ref, sem_d.at[0])
    d_copy.start()
    for k in range(first):
        part = slice(k * depth, (k + 1) * depth)
        arrivals[k].wait()
        rows = x_ref[:, :, part].reshape(m, depth)
        gate = jnp.dot(rows, g_ref[part], preferred_element_type=F32)
        upward = jnp.dot(rows, u_ref[part], preferred_element_type=F32)
        gate_ref[...] = gate if k == 0 else gate_ref[...] + gate
        up_ref[...] = upward if k == 0 else up_ref[...] + upward
    gate = gate_ref[...]
    hid_ref[...] = (gate / (1.0 + jnp.exp(-gate)) * up_ref[...]).astype(BF)
    d_copy.wait()
    departures = []
    for n in range(last):
        part = slice(n * wide, (n + 1) * wide)
        y = jnp.dot(hid_ref[...], d_ref[:, part], preferred_element_type=F32).astype(BF)
        y_ref[:, :, part] = y.reshape(units, pair, wide)
        departures.append(pltpu.make_async_copy(y_ref.at[:, :, part], out_hbm.at[:, :, part], sem_out.at[n]))
        departures[-1].start()
    for copy in departures:
        copy.wait()


def expert(x, w_gate, w_up, w_down, first, last):
    units, pair, width = x.shape
    m = units * pair
    hidden = w_gate.shape[1]
    whole = pl.BlockSpec(memory_space=pltpu.VMEM)
    far = pl.BlockSpec(memory_space=pltpu.HBM)
    return pl.pallas_call(
        expert_kernel,
        in_specs=[far, whole, whole, far],
        out_specs=far,
        out_shape=pltpu.HBM(x.shape, BF),
        scratch_shapes=[
            pltpu.VMEM(w_down.shape, BF),
            pltpu.VMEM(x.shape, BF),
            pltpu.VMEM((m, hidden), BF),
            pltpu.VMEM((m, hidden), F32),
            pltpu.VMEM((m, hidden), F32),
            pltpu.VMEM(x.shape, BF),
            pltpu.SemaphoreType.DMA((1,)),
            pltpu.SemaphoreType.DMA((first,)),
            pltpu.SemaphoreType.DMA((last,)),
        ],
        compiler_params=pltpu.CompilerParams(vmem_limit_bytes=24 * 2**20),
        cost_estimate=pl.CostEstimate(
            flops=6 * m * width * hidden, bytes_accessed=17_000_000, transcendentals=m * hidden
        ),
    )(x, w_gate, w_up, in_hbm(w_down))


def dispatch_kernel(place_ref, x_ref, out_ref):
    y = jnp.dot(place_ref[...], x_ref[...], preferred_element_type=F32).astype(BF)
    out_ref[...] = y.reshape(out_ref.shape)


def dispatch(place, x, cuts):
    m = place.shape[0]
    tokens, width = x.shape
    n = width // cuts
    return pl.pallas_call(
        dispatch_kernel,
        grid=(cuts,),
        in_specs=[pl.BlockSpec(place.shape, lambda i: (0, 0)), pl.BlockSpec((tokens, n), lambda i: (0, i))],
        out_specs=pl.BlockSpec((m // 2, 2, n), lambda i: (0, 0, i)),
        out_shape=jax.ShapeDtypeStruct((m // 2, 2, width), BF),
        compiler_params=pltpu.CompilerParams(vmem_limit_bytes=32 * 2**20),
        cost_estimate=pl.CostEstimate(
            flops=2 * m * tokens * width, bytes_accessed=2 * m * width + 2 * tokens * width, transcendentals=0
        ),
    )(place, x)


def combine_kernel(*refs):
    *in_refs, own_ref, far_ref = refs
    tok = own_ref.shape[0]
    y = None
    for factors_ref, x_ref in zip(in_refs[::2], in_refs[1::2]):
        rows = x_ref[...].reshape(factors_ref.shape[1], x_ref.shape[2])
        part = jnp.dot(factors_ref[...], rows, preferred_element_type=F32)
        y = part if y is None else y + part
    y = y[: 2 * tok] + y[2 * tok :]
    own_ref[...] = y[:tok]
    far_ref[...] = y[tok:]


def combine(parts, cuts):
    width = parts[0][1].shape[2]
    n = width // cuts
    tok = parts[0][0].shape[0] // 4
    half = pl.BlockSpec((tok, n), lambda i: (0, i))
    in_specs = []
    for factors, x in parts:
        in_specs.append(pl.BlockSpec(factors.shape, lambda i: (0, 0)))
        in_specs.append(pl.BlockSpec((x.shape[0], 2, n), lambda i: (0, 0, i)))
    rows = sum(2 * x.shape[0] for _, x in parts)
    return pl.pallas_call(
        combine_kernel,
        grid=(cuts,),
        in_specs=in_specs,
        out_specs=(half, half),
        out_shape=(jax.ShapeDtypeStruct((tok, width), F32),) * 2,
        compiler_params=pltpu.CompilerParams(vmem_limit_bytes=32 * 2**20),
        cost_estimate=pl.CostEstimate(
            flops=8 * tok * rows * width, bytes_accessed=2 * rows * width, transcendentals=0
        ),
    )(*[a for part in parts for a in part])


def project_kernel(ids_ref, own_ref, before_ref, after_ref, opposite_ref, near_ref, far_ref, out_ref, x_ref, w_ref):
    rows = own_ref.shape[0]
    group, tok = 4, out_ref.shape[1]
    parts = out_ref.shape[0] // group
    core, x = ids_ref[1], ids_ref[2]
    x_ref[:rows] = own_ref[...]
    x_ref[rows : 2 * rows] = after_ref[...]
    x_ref[2 * rows : 3 * rows] = opposite_ref[...]
    x_ref[3 * rows :] = before_ref[...]
    deep = VD // 2
    for side, ref in enumerate((near_ref, far_ref)):
        offset = (core if side == 0 else 1 - core) * deep
        for j in range(ref.shape[0]):
            w_ref[pl.ds(pl.multiple_of(j * VD + offset, deep), deep)] = ref[j]
    for d in range(group):
        y = jnp.dot(x_ref[d * rows : (d + 1) * rows], w_ref[...], preferred_element_type=F32).astype(BF)
        target = lax.rem(x + d, group)
        for e in range(parts):
            out_ref[e * group + target] = y[e * tok : (e + 1) * tok]


def project(ids, pieces, near, far, parts, width):
    rows, depth = pieces[0].shape
    whole = pl.BlockSpec(memory_space=pltpu.VMEM)
    group = 4
    return pl.pallas_call(
        project_kernel,
        in_specs=[pl.BlockSpec(memory_space=pltpu.SMEM)] + [whole] * (len(pieces) + 2),
        out_specs=whole,
        out_shape=jax.ShapeDtypeStruct((parts * group, rows // parts, width), BF),
        scratch_shapes=[pltpu.VMEM((group * rows, depth), BF), pltpu.VMEM((depth, width), BF)],
        compiler_params=pltpu.CompilerParams(vmem_limit_bytes=32 * 2**20),
        cost_estimate=pl.CostEstimate(
            flops=2 * group * rows * depth * width, bytes_accessed=2 * depth * width, transcendentals=0
        ),
    )(ids, *pieces, near, far)


def blocks_kernel(w_ref, out_ref, sems):
    wide = out_ref.shape[2]
    group = w_ref.shape[1] // wide
    copies = []
    for i in range(out_ref.shape[0]):
        first = i % group * wide
        copies.append(pltpu.make_async_copy(w_ref.at[:, first : first + wide], out_ref.at[i], sems.at[i]))
        copies[-1].start()
    for copy in copies:
        copy.wait()


def column_blocks(w, group, count):
    shape = (count, w.shape[0], w.shape[1] // group)
    return pl.pallas_call(
        blocks_kernel,
        in_specs=[pl.BlockSpec(memory_space=pltpu.VMEM)],
        out_specs=pl.BlockSpec(memory_space=pltpu.HBM),
        out_shape=pltpu.HBM(shape, w.dtype),
        scratch_shapes=[pltpu.SemaphoreType.DMA((count,))],
        cost_estimate=pl.CostEstimate(flops=0, bytes_accessed=6 * w.size, transcendentals=0),
    )(w)


def swap(mine):
    return lax.ppermute(mine, "core", SWAP)


def up(a):
    return lax.ppermute(a, "x", [(i, (i + 1) % 4) for i in range(4)])


def down(a):
    return lax.ppermute(a, "x", [(i, (i + 3) % 4) for i in range(4)])


def routing(routes, codes):
    tok = routes.shape[0]
    core = lax.axis_index("core")
    code_float = codes.astype(F32)
    mix = code_float / jnp.sum(code_float, axis=1, keepdims=True)
    routes2, mix2 = jnp.stack([routes, swap(routes)]), jnp.stack([mix, swap(mix)])
    chosen = routes2[:, :, :, None] == jnp.arange(64, dtype=jnp.int32)
    weight = jnp.sum(jnp.where(chosen, mix2[..., None], F32(0.0)), axis=2)
    has = jnp.any(chosen, axis=2)

    def of_core(a):
        a = a.reshape(2, tok, 8, 2, 4)
        return jnp.where(core == 0, a[:, :, :, 0], a[:, :, :, 1]).reshape(2, tok, 32)

    weight, has = of_core(weight), of_core(has)
    count = has.astype(jnp.int32)
    slot = jnp.cumsum(count, axis=1) - count
    place = has[:, :, :, None] & (slot[:, :, :, None] == jnp.arange(CAP, dtype=jnp.int32))
    place = place.transpose(2, 3, 0, 1)[:, :, :, None, :]
    same = jnp.arange(2)[:, None, None] == jnp.arange(2)[None, :, None]
    place = (place & same).reshape(32, CAP, 2, 2 * tok)
    place = jnp.broadcast_to(place[:, None], (32, 2, CAP, 2, 2 * tok)).reshape(64, CAP, 2, 2 * tok)
    gains = weight.transpose(2, 0, 1).reshape(32, 2 * tok)
    gains = jnp.broadcast_to(gains[:, None], (32, 2, 2 * tok)).reshape(64, 1, 1, 2 * tok)
    factors = jnp.where(place, gains, F32(0.0))
    high = lax.reduce_precision(factors, 8, 7)
    factors = jnp.concatenate([high, factors - high], axis=3).astype(BF)
    place = place.astype(BF)
    parts = []
    for slots in SLOTS:
        parts.append((place[:, slots].reshape(-1, 2 * tok), factors[:, slots].reshape(-1, 4 * tok).T))
    return parts


def local(queries, latents, w_kv, w_out, resid, norm_gain, routes, codes, w_gate, w_up, w_down):
    tok, width = resid.shape
    chips = 64
    core = lax.axis_index("core")
    group = 4
    columns = width // group
    near = lax.all_to_all(
        jnp.broadcast_to(latents[None], (8,) + latents.shape), CTX_CHIPS, split_axis=0, concat_axis=0, tiled=True
    )
    far = swap(near)
    w_blocks, _ = lax.optimization_barrier((column_blocks(w_out, group, 8), near[0, :8]))
    w_near = lax.all_to_all(w_blocks, CTX_CHIPS, split_axis=0, concat_axis=0, tiled=True)
    ids = jnp.stack([lax.axis_index(CTX), core, lax.axis_index("x")]).astype(jnp.int32)
    own = attend(ids, queries, w_kv, near, far, 4)
    opposite = lax.ppermute(own, "x", [(i, (i + 2) % 4) for i in range(4)])
    before, after, opposite, w_near = lax.optimization_barrier((up(own), down(own), opposite, w_near))
    w_far = swap(w_near)
    attn = project(ids, (own, before, after, opposite), w_near, w_far, 8, columns)
    attn = lax.all_to_all(attn, EP + ("x",), split_axis=0, concat_axis=0, tiled=True)
    attn = jnp.sum(attn.reshape(8, group, tok, columns).astype(F32), axis=0)
    attn = attn.transpose(1, 0, 2).reshape(tok, width)
    attended = (resid.astype(F32) + attn).astype(BF)
    wide = attended.astype(F32)
    meansq = jnp.mean(wide * wide, axis=1, keepdims=True)
    normed = (wide * lax.rsqrt(meansq + 1e-06) * norm_gain[None, :]).astype(BF)
    normed2 = jnp.concatenate([normed, swap(normed)], axis=0)

    def exchange(rows):
        units = rows.reshape(chips, -1, 2, width)
        units = lax.all_to_all(units, CHIPS, split_axis=0, concat_axis=0, tiled=True)
        return units.reshape(rows.shape)

    parts = routing(routes, codes)
    arrived = [exchange(dispatch(place, normed2, 2)) for place, _ in parts]
    returned = [exchange(expert(rows, w_gate[0], w_up[0], w_down[0], 2, 7)) for rows in arrived]
    mine, theirs = combine([(factors, rows) for (_, factors), rows in zip(parts, returned)], 4)
    layer_out = (wide + mine + swap(theirs)).astype(BF)
    return (attended, layer_out)


def solution(mesh):
    fine = Mesh(mesh.devices.reshape(SIZES), NAMES)
    rows = P(CTX + EP, None)
    heads = P(CTX + EP, None, None)
    placed = (
        P(CTX, EP),
        P(None, CTX),
        P(None, EP),
        P(EP + CTX, None),
        rows,
        P(),
        rows,
        rows,
        heads,
        heads,
        heads,
    )
    return jax.shard_map(local, mesh=fine, in_specs=placed, out_specs=(rows, rows), check_vma=False)
```

```python
import functools

import jax
import jax.numpy as jnp
from jax import lax
from jax.experimental import pallas as pl
from jax.experimental.pallas import tpu as pltpu
from jax.sharding import Mesh, PartitionSpec as P

NOPE = 128
VD = 128
KV_RANK = 512
TOP = 8
QK = 192
CAP = 3
SLOTS = (slice(0, 3),)

CTX = ("z_lo", "x", "core")
CTX_CHIPS = ("z_lo", "x")
EP = ("z_hi", "y")
CHIPS = ("z_lo", "x", "z_hi", "y")
SIZES = (2, 4, 2, 2, 4)
NAMES = ("z_lo", "x", "core", "z_hi", "y")
SWAP = ((0, 1), (1, 0))
BF = jnp.bfloat16
F32 = jnp.float32
LOG2E = 1.4426950408889634


def in_hbm(a):
    return pltpu.with_memory_space_constraint(a, pltpu.HBM)


def attend_kernel(
    ids_ref, q_hbm, w_hbm, near_ref, far_ref, out_ref, q_ref, w_ref, lat_ref, s_ref, latq_ref, mixed_ref, sems, *, cuts
):
    heads = w_ref.shape[1] // (NOPE + VD)
    rows = q_ref.shape[0]
    m = heads * rows
    pairs = near_ref.shape[0]
    keys = 2 * rows * pairs
    q_copy = pltpu.make_async_copy(q_hbm, q_ref, sems.at[0])
    q_copy.start()
    wide = w_ref.shape[1] // (sems.shape[0] - 1)
    w_copies = []
    for i in range(sems.shape[0] - 1):
        part = slice(i * wide, (i + 1) * wide)
        w_copies.append(pltpu.make_async_copy(w_hbm.at[:, part], w_ref.at[:, part], sems.at[1 + i]))
        w_copies[-1].start()
    for i in range(pairs):
        lat_ref[:, 2 * i * rows : (2 * i + 1) * rows] = near_ref[i]
        lat_ref[:, (2 * i + 1) * rows : (2 * i + 2) * rows] = far_ref[i]
    q_copy.wait()
    for h in range(heads):
        here = slice(h * rows, (h + 1) * rows)
        if h * (NOPE + VD) % wide == 0:
            w_copies[h * (NOPE + VD) // wide].wait()
        key_weights = w_ref[:, h * (NOPE + VD) : h * (NOPE + VD) + NOPE]
        plain = q_ref[:, h * QK : h * QK + NOPE]
        latq = lax.dot_general(plain, key_weights, (((1,), (1,)), ((), ())), preferred_element_type=F32)
        latq_ref[here, :KV_RANK] = latq.astype(BF)
        latq_ref[here, KV_RANK:] = q_ref[:, h * QK + NOPE : (h + 1) * QK]
    ctx, core = ids_ref[0], ids_ref[1]
    span = keys // cuts
    lane = lax.broadcasted_iota(jnp.int32, (m, rows), 1)
    query = lax.broadcasted_iota(jnp.int32, (m, rows), 0) % rows
    ahead = lane - query
    peak = jnp.full((m, rows), -1e30, F32)
    for j in range(cuts):
        s = jnp.dot(latq_ref[...], lat_ref[:, j * span : (j + 1) * span], preferred_element_type=F32)
        for b in range(span // rows):
            block = j * (span // rows) + b
            pos = 2 * (block // 2) + (core if block % 2 == 0 else 1 - core)
            part = s[:, b * rows : (b + 1) * rows]
            part = jnp.where(ahead <= (ctx - pos) * rows, part, F32(-1e30))
            peak = jnp.maximum(peak, part)
            s_ref[:, block * rows : (block + 1) * rows] = part
    top = jnp.max(peak, axis=1, keepdims=True)
    total = jnp.zeros((m, rows), F32)
    for j in range(cuts):
        probs = []
        for b in range(span // rows):
            first = j * span + b * rows
            p = jnp.exp2((s_ref[:, first : first + rows] - top) * (QK ** (-0.5) * LOG2E))
            total = total + p
            probs.append(p.astype(BF))
        part = lax.dot_general(
            jnp.concatenate(probs, axis=1),
            lat_ref[:KV_RANK, j * span : (j + 1) * span],
            (((1,), (1,)), ((), ())),
            preferred_element_type=F32,
        )
        mixed_ref[...] = part if j == 0 else mixed_ref[...] + part
    mixed = (mixed_ref[...] / jnp.sum(total, axis=1, keepdims=True)).astype(BF)
    for h in range(heads):
        values = w_ref[:, h * (NOPE + VD) + NOPE : (h + 1) * (NOPE + VD)]
        o = jnp.dot(mixed[h * rows : (h + 1) * rows], values, preferred_element_type=F32)
        out_ref[:, h * VD : (h + 1) * VD] = o.astype(BF)


def attend(ids, q, w_kv, near, far, cuts):
    pairs, depth, rows = near.shape
    heads = w_kv.shape[1] // (NOPE + VD)
    keys = 2 * rows * pairs
    m = heads * rows
    whole = pl.BlockSpec(memory_space=pltpu.VMEM)
    hbm = pl.BlockSpec(memory_space=pltpu.HBM)
    return pl.pallas_call(
        functools.partial(attend_kernel, cuts=cuts),
        in_specs=[pl.BlockSpec(memory_space=pltpu.SMEM), hbm, hbm, whole, whole],
        out_specs=whole,
        out_shape=jax.ShapeDtypeStruct((rows, heads * VD), BF),
        scratch_shapes=[
            pltpu.VMEM(q.shape, BF),
            pltpu.VMEM(w_kv.shape, BF),
            pltpu.VMEM((depth, keys), BF),
            pltpu.VMEM((m, keys), F32),
            pltpu.VMEM((m, depth), BF),
            pltpu.VMEM((m, KV_RANK), F32),
            pltpu.SemaphoreType.DMA((5,)),
        ],
        compiler_params=pltpu.CompilerParams(vmem_limit_bytes=28 * 2**20),
        cost_estimate=pl.CostEstimate(
            flops=2 * m * keys * (depth + KV_RANK), bytes_accessed=8_000_000, transcendentals=m * keys
        ),
    )(ids, in_hbm(q), in_hbm(w_kv), near, far)


def expert_kernel(x_hbm, g_ref, u_ref, d_hbm, out_hbm, d_ref, x_ref, hid_ref, gate_ref, up_ref, y_ref, sem_d, sem_in, sem_out):
    units, pair, width = x_ref.shape
    m = units * pair
    first, last = sem_in.shape[0], sem_out.shape[0]
    depth, wide = width // first, width // last
    arrivals = []
    for k in range(first):
        part = slice(k * depth, (k + 1) * depth)
        arrivals.append(pltpu.make_async_copy(x_hbm.at[:, :, part], x_ref.at[:, :, part], sem_in.at[k]))
        arrivals[-1].start()
    d_copy = pltpu.make_async_copy(d_hbm, d_ref, sem_d.at[0])
    d_copy.start()
    for k in range(first):
        part = slice(k * depth, (k + 1) * depth)
        arrivals[k].wait()
        rows = x_ref[:, :, part].reshape(m, depth)
        gate = jnp.dot(rows, g_ref[part], preferred_element_type=F32)
        upward = jnp.dot(rows, u_ref[part], preferred_element_type=F32)
        gate_ref[...] = gate if k == 0 else gate_ref[...] + gate
        up_ref[...] = upward if k == 0 else up_ref[...] + upward
    gate = gate_ref[...]
    hid_ref[...] = (gate / (1.0 + jnp.exp(-gate)) * up_ref[...]).astype(BF)
    d_copy.wait()
    departures = []
    for n in range(last):
        part = slice(n * wide, (n + 1) * wide)
        y = jnp.dot(hid_ref[...], d_ref[:, part], preferred_element_type=F32).astype(BF)
        y_ref[:, :, part] = y.reshape(units, pair, wide)
        departures.append(pltpu.make_async_copy(y_ref.at[:, :, part], out_hbm.at[:, :, part], sem_out.at[n]))
        departures[-1].start()
    for copy in departures:
        copy.wait()


def expert(x, w_gate, w_up, w_down, first, last):
    units, pair, width = x.shape
    m = units * pair
    hidden = w_gate.shape[1]
    whole = pl.BlockSpec(memory_space=pltpu.VMEM)
    far = pl.BlockSpec(memory_space=pltpu.HBM)
    return pl.pallas_call(
        expert_kernel,
        in_specs=[far, whole, whole, far],
        out_specs=far,
        out_shape=pltpu.HBM(x.shape, BF),
        scratch_shapes=[
            pltpu.VMEM(w_down.shape, BF),
            pltpu.VMEM(x.shape, BF),
            pltpu.VMEM((m, hidden), BF),
            pltpu.VMEM((m, hidden), F32),
            pltpu.VMEM((m, hidden), F32),
            pltpu.VMEM(x.shape, BF),
            pltpu.SemaphoreType.DMA((1,)),
            pltpu.SemaphoreType.DMA((first,)),
            pltpu.SemaphoreType.DMA((last,)),
        ],
        compiler_params=pltpu.CompilerParams(vmem_limit_bytes=24 * 2**20),
        cost_estimate=pl.CostEstimate(
            flops=6 * m * width * hidden, bytes_accessed=17_000_000, transcendentals=m * hidden
        ),
    )(x, w_gate, w_up, in_hbm(w_down))


def dispatch_kernel(place_ref, x_ref, out_ref):
    y = jnp.dot(place_ref[...], x_ref[...], preferred_element_type=F32).astype(BF)
    out_ref[...] = y.reshape(out_ref.shape)


def dispatch(place, x, cuts):
    m = place.shape[0]
    tokens, width = x.shape
    n = width // cuts
    return pl.pallas_call(
        dispatch_kernel,
        grid=(cuts,),
        in_specs=[pl.BlockSpec(place.shape, lambda i: (0, 0)), pl.BlockSpec((tokens, n), lambda i: (0, i))],
        out_specs=pl.BlockSpec((m // 2, 2, n), lambda i: (0, 0, i)),
        out_shape=jax.ShapeDtypeStruct((m // 2, 2, width), BF),
        compiler_params=pltpu.CompilerParams(vmem_limit_bytes=32 * 2**20),
        cost_estimate=pl.CostEstimate(
            flops=2 * m * tokens * width, bytes_accessed=2 * m * width + 2 * tokens * width, transcendentals=0
        ),
    )(place, x)


def combine_kernel(*refs):
    *in_refs, own_ref, far_ref = refs
    tok = own_ref.shape[0]
    y = None
    for factors_ref, x_ref in zip(in_refs[::2], in_refs[1::2]):
        rows = x_ref[...].reshape(factors_ref.shape[1], x_ref.shape[2])
        part = jnp.dot(factors_ref[...], rows, preferred_element_type=F32)
        y = part if y is None else y + part
    y = y[: 2 * tok] + y[2 * tok :]
    own_ref[...] = y[:tok]
    far_ref[...] = y[tok:]


def combine(parts, cuts):
    width = parts[0][1].shape[2]
    n = width // cuts
    tok = parts[0][0].shape[0] // 4
    half = pl.BlockSpec((tok, n), lambda i: (0, i))
    in_specs = []
    for factors, x in parts:
        in_specs.append(pl.BlockSpec(factors.shape, lambda i: (0, 0)))
        in_specs.append(pl.BlockSpec((x.shape[0], 2, n), lambda i: (0, 0, i)))
    rows = sum(2 * x.shape[0] for _, x in parts)
    return pl.pallas_call(
        combine_kernel,
        grid=(cuts,),
        in_specs=in_specs,
        out_specs=(half, half),
        out_shape=(jax.ShapeDtypeStruct((tok, width), F32),) * 2,
        compiler_params=pltpu.CompilerParams(vmem_limit_bytes=32 * 2**20),
        cost_estimate=pl.CostEstimate(
            flops=8 * tok * rows * width, bytes_accessed=2 * rows * width, transcendentals=0
        ),
    )(*[a for part in parts for a in part])


def project_kernel(ids_ref, own_ref, before_ref, after_ref, opposite_ref, near_ref, far_ref, out_ref, x_ref, w_ref):
    rows = own_ref.shape[0]
    group, tok = 4, out_ref.shape[1]
    parts = out_ref.shape[0] // group
    core, x = ids_ref[1], ids_ref[2]
    x_ref[:rows] = own_ref[...]
    x_ref[rows : 2 * rows] = after_ref[...]
    x_ref[2 * rows : 3 * rows] = opposite_ref[...]
    x_ref[3 * rows :] = before_ref[...]
    deep = VD // 2
    for side, ref in enumerate((near_ref, far_ref)):
        offset = (core if side == 0 else 1 - core) * deep
        for j in range(ref.shape[0]):
            w_ref[pl.ds(pl.multiple_of(j * VD + offset, deep), deep)] = ref[j]
    for d in range(group):
        y = jnp.dot(x_ref[d * rows : (d + 1) * rows], w_ref[...], preferred_element_type=F32).astype(BF)
        target = lax.rem(x + d, group)
        for e in range(parts):
            out_ref[e * group + target] = y[e * tok : (e + 1) * tok]


def project(ids, pieces, near, far, parts, width):
    rows, depth = pieces[0].shape
    whole = pl.BlockSpec(memory_space=pltpu.VMEM)
    group = 4
    return pl.pallas_call(
        project_kernel,
        in_specs=[pl.BlockSpec(memory_space=pltpu.SMEM)] + [whole] * (len(pieces) + 2),
        out_specs=whole,
        out_shape=jax.ShapeDtypeStruct((parts * group, rows // parts, width), BF),
        scratch_shapes=[pltpu.VMEM((group * rows, depth), BF), pltpu.VMEM((depth, width), BF)],
        compiler_params=pltpu.CompilerParams(vmem_limit_bytes=32 * 2**20),
        cost_estimate=pl.CostEstimate(
            flops=2 * group * rows * depth * width, bytes_accessed=2 * depth * width, transcendentals=0
        ),
    )(ids, *pieces, near, far)


def blocks_kernel(w_ref, out_ref, sems):
    wide = out_ref.shape[2]
    group = w_ref.shape[1] // wide
    copies = []
    for i in range(out_ref.shape[0]):
        first = i % group * wide
        copies.append(pltpu.make_async_copy(w_ref.at[:, first : first + wide], out_ref.at[i], sems.at[i]))
        copies[-1].start()
    for copy in copies:
        copy.wait()


def column_blocks(w, group, count):
    shape = (count, w.shape[0], w.shape[1] // group)
    return pl.pallas_call(
        blocks_kernel,
        in_specs=[pl.BlockSpec(memory_space=pltpu.VMEM)],
        out_specs=pl.BlockSpec(memory_space=pltpu.HBM),
        out_shape=pltpu.HBM(shape, w.dtype),
        scratch_shapes=[pltpu.SemaphoreType.DMA((count,))],
        cost_estimate=pl.CostEstimate(flops=0, bytes_accessed=60_000_000, transcendentals=0),
    )(w)


def swap(mine):
    return lax.ppermute(mine, "core", SWAP)


def up(a):
    return lax.ppermute(a, "x", [(i, (i + 1) % 4) for i in range(4)])


def down(a):
    return lax.ppermute(a, "x", [(i, (i + 3) % 4) for i in range(4)])


def routing(routes, codes):
    tok = routes.shape[0]
    core = lax.axis_index("core")
    code_float = codes.astype(F32)
    mix = code_float / jnp.sum(code_float, axis=1, keepdims=True)
    routes2, mix2 = jnp.stack([routes, swap(routes)]), jnp.stack([mix, swap(mix)])
    chosen = routes2[:, :, :, None] == jnp.arange(64, dtype=jnp.int32)
    weight = jnp.sum(jnp.where(chosen, mix2[..., None], F32(0.0)), axis=2)
    has = jnp.any(chosen, axis=2)

    def of_core(a):
        a = a.reshape(2, tok, 8, 2, 4)
        return jnp.where(core == 0, a[:, :, :, 0], a[:, :, :, 1]).reshape(2, tok, 32)

    weight, has = of_core(weight), of_core(has)
    count = has.astype(jnp.int32)
    slot = jnp.cumsum(count, axis=1) - count
    place = has[:, :, :, None] & (slot[:, :, :, None] == jnp.arange(CAP, dtype=jnp.int32))
    place = place.transpose(2, 3, 0, 1)[:, :, :, None, :]
    same = jnp.arange(2)[:, None, None] == jnp.arange(2)[None, :, None]
    place = (place & same).reshape(32, CAP, 2, 2 * tok)
    place = jnp.broadcast_to(place[:, None], (32, 2, CAP, 2, 2 * tok)).reshape(64, CAP, 2, 2 * tok)
    gains = weight.transpose(2, 0, 1).reshape(32, 2 * tok)
    gains = jnp.broadcast_to(gains[:, None], (32, 2, 2 * tok)).reshape(64, 1, 1, 2 * tok)
    factors = jnp.where(place, gains, F32(0.0))
    high = lax.reduce_precision(factors, 8, 7)
    factors = jnp.concatenate([high, factors - high], axis=3).astype(BF)
    place = place.astype(BF)
    parts = []
    for slots in SLOTS:
        parts.append((place[:, slots].reshape(-1, 2 * tok), factors[:, slots].reshape(-1, 4 * tok).T))
    return parts


def local(queries, latents, w_kv, w_out, resid, norm_gain, routes, codes, w_gate, w_up, w_down):
    tok, width = resid.shape
    chips = 64
    core = lax.axis_index("core")
    group = 4
    columns = width // group
    near = lax.all_to_all(
        jnp.broadcast_to(latents[None], (8,) + latents.shape), CTX_CHIPS, split_axis=0, concat_axis=0, tiled=True
    )
    far = swap(near)
    w_blocks, _ = lax.optimization_barrier((column_blocks(w_out, group, 8), near[0, :8]))
    w_near = lax.all_to_all(w_blocks, CTX_CHIPS, split_axis=0, concat_axis=0, tiled=True)
    ids = jnp.stack([lax.axis_index(CTX), core, lax.axis_index("x")]).astype(jnp.int32)
    own = attend(ids, queries, w_kv, near, far, 4)
    opposite = lax.ppermute(own, "x", [(i, (i + 2) % 4) for i in range(4)])
    before, after = up(own), down(own)
    opposite, w_near = lax.optimization_barrier((opposite, w_near))
    w_far = swap(w_near)
    attn = project(ids, (own, before, after, opposite), w_near, w_far, 8, columns)
    attn = lax.all_to_all(attn, EP + ("x",), split_axis=0, concat_axis=0, tiled=True)
    attn = jnp.sum(attn.reshape(8, group, tok, columns).astype(F32), axis=0)
    attn = attn.transpose(1, 0, 2).reshape(tok, width)
    attended = (resid.astype(F32) + attn).astype(BF)
    wide = attended.astype(F32)
    meansq = jnp.mean(wide * wide, axis=1, keepdims=True)
    normed = (wide * lax.rsqrt(meansq + 1e-06) * norm_gain[None, :]).astype(BF)
    normed2 = jnp.concatenate([normed, swap(normed)], axis=0)

    def exchange(rows):
        units = rows.reshape(chips, -1, 2, width)
        units = lax.all_to_all(units, CHIPS, split_axis=0, concat_axis=0, tiled=True)
        return units.reshape(rows.shape)

    parts = routing(routes, codes)
    arrived = [exchange(dispatch(place, normed2, 2)) for place, _ in parts]
    returned = [exchange(expert(rows, w_gate[0], w_up[0], w_down[0], 2, 7)) for rows in arrived]
    mine, theirs = combine([(factors, rows) for (_, factors), rows in zip(parts, returned)], 4)
    layer_out = (wide + mine + swap(theirs)).astype(BF)
    return (attended, layer_out)


def solution(mesh):
    fine = Mesh(mesh.devices.reshape(SIZES), NAMES)
    rows = P(CTX + EP, None)
    heads = P(CTX + EP, None, None)
    placed = (
        P(CTX, EP),
        P(None, CTX),
        P(None, EP),
        P(EP + CTX, None),
        rows,
        P(),
        rows,
        rows,
        heads,
        heads,
        heads,
    )
    return jax.shard_map(local, mesh=fine, in_specs=placed, out_specs=(rows, rows), check_vma=False)
```

```python
import functools

import jax
import jax.numpy as jnp
from jax import lax
from jax.experimental import pallas as pl
from jax.experimental.pallas import tpu as pltpu
from jax.sharding import Mesh, PartitionSpec as P

NOPE = 128
VD = 128
KV_RANK = 512
TOP = 8
QK = 192
CAP = 3
SLOTS = (slice(0, 3),)

CTX = ("z_lo", "x", "core")
CTX_CHIPS = ("x", "z_lo")
EP = ("z_hi", "y")
CHIPS = ("z_hi", "z_lo", "x", "y")
SIZES = (2, 4, 2, 2, 4)
NAMES = ("z_lo", "x", "core", "z_hi", "y")
SWAP = ((0, 1), (1, 0))
BF = jnp.bfloat16
F32 = jnp.float32
LOG2E = 1.4426950408889634


def chip_number(i):
    return i % 2 * 4 + i // 2


def in_hbm(a):
    return pltpu.with_memory_space_constraint(a, pltpu.HBM)


def attend_kernel(
    ids_ref, q_hbm, w_hbm, near_ref, far_ref, out_ref, q_ref, w_ref, lat_ref, s_ref, latq_ref, mixed_ref, sems, *, cuts
):
    heads = w_ref.shape[1] // (NOPE + VD)
    rows = q_ref.shape[0]
    m = heads * rows
    pairs = near_ref.shape[0]
    keys = 2 * rows * pairs
    q_copy = pltpu.make_async_copy(q_hbm, q_ref, sems.at[0])
    w_copy = pltpu.make_async_copy(w_hbm, w_ref, sems.at[1])
    q_copy.start()
    w_copy.start()
    for i in range(pairs):
        lat_ref[:, 2 * i * rows : (2 * i + 1) * rows] = near_ref[i]
        lat_ref[:, (2 * i + 1) * rows : (2 * i + 2) * rows] = far_ref[i]
    q_copy.wait()
    w_copy.wait()
    for h in range(heads):
        here = slice(h * rows, (h + 1) * rows)
        key_weights = w_ref[:, h * (NOPE + VD) : h * (NOPE + VD) + NOPE]
        plain = q_ref[:, h * QK : h * QK + NOPE]
        latq = lax.dot_general(plain, key_weights, (((1,), (1,)), ((), ())), preferred_element_type=F32)
        latq_ref[here, :KV_RANK] = latq.astype(BF)
        latq_ref[here, KV_RANK:] = q_ref[:, h * QK + NOPE : (h + 1) * QK]
    ctx, core = ids_ref[0], ids_ref[1]
    span = keys // cuts
    lane = lax.broadcasted_iota(jnp.int32, (m, rows), 1)
    query = lax.broadcasted_iota(jnp.int32, (m, rows), 0) % rows
    ahead = lane - query
    peak = jnp.full((m, rows), -1e30, F32)
    for j in range(cuts):
        s = jnp.dot(latq_ref[...], lat_ref[:, j * span : (j + 1) * span], preferred_element_type=F32)
        for b in range(span // rows):
            block = j * (span // rows) + b
            pos = 2 * chip_number(block // 2) + (core if block % 2 == 0 else 1 - core)
            part = s[:, b * rows : (b + 1) * rows]
            part = jnp.where(ahead <= (ctx - pos) * rows, part, F32(-1e30))
            peak = jnp.maximum(peak, part)
            s_ref[:, block * rows : (block + 1) * rows] = part
    top = jnp.max(peak, axis=1, keepdims=True)
    total = jnp.zeros((m, rows), F32)
    for j in range(cuts):
        probs = []
        for b in range(span // rows):
            first = j * span + b * rows
            p = jnp.exp2((s_ref[:, first : first + rows] - top) * (QK ** (-0.5) * LOG2E))
            total = total + p
            probs.append(p.astype(BF))
        part = lax.dot_general(
            jnp.concatenate(probs, axis=1),
            lat_ref[:KV_RANK, j * span : (j + 1) * span],
            (((1,), (1,)), ((), ())),
            preferred_element_type=F32,
        )
        mixed_ref[...] = part if j == 0 else mixed_ref[...] + part
    mixed = (mixed_ref[...] / jnp.sum(total, axis=1, keepdims=True)).astype(BF)
    for h in range(heads):
        values = w_ref[:, h * (NOPE + VD) + NOPE : (h + 1) * (NOPE + VD)]
        o = jnp.dot(mixed[h * rows : (h + 1) * rows], values, preferred_element_type=F32)
        out_ref[:, h * VD : (h + 1) * VD] = o.astype(BF)


def attend(ids, q, w_kv, near, far, cuts):
    pairs, depth, rows = near.shape
    heads = w_kv.shape[1] // (NOPE + VD)
    keys = 2 * rows * pairs
    m = heads * rows
    whole = pl.BlockSpec(memory_space=pltpu.VMEM)
    hbm = pl.BlockSpec(memory_space=pltpu.HBM)
    return pl.pallas_call(
        functools.partial(attend_kernel, cuts=cuts),
        in_specs=[pl.BlockSpec(memory_space=pltpu.SMEM), hbm, hbm, whole, whole],
        out_specs=whole,
        out_shape=jax.ShapeDtypeStruct((rows, heads * VD), BF),
        scratch_shapes=[
            pltpu.VMEM(q.shape, BF),
            pltpu.VMEM(w_kv.shape, BF),
            pltpu.VMEM((depth, keys), BF),
            pltpu.VMEM((m, keys), F32),
            pltpu.VMEM((m, depth), BF),
            pltpu.VMEM((m, KV_RANK), F32),
            pltpu.SemaphoreType.DMA((2,)),
        ],
        compiler_params=pltpu.CompilerParams(vmem_limit_bytes=28 * 2**20),
        cost_estimate=pl.CostEstimate(
            flops=2 * m * keys * (depth + KV_RANK), bytes_accessed=8_000_000, transcendentals=m * keys
        ),
    )(ids, in_hbm(q), in_hbm(w_kv), near, far)


def expert_kernel(x_hbm, g_ref, u_ref, d_hbm, out_hbm, d_ref, x_ref, hid_ref, gate_ref, up_ref, y_ref, sem_d, sem_in, sem_out):
    units, pair, width = x_ref.shape
    m = units * pair
    first, last = sem_in.shape[0], sem_out.shape[0]
    depth, wide = width // first, width // last
    arrivals = []
    for k in range(first):
        part = slice(k * depth, (k + 1) * depth)
        arrivals.append(pltpu.make_async_copy(x_hbm.at[:, :, part], x_ref.at[:, :, part], sem_in.at[k]))
        arrivals[-1].start()
    d_copy = pltpu.make_async_copy(d_hbm, d_ref, sem_d.at[0])
    d_copy.start()
    for k in range(first):
        part = slice(k * depth, (k + 1) * depth)
        arrivals[k].wait()
        rows = x_ref[:, :, part].reshape(m, depth)
        gate = jnp.dot(rows, g_ref[part], preferred_element_type=F32)
        upward = jnp.dot(rows, u_ref[part], preferred_element_type=F32)
        gate_ref[...] = gate if k == 0 else gate_ref[...] + gate
        up_ref[...] = upward if k == 0 else up_ref[...] + upward
    gate = gate_ref[...]
    hid_ref[...] = (gate / (1.0 + jnp.exp(-gate)) * up_ref[...]).astype(BF)
    d_copy.wait()
    departures = []
    for n in range(last):
        part = slice(n * wide, (n + 1) * wide)
        y = jnp.dot(hid_ref[...], d_ref[:, part], preferred_element_type=F32).astype(BF)
        y_ref[:, :, part] = y.reshape(units, pair, wide)
        departures.append(pltpu.make_async_copy(y_ref.at[:, :, part], out_hbm.at[:, :, part], sem_out.at[n]))
        departures[-1].start()
    for copy in departures:
        copy.wait()


def expert(x, w_gate, w_up, w_down, first, last):
    units, pair, width = x.shape
    m = units * pair
    hidden = w_gate.shape[1]
    whole = pl.BlockSpec(memory_space=pltpu.VMEM)
    far = pl.BlockSpec(memory_space=pltpu.HBM)
    return pl.pallas_call(
        expert_kernel,
        in_specs=[far, whole, whole, far],
        out_specs=far,
        out_shape=pltpu.HBM(x.shape, BF),
        scratch_shapes=[
            pltpu.VMEM(w_down.shape, BF),
            pltpu.VMEM(x.shape, BF),
            pltpu.VMEM((m, hidden), BF),
            pltpu.VMEM((m, hidden), F32),
            pltpu.VMEM((m, hidden), F32),
            pltpu.VMEM(x.shape, BF),
            pltpu.SemaphoreType.DMA((1,)),
            pltpu.SemaphoreType.DMA((first,)),
            pltpu.SemaphoreType.DMA((last,)),
        ],
        compiler_params=pltpu.CompilerParams(vmem_limit_bytes=24 * 2**20),
        cost_estimate=pl.CostEstimate(
            flops=6 * m * width * hidden, bytes_accessed=17_000_000, transcendentals=m * hidden
        ),
    )(x, w_gate, w_up, in_hbm(w_down))


def dispatch_kernel(place_ref, x_ref, out_ref):
    y = jnp.dot(place_ref[...], x_ref[...], preferred_element_type=F32).astype(BF)
    out_ref[...] = y.reshape(out_ref.shape)


def dispatch(place, x, cuts):
    m = place.shape[0]
    tokens, width = x.shape
    n = width // cuts
    return pl.pallas_call(
        dispatch_kernel,
        grid=(cuts,),
        in_specs=[pl.BlockSpec(place.shape, lambda i: (0, 0)), pl.BlockSpec((tokens, n), lambda i: (0, i))],
        out_specs=pl.BlockSpec((m // 2, 2, n), lambda i: (0, 0, i)),
        out_shape=jax.ShapeDtypeStruct((m // 2, 2, width), BF),
        compiler_params=pltpu.CompilerParams(vmem_limit_bytes=32 * 2**20),
        cost_estimate=pl.CostEstimate(
            flops=2 * m * tokens * width, bytes_accessed=2 * m * width + 2 * tokens * width, transcendentals=0
        ),
    )(place, x)


def combine_kernel(*refs):
    *in_refs, own_ref, far_ref = refs
    tok = own_ref.shape[0]
    y = None
    for factors_ref, x_ref in zip(in_refs[::2], in_refs[1::2]):
        rows = x_ref[...].reshape(factors_ref.shape[1], x_ref.shape[2])
        part = jnp.dot(factors_ref[...], rows, preferred_element_type=F32)
        y = part if y is None else y + part
    y = y[: 2 * tok] + y[2 * tok :]
    own_ref[...] = y[:tok]
    far_ref[...] = y[tok:]


def combine(parts, cuts):
    width = parts[0][1].shape[2]
    n = width // cuts
    tok = parts[0][0].shape[0] // 4
    half = pl.BlockSpec((tok, n), lambda i: (0, i))
    in_specs = []
    for factors, x in parts:
        in_specs.append(pl.BlockSpec(factors.shape, lambda i: (0, 0)))
        in_specs.append(pl.BlockSpec((x.shape[0], 2, n), lambda i: (0, 0, i)))
    rows = sum(2 * x.shape[0] for _, x in parts)
    return pl.pallas_call(
        combine_kernel,
        grid=(cuts,),
        in_specs=in_specs,
        out_specs=(half, half),
        out_shape=(jax.ShapeDtypeStruct((tok, width), F32),) * 2,
        compiler_params=pltpu.CompilerParams(vmem_limit_bytes=32 * 2**20),
        cost_estimate=pl.CostEstimate(
            flops=8 * tok * rows * width, bytes_accessed=2 * rows * width, transcendentals=0
        ),
    )(*[a for part in parts for a in part])


def project_kernel(ids_ref, own_ref, before_ref, after_ref, left_ref, right_ref, near_ref, far_ref, out_ref, x_ref, w_ref):
    rows = own_ref.shape[0]
    group, tok = 4, out_ref.shape[1]
    parts = out_ref.shape[0] // group
    core, x = ids_ref[1], ids_ref[2]
    half = left_ref.shape[1]
    x_ref[:rows] = own_ref[...]
    x_ref[rows : 2 * rows] = after_ref[...]
    x_ref[2 * rows : 3 * rows, :half] = left_ref[...]
    x_ref[2 * rows : 3 * rows, half:] = right_ref[...]
    x_ref[3 * rows :] = before_ref[...]
    deep = VD // 2
    for side, ref in enumerate((near_ref, far_ref)):
        offset = (core if side == 0 else 1 - core) * deep
        for j in range(ref.shape[0]):
            w_ref[pl.ds(pl.multiple_of(chip_number(j) * VD + offset, deep), deep)] = ref[j]
    for d in range(group):
        y = jnp.dot(x_ref[d * rows : (d + 1) * rows], w_ref[...], preferred_element_type=F32).astype(BF)
        target = lax.rem(x + d, group)
        for e in range(parts):
            out_ref[e * group + target] = y[e * tok : (e + 1) * tok]


def project(ids, pieces, near, far, parts, width):
    rows, depth = pieces[0].shape
    whole = pl.BlockSpec(memory_space=pltpu.VMEM)
    group = 4
    return pl.pallas_call(
        project_kernel,
        in_specs=[pl.BlockSpec(memory_space=pltpu.SMEM)] + [whole] * (len(pieces) + 2),
        out_specs=whole,
        out_shape=jax.ShapeDtypeStruct((parts * group, rows // parts, width), BF),
        scratch_shapes=[pltpu.VMEM((group * rows, depth), BF), pltpu.VMEM((depth, width), BF)],
        compiler_params=pltpu.CompilerParams(vmem_limit_bytes=32 * 2**20),
        cost_estimate=pl.CostEstimate(
            flops=2 * group * rows * depth * width, bytes_accessed=2 * depth * width, transcendentals=0
        ),
    )(ids, *pieces, near, far)


def blocks_kernel(w_ref, out_ref, sems):
    wide = out_ref.shape[2]
    group = w_ref.shape[1] // wide
    copies = []
    for i in range(out_ref.shape[0]):
        first = i // (out_ref.shape[0] // group) * wide
        copies.append(pltpu.make_async_copy(w_ref.at[:, first : first + wide], out_ref.at[i], sems.at[i]))
        copies[-1].start()
    for copy in copies:
        copy.wait()


def column_blocks(w, group, count):
    shape = (count, w.shape[0], w.shape[1] // group)
    return pl.pallas_call(
        blocks_kernel,
        in_specs=[pl.BlockSpec(memory_space=pltpu.VMEM)],
        out_specs=pl.BlockSpec(memory_space=pltpu.HBM),
        out_shape=pltpu.HBM(shape, w.dtype),
        scratch_shapes=[pltpu.SemaphoreType.DMA((count,))],
        cost_estimate=pl.CostEstimate(flops=0, bytes_accessed=6 * w.size, transcendentals=0),
    )(w)


def swap(mine):
    return lax.ppermute(mine, "core", SWAP)


def up(a):
    return lax.ppermute(a, "x", [(i, (i + 1) % 4) for i in range(4)])


def down(a):
    return lax.ppermute(a, "x", [(i, (i + 3) % 4) for i in range(4)])


def routing(routes, codes):
    tok = routes.shape[0]
    core = lax.axis_index("core")
    code_float = codes.astype(F32)
    mix = code_float / jnp.sum(code_float, axis=1, keepdims=True)
    routes2, mix2 = jnp.stack([routes, swap(routes)]), jnp.stack([mix, swap(mix)])
    chosen = routes2[:, :, :, None] == jnp.arange(64, dtype=jnp.int32)
    weight = jnp.sum(jnp.where(chosen, mix2[..., None], F32(0.0)), axis=2)
    has = jnp.any(chosen, axis=2)

    def of_core(a):
        a = a.reshape(2, tok, 8, 2, 4)
        a = jnp.where(core == 0, a[:, :, :, 0], a[:, :, :, 1])
        return a.reshape(2, tok, 8, 2, 2).transpose(0, 1, 3, 2, 4).reshape(2, tok, 32)

    weight, has = of_core(weight), of_core(has)
    count = has.astype(jnp.int32)
    slot = jnp.cumsum(count, axis=1) - count
    place = has[:, :, :, None] & (slot[:, :, :, None] == jnp.arange(CAP, dtype=jnp.int32))
    place = place.transpose(2, 3, 0, 1)[:, :, :, None, :]
    same = jnp.arange(2)[:, None, None] == jnp.arange(2)[None, :, None]
    place = (place & same).reshape(32, CAP, 2, 2 * tok)
    place = jnp.broadcast_to(place[:, None], (32, 2, CAP, 2, 2 * tok)).reshape(64, CAP, 2, 2 * tok)
    gains = weight.transpose(2, 0, 1).reshape(32, 2 * tok)
    gains = jnp.broadcast_to(gains[:, None], (32, 2, 2 * tok)).reshape(64, 1, 1, 2 * tok)
    factors = jnp.where(place, gains, F32(0.0))
    high = lax.reduce_precision(factors, 8, 7)
    factors = jnp.concatenate([high, factors - high], axis=3).astype(BF)
    place = place.astype(BF)
    parts = []
    for slots in SLOTS:
        parts.append((place[:, slots].reshape(-1, 2 * tok), factors[:, slots].reshape(-1, 4 * tok).T))
    return parts


def local(queries, latents, w_kv, w_out, resid, norm_gain, routes, codes, w_gate, w_up, w_down):
    tok, width = resid.shape
    chips = 64
    core = lax.axis_index("core")
    group = 4
    columns = width // group
    near = lax.all_to_all(
        jnp.broadcast_to(latents[None], (8,) + latents.shape), CTX_CHIPS, split_axis=0, concat_axis=0, tiled=True
    )
    far = swap(near)
    w_blocks, _ = lax.optimization_barrier((column_blocks(w_out, group, 8), near[0, :8]))
    w_near = lax.all_to_all(w_blocks, CTX_CHIPS, split_axis=0, concat_axis=0, tiled=True)
    ids = jnp.stack([lax.axis_index(CTX), core, lax.axis_index("x")]).astype(jnp.int32)
    own = attend(ids, queries, w_kv, near, far, 4)
    before, after, w_near = lax.optimization_barrier((up(own), down(own), w_near))
    w_far = swap(w_near)
    half = own.shape[1] // 2
    left, right = up(before[:, :half]), down(after[:, half:])
    attn = project(ids, (own, before, after, left, right), w_near, w_far, 8, columns)
    attn = lax.all_to_all(attn, EP + ("x",), split_axis=0, concat_axis=0, tiled=True)
    attn = jnp.sum(attn.reshape(8, group, tok, columns).astype(F32), axis=0)
    attn = attn.transpose(1, 0, 2).reshape(tok, width)
    attended = (resid.astype(F32) + attn).astype(BF)
    wide = attended.astype(F32)
    meansq = jnp.mean(wide * wide, axis=1, keepdims=True)
    normed = (wide * lax.rsqrt(meansq + 1e-06) * norm_gain[None, :]).astype(BF)
    normed2 = jnp.concatenate([normed, swap(normed)], axis=0)

    def exchange(rows):
        units = rows.reshape(chips, -1, 2, width)
        units = lax.all_to_all(units, CHIPS, split_axis=0, concat_axis=0, tiled=True)
        return units.reshape(rows.shape)

    parts = routing(routes, codes)
    arrived = [exchange(dispatch(place, normed2, 2)) for place, _ in parts]
    returned = [exchange(expert(rows, w_gate[0], w_up[0], w_down[0], 2, 7)) for rows in arrived]
    mine, theirs = combine([(factors, rows) for (_, factors), rows in zip(parts, returned)], 4)
    layer_out = (wide + mine + swap(theirs)).astype(BF)
    return (attended, layer_out)


def solution(mesh):
    fine = Mesh(mesh.devices.reshape(SIZES), NAMES)
    rows = P(CTX + EP, None)
    heads = P(CTX + EP, None, None)
    placed = (
        P(CTX, EP),
        P(None, CTX),
        P(None, EP),
        P(EP + CTX, None),
        rows,
        P(),
        rows,
        rows,
        heads,
        heads,
        heads,
    )
    return jax.shard_map(local, mesh=fine, in_specs=placed, out_specs=(rows, rows), check_vma=False)
```

```python
import functools

import jax
import jax.numpy as jnp
from jax import lax
from jax.experimental import pallas as pl
from jax.experimental.pallas import tpu as pltpu
from jax.sharding import Mesh, PartitionSpec as P

NOPE = 128
VD = 128
KV_RANK = 512
TOP = 8
QK = 192
CAP = 3
SLOTS = (slice(0, 3),)

CTX = ("z_lo", "x", "core")
CTX_CHIPS = ("x", "z_lo")
EP = ("z_hi", "y")
CHIPS = ("z_hi", "z_lo", "x", "y")
SIZES = (2, 4, 2, 2, 4)
NAMES = ("z_lo", "x", "core", "z_hi", "y")
SWAP = ((0, 1), (1, 0))
BF = jnp.bfloat16
F32 = jnp.float32
LOG2E = 1.4426950408889634


def chip_number(i):
    return i % 2 * 4 + i // 2


def in_hbm(a):
    return pltpu.with_memory_space_constraint(a, pltpu.HBM)


def attend_kernel(
    ids_ref, q_hbm, w_hbm, near_ref, far_ref, out_ref, q_ref, w_ref, lat_ref, s_ref, latq_ref, mixed_ref, sems, *, cuts
):
    heads = w_ref.shape[1] // (NOPE + VD)
    rows = q_ref.shape[0]
    m = heads * rows
    pairs = near_ref.shape[0]
    keys = 2 * rows * pairs
    q_copy = pltpu.make_async_copy(q_hbm, q_ref, sems.at[0])
    w_copy = pltpu.make_async_copy(w_hbm, w_ref, sems.at[1])
    q_copy.start()
    w_copy.start()
    for i in range(pairs):
        lat_ref[:, 2 * i * rows : (2 * i + 1) * rows] = near_ref[i]
        lat_ref[:, (2 * i + 1) * rows : (2 * i + 2) * rows] = far_ref[i]
    q_copy.wait()
    w_copy.wait()
    for h in range(heads):
        here = slice(h * rows, (h + 1) * rows)
        key_weights = w_ref[:, h * (NOPE + VD) : h * (NOPE + VD) + NOPE]
        plain = q_ref[:, h * QK : h * QK + NOPE]
        latq = lax.dot_general(plain, key_weights, (((1,), (1,)), ((), ())), preferred_element_type=F32)
        latq_ref[here, :KV_RANK] = latq.astype(BF)
        latq_ref[here, KV_RANK:] = q_ref[:, h * QK + NOPE : (h + 1) * QK]
    ctx, core = ids_ref[0], ids_ref[1]
    span = keys // cuts
    lane = lax.broadcasted_iota(jnp.int32, (m, rows), 1)
    query = lax.broadcasted_iota(jnp.int32, (m, rows), 0) % rows
    ahead = lane - query
    peak = jnp.full((m, rows), -1e30, F32)
    for j in range(cuts):
        s = jnp.dot(latq_ref[...], lat_ref[:, j * span : (j + 1) * span], preferred_element_type=F32)
        for b in range(span // rows):
            block = j * (span // rows) + b
            pos = 2 * chip_number(block // 2) + (core if block % 2 == 0 else 1 - core)
            part = s[:, b * rows : (b + 1) * rows]
            part = jnp.where(ahead <= (ctx - pos) * rows, part, F32(-1e30))
            peak = jnp.maximum(peak, part)
            s_ref[:, block * rows : (block + 1) * rows] = part
    top = jnp.max(peak, axis=1, keepdims=True)
    total = jnp.zeros((m, rows), F32)
    for j in range(cuts):
        probs = []
        for b in range(span // rows):
            first = j * span + b * rows
            p = jnp.exp2((s_ref[:, first : first + rows] - top) * (QK ** (-0.5) * LOG2E))
            total = total + p
            probs.append(p.astype(BF))
        part = lax.dot_general(
            jnp.concatenate(probs, axis=1),
            lat_ref[:KV_RANK, j * span : (j + 1) * span],
            (((1,), (1,)), ((), ())),
            preferred_element_type=F32,
        )
        mixed_ref[...] = part if j == 0 else mixed_ref[...] + part
    mixed = (mixed_ref[...] / jnp.sum(total, axis=1, keepdims=True)).astype(BF)
    for h in range(heads):
        values = w_ref[:, h * (NOPE + VD) + NOPE : (h + 1) * (NOPE + VD)]
        o = jnp.dot(mixed[h * rows : (h + 1) * rows], values, preferred_element_type=F32)
        out_ref[:, h * VD : (h + 1) * VD] = o.astype(BF)


def attend(ids, q, w_kv, near, far, cuts):
    pairs, depth, rows = near.shape
    heads = w_kv.shape[1] // (NOPE + VD)
    keys = 2 * rows * pairs
    m = heads * rows
    whole = pl.BlockSpec(memory_space=pltpu.VMEM)
    hbm = pl.BlockSpec(memory_space=pltpu.HBM)
    return pl.pallas_call(
        functools.partial(attend_kernel, cuts=cuts),
        in_specs=[pl.BlockSpec(memory_space=pltpu.SMEM), hbm, hbm, whole, whole],
        out_specs=whole,
        out_shape=jax.ShapeDtypeStruct((rows, heads * VD), BF),
        scratch_shapes=[
            pltpu.VMEM(q.shape, BF),
            pltpu.VMEM(w_kv.shape, BF),
            pltpu.VMEM((depth, keys), BF),
            pltpu.VMEM((m, keys), F32),
            pltpu.VMEM((m, depth), BF),
            pltpu.VMEM((m, KV_RANK), F32),
            pltpu.SemaphoreType.DMA((2,)),
        ],
        compiler_params=pltpu.CompilerParams(vmem_limit_bytes=28 * 2**20),
        cost_estimate=pl.CostEstimate(
            flops=2 * m * keys * (depth + KV_RANK), bytes_accessed=8_000_000, transcendentals=m * keys
        ),
    )(ids, in_hbm(q), in_hbm(w_kv), near, far)


def expert_kernel(x_hbm, g_ref, u_ref, d_hbm, out_hbm, d_ref, x_ref, hid_ref, gate_ref, up_ref, y_ref, sem_d, sem_in, sem_out):
    units, pair, width = x_ref.shape
    m = units * pair
    first, last = sem_in.shape[0], sem_out.shape[0]
    depth, wide = width // first, width // last
    arrivals = []
    for k in range(first):
        part = slice(k * depth, (k + 1) * depth)
        arrivals.append(pltpu.make_async_copy(x_hbm.at[:, :, part], x_ref.at[:, :, part], sem_in.at[k]))
        arrivals[-1].start()
    d_copy = pltpu.make_async_copy(d_hbm, d_ref, sem_d.at[0])
    d_copy.start()
    for k in range(first):
        part = slice(k * depth, (k + 1) * depth)
        arrivals[k].wait()
        rows = x_ref[:, :, part].reshape(m, depth)
        gate = jnp.dot(rows, g_ref[part], preferred_element_type=F32)
        upward = jnp.dot(rows, u_ref[part], preferred_element_type=F32)
        gate_ref[...] = gate if k == 0 else gate_ref[...] + gate
        up_ref[...] = upward if k == 0 else up_ref[...] + upward
    gate = gate_ref[...]
    hid_ref[...] = (gate / (1.0 + jnp.exp(-gate)) * up_ref[...]).astype(BF)
    d_copy.wait()
    departures = []
    for n in range(last):
        part = slice(n * wide, (n + 1) * wide)
        y = jnp.dot(hid_ref[...], d_ref[:, part], preferred_element_type=F32).astype(BF)
        y_ref[:, :, part] = y.reshape(units, pair, wide)
        departures.append(pltpu.make_async_copy(y_ref.at[:, :, part], out_hbm.at[:, :, part], sem_out.at[n]))
        departures[-1].start()
    for copy in departures:
        copy.wait()


def expert(x, w_gate, w_up, w_down, first, last):
    units, pair, width = x.shape
    m = units * pair
    hidden = w_gate.shape[1]
    whole = pl.BlockSpec(memory_space=pltpu.VMEM)
    far = pl.BlockSpec(memory_space=pltpu.HBM)
    return pl.pallas_call(
        expert_kernel,
        in_specs=[far, whole, whole, far],
        out_specs=far,
        out_shape=pltpu.HBM(x.shape, BF),
        scratch_shapes=[
            pltpu.VMEM(w_down.shape, BF),
            pltpu.VMEM(x.shape, BF),
            pltpu.VMEM((m, hidden), BF),
            pltpu.VMEM((m, hidden), F32),
            pltpu.VMEM((m, hidden), F32),
            pltpu.VMEM(x.shape, BF),
            pltpu.SemaphoreType.DMA((1,)),
            pltpu.SemaphoreType.DMA((first,)),
            pltpu.SemaphoreType.DMA((last,)),
        ],
        compiler_params=pltpu.CompilerParams(vmem_limit_bytes=24 * 2**20),
        cost_estimate=pl.CostEstimate(
            flops=6 * m * width * hidden, bytes_accessed=17_000_000, transcendentals=m * hidden
        ),
    )(x, w_gate, w_up, in_hbm(w_down))


def dispatch_kernel(place_ref, x_ref, out_ref):
    y = jnp.dot(place_ref[...], x_ref[...], preferred_element_type=F32).astype(BF)
    out_ref[...] = y.reshape(out_ref.shape)


def dispatch(place, x, cuts):
    m = place.shape[0]
    tokens, width = x.shape
    n = width // cuts
    return pl.pallas_call(
        dispatch_kernel,
        grid=(cuts,),
        in_specs=[pl.BlockSpec(place.shape, lambda i: (0, 0)), pl.BlockSpec((tokens, n), lambda i: (0, i))],
        out_specs=pl.BlockSpec((m // 2, 2, n), lambda i: (0, 0, i)),
        out_shape=jax.ShapeDtypeStruct((m // 2, 2, width), BF),
        compiler_params=pltpu.CompilerParams(vmem_limit_bytes=32 * 2**20),
        cost_estimate=pl.CostEstimate(
            flops=2 * m * tokens * width, bytes_accessed=2 * m * width + 2 * tokens * width, transcendentals=0
        ),
    )(place, x)


def combine_kernel(*refs):
    *in_refs, own_ref, far_ref = refs
    tok = own_ref.shape[0]
    y = None
    for factors_ref, x_ref in zip(in_refs[::2], in_refs[1::2]):
        rows = x_ref[...].reshape(factors_ref.shape[1], x_ref.shape[2])
        part = jnp.dot(factors_ref[...], rows, preferred_element_type=F32)
        y = part if y is None else y + part
    y = y[: 2 * tok] + y[2 * tok :]
    own_ref[...] = y[:tok]
    far_ref[...] = y[tok:]


def combine(parts, cuts):
    width = parts[0][1].shape[2]
    n = width // cuts
    tok = parts[0][0].shape[0] // 4
    half = pl.BlockSpec((tok, n), lambda i: (0, i))
    in_specs = []
    for factors, x in parts:
        in_specs.append(pl.BlockSpec(factors.shape, lambda i: (0, 0)))
        in_specs.append(pl.BlockSpec((x.shape[0], 2, n), lambda i: (0, 0, i)))
    rows = sum(2 * x.shape[0] for _, x in parts)
    return pl.pallas_call(
        combine_kernel,
        grid=(cuts,),
        in_specs=in_specs,
        out_specs=(half, half),
        out_shape=(jax.ShapeDtypeStruct((tok, width), F32),) * 2,
        compiler_params=pltpu.CompilerParams(vmem_limit_bytes=32 * 2**20),
        cost_estimate=pl.CostEstimate(
            flops=8 * tok * rows * width, bytes_accessed=2 * rows * width, transcendentals=0
        ),
    )(*[a for part in parts for a in part])


def project_kernel(ids_ref, own_ref, before_ref, after_ref, left_ref, right_ref, *refs):
    *block_refs, out_ref, x_ref, w_ref = refs
    rows = own_ref.shape[0]
    group, tok = 4, out_ref.shape[1]
    parts = out_ref.shape[0] // group
    core, x = ids_ref[1], ids_ref[2]
    half = left_ref.shape[1]
    x_ref[:rows] = own_ref[...]
    x_ref[rows : 2 * rows] = after_ref[...]
    x_ref[2 * rows : 3 * rows, :half] = left_ref[...]
    x_ref[2 * rows : 3 * rows, half:] = right_ref[...]
    x_ref[3 * rows :] = before_ref[...]
    deep = VD // 2
    z = lax.div(ids_ref[0], 2 * group)
    for i, ref in enumerate(block_refs):
        offset = (core if i < 2 else 1 - core) * deep
        plane = (z if i % 2 == 0 else 1 - z) * group
        for j in range(group):
            w_ref[pl.ds(pl.multiple_of((plane + j) * VD + offset, deep), deep)] = ref[j]
    for d in range(group):
        y = jnp.dot(x_ref[d * rows : (d + 1) * rows], w_ref[...], preferred_element_type=F32).astype(BF)
        target = lax.rem(x + d, group)
        for e in range(parts):
            out_ref[e * group + target] = y[e * tok : (e + 1) * tok]


def project(ids, pieces, blocks, parts, width):
    rows, depth = pieces[0].shape
    whole = pl.BlockSpec(memory_space=pltpu.VMEM)
    group = 4
    return pl.pallas_call(
        project_kernel,
        in_specs=[pl.BlockSpec(memory_space=pltpu.SMEM)] + [whole] * (len(pieces) + len(blocks)),
        out_specs=whole,
        out_shape=jax.ShapeDtypeStruct((parts * group, rows // parts, width), BF),
        scratch_shapes=[pltpu.VMEM((group * rows, depth), BF), pltpu.VMEM((depth, width), BF)],
        compiler_params=pltpu.CompilerParams(vmem_limit_bytes=32 * 2**20),
        cost_estimate=pl.CostEstimate(
            flops=2 * group * rows * depth * width, bytes_accessed=2 * depth * width, transcendentals=0
        ),
    )(ids, *pieces, *blocks)


def blocks_kernel(w_ref, out_ref, sems):
    wide = out_ref.shape[2]
    copies = []
    for i in range(out_ref.shape[0]):
        first = i * wide
        copies.append(pltpu.make_async_copy(w_ref.at[:, first : first + wide], out_ref.at[i], sems.at[i]))
        copies[-1].start()
    for copy in copies:
        copy.wait()


def column_blocks(w, count):
    shape = (count, w.shape[0], w.shape[1] // count)
    return pl.pallas_call(
        blocks_kernel,
        in_specs=[pl.BlockSpec(memory_space=pltpu.VMEM)],
        out_specs=pl.BlockSpec(memory_space=pltpu.HBM),
        out_shape=pltpu.HBM(shape, w.dtype),
        scratch_shapes=[pltpu.SemaphoreType.DMA((count,))],
        cost_estimate=pl.CostEstimate(flops=0, bytes_accessed=6 * w.size, transcendentals=0),
    )(w)


def swap(mine):
    return lax.ppermute(mine, "core", SWAP)


def up(a):
    return lax.ppermute(a, "x", [(i, (i + 1) % 4) for i in range(4)])


def down(a):
    return lax.ppermute(a, "x", [(i, (i + 3) % 4) for i in range(4)])


def routing(routes, codes):
    tok = routes.shape[0]
    core = lax.axis_index("core")
    code_float = codes.astype(F32)
    mix = code_float / jnp.sum(code_float, axis=1, keepdims=True)
    routes2, mix2 = jnp.stack([routes, swap(routes)]), jnp.stack([mix, swap(mix)])
    chosen = routes2[:, :, :, None] == jnp.arange(64, dtype=jnp.int32)
    weight = jnp.sum(jnp.where(chosen, mix2[..., None], F32(0.0)), axis=2)
    has = jnp.any(chosen, axis=2)

    def of_core(a):
        a = a.reshape(2, tok, 8, 2, 4)
        a = jnp.where(core == 0, a[:, :, :, 0], a[:, :, :, 1])
        return a.reshape(2, tok, 8, 2, 2).transpose(0, 1, 3, 2, 4).reshape(2, tok, 32)

    weight, has = of_core(weight), of_core(has)
    count = has.astype(jnp.int32)
    slot = jnp.cumsum(count, axis=1) - count
    place = has[:, :, :, None] & (slot[:, :, :, None] == jnp.arange(CAP, dtype=jnp.int32))
    place = place.transpose(2, 3, 0, 1)[:, :, :, None, :]
    same = jnp.arange(2)[:, None, None] == jnp.arange(2)[None, :, None]
    place = (place & same).reshape(32, CAP, 2, 2 * tok)
    place = jnp.broadcast_to(place[:, None], (32, 2, CAP, 2, 2 * tok)).reshape(64, CAP, 2, 2 * tok)
    gains = weight.transpose(2, 0, 1).reshape(32, 2 * tok)
    gains = jnp.broadcast_to(gains[:, None], (32, 2, 2 * tok)).reshape(64, 1, 1, 2 * tok)
    factors = jnp.where(place, gains, F32(0.0))
    high = lax.reduce_precision(factors, 8, 7)
    factors = jnp.concatenate([high, factors - high], axis=3).astype(BF)
    place = place.astype(BF)
    parts = []
    for slots in SLOTS:
        parts.append((place[:, slots].reshape(-1, 2 * tok), factors[:, slots].reshape(-1, 4 * tok).T))
    return parts


def local(queries, latents, w_kv, w_out, resid, norm_gain, routes, codes, w_gate, w_up, w_down):
    tok, width = resid.shape
    chips = 64
    core = lax.axis_index("core")
    group = 4
    columns = width // group
    near = lax.all_to_all(
        jnp.broadcast_to(latents[None], (8,) + latents.shape), CTX_CHIPS, split_axis=0, concat_axis=0, tiled=True
    )
    far = swap(near)
    w_blocks, _ = lax.optimization_barrier((column_blocks(w_out, group), near[0, :8]))
    w_near = lax.all_to_all(w_blocks, "x", split_axis=0, concat_axis=0, tiled=True)
    ids = jnp.stack([lax.axis_index(CTX), core, lax.axis_index("x")]).astype(jnp.int32)
    own = attend(ids, queries, w_kv, near, far, 4)
    own, w_near = lax.optimization_barrier((own, w_near))
    w_mate = lax.ppermute(w_near, "z_lo", SWAP)
    before, after = up(own), down(own)
    half = own.shape[1] // 2
    left, right = up(before[:, :half]), down(after[:, half:])
    blocks = (w_near, w_mate, swap(w_near), swap(w_mate))
    attn = project(ids, (own, before, after, left, right), blocks, 8, columns)
    attn = lax.all_to_all(attn, EP + ("x",), split_axis=0, concat_axis=0, tiled=True)
    attn = jnp.sum(attn.reshape(8, group, tok, columns).astype(F32), axis=0)
    attn = attn.transpose(1, 0, 2).reshape(tok, width)
    attended = (resid.astype(F32) + attn).astype(BF)
    wide = attended.astype(F32)
    meansq = jnp.mean(wide * wide, axis=1, keepdims=True)
    normed = (wide * lax.rsqrt(meansq + 1e-06) * norm_gain[None, :]).astype(BF)
    normed2 = jnp.concatenate([normed, swap(normed)], axis=0)

    def exchange(rows):
        units = rows.reshape(chips, -1, 2, width)
        units = lax.all_to_all(units, CHIPS, split_axis=0, concat_axis=0, tiled=True)
        return units.reshape(rows.shape)

    parts = routing(routes, codes)
    arrived = [exchange(dispatch(place, normed2, 2)) for place, _ in parts]
    returned = [exchange(expert(rows, w_gate[0], w_up[0], w_down[0], 2, 7)) for rows in arrived]
    mine, theirs = combine([(factors, rows) for (_, factors), rows in zip(parts, returned)], 4)
    layer_out = (wide + mine + swap(theirs)).astype(BF)
    return (attended, layer_out)


def solution(mesh):
    fine = Mesh(mesh.devices.reshape(SIZES), NAMES)
    rows = P(CTX + EP, None)
    heads = P(CTX + EP, None, None)
    placed = (
        P(CTX, EP),
        P(None, CTX),
        P(None, EP),
        P(EP + CTX, None),
        rows,
        P(),
        rows,
        rows,
        heads,
        heads,
        heads,
    )
    return jax.shard_map(local, mesh=fine, in_specs=placed, out_specs=(rows, rows), check_vma=False)
```

```python
import functools

import jax
import jax.numpy as jnp
from jax import lax
from jax.experimental import pallas as pl
from jax.experimental.pallas import tpu as pltpu
from jax.sharding import Mesh, PartitionSpec as P

NOPE = 128
VD = 128
KV_RANK = 512
TOP = 8
QK = 192
CAP = 3
SLOTS = (slice(0, 3),)

CTX = ("z_lo", "x", "core")
CTX_CHIPS = ("x", "z_lo")
EP = ("z_hi", "y")
CHIPS = ("z_hi", "z_lo", "x", "y")
SIZES = (2, 4, 2, 2, 4)
NAMES = ("z_lo", "x", "core", "z_hi", "y")
SWAP = ((0, 1), (1, 0))
BF = jnp.bfloat16
F32 = jnp.float32
LOG2E = 1.4426950408889634


def chip_number(i):
    return i % 2 * 4 + i // 2


def in_hbm(a):
    return pltpu.with_memory_space_constraint(a, pltpu.HBM)


def attend_kernel(
    ids_ref, q_hbm, w_hbm, near_ref, far_ref, out_ref, q_ref, w_ref, lat_ref, s_ref, latq_ref, mixed_ref, sems, *, cuts
):
    heads = w_ref.shape[1] // (NOPE + VD)
    rows = q_ref.shape[0]
    m = heads * rows
    pairs = near_ref.shape[0]
    keys = 2 * rows * pairs
    q_copy = pltpu.make_async_copy(q_hbm, q_ref, sems.at[0])
    w_copy = pltpu.make_async_copy(w_hbm, w_ref, sems.at[1])
    q_copy.start()
    w_copy.start()
    for i in range(pairs):
        lat_ref[:, 2 * i * rows : (2 * i + 1) * rows] = near_ref[i]
        lat_ref[:, (2 * i + 1) * rows : (2 * i + 2) * rows] = far_ref[i]
    q_copy.wait()
    w_copy.wait()
    for h in range(heads):
        here = slice(h * rows, (h + 1) * rows)
        key_weights = w_ref[:, h * (NOPE + VD) : h * (NOPE + VD) + NOPE]
        plain = q_ref[:, h * QK : h * QK + NOPE]
        latq = lax.dot_general(plain, key_weights, (((1,), (1,)), ((), ())), preferred_element_type=F32)
        latq_ref[here, :KV_RANK] = latq.astype(BF)
        latq_ref[here, KV_RANK:] = q_ref[:, h * QK + NOPE : (h + 1) * QK]
    ctx, core = ids_ref[0], ids_ref[1]
    span = keys // cuts
    lane = lax.broadcasted_iota(jnp.int32, (m, rows), 1)
    query = lax.broadcasted_iota(jnp.int32, (m, rows), 0) % rows
    ahead = lane - query
    peak = jnp.full((m, rows), -1e30, F32)
    for j in range(cuts):
        s = jnp.dot(latq_ref[...], lat_ref[:, j * span : (j + 1) * span], preferred_element_type=F32)
        for b in range(span // rows):
            block = j * (span // rows) + b
            pos = 2 * chip_number(block // 2) + (core if block % 2 == 0 else 1 - core)
            part = s[:, b * rows : (b + 1) * rows]
            part = jnp.where(ahead <= (ctx - pos) * rows, part, F32(-1e30))
            peak = jnp.maximum(peak, part)
            s_ref[:, block * rows : (block + 1) * rows] = part
    top = jnp.max(peak, axis=1, keepdims=True)
    total = jnp.zeros((m, rows), F32)
    for j in range(cuts):
        probs = []
        for b in range(span // rows):
            first = j * span + b * rows
            p = jnp.exp2((s_ref[:, first : first + rows] - top) * (QK ** (-0.5) * LOG2E))
            total = total + p
            probs.append(p.astype(BF))
        part = lax.dot_general(
            jnp.concatenate(probs, axis=1),
            lat_ref[:KV_RANK, j * span : (j + 1) * span],
            (((1,), (1,)), ((), ())),
            preferred_element_type=F32,
        )
        mixed_ref[...] = part if j == 0 else mixed_ref[...] + part
    mixed = (mixed_ref[...] / jnp.sum(total, axis=1, keepdims=True)).astype(BF)
    for h in range(heads):
        values = w_ref[:, h * (NOPE + VD) + NOPE : (h + 1) * (NOPE + VD)]
        o = jnp.dot(mixed[h * rows : (h + 1) * rows], values, preferred_element_type=F32)
        out_ref[:, h * VD : (h + 1) * VD] = o.astype(BF)


def attend(ids, q, w_kv, near, far, cuts):
    pairs, depth, rows = near.shape
    heads = w_kv.shape[1] // (NOPE + VD)
    keys = 2 * rows * pairs
    m = heads * rows
    whole = pl.BlockSpec(memory_space=pltpu.VMEM)
    hbm = pl.BlockSpec(memory_space=pltpu.HBM)
    return pl.pallas_call(
        functools.partial(attend_kernel, cuts=cuts),
        in_specs=[pl.BlockSpec(memory_space=pltpu.SMEM), hbm, hbm, whole, whole],
        out_specs=whole,
        out_shape=jax.ShapeDtypeStruct((rows, heads * VD), BF),
        scratch_shapes=[
            pltpu.VMEM(q.shape, BF),
            pltpu.VMEM(w_kv.shape, BF),
            pltpu.VMEM((depth, keys), BF),
            pltpu.VMEM((m, keys), F32),
            pltpu.VMEM((m, depth), BF),
            pltpu.VMEM((m, KV_RANK), F32),
            pltpu.SemaphoreType.DMA((2,)),
        ],
        compiler_params=pltpu.CompilerParams(vmem_limit_bytes=28 * 2**20),
        cost_estimate=pl.CostEstimate(
            flops=2 * m * keys * (depth + KV_RANK), bytes_accessed=8_000_000, transcendentals=m * keys
        ),
    )(ids, in_hbm(q), in_hbm(w_kv), near, far)


def expert_kernel(x_hbm, g_ref, u_ref, d_hbm, out_hbm, d_ref, x_ref, hid_ref, gate_ref, up_ref, y_ref, sem_d, sem_in, sem_out):
    units, pair, width = x_ref.shape
    m = units * pair
    first, last = sem_in.shape[0], sem_out.shape[0]
    depth, wide = width // first, width // last
    arrivals = []
    for k in range(first):
        part = slice(k * depth, (k + 1) * depth)
        arrivals.append(pltpu.make_async_copy(x_hbm.at[:, :, part], x_ref.at[:, :, part], sem_in.at[k]))
        arrivals[-1].start()
    d_copy = pltpu.make_async_copy(d_hbm, d_ref, sem_d.at[0])
    d_copy.start()
    for k in range(first):
        part = slice(k * depth, (k + 1) * depth)
        arrivals[k].wait()
        rows = x_ref[:, :, part].reshape(m, depth)
        gate = jnp.dot(rows, g_ref[part], preferred_element_type=F32)
        upward = jnp.dot(rows, u_ref[part], preferred_element_type=F32)
        gate_ref[...] = gate if k == 0 else gate_ref[...] + gate
        up_ref[...] = upward if k == 0 else up_ref[...] + upward
    gate = gate_ref[...]
    hid_ref[...] = (gate / (1.0 + jnp.exp(-gate)) * up_ref[...]).astype(BF)
    d_copy.wait()
    departures = []
    for n in range(last):
        part = slice(n * wide, (n + 1) * wide)
        y = jnp.dot(hid_ref[...], d_ref[:, part], preferred_element_type=F32).astype(BF)
        y_ref[:, :, part] = y.reshape(units, pair, wide)
        departures.append(pltpu.make_async_copy(y_ref.at[:, :, part], out_hbm.at[:, :, part], sem_out.at[n]))
        departures[-1].start()
    for copy in departures:
        copy.wait()


def expert(x, w_gate, w_up, w_down, first, last):
    units, pair, width = x.shape
    m = units * pair
    hidden = w_gate.shape[1]
    whole = pl.BlockSpec(memory_space=pltpu.VMEM)
    far = pl.BlockSpec(memory_space=pltpu.HBM)
    return pl.pallas_call(
        expert_kernel,
        in_specs=[far, whole, whole, far],
        out_specs=far,
        out_shape=pltpu.HBM(x.shape, BF),
        scratch_shapes=[
            pltpu.VMEM(w_down.shape, BF),
            pltpu.VMEM(x.shape, BF),
            pltpu.VMEM((m, hidden), BF),
            pltpu.VMEM((m, hidden), F32),
            pltpu.VMEM((m, hidden), F32),
            pltpu.VMEM(x.shape, BF),
            pltpu.SemaphoreType.DMA((1,)),
            pltpu.SemaphoreType.DMA((first,)),
            pltpu.SemaphoreType.DMA((last,)),
        ],
        compiler_params=pltpu.CompilerParams(vmem_limit_bytes=24 * 2**20),
        cost_estimate=pl.CostEstimate(
            flops=6 * m * width * hidden, bytes_accessed=17_000_000, transcendentals=m * hidden
        ),
    )(x, w_gate, w_up, in_hbm(w_down))


def dispatch_kernel(place_ref, x_ref, out_ref):
    y = jnp.dot(place_ref[...], x_ref[...], preferred_element_type=F32).astype(BF)
    out_ref[...] = y.reshape(out_ref.shape)


def dispatch(place, x, cuts):
    m = place.shape[0]
    tokens, width = x.shape
    n = width // cuts
    return pl.pallas_call(
        dispatch_kernel,
        grid=(cuts,),
        in_specs=[pl.BlockSpec(place.shape, lambda i: (0, 0)), pl.BlockSpec((tokens, n), lambda i: (0, i))],
        out_specs=pl.BlockSpec((m // 2, 2, n), lambda i: (0, 0, i)),
        out_shape=jax.ShapeDtypeStruct((m // 2, 2, width), BF),
        compiler_params=pltpu.CompilerParams(vmem_limit_bytes=32 * 2**20),
        cost_estimate=pl.CostEstimate(
            flops=2 * m * tokens * width, bytes_accessed=2 * m * width + 2 * tokens * width, transcendentals=0
        ),
    )(place, x)


def combine_kernel(*refs):
    *in_refs, own_ref, far_ref = refs
    tok = own_ref.shape[0]
    y = None
    for factors_ref, x_ref in zip(in_refs[::2], in_refs[1::2]):
        rows = x_ref[...].reshape(factors_ref.shape[1], x_ref.shape[2])
        part = jnp.dot(factors_ref[...], rows, preferred_element_type=F32)
        y = part if y is None else y + part
    y = y[: 2 * tok] + y[2 * tok :]
    own_ref[...] = y[:tok]
    far_ref[...] = y[tok:]


def combine(parts, cuts):
    width = parts[0][1].shape[2]
    n = width // cuts
    tok = parts[0][0].shape[0] // 4
    half = pl.BlockSpec((tok, n), lambda i: (0, i))
    in_specs = []
    for factors, x in parts:
        in_specs.append(pl.BlockSpec(factors.shape, lambda i: (0, 0)))
        in_specs.append(pl.BlockSpec((x.shape[0], 2, n), lambda i: (0, 0, i)))
    rows = sum(2 * x.shape[0] for _, x in parts)
    return pl.pallas_call(
        combine_kernel,
        grid=(cuts,),
        in_specs=in_specs,
        out_specs=(half, half),
        out_shape=(jax.ShapeDtypeStruct((tok, width), F32),) * 2,
        compiler_params=pltpu.CompilerParams(vmem_limit_bytes=32 * 2**20),
        cost_estimate=pl.CostEstimate(
            flops=8 * tok * rows * width, bytes_accessed=2 * rows * width, transcendentals=0
        ),
    )(*[a for part in parts for a in part])


def project_kernel(ids_ref, own_ref, before_ref, after_ref, left_ref, right_ref, *refs):
    *block_refs, out_ref, x_ref, w_ref = refs
    rows = own_ref.shape[0]
    group, tok = 4, out_ref.shape[1]
    parts = out_ref.shape[0] // group
    core, x = ids_ref[1], ids_ref[2]
    half = left_ref.shape[1]
    x_ref[:rows] = own_ref[...]
    x_ref[rows : 2 * rows] = after_ref[...]
    x_ref[2 * rows : 3 * rows, :half] = left_ref[...]
    x_ref[2 * rows : 3 * rows, half:] = right_ref[...]
    x_ref[3 * rows :] = before_ref[...]
    deep = VD // 2
    z = lax.div(ids_ref[0], 2 * group)
    for i, ref in enumerate(block_refs):
        offset = (core if i < 2 else 1 - core) * deep
        plane = (z if i % 2 == 0 else 1 - z) * group
        for j in range(group):
            w_ref[pl.ds(pl.multiple_of((plane + j) * VD + offset, deep), deep)] = ref[j]
    for d in range(group):
        y = jnp.dot(x_ref[d * rows : (d + 1) * rows], w_ref[...], preferred_element_type=F32).astype(BF)
        target = lax.rem(x + d, group)
        for e in range(parts):
            out_ref[e * group + target] = y[e * tok : (e + 1) * tok]


def project(ids, pieces, blocks, parts, width):
    rows, depth = pieces[0].shape
    whole = pl.BlockSpec(memory_space=pltpu.VMEM)
    group = 4
    return pl.pallas_call(
        project_kernel,
        in_specs=[pl.BlockSpec(memory_space=pltpu.SMEM)] + [whole] * (len(pieces) + len(blocks)),
        out_specs=whole,
        out_shape=jax.ShapeDtypeStruct((parts * group, rows // parts, width), BF),
        scratch_shapes=[pltpu.VMEM((group * rows, depth), BF), pltpu.VMEM((depth, width), BF)],
        compiler_params=pltpu.CompilerParams(vmem_limit_bytes=32 * 2**20),
        cost_estimate=pl.CostEstimate(
            flops=2 * group * rows * depth * width, bytes_accessed=2 * depth * width, transcendentals=0
        ),
    )(ids, *pieces, *blocks)


def blocks_kernel(w_ref, out_ref, sems):
    wide = out_ref.shape[2]
    copies = []
    for i in range(out_ref.shape[0]):
        first = i * wide
        copies.append(pltpu.make_async_copy(w_ref.at[:, first : first + wide], out_ref.at[i], sems.at[i]))
        copies[-1].start()
    for copy in copies:
        copy.wait()


def column_blocks(w, count):
    shape = (count, w.shape[0], w.shape[1] // count)
    return pl.pallas_call(
        blocks_kernel,
        in_specs=[pl.BlockSpec(memory_space=pltpu.VMEM)],
        out_specs=pl.BlockSpec(memory_space=pltpu.HBM),
        out_shape=pltpu.HBM(shape, w.dtype),
        scratch_shapes=[pltpu.SemaphoreType.DMA((count,))],
        cost_estimate=pl.CostEstimate(flops=0, bytes_accessed=6 * w.size, transcendentals=0),
    )(w)


def swap(mine):
    return lax.ppermute(mine, "core", SWAP)


def up(a):
    return lax.ppermute(a, "x", [(i, (i + 1) % 4) for i in range(4)])


def down(a):
    return lax.ppermute(a, "x", [(i, (i + 3) % 4) for i in range(4)])


def routing(routes, codes):
    tok = routes.shape[0]
    core = lax.axis_index("core")
    code_float = codes.astype(F32)
    mix = code_float / jnp.sum(code_float, axis=1, keepdims=True)
    routes2, mix2 = jnp.stack([routes, swap(routes)]), jnp.stack([mix, swap(mix)])
    chosen = routes2[:, :, :, None] == jnp.arange(64, dtype=jnp.int32)
    weight = jnp.sum(jnp.where(chosen, mix2[..., None], F32(0.0)), axis=2)
    has = jnp.any(chosen, axis=2)

    def of_core(a):
        a = a.reshape(2, tok, 8, 2, 4)
        a = jnp.where(core == 0, a[:, :, :, 0], a[:, :, :, 1])
        return a.reshape(2, tok, 8, 2, 2).transpose(0, 1, 3, 2, 4).reshape(2, tok, 32)

    weight, has = of_core(weight), of_core(has)
    count = has.astype(jnp.int32)
    slot = jnp.cumsum(count, axis=1) - count
    place = has[:, :, :, None] & (slot[:, :, :, None] == jnp.arange(CAP, dtype=jnp.int32))
    place = place.transpose(2, 3, 0, 1)[:, :, :, None, :]
    same = jnp.arange(2)[:, None, None] == jnp.arange(2)[None, :, None]
    place = (place & same).reshape(32, CAP, 2, 2 * tok)
    place = jnp.broadcast_to(place[:, None], (32, 2, CAP, 2, 2 * tok)).reshape(64, CAP, 2, 2 * tok)
    gains = weight.transpose(2, 0, 1).reshape(32, 2 * tok)
    gains = jnp.broadcast_to(gains[:, None], (32, 2, 2 * tok)).reshape(64, 1, 1, 2 * tok)
    factors = jnp.where(place, gains, F32(0.0))
    high = lax.reduce_precision(factors, 8, 7)
    factors = jnp.concatenate([high, factors - high], axis=3).astype(BF)
    place = place.astype(BF)
    parts = []
    for slots in SLOTS:
        parts.append((place[:, slots].reshape(-1, 2 * tok), factors[:, slots].reshape(-1, 4 * tok).T))
    return parts


def local(queries, latents, w_kv, w_out, resid, norm_gain, routes, codes, w_gate, w_up, w_down):
    tok, width = resid.shape
    chips = 64
    core = lax.axis_index("core")
    group = 4
    columns = width // group
    near = lax.all_to_all(
        jnp.broadcast_to(latents[None], (8,) + latents.shape), CTX_CHIPS, split_axis=0, concat_axis=0, tiled=True
    )
    far = swap(near)
    w_blocks, _ = lax.optimization_barrier((column_blocks(w_out, group), near[0, :8]))
    w_near = lax.all_to_all(w_blocks, "x", split_axis=0, concat_axis=0, tiled=True)
    ids = jnp.stack([lax.axis_index(CTX), core, lax.axis_index("x")]).astype(jnp.int32)
    own = attend(ids, queries, w_kv, near, far, 4)
    own, w_near = lax.optimization_barrier((own, w_near))
    before, after, w_mate = lax.optimization_barrier((up(own), down(own), lax.ppermute(w_near, "z_lo", SWAP)))
    half = own.shape[1] // 2
    left, right = up(before[:, :half]), down(after[:, half:])
    blocks = (w_near, w_mate, swap(w_near), swap(w_mate))
    attn = project(ids, (own, before, after, left, right), blocks, 8, columns)
    attn = lax.all_to_all(attn, EP + ("x",), split_axis=0, concat_axis=0, tiled=True)
    attn = jnp.sum(attn.reshape(8, group, tok, columns).astype(F32), axis=0)
    attn = attn.transpose(1, 0, 2).reshape(tok, width)
    attended = (resid.astype(F32) + attn).astype(BF)
    wide = attended.astype(F32)
    meansq = jnp.mean(wide * wide, axis=1, keepdims=True)
    normed = (wide * lax.rsqrt(meansq + 1e-06) * norm_gain[None, :]).astype(BF)
    normed2 = jnp.concatenate([normed, swap(normed)], axis=0)

    def exchange(rows):
        units = rows.reshape(chips, -1, 2, width)
        units = lax.all_to_all(units, CHIPS, split_axis=0, concat_axis=0, tiled=True)
        return units.reshape(rows.shape)

    parts = routing(routes, codes)
    arrived = [exchange(dispatch(place, normed2, 2)) for place, _ in parts]
    returned = [exchange(expert(rows, w_gate[0], w_up[0], w_down[0], 2, 7)) for rows in arrived]
    mine, theirs = combine([(factors, rows) for (_, factors), rows in zip(parts, returned)], 4)
    layer_out = (wide + mine + swap(theirs)).astype(BF)
    return (attended, layer_out)


def solution(mesh):
    fine = Mesh(mesh.devices.reshape(SIZES), NAMES)
    rows = P(CTX + EP, None)
    heads = P(CTX + EP, None, None)
    placed = (
        P(CTX, EP),
        P(None, CTX),
        P(None, EP),
        P(EP + CTX, None),
        rows,
        P(),
        rows,
        rows,
        heads,
        heads,
        heads,
    )
    return jax.shard_map(local, mesh=fine, in_specs=placed, out_specs=(rows, rows), check_vma=False)
```

```python
import functools

import jax
import jax.numpy as jnp
from jax import lax
from jax.experimental import pallas as pl
from jax.experimental.pallas import tpu as pltpu
from jax.sharding import Mesh, PartitionSpec as P

NOPE = 128
VD = 128
KV_RANK = 512
TOP = 8
QK = 192
CAP = 3
SLOTS = (slice(0, 3),)

CTX = ("z_lo", "x", "core")
CTX_CHIPS = ("x", "z_lo")
EP = ("z_hi", "y")
CHIPS = ("z_hi", "z_lo", "x", "y")
SIZES = (2, 4, 2, 2, 4)
NAMES = ("z_lo", "x", "core", "z_hi", "y")
SWAP = ((0, 1), (1, 0))
BF = jnp.bfloat16
F32 = jnp.float32
LOG2E = 1.4426950408889634


def chip_number(i):
    return i % 2 * 4 + i // 2


def in_hbm(a):
    return pltpu.with_memory_space_constraint(a, pltpu.HBM)


def attend_kernel(
    ids_ref, q_hbm, w_hbm, near_ref, far_ref, out_ref, q_ref, w_ref, lat_ref, s_ref, latq_ref, mixed_ref, sems, *, cuts
):
    heads = w_ref.shape[1] // (NOPE + VD)
    rows = q_ref.shape[0]
    m = heads * rows
    pairs = near_ref.shape[0]
    keys = 2 * rows * pairs
    q_copy = pltpu.make_async_copy(q_hbm, q_ref, sems.at[0])
    w_copy = pltpu.make_async_copy(w_hbm, w_ref, sems.at[1])
    q_copy.start()
    w_copy.start()
    for i in range(pairs):
        lat_ref[:, 2 * i * rows : (2 * i + 1) * rows] = near_ref[i]
        lat_ref[:, (2 * i + 1) * rows : (2 * i + 2) * rows] = far_ref[i]
    q_copy.wait()
    w_copy.wait()
    for h in range(heads):
        here = slice(h * rows, (h + 1) * rows)
        key_weights = w_ref[:, h * (NOPE + VD) : h * (NOPE + VD) + NOPE]
        plain = q_ref[:, h * QK : h * QK + NOPE]
        latq = lax.dot_general(plain, key_weights, (((1,), (1,)), ((), ())), preferred_element_type=F32)
        latq_ref[here, :KV_RANK] = latq.astype(BF)
        latq_ref[here, KV_RANK:] = q_ref[:, h * QK + NOPE : (h + 1) * QK]
    ctx, core = ids_ref[0], ids_ref[1]
    span = keys // cuts
    lane = lax.broadcasted_iota(jnp.int32, (m, rows), 1)
    query = lax.broadcasted_iota(jnp.int32, (m, rows), 0) % rows
    ahead = lane - query
    peak = jnp.full((m, rows), -1e30, F32)
    for j in range(cuts):
        s = jnp.dot(latq_ref[...], lat_ref[:, j * span : (j + 1) * span], preferred_element_type=F32)
        for b in range(span // rows):
            block = j * (span // rows) + b
            pos = 2 * chip_number(block // 2) + (core if block % 2 == 0 else 1 - core)
            part = s[:, b * rows : (b + 1) * rows]
            part = jnp.where(ahead <= (ctx - pos) * rows, part, F32(-1e30))
            peak = jnp.maximum(peak, part)
            s_ref[:, block * rows : (block + 1) * rows] = part
    top = jnp.max(peak, axis=1, keepdims=True)
    total = jnp.zeros((m, rows), F32)
    for j in range(cuts):
        probs = []
        for b in range(span // rows):
            first = j * span + b * rows
            p = jnp.exp2((s_ref[:, first : first + rows] - top) * (QK ** (-0.5) * LOG2E))
            total = total + p
            probs.append(p.astype(BF))
        part = lax.dot_general(
            jnp.concatenate(probs, axis=1),
            lat_ref[:KV_RANK, j * span : (j + 1) * span],
            (((1,), (1,)), ((), ())),
            preferred_element_type=F32,
        )
        mixed_ref[...] = part if j == 0 else mixed_ref[...] + part
    mixed = (mixed_ref[...] / jnp.sum(total, axis=1, keepdims=True)).astype(BF)
    for h in range(heads):
        values = w_ref[:, h * (NOPE + VD) + NOPE : (h + 1) * (NOPE + VD)]
        o = jnp.dot(mixed[h * rows : (h + 1) * rows], values, preferred_element_type=F32)
        out_ref[:, h * VD : (h + 1) * VD] = o.astype(BF)


def attend(ids, q, w_kv, near, far, cuts):
    pairs, depth, rows = near.shape
    heads = w_kv.shape[1] // (NOPE + VD)
    keys = 2 * rows * pairs
    m = heads * rows
    whole = pl.BlockSpec(memory_space=pltpu.VMEM)
    hbm = pl.BlockSpec(memory_space=pltpu.HBM)
    return pl.pallas_call(
        functools.partial(attend_kernel, cuts=cuts),
        in_specs=[pl.BlockSpec(memory_space=pltpu.SMEM), hbm, hbm, whole, whole],
        out_specs=whole,
        out_shape=jax.ShapeDtypeStruct((rows, heads * VD), BF),
        scratch_shapes=[
            pltpu.VMEM(q.shape, BF),
            pltpu.VMEM(w_kv.shape, BF),
            pltpu.VMEM((depth, keys), BF),
            pltpu.VMEM((m, keys), F32),
            pltpu.VMEM((m, depth), BF),
            pltpu.VMEM((m, KV_RANK), F32),
            pltpu.SemaphoreType.DMA((2,)),
        ],
        compiler_params=pltpu.CompilerParams(vmem_limit_bytes=28 * 2**20),
        cost_estimate=pl.CostEstimate(
            flops=2 * m * keys * (depth + KV_RANK), bytes_accessed=8_000_000, transcendentals=m * keys
        ),
    )(ids, in_hbm(q), in_hbm(w_kv), near, far)


def expert_kernel(x_hbm, g_ref, u_ref, d_hbm, out_hbm, d_ref, x_ref, hid_ref, gate_ref, up_ref, y_ref, sem_d, sem_in, sem_out):
    units, pair, width = x_ref.shape
    m = units * pair
    first, last = sem_in.shape[0], sem_out.shape[0]
    depth, wide = width // first, width // last
    arrivals = []
    for k in range(first):
        part = slice(k * depth, (k + 1) * depth)
        arrivals.append(pltpu.make_async_copy(x_hbm.at[:, :, part], x_ref.at[:, :, part], sem_in.at[k]))
        arrivals[-1].start()
    d_copy = pltpu.make_async_copy(d_hbm, d_ref, sem_d.at[0])
    d_copy.start()
    for k in range(first):
        part = slice(k * depth, (k + 1) * depth)
        arrivals[k].wait()
        rows = x_ref[:, :, part].reshape(m, depth)
        gate = jnp.dot(rows, g_ref[part], preferred_element_type=F32)
        upward = jnp.dot(rows, u_ref[part], preferred_element_type=F32)
        gate_ref[...] = gate if k == 0 else gate_ref[...] + gate
        up_ref[...] = upward if k == 0 else up_ref[...] + upward
    gate = gate_ref[...]
    hid_ref[...] = (gate / (1.0 + jnp.exp(-gate)) * up_ref[...]).astype(BF)
    d_copy.wait()
    departures = []
    for n in range(last):
        part = slice(n * wide, (n + 1) * wide)
        y = jnp.dot(hid_ref[...], d_ref[:, part], preferred_element_type=F32).astype(BF)
        y_ref[:, :, part] = y.reshape(units, pair, wide)
        departures.append(pltpu.make_async_copy(y_ref.at[:, :, part], out_hbm.at[:, :, part], sem_out.at[n]))
        departures[-1].start()
    for copy in departures:
        copy.wait()


def expert(x, w_gate, w_up, w_down, first, last):
    units, pair, width = x.shape
    m = units * pair
    hidden = w_gate.shape[1]
    whole = pl.BlockSpec(memory_space=pltpu.VMEM)
    far = pl.BlockSpec(memory_space=pltpu.HBM)
    return pl.pallas_call(
        expert_kernel,
        in_specs=[far, whole, whole, far],
        out_specs=far,
        out_shape=pltpu.HBM(x.shape, BF),
        scratch_shapes=[
            pltpu.VMEM(w_down.shape, BF),
            pltpu.VMEM(x.shape, BF),
            pltpu.VMEM((m, hidden), BF),
            pltpu.VMEM((m, hidden), F32),
            pltpu.VMEM((m, hidden), F32),
            pltpu.VMEM(x.shape, BF),
            pltpu.SemaphoreType.DMA((1,)),
            pltpu.SemaphoreType.DMA((first,)),
            pltpu.SemaphoreType.DMA((last,)),
        ],
        compiler_params=pltpu.CompilerParams(vmem_limit_bytes=24 * 2**20),
        cost_estimate=pl.CostEstimate(
            flops=6 * m * width * hidden, bytes_accessed=17_000_000, transcendentals=m * hidden
        ),
    )(x, w_gate, w_up, in_hbm(w_down))


def dispatch_kernel(place_ref, x_ref, out_ref):
    y = jnp.dot(place_ref[...], x_ref[...], preferred_element_type=F32).astype(BF)
    out_ref[...] = y.reshape(out_ref.shape)


def dispatch(place, x, cuts):
    m = place.shape[0]
    tokens, width = x.shape
    n = width // cuts
    return pl.pallas_call(
        dispatch_kernel,
        grid=(cuts,),
        in_specs=[pl.BlockSpec(place.shape, lambda i: (0, 0)), pl.BlockSpec((tokens, n), lambda i: (0, i))],
        out_specs=pl.BlockSpec((m // 2, 2, n), lambda i: (0, 0, i)),
        out_shape=jax.ShapeDtypeStruct((m // 2, 2, width), BF),
        compiler_params=pltpu.CompilerParams(vmem_limit_bytes=32 * 2**20),
        cost_estimate=pl.CostEstimate(
            flops=2 * m * tokens * width, bytes_accessed=2 * m * width + 2 * tokens * width, transcendentals=0
        ),
    )(place, x)


def combine_kernel(*refs):
    *in_refs, own_ref, far_ref = refs
    tok = own_ref.shape[0]
    y = None
    for factors_ref, x_ref in zip(in_refs[::2], in_refs[1::2]):
        rows = x_ref[...].reshape(factors_ref.shape[1], x_ref.shape[2])
        part = jnp.dot(factors_ref[...], rows, preferred_element_type=F32)
        y = part if y is None else y + part
    y = y[: 2 * tok] + y[2 * tok :]
    own_ref[...] = y[:tok]
    far_ref[...] = y[tok:]


def combine(parts, cuts):
    width = parts[0][1].shape[2]
    n = width // cuts
    tok = parts[0][0].shape[0] // 4
    half = pl.BlockSpec((tok, n), lambda i: (0, i))
    in_specs = []
    for factors, x in parts:
        in_specs.append(pl.BlockSpec(factors.shape, lambda i: (0, 0)))
        in_specs.append(pl.BlockSpec((x.shape[0], 2, n), lambda i: (0, 0, i)))
    rows = sum(2 * x.shape[0] for _, x in parts)
    return pl.pallas_call(
        combine_kernel,
        grid=(cuts,),
        in_specs=in_specs,
        out_specs=(half, half),
        out_shape=(jax.ShapeDtypeStruct((tok, width), F32),) * 2,
        compiler_params=pltpu.CompilerParams(vmem_limit_bytes=32 * 2**20),
        cost_estimate=pl.CostEstimate(
            flops=8 * tok * rows * width, bytes_accessed=2 * rows * width, transcendentals=0
        ),
    )(*[a for part in parts for a in part])


def project_kernel(ids_ref, own_ref, before_ref, after_ref, opposite_ref, *refs):
    *block_refs, out_ref, x_ref, w_ref = refs
    rows = own_ref.shape[0]
    group, tok = 4, out_ref.shape[1]
    parts = out_ref.shape[0] // group
    core, x = ids_ref[1], ids_ref[2]
    x_ref[:rows] = own_ref[...]
    x_ref[rows : 2 * rows] = after_ref[...]
    x_ref[2 * rows : 3 * rows] = opposite_ref[...]
    x_ref[3 * rows :] = before_ref[...]
    deep = VD // 2
    z = lax.div(ids_ref[0], 2 * group)
    for i, ref in enumerate(block_refs):
        offset = (core if i < 2 else 1 - core) * deep
        plane = (z if i % 2 == 0 else 1 - z) * group
        for j in range(group):
            w_ref[pl.ds(pl.multiple_of((plane + j) * VD + offset, deep), deep)] = ref[j]
    for d in range(group):
        y = jnp.dot(x_ref[d * rows : (d + 1) * rows], w_ref[...], preferred_element_type=F32).astype(BF)
        target = lax.rem(x + d, group)
        for e in range(parts):
            out_ref[e * group + target] = y[e * tok : (e + 1) * tok]


def project(ids, pieces, blocks, parts, width):
    rows, depth = pieces[0].shape
    whole = pl.BlockSpec(memory_space=pltpu.VMEM)
    group = 4
    return pl.pallas_call(
        project_kernel,
        in_specs=[pl.BlockSpec(memory_space=pltpu.SMEM)] + [whole] * (len(pieces) + len(blocks)),
        out_specs=whole,
        out_shape=jax.ShapeDtypeStruct((parts * group, rows // parts, width), BF),
        scratch_shapes=[pltpu.VMEM((group * rows, depth), BF), pltpu.VMEM((depth, width), BF)],
        compiler_params=pltpu.CompilerParams(vmem_limit_bytes=32 * 2**20),
        cost_estimate=pl.CostEstimate(
            flops=2 * group * rows * depth * width, bytes_accessed=2 * depth * width, transcendentals=0
        ),
    )(ids, *pieces, *blocks)


def blocks_kernel(w_ref, out_ref, sems):
    wide = out_ref.shape[2]
    copies = []
    for i in range(out_ref.shape[0]):
        first = i * wide
        copies.append(pltpu.make_async_copy(w_ref.at[:, first : first + wide], out_ref.at[i], sems.at[i]))
        copies[-1].start()
    for copy in copies:
        copy.wait()


def column_blocks(w, count):
    shape = (count, w.shape[0], w.shape[1] // count)
    return pl.pallas_call(
        blocks_kernel,
        in_specs=[pl.BlockSpec(memory_space=pltpu.VMEM)],
        out_specs=pl.BlockSpec(memory_space=pltpu.HBM),
        out_shape=pltpu.HBM(shape, w.dtype),
        scratch_shapes=[pltpu.SemaphoreType.DMA((count,))],
        cost_estimate=pl.CostEstimate(flops=0, bytes_accessed=6 * w.size, transcendentals=0),
    )(w)


def swap(mine):
    return lax.ppermute(mine, "core", SWAP)


def up(a):
    return lax.ppermute(a, "x", [(i, (i + 1) % 4) for i in range(4)])


def down(a):
    return lax.ppermute(a, "x", [(i, (i + 3) % 4) for i in range(4)])


def routing(routes, codes):
    tok = routes.shape[0]
    core = lax.axis_index("core")
    code_float = codes.astype(F32)
    mix = code_float / jnp.sum(code_float, axis=1, keepdims=True)
    routes2, mix2 = jnp.stack([routes, swap(routes)]), jnp.stack([mix, swap(mix)])
    chosen = routes2[:, :, :, None] == jnp.arange(64, dtype=jnp.int32)
    weight = jnp.sum(jnp.where(chosen, mix2[..., None], F32(0.0)), axis=2)
    has = jnp.any(chosen, axis=2)

    def of_core(a):
        a = a.reshape(2, tok, 8, 2, 4)
        a = jnp.where(core == 0, a[:, :, :, 0], a[:, :, :, 1])
        return a.reshape(2, tok, 8, 2, 2).transpose(0, 1, 3, 2, 4).reshape(2, tok, 32)

    weight, has = of_core(weight), of_core(has)
    count = has.astype(jnp.int32)
    slot = jnp.cumsum(count, axis=1) - count
    place = has[:, :, :, None] & (slot[:, :, :, None] == jnp.arange(CAP, dtype=jnp.int32))
    place = place.transpose(2, 3, 0, 1)[:, :, :, None, :]
    same = jnp.arange(2)[:, None, None] == jnp.arange(2)[None, :, None]
    place = (place & same).reshape(32, CAP, 2, 2 * tok)
    place = jnp.broadcast_to(place[:, None], (32, 2, CAP, 2, 2 * tok)).reshape(64, CAP, 2, 2 * tok)
    gains = weight.transpose(2, 0, 1).reshape(32, 2 * tok)
    gains = jnp.broadcast_to(gains[:, None], (32, 2, 2 * tok)).reshape(64, 1, 1, 2 * tok)
    factors = jnp.where(place, gains, F32(0.0))
    high = lax.reduce_precision(factors, 8, 7)
    factors = jnp.concatenate([high, factors - high], axis=3).astype(BF)
    place = place.astype(BF)
    parts = []
    for slots in SLOTS:
        parts.append((place[:, slots].reshape(-1, 2 * tok), factors[:, slots].reshape(-1, 4 * tok).T))
    return parts


def local(queries, latents, w_kv, w_out, resid, norm_gain, routes, codes, w_gate, w_up, w_down):
    tok, width = resid.shape
    chips = 64
    core = lax.axis_index("core")
    group = 4
    columns = width // group
    near = lax.all_to_all(
        jnp.broadcast_to(latents[None], (8,) + latents.shape), CTX_CHIPS, split_axis=0, concat_axis=0, tiled=True
    )
    far = swap(near)
    w_blocks, _ = lax.optimization_barrier((column_blocks(w_out, group), near[0, :8]))
    w_near = lax.all_to_all(w_blocks, "x", split_axis=0, concat_axis=0, tiled=True)
    ids = jnp.stack([lax.axis_index(CTX), core, lax.axis_index("x")]).astype(jnp.int32)
    own = attend(ids, queries, w_kv, near, far, 4)
    own, w_near = lax.optimization_barrier((own, w_near))
    opposite = lax.ppermute(own, "x", [(i, (i + 2) % 4) for i in range(4)])
    mate = lax.ppermute(w_near, "z_lo", SWAP)
    before, after, opposite, w_mate = lax.optimization_barrier((up(own), down(own), opposite, mate))
    blocks = (w_near, w_mate, swap(w_near), swap(w_mate))
    attn = project(ids, (own, before, after, opposite), blocks, 8, columns)
    attn = lax.all_to_all(attn, EP + ("x",), split_axis=0, concat_axis=0, tiled=True)
    attn = jnp.sum(attn.reshape(8, group, tok, columns).astype(F32), axis=0)
    attn = attn.transpose(1, 0, 2).reshape(tok, width)
    attended = (resid.astype(F32) + attn).astype(BF)
    wide = attended.astype(F32)
    meansq = jnp.mean(wide * wide, axis=1, keepdims=True)
    normed = (wide * lax.rsqrt(meansq + 1e-06) * norm_gain[None, :]).astype(BF)
    normed2 = jnp.concatenate([normed, swap(normed)], axis=0)

    def exchange(rows):
        units = rows.reshape(chips, -1, 2, width)
        units = lax.all_to_all(units, CHIPS, split_axis=0, concat_axis=0, tiled=True)
        return units.reshape(rows.shape)

    parts = routing(routes, codes)
    arrived = [exchange(dispatch(place, normed2, 2)) for place, _ in parts]
    returned = [exchange(expert(rows, w_gate[0], w_up[0], w_down[0], 2, 7)) for rows in arrived]
    mine, theirs = combine([(factors, rows) for (_, factors), rows in zip(parts, returned)], 4)
    layer_out = (wide + mine + swap(theirs)).astype(BF)
    return (attended, layer_out)


def solution(mesh):
    fine = Mesh(mesh.devices.reshape(SIZES), NAMES)
    rows = P(CTX + EP, None)
    heads = P(CTX + EP, None, None)
    placed = (
        P(CTX, EP),
        P(None, CTX),
        P(None, EP),
        P(EP + CTX, None),
        rows,
        P(),
        rows,
        rows,
        heads,
        heads,
        heads,
    )
    return jax.shard_map(local, mesh=fine, in_specs=placed, out_specs=(rows, rows), check_vma=False)
```

```python
import functools

import jax
import jax.numpy as jnp
from jax import lax
from jax.experimental import pallas as pl
from jax.experimental.pallas import tpu as pltpu
from jax.sharding import Mesh, PartitionSpec as P

NOPE = 128
VD = 128
KV_RANK = 512
TOP = 8
QK = 192
CAP = 3
SLOTS = (slice(0, 3),)

CTX = ("z_lo", "x", "core")
CTX_CHIPS = ("x", "z_lo")
EP = ("z_hi", "y")
CHIPS = ("z_hi", "z_lo", "x", "y")
SIZES = (2, 4, 2, 2, 4)
NAMES = ("z_lo", "x", "core", "z_hi", "y")
SWAP = ((0, 1), (1, 0))
BF = jnp.bfloat16
F32 = jnp.float32
LOG2E = 1.4426950408889634


def chip_number(i):
    return i % 2 * 4 + i // 2


def in_hbm(a):
    return pltpu.with_memory_space_constraint(a, pltpu.HBM)


def attend_kernel(
    ids_ref, q_hbm, w_hbm, near_ref, far_ref, out_ref, q_ref, w_ref, lat_ref, s_ref, latq_ref, mixed_ref, sems, *, cuts
):
    heads = w_ref.shape[1] // (NOPE + VD)
    rows = q_ref.shape[0]
    m = heads * rows
    pairs = near_ref.shape[0]
    keys = 2 * rows * pairs
    q_copy = pltpu.make_async_copy(q_hbm, q_ref, sems.at[0])
    w_copy = pltpu.make_async_copy(w_hbm, w_ref, sems.at[1])
    q_copy.start()
    w_copy.start()
    for i in range(pairs):
        lat_ref[:, 2 * i * rows : (2 * i + 1) * rows] = near_ref[i]
        lat_ref[:, (2 * i + 1) * rows : (2 * i + 2) * rows] = far_ref[i]
    q_copy.wait()
    w_copy.wait()
    for h in range(heads):
        here = slice(h * rows, (h + 1) * rows)
        key_weights = w_ref[:, h * (NOPE + VD) : h * (NOPE + VD) + NOPE]
        plain = q_ref[:, h * QK : h * QK + NOPE]
        latq = lax.dot_general(plain, key_weights, (((1,), (1,)), ((), ())), preferred_element_type=F32)
        latq_ref[here, :KV_RANK] = latq.astype(BF)
        latq_ref[here, KV_RANK:] = q_ref[:, h * QK + NOPE : (h + 1) * QK]
    ctx, core = ids_ref[0], ids_ref[1]
    span = keys // cuts
    lane = lax.broadcasted_iota(jnp.int32, (m, rows), 1)
    query = lax.broadcasted_iota(jnp.int32, (m, rows), 0) % rows
    ahead = lane - query
    peak = jnp.full((m, rows), -1e30, F32)
    for j in range(cuts):
        s = jnp.dot(latq_ref[...], lat_ref[:, j * span : (j + 1) * span], preferred_element_type=F32)
        for b in range(span // rows):
            block = j * (span // rows) + b
            pos = 2 * chip_number(block // 2) + (core if block % 2 == 0 else 1 - core)
            part = s[:, b * rows : (b + 1) * rows]
            part = jnp.where(ahead <= (ctx - pos) * rows, part, F32(-1e30))
            peak = jnp.maximum(peak, part)
            s_ref[:, block * rows : (block + 1) * rows] = part
    top = jnp.max(peak, axis=1, keepdims=True)
    total = jnp.zeros((m, rows), F32)
    for j in range(cuts):
        probs = []
        for b in range(span // rows):
            first = j * span + b * rows
            p = jnp.exp2((s_ref[:, first : first + rows] - top) * (QK ** (-0.5) * LOG2E))
            total = total + p
            probs.append(p.astype(BF))
        part = lax.dot_general(
            jnp.concatenate(probs, axis=1),
            lat_ref[:KV_RANK, j * span : (j + 1) * span],
            (((1,), (1,)), ((), ())),
            preferred_element_type=F32,
        )
        mixed_ref[...] = part if j == 0 else mixed_ref[...] + part
    mixed = (mixed_ref[...] / jnp.sum(total, axis=1, keepdims=True)).astype(BF)
    for h in range(heads):
        values = w_ref[:, h * (NOPE + VD) + NOPE : (h + 1) * (NOPE + VD)]
        o = jnp.dot(mixed[h * rows : (h + 1) * rows], values, preferred_element_type=F32)
        out_ref[:, h * VD : (h + 1) * VD] = o.astype(BF)


def attend(ids, q, w_kv, near, far, cuts):
    pairs, depth, rows = near.shape
    heads = w_kv.shape[1] // (NOPE + VD)
    keys = 2 * rows * pairs
    m = heads * rows
    whole = pl.BlockSpec(memory_space=pltpu.VMEM)
    hbm = pl.BlockSpec(memory_space=pltpu.HBM)
    return pl.pallas_call(
        functools.partial(attend_kernel, cuts=cuts),
        in_specs=[pl.BlockSpec(memory_space=pltpu.SMEM), hbm, hbm, whole, whole],
        out_specs=whole,
        out_shape=jax.ShapeDtypeStruct((rows, heads * VD), BF),
        scratch_shapes=[
            pltpu.VMEM(q.shape, BF),
            pltpu.VMEM(w_kv.shape, BF),
            pltpu.VMEM((depth, keys), BF),
            pltpu.VMEM((m, keys), F32),
            pltpu.VMEM((m, depth), BF),
            pltpu.VMEM((m, KV_RANK), F32),
            pltpu.SemaphoreType.DMA((2,)),
        ],
        compiler_params=pltpu.CompilerParams(vmem_limit_bytes=28 * 2**20),
        cost_estimate=pl.CostEstimate(
            flops=2 * m * keys * (depth + KV_RANK), bytes_accessed=8_000_000, transcendentals=m * keys
        ),
    )(ids, in_hbm(q), in_hbm(w_kv), near, far)


def expert_kernel(x_hbm, g_ref, u_ref, d_hbm, out_hbm, d_ref, x_ref, hid_ref, gate_ref, up_ref, y_ref, sem_d, sem_in, sem_out):
    units, pair, width = x_ref.shape
    m = units * pair
    first, last = sem_in.shape[0], sem_out.shape[0]
    depth, wide = width // first, width // last
    arrivals = []
    for k in range(first):
        part = slice(k * depth, (k + 1) * depth)
        arrivals.append(pltpu.make_async_copy(x_hbm.at[:, :, part], x_ref.at[:, :, part], sem_in.at[k]))
        arrivals[-1].start()
    d_copy = pltpu.make_async_copy(d_hbm, d_ref, sem_d.at[0])
    d_copy.start()
    for k in range(first):
        part = slice(k * depth, (k + 1) * depth)
        arrivals[k].wait()
        rows = x_ref[:, :, part].reshape(m, depth)
        gate = jnp.dot(rows, g_ref[part], preferred_element_type=F32)
        upward = jnp.dot(rows, u_ref[part], preferred_element_type=F32)
        gate_ref[...] = gate if k == 0 else gate_ref[...] + gate
        up_ref[...] = upward if k == 0 else up_ref[...] + upward
    gate = gate_ref[...]
    hid_ref[...] = (gate / (1.0 + jnp.exp(-gate)) * up_ref[...]).astype(BF)
    d_copy.wait()
    departures = []
    for n in range(last):
        part = slice(n * wide, (n + 1) * wide)
        y = jnp.dot(hid_ref[...], d_ref[:, part], preferred_element_type=F32).astype(BF)
        y_ref[:, :, part] = y.reshape(units, pair, wide)
        departures.append(pltpu.make_async_copy(y_ref.at[:, :, part], out_hbm.at[:, :, part], sem_out.at[n]))
        departures[-1].start()
    for copy in departures:
        copy.wait()


def expert(x, w_gate, w_up, w_down, first, last):
    units, pair, width = x.shape
    m = units * pair
    hidden = w_gate.shape[1]
    whole = pl.BlockSpec(memory_space=pltpu.VMEM)
    far = pl.BlockSpec(memory_space=pltpu.HBM)
    return pl.pallas_call(
        expert_kernel,
        in_specs=[far, whole, whole, far],
        out_specs=far,
        out_shape=pltpu.HBM(x.shape, BF),
        scratch_shapes=[
            pltpu.VMEM(w_down.shape, BF),
            pltpu.VMEM(x.shape, BF),
            pltpu.VMEM((m, hidden), BF),
            pltpu.VMEM((m, hidden), F32),
            pltpu.VMEM((m, hidden), F32),
            pltpu.VMEM(x.shape, BF),
            pltpu.SemaphoreType.DMA((1,)),
            pltpu.SemaphoreType.DMA((first,)),
            pltpu.SemaphoreType.DMA((last,)),
        ],
        compiler_params=pltpu.CompilerParams(vmem_limit_bytes=24 * 2**20),
        cost_estimate=pl.CostEstimate(
            flops=6 * m * width * hidden, bytes_accessed=17_000_000, transcendentals=m * hidden
        ),
    )(x, w_gate, w_up, in_hbm(w_down))


def dispatch_kernel(place_ref, x_ref, out_ref):
    y = jnp.dot(place_ref[...], x_ref[...], preferred_element_type=F32).astype(BF)
    out_ref[...] = y.reshape(out_ref.shape)


def dispatch(place, x, cuts):
    m = place.shape[0]
    tokens, width = x.shape
    n = width // cuts
    return pl.pallas_call(
        dispatch_kernel,
        grid=(cuts,),
        in_specs=[pl.BlockSpec(place.shape, lambda i: (0, 0)), pl.BlockSpec((tokens, n), lambda i: (0, i))],
        out_specs=pl.BlockSpec((m // 2, 2, n), lambda i: (0, 0, i)),
        out_shape=jax.ShapeDtypeStruct((m // 2, 2, width), BF),
        compiler_params=pltpu.CompilerParams(vmem_limit_bytes=32 * 2**20),
        cost_estimate=pl.CostEstimate(
            flops=2 * m * tokens * width, bytes_accessed=2 * m * width + 2 * tokens * width, transcendentals=0
        ),
    )(place, x)


def combine_kernel(*refs):
    *in_refs, own_ref, far_ref = refs
    tok = own_ref.shape[0]
    y = None
    for factors_ref, x_ref in zip(in_refs[::2], in_refs[1::2]):
        rows = x_ref[...].reshape(factors_ref.shape[1], x_ref.shape[2])
        part = jnp.dot(factors_ref[...], rows, preferred_element_type=F32)
        y = part if y is None else y + part
    y = y[: 2 * tok] + y[2 * tok :]
    own_ref[...] = y[:tok]
    far_ref[...] = y[tok:]


def combine(parts, cuts):
    width = parts[0][1].shape[2]
    n = width // cuts
    tok = parts[0][0].shape[0] // 4
    half = pl.BlockSpec((tok, n), lambda i: (0, i))
    in_specs = []
    for factors, x in parts:
        in_specs.append(pl.BlockSpec(factors.shape, lambda i: (0, 0)))
        in_specs.append(pl.BlockSpec((x.shape[0], 2, n), lambda i: (0, 0, i)))
    rows = sum(2 * x.shape[0] for _, x in parts)
    return pl.pallas_call(
        combine_kernel,
        grid=(cuts,),
        in_specs=in_specs,
        out_specs=(half, half),
        out_shape=(jax.ShapeDtypeStruct((tok, width), F32),) * 2,
        compiler_params=pltpu.CompilerParams(vmem_limit_bytes=32 * 2**20),
        cost_estimate=pl.CostEstimate(
            flops=8 * tok * rows * width, bytes_accessed=2 * rows * width, transcendentals=0
        ),
    )(*[a for part in parts for a in part])


def project_kernel(ids_ref, own_ref, before_ref, after_ref, left_ref, right_ref, near_ref, far_ref, out_ref, x_ref, w_ref):
    rows = own_ref.shape[0]
    group, tok = 4, out_ref.shape[1]
    parts = out_ref.shape[0] // group
    core, x = ids_ref[1], ids_ref[2]
    half = left_ref.shape[1]
    x_ref[:rows] = own_ref[...]
    x_ref[rows : 2 * rows] = after_ref[...]
    x_ref[2 * rows : 3 * rows, :half] = left_ref[...]
    x_ref[2 * rows : 3 * rows, half:] = right_ref[...]
    x_ref[3 * rows :] = before_ref[...]
    deep = VD // 2
    for side, ref in enumerate((near_ref, far_ref)):
        offset = (core if side == 0 else 1 - core) * deep
        for j in range(ref.shape[0]):
            w_ref[pl.ds(pl.multiple_of(chip_number(j) * VD + offset, deep), deep)] = ref[j]
    for d in range(group):
        y = jnp.dot(x_ref[d * rows : (d + 1) * rows], w_ref[...], preferred_element_type=F32).astype(BF)
        target = lax.rem(x + d, group)
        for e in range(parts):
            out_ref[e * group + target] = y[e * tok : (e + 1) * tok]


def project(ids, pieces, near, far, parts, width):
    rows, depth = pieces[0].shape
    whole = pl.BlockSpec(memory_space=pltpu.VMEM)
    group = 4
    return pl.pallas_call(
        project_kernel,
        in_specs=[pl.BlockSpec(memory_space=pltpu.SMEM)] + [whole] * (len(pieces) + 2),
        out_specs=whole,
        out_shape=jax.ShapeDtypeStruct((parts * group, rows // parts, width), BF),
        scratch_shapes=[pltpu.VMEM((group * rows, depth), BF), pltpu.VMEM((depth, width), BF)],
        compiler_params=pltpu.CompilerParams(vmem_limit_bytes=32 * 2**20),
        cost_estimate=pl.CostEstimate(
            flops=2 * group * rows * depth * width, bytes_accessed=2 * depth * width, transcendentals=0
        ),
    )(ids, *pieces, near, far)


def blocks_kernel(w_ref, out_ref, sems):
    wide = out_ref.shape[2]
    group = w_ref.shape[1] // wide
    copies = []
    for i in range(out_ref.shape[0]):
        first = i // (out_ref.shape[0] // group) * wide
        copies.append(pltpu.make_async_copy(w_ref.at[:, first : first + wide], out_ref.at[i], sems.at[i]))
        copies[-1].start()
    for copy in copies:
        copy.wait()


def column_blocks(w, group, count):
    shape = (count, w.shape[0], w.shape[1] // group)
    return pl.pallas_call(
        blocks_kernel,
        in_specs=[pl.BlockSpec(memory_space=pltpu.VMEM)],
        out_specs=pl.BlockSpec(memory_space=pltpu.HBM),
        out_shape=pltpu.HBM(shape, w.dtype),
        scratch_shapes=[pltpu.SemaphoreType.DMA((count,))],
        cost_estimate=pl.CostEstimate(flops=0, bytes_accessed=6 * w.size, transcendentals=0),
    )(w)


def swap(mine):
    return lax.ppermute(mine, "core", SWAP)


def up(a):
    return lax.ppermute(a, "x", [(i, (i + 1) % 4) for i in range(4)])


def down(a):
    return lax.ppermute(a, "x", [(i, (i + 3) % 4) for i in range(4)])


def routing(routes, codes):
    tok = routes.shape[0]
    core = lax.axis_index("core")
    code_float = codes.astype(F32)
    mix = code_float / jnp.sum(code_float, axis=1, keepdims=True)
    routes2, mix2 = jnp.stack([routes, swap(routes)]), jnp.stack([mix, swap(mix)])
    chosen = routes2[:, :, :, None] == jnp.arange(64, dtype=jnp.int32)
    weight = jnp.sum(jnp.where(chosen, mix2[..., None], F32(0.0)), axis=2)
    has = jnp.any(chosen, axis=2)

    def of_core(a):
        a = a.reshape(2, tok, 8, 2, 4)
        a = jnp.where(core == 0, a[:, :, :, 0], a[:, :, :, 1])
        return a.reshape(2, tok, 8, 2, 2).transpose(0, 1, 3, 2, 4).reshape(2, tok, 32)

    weight, has = of_core(weight), of_core(has)
    count = has.astype(jnp.int32)
    slot = jnp.cumsum(count, axis=1) - count
    place = has[:, :, :, None] & (slot[:, :, :, None] == jnp.arange(CAP, dtype=jnp.int32))
    place = place.transpose(2, 3, 0, 1)[:, :, :, None, :]
    same = jnp.arange(2)[:, None, None] == jnp.arange(2)[None, :, None]
    place = (place & same).reshape(32, CAP, 2, 2 * tok)
    place = jnp.broadcast_to(place[:, None], (32, 2, CAP, 2, 2 * tok)).reshape(64, CAP, 2, 2 * tok)
    gains = weight.transpose(2, 0, 1).reshape(32, 2 * tok)
    gains = jnp.broadcast_to(gains[:, None], (32, 2, 2 * tok)).reshape(64, 1, 1, 2 * tok)
    factors = jnp.where(place, gains, F32(0.0))
    high = lax.reduce_precision(factors, 8, 7)
    factors = jnp.concatenate([high, factors - high], axis=3).astype(BF)
    place = place.astype(BF)
    parts = []
    for slots in SLOTS:
        parts.append((place[:, slots].reshape(-1, 2 * tok), factors[:, slots].reshape(-1, 4 * tok).T))
    return parts


def local(queries, latents, w_kv, w_out, resid, norm_gain, routes, codes, w_gate, w_up, w_down):
    tok, width = resid.shape
    chips = 64
    core = lax.axis_index("core")
    group = 4
    columns = width // group
    near = lax.all_to_all(
        jnp.broadcast_to(latents[None], (8,) + latents.shape), CTX_CHIPS, split_axis=0, concat_axis=0, tiled=True
    )
    far = swap(near)
    w_blocks, _ = lax.optimization_barrier((column_blocks(w_out, group, 8), near[0, :8]))
    w_near = lax.all_to_all(w_blocks, CTX_CHIPS, split_axis=0, concat_axis=0, tiled=True)
    ids = jnp.stack([lax.axis_index(CTX), core, lax.axis_index("x")]).astype(jnp.int32)
    parts = routing(routes, codes)
    ids, parts = lax.optimization_barrier((ids, parts))
    own = attend(ids, queries, w_kv, near, far, 4)
    before, after, w_near = lax.optimization_barrier((up(own), down(own), w_near))
    w_far = swap(w_near)
    half = own.shape[1] // 2
    left, right = up(before[:, :half]), down(after[:, half:])
    attn = project(ids, (own, before, after, left, right), w_near, w_far, 8, columns)
    attn = lax.all_to_all(attn, EP + ("x",), split_axis=0, concat_axis=0, tiled=True)
    attn = jnp.sum(attn.reshape(8, group, tok, columns).astype(F32), axis=0)
    attn = attn.transpose(1, 0, 2).reshape(tok, width)
    attended = (resid.astype(F32) + attn).astype(BF)
    wide = attended.astype(F32)
    meansq = jnp.mean(wide * wide, axis=1, keepdims=True)
    normed = (wide * lax.rsqrt(meansq + 1e-06) * norm_gain[None, :]).astype(BF)
    normed2 = jnp.concatenate([normed, swap(normed)], axis=0)

    def exchange(rows):
        units = rows.reshape(chips, -1, 2, width)
        units = lax.all_to_all(units, CHIPS, split_axis=0, concat_axis=0, tiled=True)
        return units.reshape(rows.shape)

    arrived = [exchange(dispatch(place, normed2, 2)) for place, _ in parts]
    returned = [exchange(expert(rows, w_gate[0], w_up[0], w_down[0], 2, 7)) for rows in arrived]
    mine, theirs = combine([(factors, rows) for (_, factors), rows in zip(parts, returned)], 4)
    layer_out = (wide + mine + swap(theirs)).astype(BF)
    return (attended, layer_out)


def solution(mesh):
    fine = Mesh(mesh.devices.reshape(SIZES), NAMES)
    rows = P(CTX + EP, None)
    heads = P(CTX + EP, None, None)
    placed = (
        P(CTX, EP),
        P(None, CTX),
        P(None, EP),
        P(EP + CTX, None),
        rows,
        P(),
        rows,
        rows,
        heads,
        heads,
        heads,
    )
    return jax.shard_map(local, mesh=fine, in_specs=placed, out_specs=(rows, rows), check_vma=False)
```
